128 devices in a mesh: ctx: 16 (over y, x), tp: 8 (over z, core).
Axes of the slice: x: 4, y: 4, z: 4, core: 2. Of those that a mesh axis runs over, the one named last changes fastest.
Arguments:
- hidden_in: bfloat16 [8192, 2048], P('ctx'), may hold values from -6 to 6
- norm_gains: float32 [2, 2048], replicated, may hold values from 0.5 to 1.5
- w_in: bfloat16 [2048, 8, 896], P(None, 'tp'), may hold values from -0.125 to 0.125
- w_shared: bfloat16 [2048, 1024], replicated, may hold values from -0.125 to 0.125
- w_dt: bfloat16 [2048, 48], P(None, 'tp'), may hold values from -0.125 to 0.125
- head_params: float32 [3, 48], P(None, 'tp'), as said below
- w_out: bfloat16 [8, 512, 2048], P('tp'), may hold values from -0.25 to 0.25
- w_gu: bfloat16 [2048, 2, 4096], P(None, None, 'tp'), may hold values from -0.125 to 0.125
- w_down: bfloat16 [4096, 2048], P('tp'), may hold values from -0.09375 to 0.09375
- a_in: bfloat16 [2048, 128], replicated, may hold values from -0.125 to 0.125
- b_in: bfloat16 [128, 8, 896], P(None, 'tp'), may hold values from -0.75 to 0.75
- a_sh: bfloat16 [2048, 128], replicated, may hold values from -0.125 to 0.125
- b_sh: bfloat16 [128, 1024], replicated, may hold values from -0.75 to 0.75
- a_out: bfloat16 [8, 512, 128], P('tp'), may hold values from -0.125 to 0.125
- b_out: bfloat16 [128, 2048], replicated, may hold values from -0.75 to 0.75
- a_gu: bfloat16 [2048, 128], replicated, may hold values from -0.125 to 0.125
- b_gu: bfloat16 [128, 2, 4096], P(None, None, 'tp'), may hold values from -0.75 to 0.75
- a_dn: bfloat16 [4096, 128], P('tp'), may hold values from -0.09375 to 0.09375
- b_dn: bfloat16 [128, 2048], replicated, may hold values from -0.75 to 0.75
- adapter_ids: int32 [4], replicated, may hold values from 0 to 7
- doc_lengths: int32 [4], replicated, may hold values from 1 to 7936, 8192 in all
- out_grad: bfloat16 [8192, 2048], P('ctx'), may hold values from -6 to 6
Outputs:
- mixed: float32 [8192, 2048], P('ctx')
- input_grad: float32 [8192, 2048], P('ctx')
- grad_norm_gains: float32 [2, 2048], P(None, 'ctx')
- grad_w_in: float32 [2048, 8, 896], P('ctx', 'tp')
- grad_w_shared: float32 [2048, 1024], P('ctx')
- grad_w_dt: float32 [2048, 48], P('ctx', 'tp')
- grad_head_params: float32 [3, 48], P(None, 'tp')
- grad_w_out: float32 [8, 512, 2048], P('tp', None, 'ctx')
- grad_w_gu: float32 [2048, 2, 4096], P('ctx', None, 'tp')
- grad_w_down: float32 [4096, 2048], P('tp', 'ctx')
- grad_a_in: float32 [2048, 128], P(('ctx', 'tp'))
- grad_b_in: float32 [128, 8, 896], P('ctx', 'tp')
- grad_a_sh: float32 [2048, 128], P('ctx')
- grad_b_sh: float32 [128, 1024], P('ctx')
- grad_a_out: float32 [8, 512, 128], P('tp', 'ctx')
- grad_b_out: float32 [128, 2048], P(None, ('ctx', 'tp'))
- grad_a_gu: float32 [2048, 128], P(('ctx', 'tp'))
- grad_b_gu: float32 [128, 2, 4096], P('ctx', None, 'tp')
- grad_a_dn: float32 [4096, 128], P('tp', 'ctx')
- grad_b_dn: float32 [128, 2048], P(None, ('ctx', 'tp'))
The draws below stay inside these ranges and needn't reach their ends.
Inputs may be any that keep to these rules, and one draw needn't show every extreme that they name: `doc_lengths`: the lengths sum to 8192; one sequence is 7936 tokens long. `head_params`: row 0: step biases, row 1: logarithms of decay scales, row 2: skip factors.
All inputs are finite; a program needn't handle non-finite values.
Results may differ from the reference program's by a relative error of at most 0.03.
Values may be sent and summed in bfloat16 or wider, within the bound.
A program may use at most 192 MiB of HBM per device.

```python
import math
import jax
import jax.numpy as jnp
import numpy as np
from jax import lax

D = 2048
MHEADS = 48
MHEAD = 64
STATE = 256
QHEADS = 8
KVH = 2
HD = 128
FF = 4096
RANK = 16
NADAPT = 8
SEQS = 4
TOK_DEV = 512
TOKENS = 8192
AR = 128
SH = 1024
CI_DEV = 896
CO_DEV = 512
N_TP = 8


def draw_head_params(key, part):
    key = jax.random.fold_in(key, 7)
    key_scale, key_rate, key_skip = jax.random.split(key, 3)
    log_scale = jax.random.uniform(key_scale, (MHEADS,), jnp.float32, -1.0, 1.0)
    fastest = math.log(1.0 / 30.0)
    log_rate = jax.random.uniform(key_rate, (MHEADS,), jnp.float32, math.log(0.25 / TOKENS), fastest)
    step_bias = log_rate - log_scale - 0.5
    skip_factor = jax.random.uniform(key_skip, (MHEADS,), jnp.float32, 0.5, 1.5)
    return jnp.stack([step_bias, log_scale, skip_factor])


def place_ends(values, key, least, top_value):
    dims = values.shape
    place = [jax.random.randint(jax.random.fold_in(key, axis), (), 0, dims[axis]) for axis in range(len(dims))]
    values = values.at[tuple(place)].set(least)
    longest = dims.index(max(dims))
    place[longest] = (place[longest] + 1) % dims[longest]
    return values.at[tuple(place)].set(top_value)


def levels(rng, extent, cuts, low, largest):
    factor_of = 1.0
    for dim, parts in cuts:
        heights = jax.random.uniform(jax.random.fold_in(jax.random.fold_in(rng, 6), dim), (parts,), jnp.float32, low / len(cuts), largest / len(cuts))
        factor_of = factor_of * jnp.repeat(jnp.exp(heights), extent[dim] // parts).reshape((-1,) + (1,) * (len(extent) - 1 - dim))
    return factor_of


def profile(amount, total, bound, skew):
    weights = [(1 << 20) // math.isqrt(standing ** skew) + 1 for standing in range(2, amount + 1)]
    surplus, holding = total - bound - (amount - 1), [1] * (amount - 1)
    while surplus > 0:
        free = [i for i in range(amount - 1) if holding[i] < bound]
        pool, budget = sum([weights[i] for i in free]), surplus
        for i in free:
            extra = min(bound - holding[i], max(1, budget * weights[i] // pool), surplus)
            holding[i] = holding[i] + extra
            surplus = surplus - extra
    return np.array([bound] + holding)


def ragged(key, count, total, bound, slope):
    if count == 2:
        one = jax.random.randint(key, (), max(1, total - bound), min(bound, total - 1) + 1)
        return jnp.stack([one, total - one])
    lengths = jnp.asarray(profile(count, total, bound, slope), jnp.int32)
    twos = (count - 1) // 2
    giver, taker = lengths[1:1 + 2 * twos:2], lengths[2:2 + 2 * twos:2]
    room = jnp.minimum(giver - 1, bound - taker)
    moved = jax.random.randint(jax.random.fold_in(key, 1), (twos,), 0, 1 << 20) % (room + 1)
    lengths = lengths.at[1:1 + 2 * twos:2].set(giver - moved).at[2:2 + 2 * twos:2].set(taker + moved)
    return lengths[jax.random.permutation(jax.random.fold_in(key, 2), count)]


def scatter_about(rng, dims, deviation, reach, shards=(), kind=jnp.bfloat16):
    values = jax.random.normal(rng, dims, jnp.float32) * deviation
    if len(shards) > 0:
        values = levels(rng, dims, shards, -0.22, 0.18) * values
    return jnp.clip(values, min=-reach, max=reach).astype(kind)


def setup_inputs(seed: int = 0) -> dict:
    keys = jax.random.split(jax.random.key(seed), 23)
    return {
        "hidden_in": scatter_about(keys[0], (TOKENS, D), 1.0, 6.0, ((0, 16),)),
        "norm_gains": jnp.clip(1.0 + 0.1 * jax.random.normal(keys[1], (2, D), jnp.float32), 0.5, 1.5),
        "w_in": scatter_about(keys[2], (D, N_TP, CI_DEV), D ** -0.5, 0.125, ((1, 8),)),
        "w_shared": scatter_about(keys[3], (D, SH), D ** -0.5, 0.125),
        "w_dt": scatter_about(keys[4], (D, MHEADS), D ** -0.5, 0.125, ((1, 8),)),
        "head_params": draw_head_params(jax.random.fold_in(keys[22], 71), 0),
        "w_out": scatter_about(keys[6], (N_TP, CO_DEV, D), (D // 4) ** -0.5, 0.25, ((0, 8),)),
        "w_gu": scatter_about(keys[7], (D, 2, FF), D ** -0.5, 0.125, ((2, 8),)),
        "w_down": scatter_about(keys[8], (FF, D), FF ** -0.5, 0.09375, ((0, 8),)),
        "a_in": scatter_about(keys[9], (D, AR), D ** -0.5, 0.125),
        "b_in": scatter_about(keys[10], (AR, N_TP, CI_DEV), (4 * RANK) ** -0.5, 0.75, ((1, 8),)),
        "a_sh": scatter_about(keys[11], (D, AR), D ** -0.5, 0.125),
        "b_sh": scatter_about(keys[12], (AR, SH), (4 * RANK) ** -0.5, 0.75),
        "a_out": scatter_about(keys[13], (N_TP, CO_DEV, AR), D ** -0.5, 0.125, ((0, 8),)),
        "b_out": scatter_about(keys[14], (AR, D), (4 * RANK) ** -0.5, 0.75),
        "a_gu": scatter_about(keys[15], (D, AR), D ** -0.5, 0.125),
        "b_gu": scatter_about(keys[16], (AR, 2, FF), (4 * RANK) ** -0.5, 0.75, ((2, 8),)),
        "a_dn": scatter_about(keys[17], (FF, AR), FF ** -0.5, 0.09375, ((0, 8),)),
        "b_dn": scatter_about(keys[18], (AR, D), (4 * RANK) ** -0.5, 0.75),
        "adapter_ids": place_ends(jax.random.randint(keys[19], (SEQS,), 0, NADAPT), jax.random.fold_in(keys[19], 1), 0, NADAPT - 1).astype(jnp.int32),
        "doc_lengths": ragged(keys[20], SEQS, TOKENS, TOKENS - TOK_DEV // 2, 0).astype(jnp.int32),
        "out_grad": scatter_about(keys[21], (TOKENS, D), 1.0, 6.0, ((0, 16),)),
    }


NORM_EPSILON = 1e-06

@jax.custom_vjp
def low(v):
    return lax.optimization_barrier(v.astype(jnp.bfloat16)).astype(jnp.float32)

@jax.custom_vjp
def low_back(v):
    return v

def low_keep(v):
    return (low(v), None)

def low_pass(kept, grad):
    return (grad,)

def back_keep(v):
    return (v, None)

def back_low(kept, grad):
    return (low(grad),)
low.defvjp(low_keep, low_pass)
low_back.defvjp(back_keep, back_low)

def exact_dot(left_side, right_side):
    return jnp.dot(left_side, right_side, precision=lax.Precision.HIGHEST)

def norm_apply(values, gain_row):
    return values * lax.rsqrt(lax.optimization_barrier(jnp.mean(values * values, axis=-1, keepdims=True)) + NORM_EPSILON) * gain_row

def soft_plus(values):
    return jnp.maximum(values, 0.0) + jnp.log1p(jnp.exp(-jnp.abs(values)))

def doc_index(positions, doc_lengths):
    bounds = jnp.cumsum(doc_lengths)
    return lax.optimization_barrier(jnp.sum((positions[:, None] >= bounds[None, :]).astype(jnp.int32), axis=1))

def adapter_mask(doc_ids, adapter_ids, columns):
    seq_count = adapter_ids.shape[0]
    chosen = lax.optimization_barrier(jnp.sum(jnp.where(doc_ids[:, None] == jnp.arange(seq_count)[None, :], adapter_ids[None, :], 0), axis=1))
    return (chosen[:, None] == jnp.arange(columns)[None, :] // RANK).astype(jnp.float32)

def decay_terms(dt_raw, head_params):
    step_size = soft_plus(dt_raw + head_params[0])
    return (step_size, jnp.cumsum(-step_size * jnp.exp(head_params[1]), axis=0))

def ssd_inner(values, b_matrix, c_matrix, dt_raw, head_params, doc_ids, doc_before):
    step_size, decay_sum = decay_terms(dt_raw, head_params)
    row_order = jnp.arange(values.shape[0])
    allowed = (row_order[:, None] >= row_order[None, :]) & (doc_ids[:, None] == doc_ids[None, :])
    decay_gap = jnp.where(allowed[:, :, None], decay_sum[:, None, :] - decay_sum[None, :, :], 0.0)
    weights = jnp.where(allowed[:, :, None], jnp.exp(decay_gap), 0.0) * step_size[None, :, :]
    intersection = jnp.dot(c_matrix, b_matrix.T, precision=lax.Precision.HIGHEST)
    mixing = intersection[:, :, None] * weights
    output = jnp.einsum('tsh,shp->thp', mixing, values, precision=lax.Precision.HIGHEST)
    output = output + head_params[2][None, :, None] * values
    tail_weight = jnp.where((doc_ids == doc_ids[-1])[:, None], jnp.exp(decay_sum[-1][None, :] - decay_sum), 0.0) * step_size
    state_out = jnp.einsum('sn,shp->hnp', b_matrix, tail_weight[:, :, None] * values, precision=lax.Precision.HIGHEST)
    carried = (doc_ids[-1] == doc_before).astype(values.dtype)
    return (output, state_out, jnp.exp(decay_sum[-1]) * carried)

def ssd_cross(c_matrix, dt_raw, head_params, entering, doc_ids, doc_before):
    step_size, decay_sum = decay_terms(dt_raw, head_params)
    carried = (doc_ids == doc_before).astype(c_matrix.dtype)
    reach_weight = jnp.exp(decay_sum) * carried[:, None]
    return jnp.einsum('tn,hnp->thp', c_matrix, entering, precision=lax.Precision.HIGHEST) * reach_weight[:, :, None]

def mamba_mixer(values, b_matrix, c_matrix, dt_raw, head_params, doc_ids, doc_lengths):
    block_count = TOKENS // TOK_DEV
    starts = jnp.arange(block_count, dtype=jnp.int32) * TOK_DEV
    before_ids = doc_index(jnp.maximum(starts - 1, 0), doc_lengths)

    def one_block(entering, pieces):
        block_values, block_b, block_c, block_dt, block_docs, block_before = pieces
        output, state_out, decay_total = ssd_inner(block_values, block_b, block_c, block_dt, head_params, block_docs, block_before)
        output = output + ssd_cross(block_c, block_dt, head_params, entering, block_docs, block_before)
        return (decay_total[:, None, None] * entering + state_out, output)

    def by_block(array_in):
        return array_in.reshape((block_count, TOK_DEV) + array_in.shape[1:])
    initial = jnp.zeros((MHEADS, STATE, MHEAD), jnp.float32)
    _, outputs = lax.scan(jax.checkpoint(one_block), initial, (by_block(values), by_block(b_matrix), by_block(c_matrix), by_block(dt_raw), by_block(doc_ids), before_ids))
    return outputs.reshape(values.shape)

def attention(queries, keys_all, values_all, doc_ids):
    query_block = min(TOKENS, 512)
    block_count = TOKENS // query_block
    positions = jnp.arange(TOKENS, dtype=jnp.int32)
    expand = QHEADS // KVH
    wide_keys = jnp.repeat(keys_all, expand, axis=1)
    wide_values = jnp.repeat(values_all, expand, axis=1)
    scale_factor = HD ** (-0.5)

    def one_block(pieces):
        block_q, block_pos, block_docs = pieces
        scores = jnp.einsum('rhd,nhd->hrn', block_q, wide_keys, precision=lax.Precision.HIGHEST) * scale_factor
        scores = low_back(scores)
        allowed = (block_pos[:, None] >= positions[None, :]) & (block_docs[:, None] == doc_ids[None, :])
        scores = jnp.where(allowed[None], scores, -1e+30)
        top_score = lax.optimization_barrier(jnp.max(scores, axis=-1, keepdims=True))
        expos = jnp.exp(scores - top_score)
        probs = expos / lax.optimization_barrier(jnp.sum(expos, axis=-1, keepdims=True))
        return jnp.einsum('hrn,nhd->rhd', low(probs), wide_values, precision=lax.Precision.HIGHEST)
    outputs = lax.map(jax.checkpoint(one_block), (queries.reshape(block_count, query_block, QHEADS, HD), positions.reshape(block_count, query_block), doc_ids.reshape(block_count, query_block)))
    return outputs.reshape(TOKENS, QHEADS * HD)

def adapted(inputs, weight, down_map, up_map, adapter_rows):
    return exact_dot(inputs, weight) + exact_dot(exact_dot(inputs, down_map) * adapter_rows, up_map)

def forward(arrays, doc_ids, doc_lengths, adapter_rows):
    source, norm_gains, w_in, w_shared, w_dt, head_params, w_out, w_gu, w_down, a_in, b_in, a_sh, b_sh, a_out, b_out, a_gu, b_gu, a_dn, b_dn = arrays
    inner_dev = MHEADS // N_TP * MHEAD
    normed_one = low(norm_apply(source, norm_gains[0]))
    h_one = low_back(low(adapted(normed_one, w_in.reshape(D, -1), a_in, b_in.reshape(NADAPT * RANK, -1), adapter_rows)))
    h_one = h_one.reshape(TOKENS, N_TP, -1)
    gate_ssm = h_one[:, :, :inner_dev].reshape(TOKENS, MHEADS, MHEAD)
    values = h_one[:, :, inner_dev:2 * inner_dev].reshape(TOKENS, MHEADS, MHEAD)
    queries = h_one[:, :, 2 * inner_dev:].reshape(TOKENS, QHEADS, HD)
    h_two = low_back(low(adapted(normed_one, w_shared, a_sh, b_sh, adapter_rows)))
    b_matrix = h_two[:, :STATE]
    c_matrix = h_two[:, STATE:2 * STATE]
    keys_all = h_two[:, 2 * STATE:2 * STATE + KVH * HD].reshape(TOKENS, KVH, HD)
    values_all = h_two[:, 2 * STATE + KVH * HD:].reshape(TOKENS, KVH, HD)
    dt_raw = exact_dot(normed_one, w_dt)
    ssd_out = mamba_mixer(values, b_matrix, c_matrix, dt_raw, head_params, doc_ids, doc_lengths)
    gated_ssm = ssd_out * (gate_ssm * jax.nn.sigmoid(gate_ssm))
    attended = attention(queries, keys_all, values_all, doc_ids)
    merged = jnp.concatenate([gated_ssm.reshape(TOKENS, N_TP, -1), attended.reshape(TOKENS, N_TP, -1)], axis=2).reshape(TOKENS, -1)
    merged = low_back(low(merged))
    mixer_out = low_back(adapted(merged, w_out.reshape(-1, D), a_out.reshape(-1, NADAPT * RANK), b_out, adapter_rows))
    residual = source + mixer_out
    normed_two = low(norm_apply(residual, norm_gains[1]))
    h_gu = low_back(low(adapted(normed_two, w_gu.reshape(D, -1), a_gu, b_gu.reshape(NADAPT * RANK, -1), adapter_rows)))
    h_gu = h_gu.reshape(TOKENS, 2, FF)
    gate_mlp = h_gu[:, 0]
    act_mlp = low_back(low(gate_mlp * jax.nn.sigmoid(gate_mlp) * h_gu[:, 1]))
    mlp_out = low_back(adapted(act_mlp, w_down, a_dn, b_dn, adapter_rows))
    return residual + mlp_out

def reference(hidden_in, norm_gains, w_in, w_shared, w_dt, head_params, w_out, w_gu, w_down, a_in, b_in, a_sh, b_sh, a_out, b_out, a_gu, b_gu, a_dn, b_dn, adapter_ids, doc_lengths, out_grad):
    positions = jnp.arange(TOKENS, dtype=jnp.int32)
    doc_ids = doc_index(positions, doc_lengths)
    adapter_rows = adapter_mask(doc_ids, adapter_ids, NADAPT * RANK)
    given_arrays = (hidden_in, norm_gains, w_in, w_shared, w_dt, head_params, w_out, w_gu, w_down, a_in, b_in, a_sh, b_sh, a_out, b_out, a_gu, b_gu, a_dn, b_dn)
    floats = tuple((array_in.astype(jnp.float32) for array_in in given_arrays))

    def whole_layer(arrays):
        return forward(arrays, doc_ids, doc_lengths, adapter_rows)
    result, pullback = jax.vjp(whole_layer, floats)
    grads = pullback(out_grad.astype(jnp.float32))[0]
    return (result, grads[0], grads[1], grads[2], grads[3], grads[4], grads[5], grads[6], grads[7], grads[8], grads[9], grads[10], grads[11], grads[12], grads[13], grads[14], grads[15], grads[16], grads[17], grads[18])
```

```python
import functools

import jax
import jax.numpy as jnp
from jax import lax
from jax.experimental import pallas as pl
from jax.experimental.pallas import tpu as pltpu
from jax.sharding import PartitionSpec as P

MHEAD = 64
STATE = 256
QHEADS = 8
KVH = 2
HD = 128
RANK = 16
NORM_EPSILON = 1e-06

MESH = pl.DeviceIdType.MESH
VM = pl.BlockSpec(memory_space=pltpu.VMEM)
SM = pl.BlockSpec(memory_space=pltpu.SMEM)
BF = jnp.bfloat16
F32 = jnp.float32
DMA = pltpu.SemaphoreType.DMA
OFFSETS = (2, 1, 3)


def call(kernel, outs, ins, scratch, cid, name):
    return pl.pallas_call(
        kernel,
        out_shape=[jax.ShapeDtypeStruct(s, d) for s, d in outs],
        in_specs=[VM] * len(ins),
        out_specs=[VM] * len(outs),
        scratch_shapes=scratch,
        compiler_params=pltpu.CompilerParams(
            collective_id=cid, has_side_effects=True, vmem_limit_bytes=56 << 20
        ),
        name=name,
    )(*ins)


def greet(peers):
    barrier = pltpu.get_barrier_semaphore()
    for peer in peers:
        pl.semaphore_signal(barrier, inc=1, device_id=peer, device_id_type=MESH)
    pl.semaphore_wait(barrier, len(peers))


def send(src, dst, sems, slot, peer):
    cp = pltpu.make_async_remote_copy(
        src_ref=src,
        dst_ref=dst,
        send_sem=sems[0].at[slot],
        recv_sem=sems[1].at[slot],
        device_id=peer,
        device_id_type=MESH,
    )
    cp.start()
    return cp


def pair(*shape):
    return [DMA(shape), DMA(shape)]


def tp_place():
    ctx = lax.axis_index("ctx")
    tp = lax.axis_index("tp")
    return ctx, tp, tp // 2, tp % 2


def tp_peers(ctx, tp, z, c):
    return [(ctx, ((z + d) % 4) * 2 + c) for d in (1, 2, 3)] + [(ctx, z * 2 + 1 - c)]


def reduce_bufs(rows, width):
    return [
        pltpu.VMEM((4, rows, width), BF),
        pltpu.VMEM((3, rows, width), BF),
        pltpu.VMEM((3, rows, width), BF),
        *pair(4),
        *pair(3),
    ]


def reduce_start(part, bufs, place):
    sib, snd, rcv, s1s, s1r, s2s, s2r = bufs
    ctx, tp, z, c = place
    mate = (ctx, z * 2 + 1 - c)
    return [
        send(part.at[((z + off) % 4) * 2 + 1 - c], sib.at[k], (s1s, s1r), k, mate)
        for k, off in enumerate(OFFSETS + (0,))
    ]


def reduce_middle(part, bufs, place, first):
    sib, snd, rcv, s1s, s1r, s2s, s2r = bufs
    ctx, tp, z, c = place
    second = []
    for k, off in enumerate(OFFSETS):
        to = ((z + off) % 4) * 2 + c
        first[k].wait_recv()
        snd[k] = (part[to].astype(F32) + sib[k].astype(F32)).astype(BF)
        second.append(send(snd.at[k], rcv.at[k], (s2s, s2r), k, (ctx, to)))
    return second


def reduce_end(part, bufs, place, first, second):
    sib, snd, rcv = bufs[:3]
    first[3].wait_recv()
    total = part[place[1]].astype(F32) + sib[3].astype(F32)
    for k in range(3):
        second[k].wait_recv()
        total = total + rcv[k].astype(F32)
    for cp in first + second:
        cp.wait_send()
    return total


def share_sems():
    return [*pair(3), *pair(4)]


def share_start(out, sems, place):
    ctx, tp, z, c = place
    copies = [
        send(out.at[tp], out.at[tp], sems[:2], k, (ctx, ((z + off) % 4) * 2 + c))
        for k, off in enumerate(OFFSETS)
    ]
    return copies, send(out.at[tp], out.at[tp], sems[2:], 3, (ctx, z * 2 + 1 - c))


def share_end(out, sems, place, started):
    ctx, tp, z, c = place
    copies, own = started
    passed = [own]
    for k, off in sorted(enumerate(OFFSETS), key=lambda t: t[1] == 2):
        copies[k].wait_recv()
        at = ((z + 4 - off) % 4) * 2 + c
        passed.append(send(out.at[at], out.at[at], sems[2:], k, (ctx, z * 2 + 1 - c)))
    for cp in passed:
        cp.wait_recv()
    for cp in copies + passed:
        cp.wait_send()


def norm_scale(v):
    return lax.rsqrt(jnp.mean(v * v, axis=-1, keepdims=True) + NORM_EPSILON)


def norm_back(v, gain, grad):
    r = norm_scale(v)
    pulled = grad * gain
    inner = jnp.mean(pulled * v, axis=-1, keepdims=True)
    grad_v = r * pulled - v * (r * r * r) * inner
    return grad_v, jnp.sum(grad * v * r, axis=0, keepdims=True)


def dot(a, b):
    return jnp.dot(a, b, preferred_element_type=F32)


def dot_nt(a, b):
    return lax.dot_general(a, b, (((1,), (1,)), ((), ())), preferred_element_type=F32)


def dot_tn(a, b):
    return lax.dot_general(a, b, (((0,), (0,)), ((), ())), preferred_element_type=F32)


def mixer_kernel(part, source, gain, b_out, out, resid, *scratch):
    width = source.shape[1]
    place = tp_place()
    greet(tp_peers(*place))
    bufs, sems = scratch[:7], scratch[7:]
    first = reduce_start(part, bufs, place)
    total = reduce_end(part, bufs, place, first, reduce_middle(part, bufs, place, first))
    low = total[:, width:].astype(BF)
    residual = source[...].astype(F32) + total[:, :width] + dot(low, b_out[...])
    resid[...] = residual
    normed = residual * norm_scale(residual) * gain[...]
    out[place[1], :, :width] = normed.astype(BF)
    out[place[1], :, width:] = low
    share_end(out, sems, place, share_start(out, sems, place))


def mixer_exchange(part, source, gain, b_out):
    _, rows, wide = part.shape
    return call(
        mixer_kernel,
        [(part.shape, BF), (source.shape, F32)],
        [part, source, gain, b_out],
        reduce_bufs(rows, wide) + share_sems(),
        1,
        "mixer_exchange",
    )


def mlp_kernel(part, resid, gain, out_grad, b_dn, a_gu, mask, out, grad_resid, gain_part, *scratch):
    width = resid.shape[1]
    rank = a_gu.shape[1]
    wide = width + rank
    place = tp_place()
    tp = place[1]
    greet(tp_peers(*place))
    bufs, sems = scratch[:7], scratch[7:]
    first = reduce_start(part, bufs, place)
    total = reduce_end(part, bufs, place, first, reduce_middle(part, bufs, place, first))
    low_gu = (total[:, width:wide] * mask[...]).astype(BF)
    low_dn = total[:, wide + width :].astype(BF)
    residual = resid[...]
    grad = total[:, :width] + dot_nt(low_gu, a_gu[...])
    grad_v, grad_gain = norm_back(residual, gain[...], grad)
    grad_r = out_grad[...].astype(F32) + grad_v
    grad_resid[...] = grad_r
    gain_part[...] = grad_gain
    mixed = residual + total[:, wide : wide + width] + dot(low_dn, b_dn[...])
    out[tp, :, :width] = grad_r.astype(BF)
    out[tp, :, width:wide] = low_gu
    out[tp, :, wide : wide + width] = mixed.astype(BF)
    out[tp, :, wide + width :] = low_dn
    share_end(out, sems, place, share_start(out, sems, place))


def mlp_exchange(part, resid, gain, out_grad, b_dn, a_gu, mask):
    _, rows, wide = part.shape
    return call(
        mlp_kernel,
        [(part.shape, BF), (resid.shape, F32), (gain.shape, F32)],
        [part, resid, gain, out_grad, b_dn, a_gu, mask],
        reduce_bufs(rows, wide) + share_sems(),
        2,
        "mlp_exchange",
    )


def input_kernel(
    part, part_two, source, gain, grad_resid, a_in, a_sh, mask, gain_two, out, gains, two, *scratch
):
    width = source.shape[1]
    rank = a_in.shape[1]
    place = tp_place()
    tp = place[1]
    greet(tp_peers(*place))
    bufs, more, sems, sems_g = scratch[:7], scratch[7:14], scratch[14:18], scratch[18:]
    first = reduce_start(part, bufs, place)
    first_two = reduce_start(part_two, more, place)
    second = reduce_middle(part, bufs, place, first)
    second_two = reduce_middle(part_two, more, place, first_two)
    total = reduce_end(part, bufs, place, first, second)
    low_in = (total[:, width : width + rank] * mask[...]).astype(BF)
    low_sh = (total[:, width + rank :] * mask[...]).astype(BF)
    grad = total[:, :width] + dot_nt(low_in, a_in[...]) + dot_nt(low_sh, a_sh[...])
    grad_v, grad_gain = norm_back(source[...].astype(F32), gain[...], grad)
    out[tp, :, :width] = (grad_resid[...] + grad_v).astype(BF)
    out[tp, :, width : width + rank] = low_in
    out[tp, :, width + rank :] = low_sh
    gains[tp, 0:1] = grad_gain
    gains[tp, 1:2] = gain_two[...]
    gains[tp, 2:8] = jnp.zeros((6, width), F32)
    started = share_start(out, sems, place)
    started_g = share_start(gains, sems_g, place)
    two[...] = reduce_end(part_two, more, place, first_two, second_two).astype(BF)
    share_end(out, sems, place, started)
    share_end(gains, sems_g, place, started_g)


def input_exchange(part, part_two, source, gain, grad_resid, a_in, a_sh, mask, gain_two):
    _, rows, wide = part.shape
    _, tall, cols = part_two.shape
    return call(
        input_kernel,
        [(part.shape, BF), ((8, 8, source.shape[1]), F32), ((tall, cols), BF)],
        [part, part_two, source, gain, grad_resid, a_in, a_sh, mask, gain_two],
        reduce_bufs(rows, wide) + reduce_bufs(tall, cols) + share_sems() + share_sems(),
        3,
        "input_exchange",
    )


def ctx_place():
    ctx = lax.axis_index("ctx")
    return ctx, lax.axis_index("tp"), ctx // 4, ctx % 4


def spot(h, fast, slow):
    return slow * 4 + fast if h == 0 else fast * 4 + slow


def scatter_bufs(rows, width):
    most = max(rows - rows // 32 * 16, rows // 32 * 16)
    return [
        pltpu.VMEM((2, 3, most, width), BF),
        pltpu.VMEM((2, 3, 4, most, width), BF),
        pltpu.VMEM((2, 3, most, width), BF),
        *pair(2, 3, 4),
        *pair(2, 3),
    ]


def spans_of(rows):
    half = rows // 32 * 16
    return ((0, half), (half, rows - half))


def scatter_start(part, bufs, place):
    mid, r1, r2, s1s, s1r, s2s, s2r = bufs
    ctx, tp, y, x = place
    spans = spans_of(part.shape[1])
    first = {}
    for j in OFFSETS + (0,):
        for off in OFFSETS:
            for h in (0, 1):
                fast, slow = ((x, y), (y, x))[h]
                lo, size = spans[h]
                to = (fast + off) % 4
                first[h, off, j] = send(
                    part.at[spot(h, to, (slow + j) % 4), pl.ds(lo, size)],
                    r1.at[h, off - 1, j, pl.ds(0, size)],
                    (s1s, s1r),
                    (h, off - 1, j),
                    (spot(h, to, slow), tp),
                )
    return first


def scatter_middle(part, out, bufs, place, first):
    mid, r1, r2, s1s, s1r, s2s, s2r = bufs
    ctx, tp, y, x = place
    spans = spans_of(part.shape[1])
    second = {}
    for j in OFFSETS + (0,):
        for h in (0, 1):
            fast, slow = ((x, y), (y, x))[h]
            lo, size = spans[h]
            for off in OFFSETS:
                first[h, off, j].wait_recv()
            total = part[spot(h, fast, (slow + j) % 4), pl.ds(lo, size)].astype(F32)
            for off in (1, 2, 3):
                total = total + r1[h, off - 1, j, pl.ds(0, size)].astype(F32)
            if j == 0:
                out[pl.ds(lo, size)] = total
            else:
                mid[h, j - 1, pl.ds(0, size)] = total.astype(BF)
                second[h, j] = send(
                    mid.at[h, j - 1, pl.ds(0, size)],
                    r2.at[h, j - 1, pl.ds(0, size)],
                    (s2s, s2r),
                    (h, j - 1),
                    (spot(h, fast, (slow + j) % 4), tp),
                )
    return second


def scatter_end(part, out, bufs, first, second):
    r2 = bufs[2]
    for h, (lo, size) in enumerate(spans_of(part.shape[1])):
        for j in OFFSETS:
            second[h, j].wait_recv()
        total = out[pl.ds(lo, size)]
        for j in (1, 2, 3):
            total = total + r2[h, j - 1, pl.ds(0, size)].astype(F32)
        out[pl.ds(lo, size)] = total
    for cp in list(first.values()) + list(second.values()):
        cp.wait_send()


def ctx_peers(ctx, tp):
    return [((ctx + d) % 16, tp) for d in range(1, 16)]


def swap_start(src, dst, sems, place):
    ctx, tp = place[:2]
    return [
        send(src.at[(ctx + d) % 16], dst.at[ctx], sems, d - 1, ((ctx + d) % 16, tp))
        for d in range(1, 16)
    ]


def prefix_into(order, got, ent):
    running = jnp.zeros(ent.shape[1:], F32)
    for i in order:
        ent[i] = running
        running = got[i, 0:16] + got[i, 16:17] * running


def front_kernel(msg, kv, entering, kv_all, got, ent, *sems):
    place = ctx_place()
    ctx, tp, y, x = place
    c = tp % 2
    mate = (ctx, tp + 1 - 2 * c)
    greet(ctx_peers(ctx, tp) + [mate])
    s_one, s_two, s_kv1, s_kv2, s_m1, s_m2 = [sems[2 * k : 2 * k + 2] for k in range(6)]
    one = swap_start(msg, got, s_one, place)
    half = kv.shape[0] // 2
    part = half // 2
    base = pl.multiple_of(c * half, half)
    span = [pl.ds(pl.multiple_of(base + h * part, part), part) for h in (0, 1)]
    kv1 = {}
    for off in OFFSETS:
        for h in (0, 1):
            fast, slow = ((x, y), (y, x))[h]
            kv1[h, off] = send(
                kv.at[span[h]],
                kv_all.at[ctx, span[h]],
                s_kv1,
                (h, off - 1),
                (spot(h, (fast + off) % 4, slow), tp),
            )
    kv_all[ctx] = kv[...]
    got[ctx] = msg[ctx]
    for cp in one:
        cp.wait_recv()
    prefix_into(range(16), got, ent)
    two = swap_start(ent, entering, s_two, place)
    entering[ctx] = ent[ctx]
    kv2, to_mate = {}, []
    for off in OFFSETS:
        for h in (0, 1):
            kv1[h, off].wait_recv()
    for h in (0, 1):
        fast, slow = ((x, y), (y, x))[h]
        for off in OFFSETS:
            for k in range(4):
                at = spot(h, k, slow)
                kv2[h, off, k] = send(
                    kv_all.at[at, span[h]],
                    kv_all.at[at, span[h]],
                    s_kv2,
                    (h, off - 1, k),
                    (spot(h, fast, (slow + off) % 4), tp),
                )
    for off in OFFSETS:
        for h in (0, 1):
            fast, slow = ((x, y), (y, x))[h]
            at = spot(h, (fast + 4 - off) % 4, slow)
            to_mate.append(
                send(kv_all.at[at, span[h]], kv_all.at[at, span[h]], s_m1, (h, off - 1), mate)
            )
    for off in OFFSETS:
        for h in (0, 1):
            fast, slow = ((x, y), (y, x))[h]
            for k in range(4):
                kv2[h, off, k].wait_recv()
                at = spot(h, k, (slow + 4 - off) % 4)
                to_mate.append(
                    send(
                        kv_all.at[at, span[h]], kv_all.at[at, span[h]], s_m2, (h, off - 1, k), mate
                    )
                )
    for cp in two + to_mate:
        cp.wait_recv()
    for cp in one + two + to_mate + list(kv1.values()) + list(kv2.values()):
        cp.wait_send()


def front_exchange(msg, kv):
    _, _, width = msg.shape
    return call(
        front_kernel,
        [((16, 16, width), F32), ((16,) + kv.shape, BF)],
        [msg, kv],
        [
            pltpu.VMEM(msg.shape, F32),
            pltpu.VMEM((16, 16, width), F32),
            *pair(15),
            *pair(15),
            *pair(2, 3),
            *pair(2, 3, 4),
            *pair(2, 3),
            *pair(2, 3, 4),
        ],
        4,
        "front_exchange",
    )


def back_kernel(msg, dkv, leaving, out, got, ent, mate_buf, both, *scratch):
    place = ctx_place()
    ctx, tp, y, x = place
    c = tp % 2
    mate = (ctx, tp + 1 - 2 * c)
    greet(ctx_peers(ctx, tp) + [mate])
    s_one, s_two, s_mate, bufs = scratch[0:2], scratch[2:4], scratch[4:6], scratch[6:]
    one = swap_start(msg, got, s_one, place)
    half = dkv.shape[1] // 2
    mine = pl.ds(pl.multiple_of(c * half, half), half)
    other = pl.ds(pl.multiple_of((1 - c) * half, half), half)
    cps = [
        send(
            dkv.at[pl.ds(4 * k, 4), other], mate_buf.at[pl.ds(4 * k, 4)], s_mate, k, mate
        )
        for k in range(4)
    ]
    got[ctx] = msg[ctx]
    for k in range(4):
        cps[k].wait_recv()
        for i in range(4 * k, 4 * k + 4):
            both[i] = (dkv[i, mine].astype(F32) + mate_buf[i].astype(F32)).astype(BF)
    first = scatter_start(both, bufs, place)
    for cp in one:
        cp.wait_recv()
    prefix_into(range(15, -1, -1), got, ent)
    two = swap_start(ent, leaving, s_two, place)
    leaving[ctx] = ent[ctx]
    second = scatter_middle(both, out, bufs, place, first)
    scatter_end(both, out, bufs, first, second)
    for cp in two:
        cp.wait_recv()
    for cp in one + two + cps:
        cp.wait_send()


def back_exchange(msg, dkv):
    _, _, width = msg.shape
    _, tall, cols = dkv.shape
    half = tall // 2
    return call(
        back_kernel,
        [((16, 16, width), F32), ((half, cols), F32)],
        [msg, dkv],
        [
            pltpu.VMEM(msg.shape, F32),
            pltpu.VMEM((16, 16, width), F32),
            pltpu.VMEM((16, half, cols), BF),
            pltpu.VMEM((16, half, cols), BF),
            *pair(15),
            *pair(15),
            *pair(4),
            *scatter_bufs(half, cols),
        ],
        5,
        "back_exchange",
    )


def tail_kernel(big, small, head, big_out, small_out, shared, head_out, heads, *scratch):
    place = ctx_place()
    ctx, tp = place[:2]
    tp_at = tp_place()
    greet(ctx_peers(ctx, tp) + tp_peers(*tp_at))
    bufs, more, s_head, sems = scratch[:7], scratch[7:14], scratch[14:16], scratch[16:]
    first_s = scatter_start(small, more, place)
    first = scatter_start(big, bufs, place)
    sent = [
        send(head, heads.at[ctx], s_head, d - 1, ((ctx + d) % 16, tp)) for d in range(1, 16)
    ]
    heads[ctx] = head[...]
    second_s = scatter_middle(small, small_out, more, place, first_s)
    second = scatter_middle(big, big_out, bufs, place, first)
    scatter_end(small, small_out, more, first_s, second_s)
    shared[tp] = small_out[pl.ds(0, shared.shape[1])]
    started = share_start(shared, sems, tp_at)
    scatter_end(big, big_out, bufs, first, second)
    for cp in sent:
        cp.wait_recv()
    head_out[...] = jnp.sum(heads[...], axis=0)
    share_end(shared, sems, tp_at, started)
    for cp in sent:
        cp.wait_send()


def tail_exchange(big, small, head, shared_rows):
    _, tall, wide = big.shape
    _, rows, cols = small.shape
    return call(
        tail_kernel,
        [
            ((tall, wide), F32),
            ((rows, cols), F32),
            ((8, shared_rows, cols), F32),
            (head.shape, F32),
        ],
        [big, small, head],
        [
            pltpu.VMEM((16,) + head.shape, F32),
            *scatter_bufs(tall, wide),
            *scatter_bufs(rows, cols),
            *pair(15),
            *share_sems(),
        ],
        6,
        "tail_exchange",
    )


def flash_kernel(scale, at, q_t, kv, start, out_t, lse):
    ctx = at[0]
    block, size = kv.shape[1], q_t.shape[1]
    queries = q_t[...]
    begin = start[...]

    def step(i, carry, diagonal):
        top, total, acc = carry
        s = dot(kv[i, :, :HD], queries)
        key = i * block + lax.broadcasted_iota(jnp.int32, s.shape, 0)
        allowed = key >= begin
        if diagonal:
            allowed &= key <= ctx * block + lax.broadcasted_iota(jnp.int32, s.shape, 1)
        s = jnp.where(allowed, s * scale, -1e30)
        new = jnp.maximum(top, jnp.max(s, axis=0, keepdims=True))
        p = jnp.where(allowed, jnp.exp(s - new), 0.0)
        fade = jnp.exp(top - new)
        total = total * fade + jnp.sum(p, axis=0, keepdims=True)
        acc = acc * fade + dot_tn(kv[i, :, HD:], p.astype(BF))
        return new, total, acc

    carry = (
        jnp.full((1, size), -1e30, F32),
        jnp.zeros((1, size), F32),
        jnp.zeros((HD, size), F32),
    )
    carry = lax.fori_loop(at[1], ctx, lambda i, k: step(i, k, False), carry)
    top, total, acc = step(ctx, carry, True)
    out_t[...] = acc / total
    lse[...] = top + jnp.log(total)


def plain_call(kernel, outs, ins, specs, name):
    return pl.pallas_call(
        kernel,
        out_shape=[jax.ShapeDtypeStruct(s, d) for s, d in outs],
        in_specs=specs,
        out_specs=[VM] * len(outs),
        compiler_params=pltpu.CompilerParams(vmem_limit_bytes=56 << 20),
        name=name,
    )(*ins)


def flash_forward(at, q_t, kv, start, scale):
    return plain_call(
        functools.partial(flash_kernel, scale),
        [(q_t.shape, F32), ((1, q_t.shape[1]), F32)],
        [at, q_t, kv, start],
        [SM, VM, VM, VM],
        "flash_forward",
    )


def flash_back_kernel(scale, at, q_t, q, kv, start, lse, grad_t, grad, delta, dq_t, dkv):
    ctx = at[0]
    block = kv.shape[1]
    dkv[...] = jnp.zeros(dkv.shape, BF)
    queries_t, queries = q_t[...], q[...]
    og_t, og = grad_t[...], grad[...]
    begin, offset, low = start[...], lse[...], delta[...]

    def step(i, acc, diagonal):
        keys = kv[i, :, :HD]
        s = dot(keys, queries_t)
        key = i * block + lax.broadcasted_iota(jnp.int32, s.shape, 0)
        allowed = key >= begin
        if diagonal:
            allowed &= key <= ctx * block + lax.broadcasted_iota(jnp.int32, s.shape, 1)
        p = jnp.exp(jnp.where(allowed, s * scale - offset, -1e30))
        dp = dot(kv[i, :, HD:], og_t)
        ds = (p * (dp - low)).astype(BF)
        dkv[i, :, :HD] = (dot(ds, queries) * scale).astype(BF)
        dkv[i, :, HD:] = dot(p.astype(BF), og).astype(BF)
        return acc + dot_tn(keys, ds)

    acc = jnp.zeros(q_t.shape, F32)
    acc = lax.fori_loop(at[1], ctx, lambda i, k: step(i, k, False), acc)
    dq_t[...] = step(ctx, acc, True) * scale


def flash_backward(at, q_t, q, kv, start, lse, grad_t, grad, delta, scale):
    return plain_call(
        functools.partial(flash_back_kernel, scale),
        [(q_t.shape, F32), (kv.shape, BF)],
        [at, q_t, q, kv, start, lse, grad_t, grad, delta],
        [SM] + [VM] * 8,
        "flash_backward",
    )


def soft_plus(values):
    return jnp.maximum(values, 0.0) + jnp.log1p(jnp.exp(-jnp.abs(values)))


def doc_index(positions, doc_lengths):
    bounds = jnp.cumsum(doc_lengths)
    return jnp.sum((positions[:, None] >= bounds[None, :]).astype(jnp.int32), axis=1)


def adapter_mask(doc_ids, adapter_ids, columns):
    seq_count = adapter_ids.shape[0]
    chosen = jnp.sum(
        jnp.where(doc_ids[:, None] == jnp.arange(seq_count)[None, :], adapter_ids[None, :], 0),
        axis=1,
    )
    return (chosen[:, None] == jnp.arange(columns)[None, :] // RANK).astype(F32)


def spread(per_head):
    return jnp.repeat(per_head, MHEAD, axis=1)


def by_head(flat):
    return flat.reshape(flat.shape[0], -1, MHEAD).transpose(1, 0, 2)


def flat_heads(split):
    return split.transpose(1, 0, 2).reshape(split.shape[1], -1)


def state_message(state, decay):
    wide = jnp.repeat(decay, MHEAD)
    rows = jnp.broadcast_to(wide[None, None, :], (16, 8, wide.shape[0]))
    return jnp.concatenate([state.reshape(16, 16, -1), rows], axis=1)


def body(
    hidden_in,
    norm_gains,
    w_in,
    w_shared,
    w_dt,
    head_params,
    w_out,
    w_gu,
    w_down,
    a_in,
    b_in,
    a_sh,
    b_sh,
    a_out,
    b_out,
    a_gu,
    b_gu,
    a_dn,
    b_dn,
    adapter_ids,
    doc_lengths,
    out_grad,
):
    rows, width = hidden_in.shape
    heads = head_params.shape[1]
    inner = heads * MHEAD
    tp_count = lax.axis_size("tp")
    share = rows // tp_count
    ctx_at = lax.axis_index("ctx")
    tp_at = lax.axis_index("tp")
    positions = ctx_at * rows + jnp.arange(rows, dtype=jnp.int32)
    doc_ids = doc_index(positions, doc_lengths)
    doc_before = doc_index(jnp.maximum(positions[:1] - 1, 0), doc_lengths)[0]
    bounds = jnp.cumsum(doc_lengths)
    starts = jnp.sum(
        jnp.where(doc_ids[:, None] == jnp.arange(1, 1 + bounds.shape[0])[None, :], bounds[None, :], 0),
        axis=1,
    )
    starts_row = starts[None, :]
    at = jnp.stack([ctx_at, jnp.min(starts) // rows]).astype(jnp.int32)
    mask = adapter_mask(doc_ids, adapter_ids, a_in.shape[1])

    def rows_of(array):
        return lax.dynamic_slice_in_dim(array, tp_at * share, share, 0)

    mask_rows = rows_of(mask)
    w_in = w_in.reshape(width, -1)
    b_in = b_in.reshape(b_in.shape[0], -1)
    w_out = w_out.reshape(-1, width)
    a_out = a_out.reshape(-1, a_out.shape[2])
    w_gu = w_gu.reshape(width, -1)
    b_gu = b_gu.reshape(b_gu.shape[0], -1)
    hidden = w_down.shape[0]
    rank = a_in.shape[1]
    scale = HD ** (-0.5)
    gain_one, gain_two = norm_gains[0:1], norm_gains[1:2]
    source = hidden_in.astype(F32)
    normed_one = (source * norm_scale(source) * gain_one).astype(BF)
    low_in = (dot(normed_one, a_in) * mask).astype(BF)
    h_one = (dot(normed_one, w_in) + dot(low_in, b_in)).astype(BF)
    low_sh = (dot(normed_one, a_sh) * mask).astype(BF)
    h_two = (dot(normed_one, w_shared) + dot(low_sh, b_sh)).astype(BF)
    dt_raw = dot(normed_one, w_dt)
    gate = h_one[:, :inner].astype(F32)
    xs = h_one[:, inner : 2 * inner]
    xs_f = xs.astype(F32)
    q = h_one[:, 2 * inner :]
    q_t = q.T
    bm, cm = h_two[:, :STATE], h_two[:, STATE : 2 * STATE]
    kv_group = tp_at // (QHEADS // KVH)
    key_col = 2 * STATE + kv_group * HD
    keys_mine = lax.dynamic_slice_in_dim(h_two, key_col, HD, 1)
    vals_mine = lax.dynamic_slice_in_dim(h_two, key_col + KVH * HD, HD, 1)

    pre = dt_raw + head_params[0]
    dt = soft_plus(pre)
    rate = jnp.exp(head_params[1])
    order = jnp.arange(rows)
    tri = (order[:, None] >= order[None, :]).astype(F32)
    decay = jnp.dot(tri, -dt * rate, precision=lax.Precision.HIGHEST)
    decay_t, dt_t = decay.T, dt.T
    allowed = (order[:, None] >= order[None, :]) & (doc_ids[:, None] == doc_ids[None, :])
    gap = jnp.where(allowed[None], decay_t[:, :, None] - decay_t[:, None, :], -1e30)
    fade = jnp.exp(gap)
    inter = dot_nt(cm, bm)
    pulls = inter[None] * fade
    mixing = (pulls * dt_t[:, None, :]).astype(BF)
    xs_h = by_head(xs)
    inner_y = flat_heads(
        lax.dot_general(mixing, xs_h, (((2,), (1,)), ((0,), (0,))), preferred_element_type=F32)
    )
    tail = jnp.where(
        (doc_ids == doc_ids[-1])[:, None], jnp.exp(decay[-1][None, :] - decay), 0.0
    )
    tail_dt = tail * dt
    state_out = dot_tn(bm, (spread(tail_dt) * xs_f).astype(BF))
    total_decay = jnp.exp(decay[-1]) * (doc_ids[-1] == doc_before).astype(F32)
    entering, kv_all = front_exchange(
        state_message(state_out, total_decay), jnp.concatenate([keys_mine, vals_mine], axis=1)
    )
    entering = entering.reshape(STATE, inner)
    entering_low = entering.astype(BF)
    reach = spread(jnp.exp(decay) * (doc_ids == doc_before).astype(F32)[:, None])
    cross = dot(cm, entering_low) * reach
    skip = jnp.repeat(head_params[2], MHEAD)[None, :]
    ssd = inner_y + cross + skip * xs_f
    gate_sig = jax.nn.sigmoid(gate)
    gated = ssd * (gate * gate_sig)

    attn_t, lse = flash_forward(at, q_t, kv_all, starts_row, scale)
    merged = jnp.concatenate([gated, attn_t.T], axis=1).astype(BF)
    low_out_part = dot(merged, a_out) * mask
    mix_part = jnp.concatenate([dot(merged, w_out).astype(BF), low_out_part.astype(BF)], axis=1)
    shared_mix, resid = mixer_exchange(
        mix_part.reshape(tp_count, share, -1), rows_of(hidden_in), gain_two, b_out
    )
    shared_mix = shared_mix.reshape(rows, -1)
    normed_two, low_out = shared_mix[:, :width], shared_mix[:, width:]

    low_gu = (dot(normed_two, a_gu) * mask).astype(BF)
    h_gu = (dot(normed_two, w_gu) + dot(low_gu, b_gu)).astype(BF).astype(F32)
    gate_mlp, up = h_gu[:, :hidden], h_gu[:, hidden:]
    sig = jax.nn.sigmoid(gate_mlp)
    act = (gate_mlp * sig * up).astype(BF)
    low_dn_part = dot(act, a_dn) * mask
    mlp_part = dot(act, w_down)
    grad_low_dn = (dot_nt(out_grad, b_dn) * mask).astype(BF)
    grad_act = (dot_nt(out_grad, w_down) + dot_nt(grad_low_dn, a_dn)).astype(BF).astype(F32)
    grad_gu = jnp.concatenate(
        [grad_act * up * sig * (1.0 + gate_mlp * (1.0 - sig)), grad_act * (gate_mlp * sig)], axis=1
    ).astype(BF)
    grad_low_gu_part = dot_nt(grad_gu, b_gu)
    grad_two_part = dot_nt(grad_gu, w_gu)
    g_gu = dot_tn(normed_two, grad_gu).astype(BF).reshape(16, -1, 2 * hidden)
    g_b_gu = dot_tn(low_gu, grad_gu).astype(BF).reshape(16, -1, 2 * hidden)
    g_dn = dot_tn(out_grad, act).astype(BF).reshape(16, -1, hidden)
    g_a_dn = dot_tn(grad_low_dn, act).astype(BF).reshape(16, -1, hidden)
    early = jnp.concatenate(
        [jnp.concatenate([g_gu, g_dn], axis=2), jnp.concatenate([g_b_gu, g_a_dn], axis=2)], axis=1
    )
    early_rows = early.shape[1]
    early = lax.psum_scatter(
        early.reshape(16 * early_rows, -1), "ctx", scatter_dimension=0, tiled=True
    )
    part = jnp.concatenate(
        [
            grad_two_part.astype(BF),
            grad_low_gu_part.astype(BF),
            mlp_part.astype(BF),
            low_dn_part.astype(BF),
        ],
        axis=1,
    )
    shared_mlp, grad_resid, gain_part_two = mlp_exchange(
        part.reshape(tp_count, share, -1), resid, gain_two, rows_of(out_grad), b_dn, a_gu, mask_rows
    )
    shared_mlp = shared_mlp.reshape(rows, -1)
    wide = width + rank
    grad_mixer, grad_low_gu = shared_mlp[:, :width], shared_mlp[:, width:wide]
    mixed, low_dn = shared_mlp[:, wide : wide + width], shared_mlp[:, wide + width :]

    grad_low_out = (dot_nt(grad_mixer, b_out) * mask).astype(BF)
    grad_merged = (dot_nt(grad_mixer, w_out) + dot_nt(grad_low_out, a_out)).astype(BF)
    late = dot_tn(grad_mixer, merged).astype(BF)
    late = lax.psum_scatter(late, "ctx", scatter_dimension=0, tiled=True)
    grad_gated = grad_merged[:, :inner].astype(F32)
    grad_attn = grad_merged[:, inner:]
    grad_ssd = grad_gated * (gate * gate_sig)
    grad_gate = grad_gated * ssd * gate_sig * (1.0 + gate * (1.0 - gate_sig))
    grad_attn_t = grad_attn.T
    delta = jnp.sum(grad_attn_t.astype(F32) * attn_t, axis=0, keepdims=True)
    dq_t, dkv = flash_backward(
        at, q_t, q, kv_all, starts_row, lse, grad_attn_t, grad_attn, delta, scale
    )
    dy = grad_ssd.astype(BF)
    dy_h = by_head(dy)
    reached = (reach * grad_ssd).astype(BF)
    pull_state = dot_tn(cm, reached)
    leaving, dkv_sum = back_exchange(state_message(pull_state, total_decay), dkv)
    leaving = leaving.reshape(STATE, inner)
    leaving_low = leaving.astype(BF)
    d_mix = lax.dot_general(dy_h, xs_h, (((2,), (2,)), ((0,), (0,))), preferred_element_type=F32)
    d_inter = jnp.sum(d_mix * (fade * dt_t[:, None, :]), axis=0).astype(BF)
    weighted = d_mix * pulls
    col = jnp.sum(weighted, axis=1).T
    row = jnp.sum(weighted * dt_t[:, None, :], axis=2).T
    dx_inner = flat_heads(
        lax.dot_general(mixing, dy_h, (((1,), (1,)), ((0,), (0,))), preferred_element_type=F32)
    )
    from_state = dot(bm, leaving_low)

    def head_sums(flat):
        return jnp.sum(flat.reshape(flat.shape[0], heads, MHEAD), axis=2)

    held = head_sums(from_state * xs_f) * tail
    d_cross = head_sums(cross * grad_ssd)
    d_decay = row - col * dt + d_cross - held * dt
    d_last = jnp.sum(held * dt, axis=0) + total_decay * head_sums(
        jnp.sum(leaving * entering, axis=0)[None]
    )[0]
    d_log = jnp.dot(tri.T, d_decay, precision=lax.Precision.HIGHEST) + d_last[None, :]
    grad_dt = (col + held - rate * d_log) * jax.nn.sigmoid(pre)
    grad_x = dx_inner + spread(tail_dt) * from_state + skip * grad_ssd
    grad_bm = dot_tn(d_inter, cm) + dot_nt((spread(tail_dt) * xs_f).astype(BF), leaving_low)
    grad_cm = dot(d_inter, bm) + dot_nt(reached, entering_low)
    grad_head = jnp.stack(
        [
            jnp.sum(grad_dt, axis=0),
            -jnp.sum(dt * rate * d_log, axis=0),
            jnp.sum(head_sums(grad_ssd * xs_f), axis=0),
        ]
    )
    grad_one = jnp.concatenate([grad_gate, grad_x, dq_t.T], axis=1).astype(BF)
    half = rows // 2
    dkv_rows = lax.dynamic_update_slice_in_dim(
        jnp.zeros((rows, 2 * HD), F32), dkv_sum, (tp_at % 2) * half, 0
    ).astype(BF)
    group = (jnp.arange(KVH) == kv_group).astype(BF)[None, :, None]
    grad_two = jnp.concatenate(
        [
            grad_bm.astype(BF),
            grad_cm.astype(BF),
            (dkv_rows[:, None, :HD] * group).reshape(rows, KVH * HD),
            (dkv_rows[:, None, HD:] * group).reshape(rows, KVH * HD),
        ],
        axis=1,
    )
    grad_dt_low = grad_dt.astype(BF)
    norm_part = dot_nt(grad_one, w_in) + dot_nt(grad_two, w_shared) + dot_nt(grad_dt_low, w_dt)
    part = jnp.concatenate(
        [
            norm_part.astype(BF),
            dot_nt(grad_one, b_in).astype(BF),
            dot_nt(grad_two, b_sh).astype(BF),
        ],
        axis=1,
    )
    two_blocks = grad_two.reshape(rows, tp_count, -1).transpose(1, 0, 2)
    shared_in, gains, two_mine = input_exchange(
        part.reshape(tp_count, share, -1),
        two_blocks,
        rows_of(hidden_in),
        gain_one,
        grad_resid,
        a_in,
        a_sh,
        mask_rows,
        gain_part_two,
    )
    shared_in = shared_in.reshape(rows, -1)
    input_grad = shared_in[:, :width].astype(F32)
    grad_low_in, grad_low_sh = shared_in[:, width:wide], shared_in[:, wide:]
    gain_sum = jnp.sum(gains, axis=0)

    pad_dt = jnp.concatenate(
        [grad_one, grad_dt_low, jnp.zeros((rows, 128 - heads), BF)], axis=1
    )
    g_in = dot_tn(normed_one, pad_dt).astype(BF).reshape(16, -1, pad_dt.shape[1])
    g_b_in = dot_tn(low_in, pad_dt).astype(BF).reshape(16, -1, pad_dt.shape[1])
    big = jnp.concatenate([g_in, g_b_in, jnp.zeros_like(g_b_in)], axis=1)

    def my_slice(full):
        cut = full.astype(BF).reshape(16, tp_count, -1, full.shape[1])
        return lax.dynamic_index_in_dim(cut, tp_at, 1, keepdims=False)

    def by_ctx(full):
        return full.astype(BF).reshape(16, -1, full.shape[1])

    gain_rows = gain_sum.astype(BF).reshape(8, 16, -1).transpose(1, 0, 2)
    small = jnp.concatenate(
        [
            by_ctx(dot_tn(normed_one, two_mine)),
            my_slice(dot_tn(normed_one, grad_low_sh)),
            by_ctx(dot_tn(low_sh, two_mine)),
            gain_rows,
            by_ctx(dot_tn(merged, grad_low_out)),
            my_slice(dot_tn(normed_one, grad_low_in)),
            my_slice(dot_tn(normed_two, grad_low_gu)),
            my_slice(dot_tn(grad_mixer, low_out)),
            my_slice(dot_tn(out_grad, low_dn)),
        ],
        axis=1,
    )
    head_tile = jnp.pad(grad_head, ((0, 5), (0, 128 - heads)))
    big_sum, small_sum, shared, head_sum = tail_exchange(big, small, head_tile, 152)
    deep = width // 16
    out_shared = shared[:, :deep].transpose(1, 0, 2).reshape(deep, -1)
    out_a_sh = shared[:, deep : deep + 16].reshape(deep, -1)
    out_b_sh = shared[:, deep + 16 : deep + 24].transpose(1, 0, 2).reshape(8, -1)
    spot_at = deep + 24
    out_gain = small_sum[spot_at : spot_at + 2]
    spot_at += 8
    out_a_out = small_sum[spot_at : spot_at + 32]
    spot_at += 32
    four = [small_sum[spot_at + 16 * k : spot_at + 16 * (k + 1)] for k in range(4)]
    early = early.astype(F32)
    return (
        mixed.astype(F32),
        input_grad,
        out_gain,
        big_sum[:deep, : w_in.shape[1]].reshape(deep, 1, -1),
        out_shared,
        big_sum[:deep, w_in.shape[1] : w_in.shape[1] + heads],
        head_sum[:3, :heads],
        late.astype(F32).T[None],
        early[:deep, : 2 * hidden].reshape(deep, 2, hidden),
        early[:deep, 2 * hidden :].T,
        four[0],
        big_sum[deep : deep + 8, : w_in.shape[1]].reshape(8, 1, -1),
        out_a_sh,
        out_b_sh,
        out_a_out[None],
        four[2].T,
        four[1],
        early[deep : deep + 8, : 2 * hidden].reshape(8, 2, hidden),
        early[deep : deep + 8, 2 * hidden :].T,
        four[3].T,
    )
def solution(mesh):
    placed = (
        P("ctx", None),
        P(),
        P(None, "tp", None),
        P(),
        P(None, "tp"),
        P(None, "tp"),
        P("tp", None, None),
        P(None, None, "tp"),
        P("tp", None),
        P(),
        P(None, "tp", None),
        P(),
        P(),
        P("tp", None, None),
        P(),
        P(),
        P(None, None, "tp"),
        P("tp", None),
        P(),
        P(),
        P(),
        P("ctx", None),
    )
    return jax.shard_map(
        body,
        mesh=mesh,
        in_specs=placed,
        out_specs=(
            P("ctx", None),
            P("ctx", None),
            P(None, "ctx"),
            P("ctx", "tp", None),
            P("ctx", None),
            P("ctx", "tp"),
            P(None, "tp"),
            P("tp", None, "ctx"),
            P("ctx", None, "tp"),
            P("tp", "ctx"),
            P(("ctx", "tp"), None),
            P("ctx", "tp", None),
            P("ctx", None),
            P("ctx", None),
            P("tp", "ctx", None),
            P(None, ("ctx", "tp")),
            P(("ctx", "tp"), None),
            P("ctx", None, "tp"),
            P("tp", "ctx"),
            P(None, ("ctx", "tp")),
        ),
        check_vma=False,
    )
```

```python
import functools

import jax
import jax.numpy as jnp
from jax import lax
from jax.experimental import pallas as pl
from jax.experimental.pallas import tpu as pltpu
from jax.sharding import PartitionSpec as P

MHEAD = 64
STATE = 256
QHEADS = 8
KVH = 2
HD = 128
RANK = 16
NORM_EPSILON = 1e-06

MESH = pl.DeviceIdType.MESH
VM = pl.BlockSpec(memory_space=pltpu.VMEM)
SM = pl.BlockSpec(memory_space=pltpu.SMEM)
BF = jnp.bfloat16
F32 = jnp.float32
DMA = pltpu.SemaphoreType.DMA
OFFSETS = (2, 1, 3)


def call(kernel, outs, ins, scratch, cid, name):
    return pl.pallas_call(
        kernel,
        out_shape=[jax.ShapeDtypeStruct(s, d) for s, d in outs],
        in_specs=[VM] * len(ins),
        out_specs=[VM] * len(outs),
        scratch_shapes=scratch,
        compiler_params=pltpu.CompilerParams(
            collective_id=cid, has_side_effects=True, vmem_limit_bytes=56 << 20
        ),
        name=name,
    )(*ins)


def greet(peers):
    barrier = pltpu.get_barrier_semaphore()
    for peer in peers:
        pl.semaphore_signal(barrier, inc=1, device_id=peer, device_id_type=MESH)
    pl.semaphore_wait(barrier, len(peers))


def send(src, dst, sems, slot, peer):
    cp = pltpu.make_async_remote_copy(
        src_ref=src,
        dst_ref=dst,
        send_sem=sems[0].at[slot],
        recv_sem=sems[1].at[slot],
        device_id=peer,
        device_id_type=MESH,
    )
    cp.start()
    return cp


def pair(*shape):
    return [DMA(shape), DMA(shape)]


def tp_place():
    ctx = lax.axis_index("ctx")
    tp = lax.axis_index("tp")
    return ctx, tp, tp // 2, tp % 2


def tp_peers(ctx, tp, z, c):
    return [(ctx, ((z + d) % 4) * 2 + c) for d in (1, 2, 3)] + [(ctx, z * 2 + 1 - c)]


def reduce_bufs(rows, width):
    return [
        pltpu.VMEM((4, rows, width), BF),
        pltpu.VMEM((3, rows, width), BF),
        pltpu.VMEM((3, rows, width), BF),
        *pair(4),
        *pair(3),
    ]


def reduce_start(part, bufs, place):
    sib, snd, rcv, s1s, s1r, s2s, s2r = bufs
    ctx, tp, z, c = place
    mate = (ctx, z * 2 + 1 - c)
    return [
        send(part.at[((z + off) % 4) * 2 + 1 - c], sib.at[k], (s1s, s1r), k, mate)
        for k, off in enumerate(OFFSETS + (0,))
    ]


def reduce_middle(part, bufs, place, first):
    sib, snd, rcv, s1s, s1r, s2s, s2r = bufs
    ctx, tp, z, c = place
    second = []
    for k, off in enumerate(OFFSETS):
        to = ((z + off) % 4) * 2 + c
        first[k].wait_recv()
        snd[k] = (part[to].astype(F32) + sib[k].astype(F32)).astype(BF)
        second.append(send(snd.at[k], rcv.at[k], (s2s, s2r), k, (ctx, to)))
    return second


def reduce_end(part, bufs, place, first, second):
    sib, snd, rcv = bufs[:3]
    first[3].wait_recv()
    total = part[place[1]].astype(F32) + sib[3].astype(F32)
    for k in range(3):
        second[k].wait_recv()
        total = total + rcv[k].astype(F32)
    for cp in first + second:
        cp.wait_send()
    return total


def share_sems():
    return [*pair(3), *pair(4)]


def share_start(out, sems, place):
    ctx, tp, z, c = place
    copies = [
        send(out.at[tp], out.at[tp], sems[:2], k, (ctx, ((z + off) % 4) * 2 + c))
        for k, off in enumerate(OFFSETS)
    ]
    return copies, send(out.at[tp], out.at[tp], sems[2:], 3, (ctx, z * 2 + 1 - c))


def share_end(out, sems, place, started):
    ctx, tp, z, c = place
    copies, own = started
    passed = [own]
    for k, off in sorted(enumerate(OFFSETS), key=lambda t: t[1] == 2):
        copies[k].wait_recv()
        at = ((z + 4 - off) % 4) * 2 + c
        passed.append(send(out.at[at], out.at[at], sems[2:], k, (ctx, z * 2 + 1 - c)))
    for cp in passed:
        cp.wait_recv()
    for cp in copies + passed:
        cp.wait_send()


def norm_scale(v):
    return lax.rsqrt(jnp.mean(v * v, axis=-1, keepdims=True) + NORM_EPSILON)


def norm_back(v, gain, grad):
    r = norm_scale(v)
    pulled = grad * gain
    inner = jnp.mean(pulled * v, axis=-1, keepdims=True)
    grad_v = r * pulled - v * (r * r * r) * inner
    return grad_v, jnp.sum(grad * v * r, axis=0, keepdims=True)


def dot(a, b):
    return jnp.dot(a, b, preferred_element_type=F32)


def dot_nt(a, b):
    return lax.dot_general(a, b, (((1,), (1,)), ((), ())), preferred_element_type=F32)


def dot_tn(a, b):
    return lax.dot_general(a, b, (((0,), (0,)), ((), ())), preferred_element_type=F32)


def mixer_kernel(part, source, gain, b_out, out, resid, *scratch):
    width = source.shape[1]
    place = tp_place()
    greet(tp_peers(*place))
    bufs, sems = scratch[:7], scratch[7:]
    first = reduce_start(part, bufs, place)
    total = reduce_end(part, bufs, place, first, reduce_middle(part, bufs, place, first))
    low = total[:, width:].astype(BF)
    residual = source[...].astype(F32) + total[:, :width] + dot(low, b_out[...])
    resid[...] = residual
    normed = residual * norm_scale(residual) * gain[...]
    out[place[1], :, :width] = normed.astype(BF)
    out[place[1], :, width:] = low
    share_end(out, sems, place, share_start(out, sems, place))


def mixer_exchange(part, source, gain, b_out):
    _, rows, wide = part.shape
    return call(
        mixer_kernel,
        [(part.shape, BF), (source.shape, F32)],
        [part, source, gain, b_out],
        reduce_bufs(rows, wide) + share_sems(),
        1,
        "mixer_exchange",
    )


def cut_t(ref, j):
    return ref[:, pl.ds(pl.multiple_of(j * 128, 128), 128)].T


def eight(ref, j):
    rows = ref[pl.ds(pl.multiple_of(j * 8, 8), 8)]
    return jnp.concatenate([rows, jnp.zeros_like(rows)], axis=0)


def mlp_kernel(
    part,
    resid,
    gain,
    out_grad_rows,
    a_gu,
    mask,
    normed_two,
    grad_gu,
    out_grad,
    act,
    low_gu,
    grad_low_dn,
    out,
    grad_resid,
    gain_part,
    early,
    b_gu_sum,
    a_dn_sum,
    *scratch,
):
    width = resid.shape[1]
    wide = grad_gu.shape[1]
    place = tp_place()
    tp = place[1]
    greet(tp_peers(*place))
    bufs, sems = scratch[:7], scratch[7:]
    first = reduce_start(part, bufs, place)
    second = reduce_middle(part, bufs, place, first)
    b_gu_sum[...] = dot_tn(low_gu[...], grad_gu[...])
    a_dn_sum[...] = dot_tn(grad_low_dn[...], act[...])

    def weights(j, carry):
        early[j, 0:128, :wide] = dot(cut_t(normed_two, j), grad_gu[...]).astype(BF)
        early[j, 0:128, wide:] = dot(cut_t(out_grad, j), act[...]).astype(BF)
        early[j, 128:144, :wide] = eight(b_gu_sum, j).astype(BF)
        early[j, 128:144, wide:] = eight(a_dn_sum, j).astype(BF)
        return carry

    lax.fori_loop(0, 16, weights, 0)
    total = reduce_end(part, bufs, place, first, second)
    low = (total[:, width:] * mask[...]).astype(BF)
    grad = total[:, :width] + dot_nt(low, a_gu[...])
    grad_v, grad_gain = norm_back(resid[...], gain[...], grad)
    grad_r = out_grad_rows[...].astype(F32) + grad_v
    grad_resid[...] = grad_r
    gain_part[...] = grad_gain
    out[tp, :, :width] = grad_r.astype(BF)
    out[tp, :, width:] = low
    share_end(out, sems, place, share_start(out, sems, place))


def mlp_exchange(part, resid, gain, rows, a_gu, mask, *weights):
    _, tall, wide = part.shape
    grad_gu, act = weights[1], weights[3]
    return call(
        mlp_kernel,
        [
            (part.shape, BF),
            (resid.shape, F32),
            (gain.shape, F32),
            ((16, 144, grad_gu.shape[1] + act.shape[1]), BF),
        ],
        [part, resid, gain, rows, a_gu, mask, *weights],
        [
            pltpu.VMEM((128, grad_gu.shape[1]), F32),
            pltpu.VMEM((128, act.shape[1]), F32),
            *reduce_bufs(tall, wide),
            *share_sems(),
        ],
        2,
        "mlp_exchange",
    )


def ctx_place():
    ctx = lax.axis_index("ctx")
    return ctx, lax.axis_index("tp"), ctx // 4, ctx % 4


def spot(h, fast, slow):
    return slow * 4 + fast if h == 0 else fast * 4 + slow


def scatter_bufs(rows, width):
    most = max(rows - rows // 32 * 16, rows // 32 * 16)
    return [
        pltpu.VMEM((2, 3, most, width), BF),
        pltpu.VMEM((2, 3, 4, most, width), BF),
        pltpu.VMEM((2, 3, most, width), BF),
        *pair(2, 3, 4),
        *pair(2, 3),
    ]


def spans_of(rows):
    half = rows // 32 * 16
    return ((0, half), (half, rows - half))


def scatter_start(part, bufs, place):
    mid, r1, r2, s1s, s1r, s2s, s2r = bufs
    ctx, tp, y, x = place
    spans = spans_of(part.shape[1])
    first = {}
    for j in OFFSETS + (0,):
        for off in OFFSETS:
            for h in (0, 1):
                fast, slow = ((x, y), (y, x))[h]
                lo, size = spans[h]
                to = (fast + off) % 4
                first[h, off, j] = send(
                    part.at[spot(h, to, (slow + j) % 4), pl.ds(lo, size)],
                    r1.at[h, off - 1, j, pl.ds(0, size)],
                    (s1s, s1r),
                    (h, off - 1, j),
                    (spot(h, to, slow), tp),
                )
    return first


def scatter_middle(part, out, bufs, place, first):
    mid, r1, r2, s1s, s1r, s2s, s2r = bufs
    ctx, tp, y, x = place
    spans = spans_of(part.shape[1])
    second = {}
    for j in OFFSETS + (0,):
        for h in (0, 1):
            fast, slow = ((x, y), (y, x))[h]
            lo, size = spans[h]
            for off in OFFSETS:
                first[h, off, j].wait_recv()
            total = part[spot(h, fast, (slow + j) % 4), pl.ds(lo, size)].astype(F32)
            for off in (1, 2, 3):
                total = total + r1[h, off - 1, j, pl.ds(0, size)].astype(F32)
            if j == 0:
                out[pl.ds(lo, size)] = total
            else:
                mid[h, j - 1, pl.ds(0, size)] = total.astype(BF)
                second[h, j] = send(
                    mid.at[h, j - 1, pl.ds(0, size)],
                    r2.at[h, j - 1, pl.ds(0, size)],
                    (s2s, s2r),
                    (h, j - 1),
                    (spot(h, fast, (slow + j) % 4), tp),
                )
    return second


def scatter_end(part, out, bufs, first, second):
    r2 = bufs[2]
    for h, (lo, size) in enumerate(spans_of(part.shape[1])):
        for j in OFFSETS:
            second[h, j].wait_recv()
        total = out[pl.ds(lo, size)]
        for j in (1, 2, 3):
            total = total + r2[h, j - 1, pl.ds(0, size)].astype(F32)
        out[pl.ds(lo, size)] = total
    for cp in list(first.values()) + list(second.values()):
        cp.wait_send()


def ctx_peers(ctx, tp):
    return [((ctx + d) % 16, tp) for d in range(1, 16)]


def swap_start(src, dst, sems, place):
    ctx, tp = place[:2]
    return [
        send(src.at[(ctx + d) % 16], dst.at[ctx], sems, d - 1, ((ctx + d) % 16, tp))
        for d in range(1, 16)
    ]


def pack_state(state, decay, msg):
    width = decay.shape[1]
    msg[:, :, :width] = state[...].astype(BF)
    high = decay[...].astype(BF).astype(F32)
    low = decay[...] - high
    row = lax.broadcasted_iota(jnp.int32, (16, 128), 0)
    tile = jnp.zeros((16, 128), F32)
    count = width // 128
    for k in range(count):
        span = slice(128 * k, 128 * (k + 1))
        tile = jnp.where(row == k, high[:, span], tile)
        tile = jnp.where(row == count + k, low[:, span], tile)
    for j in range(16):
        msg[j, :, width:] = tile.astype(BF)


def prefix_into(order, got, ent):
    width = ent.shape[2]
    count = width // 128
    running = jnp.zeros(ent.shape[1:], F32)
    for i in order:
        ent[i] = running.astype(BF)
        tile = got[i, :, width:].astype(F32)
        decay = jnp.concatenate(
            [tile[k : k + 1] + tile[count + k : count + k + 1] for k in range(count)], axis=1
        )
        running = got[i, :, :width].astype(F32) + decay * running


def front_kernel(state, decay, kv, entering, kv_all, msg, got, ent, *sems):
    place = ctx_place()
    ctx, tp, y, x = place
    c = tp % 2
    mate = (ctx, tp + 1 - 2 * c)
    pack_state(state, decay, msg)
    greet(ctx_peers(ctx, tp) + [mate])
    s_one, s_two, s_kv1, s_kv2, s_m1, s_m2 = [sems[2 * k : 2 * k + 2] for k in range(6)]
    one = swap_start(msg, got, s_one, place)
    half = kv.shape[0] // 2
    part = half // 2
    base = pl.multiple_of(c * half, half)
    span = [pl.ds(pl.multiple_of(base + h * part, part), part) for h in (0, 1)]
    kv1 = {}
    for off in OFFSETS:
        for h in (0, 1):
            fast, slow = ((x, y), (y, x))[h]
            kv1[h, off] = send(
                kv.at[span[h]],
                kv_all.at[ctx, span[h]],
                s_kv1,
                (h, off - 1),
                (spot(h, (fast + off) % 4, slow), tp),
            )
    kv_all[ctx] = kv[...]
    got[ctx] = msg[ctx]
    for cp in one:
        cp.wait_recv()
    prefix_into(range(16), got, ent)
    two = swap_start(ent, entering, s_two, place)
    entering[ctx] = ent[ctx]
    kv2, to_mate = {}, []
    for off in OFFSETS:
        for h in (0, 1):
            kv1[h, off].wait_recv()
    for h in (0, 1):
        fast, slow = ((x, y), (y, x))[h]
        for off in OFFSETS:
            for k in range(4):
                at = spot(h, k, slow)
                kv2[h, off, k] = send(
                    kv_all.at[at, span[h]],
                    kv_all.at[at, span[h]],
                    s_kv2,
                    (h, off - 1, k),
                    (spot(h, fast, (slow + off) % 4), tp),
                )
    for off in OFFSETS:
        for h in (0, 1):
            fast, slow = ((x, y), (y, x))[h]
            at = spot(h, (fast + 4 - off) % 4, slow)
            to_mate.append(
                send(kv_all.at[at, span[h]], kv_all.at[at, span[h]], s_m1, (h, off - 1), mate)
            )
    for off in OFFSETS:
        for h in (0, 1):
            fast, slow = ((x, y), (y, x))[h]
            for k in range(4):
                kv2[h, off, k].wait_recv()
                at = spot(h, k, (slow + 4 - off) % 4)
                to_mate.append(
                    send(
                        kv_all.at[at, span[h]], kv_all.at[at, span[h]], s_m2, (h, off - 1, k), mate
                    )
                )
    for cp in two + to_mate:
        cp.wait_recv()
    for cp in one + two + to_mate + list(kv1.values()) + list(kv2.values()):
        cp.wait_send()


def front_exchange(state, decay, kv):
    width = decay.shape[1]
    return call(
        front_kernel,
        [((16, 16, width), BF), ((16,) + kv.shape, BF)],
        [state.reshape(16, 16, width), decay, kv],
        [
            pltpu.VMEM((16, 16, width + 128), BF),
            pltpu.VMEM((16, 16, width + 128), BF),
            pltpu.VMEM((16, 16, width), BF),
            *pair(15),
            *pair(15),
            *pair(2, 3),
            *pair(2, 3, 4),
            *pair(2, 3),
            *pair(2, 3, 4),
        ],
        4,
        "front_exchange",
    )


def back_kernel(
    state,
    decay,
    dkv,
    part,
    resid,
    b_dn,
    leaving,
    out,
    mixed,
    low_dn,
    msg,
    got,
    ent,
    mate_buf,
    both,
    gathered,
    *scratch,
):
    place = ctx_place()
    ctx, tp, y, x = place
    tp_at = tp_place()
    c = tp % 2
    mate = (ctx, tp + 1 - 2 * c)
    pack_state(state, decay, msg)
    greet(ctx_peers(ctx, tp) + tp_peers(*tp_at))
    s_one, s_two, s_mate = scratch[0:2], scratch[2:4], scratch[4:6]
    bufs, more, sems = scratch[6:13], scratch[13:20], scratch[20:]
    one = swap_start(msg, got, s_one, place)
    half = dkv.shape[1] // 2
    mine = pl.ds(pl.multiple_of(c * half, half), half)
    other = pl.ds(pl.multiple_of((1 - c) * half, half), half)
    cps = [
        send(dkv.at[pl.ds(4 * k, 4), other], mate_buf.at[pl.ds(4 * k, 4)], s_mate, k, mate)
        for k in range(4)
    ]
    first_z = reduce_start(part, more, tp_at)
    got[ctx] = msg[ctx]
    for k in range(4):
        cps[k].wait_recv()
        for i in range(4 * k, 4 * k + 4):
            both[i] = (dkv[i, mine].astype(F32) + mate_buf[i].astype(F32)).astype(BF)
    first = scatter_start(both, bufs, place)
    second_z = reduce_middle(part, more, tp_at, first_z)
    for cp in one:
        cp.wait_recv()
    prefix_into(range(15, -1, -1), got, ent)
    two = swap_start(ent, leaving, s_two, place)
    leaving[ctx] = ent[ctx]
    total = reduce_end(part, more, tp_at, first_z, second_z)
    width = resid.shape[1]
    low = total[:, width:].astype(BF)
    gathered[tp, :, :width] = (resid[...] + total[:, :width] + dot(low, b_dn[...])).astype(BF)
    gathered[tp, :, width:] = low
    started = share_start(gathered, sems, tp_at)
    second = scatter_middle(both, out, bufs, place, first)
    scatter_end(both, out, bufs, first, second)
    share_end(gathered, sems, tp_at, started)
    for k in range(8):
        mixed[k] = gathered[k, :, :width].astype(F32)
        low_dn[k] = gathered[k, :, width:]
    for cp in two:
        cp.wait_recv()
    for cp in one + two + cps:
        cp.wait_send()


def back_exchange(state, decay, dkv, part, resid, b_dn):
    width = decay.shape[1]
    _, tall, cols = dkv.shape
    _, rows, wide = part.shape
    half = tall // 2
    model = resid.shape[1]
    return call(
        back_kernel,
        [
            ((16, 16, width), BF),
            ((half, cols), F32),
            ((8, rows, model), F32),
            ((8, rows, wide - model), BF),
        ],
        [state.reshape(16, 16, width), decay, dkv, part, resid, b_dn],
        [
            pltpu.VMEM((16, 16, width + 128), BF),
            pltpu.VMEM((16, 16, width + 128), BF),
            pltpu.VMEM((16, 16, width), BF),
            pltpu.VMEM((16, half, cols), BF),
            pltpu.VMEM((16, half, cols), BF),
            pltpu.VMEM(part.shape, BF),
            *pair(15),
            *pair(15),
            *pair(4),
            *scatter_bufs(half, cols),
            *reduce_bufs(rows, wide),
            *share_sems(),
        ],
        5,
        "back_exchange",
    )


def tail_kernel(
    part,
    part_two,
    source,
    gain,
    grad_resid,
    a_in,
    a_sh,
    mask,
    gain_two,
    normed_one,
    grad_one,
    low_in,
    low_sh,
    merged,
    grad_low_out,
    normed_two,
    grad_low_gu,
    grad_mixer,
    low_out,
    out_grad,
    low_dn,
    head,
    input_grad,
    big_out,
    small_out,
    shared,
    head_out,
    gathered,
    gains,
    turned,
    big,
    small,
    b_in_sum,
    mine,
    heads,
    *scratch,
):
    width = source.shape[1]
    rank = a_in.shape[1]
    place = ctx_place()
    tp_at = tp_place()
    ctx, tp = place[:2]
    greet(ctx_peers(ctx, tp) + tp_peers(*tp_at))
    bufs_z, more_z, sems, sems_g = scratch[:7], scratch[7:14], scratch[14:18], scratch[18:22]
    bufs, more, s_head, sems_s = scratch[22:29], scratch[29:36], scratch[36:38], scratch[38:]
    first_z = reduce_start(part, bufs_z, tp_at)
    first_two = reduce_start(part_two, more_z, tp_at)
    second_z = reduce_middle(part, bufs_z, tp_at, first_z)
    second_two = reduce_middle(part_two, more_z, tp_at, first_two)
    sent = [send(head, heads.at[ctx], s_head, d - 1, ((ctx + d) % 16, tp)) for d in range(1, 16)]
    heads[ctx] = head[...]
    b_in_sum[...] = dot_tn(low_in[...], grad_one[...])

    def weights(j, carry):
        turned[j] = cut_t(normed_one, j)
        big[j, 0:128] = dot(turned[j], grad_one[...]).astype(BF)
        big[j, 128:144] = eight(b_in_sum, j).astype(BF)
        return carry

    lax.fori_loop(0, 16, weights, 0)
    first = scatter_start(big, bufs, place)
    total = reduce_end(part, bufs_z, tp_at, first_z, second_z)
    grad_low_in = (total[:, width : width + rank] * mask[...]).astype(BF)
    grad_low_sh = (total[:, width + rank :] * mask[...]).astype(BF)
    grad = total[:, :width] + dot_nt(grad_low_in, a_in[...]) + dot_nt(grad_low_sh, a_sh[...])
    grad_v, grad_gain = norm_back(source[...].astype(F32), gain[...], grad)
    gathered[tp, :, :width] = (grad_resid[...] + grad_v).astype(BF)
    gathered[tp, :, width : width + rank] = grad_low_in
    gathered[tp, :, width + rank :] = grad_low_sh
    gains[tp, 0:1] = grad_gain
    gains[tp, 1:2] = gain_two[...]
    gains[tp, 2:8] = jnp.zeros((6, width), F32)
    started = share_start(gathered, sems, tp_at)
    started_g = share_start(gains, sems_g, tp_at)

    slot = pl.ds(pl.multiple_of(tp * 16, 16), 16)
    a_out_sum = dot_tn(merged[...], grad_low_out[...])
    for j in range(16):
        small[j, 160:192] = a_out_sum[j * 32 : (j + 1) * 32].astype(BF)

    def keep(j, row, block):
        mine[...] = block
        small[j, row : row + 16] = mine[slot].astype(BF)

    for row, low, tall in (
        (208, grad_low_gu, normed_two),
        (224, low_out, grad_mixer),
        (240, low_dn, out_grad),
    ):
        low_t = low[...].T

        def maps(j, carry):
            cols = tall[:, pl.ds(pl.multiple_of(j * 128, 128), 128)]
            keep(j, row, dot(low_t, cols).T)
            return carry

        lax.fori_loop(0, 16, maps, 0)
    two = reduce_end(part_two, more_z, tp_at, first_two, second_two).astype(BF)
    b_in_sum[:, :128] = dot_tn(low_sh[...], two)

    def shared_maps(j, carry):
        small[j, 0:128] = dot(turned[j], two).astype(BF)
        return carry

    lax.fori_loop(0, 16, shared_maps, 0)
    share_end(gains, sems_g, tp_at, started_g)
    gain_sum = jnp.sum(gains[...], axis=0)
    for j in range(16):
        small[j, 144:160] = jnp.concatenate(
            [b_in_sum[8 * j : 8 * j + 8, :128], gain_sum[:, 128 * j : 128 * (j + 1)]], axis=0
        ).astype(BF)
    share_end(gathered, sems, tp_at, started)
    for row, lo in ((192, width), (128, width + rank)):
        low = gathered[:, :, lo : lo + rank].reshape(-1, rank)

        def last_maps(j, carry):
            keep(j, row, dot(turned[j], low))
            return carry

        lax.fori_loop(0, 16, last_maps, 0)
    first_s = scatter_start(small, more, place)
    second = scatter_middle(big, big_out, bufs, place, first)
    for k in range(8):
        input_grad[k] = gathered[k, :, :width].astype(F32)
    second_s = scatter_middle(small, small_out, more, place, first_s)
    scatter_end(small, small_out, more, first_s, second_s)
    shared[tp] = small_out[pl.ds(0, shared.shape[1])]
    started_s = share_start(shared, sems_s, tp_at)
    scatter_end(big, big_out, bufs, first, second)
    for cp in sent:
        cp.wait_recv()
    head_out[...] = jnp.sum(heads[...], axis=0)
    share_end(shared, sems_s, tp_at, started_s)
    for cp in sent:
        cp.wait_send()


def tail_exchange(*args):
    part, part_two, source = args[:3]
    grad_one, head = args[10], args[-1]
    _, rows, wide = part.shape
    _, tall, cols = part_two.shape
    width = source.shape[1]
    deep = grad_one.shape[1]
    return call(
        tail_kernel,
        [
            ((8, rows, width), F32),
            ((144, deep), F32),
            ((256, 128), F32),
            ((8, 152, 128), F32),
            (head.shape, F32),
        ],
        list(args),
        [
            pltpu.VMEM(part.shape, BF),
            pltpu.VMEM((8, 8, width), F32),
            pltpu.VMEM((16, 128, tall), BF),
            pltpu.VMEM((16, 144, deep), BF),
            pltpu.VMEM((16, 256, 128), BF),
            pltpu.VMEM((128, deep), F32),
            pltpu.VMEM((128, 128), F32),
            pltpu.VMEM((16,) + head.shape, F32),
            *reduce_bufs(rows, wide),
            *reduce_bufs(tall, cols),
            *share_sems(),
            *share_sems(),
            *scatter_bufs(144, deep),
            *scatter_bufs(256, 128),
            *pair(15),
            *share_sems(),
        ],
        6,
        "tail_exchange",
    )


def flash_kernel(scale, at, q_t, kv, start, out_t, lse):
    ctx = at[0]
    block, size = kv.shape[1], q_t.shape[1]
    queries = q_t[...]
    begin = start[...]

    def step(i, carry, diagonal):
        top, total, acc = carry
        s = dot(kv[i, :, :HD], queries)
        key = i * block + lax.broadcasted_iota(jnp.int32, s.shape, 0)
        allowed = key >= begin
        if diagonal:
            allowed &= key <= ctx * block + lax.broadcasted_iota(jnp.int32, s.shape, 1)
        s = jnp.where(allowed, s * scale, -1e30)
        new = jnp.maximum(top, jnp.max(s, axis=0, keepdims=True))
        p = jnp.where(allowed, jnp.exp(s - new), 0.0)
        fade = jnp.exp(top - new)
        total = total * fade + jnp.sum(p, axis=0, keepdims=True)
        acc = acc * fade + dot_tn(kv[i, :, HD:], p.astype(BF))
        return new, total, acc

    carry = (
        jnp.full((1, size), -1e30, F32),
        jnp.zeros((1, size), F32),
        jnp.zeros((HD, size), F32),
    )
    carry = lax.fori_loop(at[1], ctx, lambda i, k: step(i, k, False), carry)
    top, total, acc = step(ctx, carry, True)
    out_t[...] = acc / total
    lse[...] = top + jnp.log(total)


def plain_call(kernel, outs, ins, specs, name):
    return pl.pallas_call(
        kernel,
        out_shape=[jax.ShapeDtypeStruct(s, d) for s, d in outs],
        in_specs=specs,
        out_specs=[VM] * len(outs),
        compiler_params=pltpu.CompilerParams(vmem_limit_bytes=56 << 20),
        name=name,
    )(*ins)


def flash_forward(at, q_t, kv, start, scale):
    return plain_call(
        functools.partial(flash_kernel, scale),
        [(q_t.shape, F32), ((1, q_t.shape[1]), F32)],
        [at, q_t, kv, start],
        [SM, VM, VM, VM],
        "flash_forward",
    )


def flash_back_kernel(scale, at, q_t, q, kv, start, lse, grad_t, grad, delta, dq_t, dkv):
    ctx = at[0]
    block = kv.shape[1]
    dkv[...] = jnp.zeros(dkv.shape, BF)
    queries_t, queries = q_t[...], q[...]
    og_t, og = grad_t[...], grad[...]
    begin, offset, low = start[...], lse[...], delta[...]

    def step(i, acc, diagonal):
        keys = kv[i, :, :HD]
        s = dot(keys, queries_t)
        key = i * block + lax.broadcasted_iota(jnp.int32, s.shape, 0)
        allowed = key >= begin
        if diagonal:
            allowed &= key <= ctx * block + lax.broadcasted_iota(jnp.int32, s.shape, 1)
        p = jnp.exp(jnp.where(allowed, s * scale - offset, -1e30))
        dp = dot(kv[i, :, HD:], og_t)
        ds = (p * (dp - low)).astype(BF)
        dkv[i, :, :HD] = (dot(ds, queries) * scale).astype(BF)
        dkv[i, :, HD:] = dot(p.astype(BF), og).astype(BF)
        return acc + dot_tn(keys, ds)

    acc = jnp.zeros(q_t.shape, F32)
    acc = lax.fori_loop(at[1], ctx, lambda i, k: step(i, k, False), acc)
    dq_t[...] = step(ctx, acc, True) * scale


def flash_backward(at, q_t, q, kv, start, lse, grad_t, grad, delta, scale):
    return plain_call(
        functools.partial(flash_back_kernel, scale),
        [(q_t.shape, F32), (kv.shape, BF)],
        [at, q_t, q, kv, start, lse, grad_t, grad, delta],
        [SM] + [VM] * 8,
        "flash_backward",
    )


def soft_plus(values):
    return jnp.maximum(values, 0.0) + jnp.log1p(jnp.exp(-jnp.abs(values)))


def doc_index(positions, doc_lengths):
    bounds = jnp.cumsum(doc_lengths)
    return jnp.sum((positions[:, None] >= bounds[None, :]).astype(jnp.int32), axis=1)


def adapter_mask(doc_ids, adapter_ids, columns):
    seq_count = adapter_ids.shape[0]
    chosen = jnp.sum(
        jnp.where(doc_ids[:, None] == jnp.arange(seq_count)[None, :], adapter_ids[None, :], 0),
        axis=1,
    )
    return (chosen[:, None] == jnp.arange(columns)[None, :] // RANK).astype(F32)


def spread(per_head):
    return jnp.repeat(per_head, MHEAD, axis=1)


def by_head(flat):
    return flat.reshape(flat.shape[0], -1, MHEAD).transpose(1, 0, 2)


def flat_heads(split):
    return split.transpose(1, 0, 2).reshape(split.shape[1], -1)


def body(
    hidden_in,
    norm_gains,
    w_in,
    w_shared,
    w_dt,
    head_params,
    w_out,
    w_gu,
    w_down,
    a_in,
    b_in,
    a_sh,
    b_sh,
    a_out,
    b_out,
    a_gu,
    b_gu,
    a_dn,
    b_dn,
    adapter_ids,
    doc_lengths,
    out_grad,
):
    rows, width = hidden_in.shape
    heads = head_params.shape[1]
    inner = heads * MHEAD
    tp_count = lax.axis_size("tp")
    share = rows // tp_count
    ctx_at = lax.axis_index("ctx")
    tp_at = lax.axis_index("tp")
    positions = ctx_at * rows + jnp.arange(rows, dtype=jnp.int32)
    doc_ids = doc_index(positions, doc_lengths)
    doc_before = doc_index(jnp.maximum(positions[:1] - 1, 0), doc_lengths)[0]
    bounds = jnp.cumsum(doc_lengths)
    starts = jnp.sum(
        jnp.where(doc_ids[:, None] == jnp.arange(1, 1 + bounds.shape[0])[None, :], bounds[None, :], 0),
        axis=1,
    )
    starts_row = starts[None, :]
    at = jnp.stack([ctx_at, jnp.min(starts) // rows]).astype(jnp.int32)
    mask = adapter_mask(doc_ids, adapter_ids, a_in.shape[1])

    def rows_of(array):
        return lax.dynamic_slice_in_dim(array, tp_at * share, share, 0)

    mask_rows = rows_of(mask)
    w_in = w_in.reshape(width, -1)
    b_in = b_in.reshape(b_in.shape[0], -1)
    w_out = w_out.reshape(-1, width)
    a_out = a_out.reshape(-1, a_out.shape[2])
    w_gu = w_gu.reshape(width, -1)
    b_gu = b_gu.reshape(b_gu.shape[0], -1)
    hidden = w_down.shape[0]
    rank = a_in.shape[1]
    scale = HD ** (-0.5)
    gain_one, gain_two = norm_gains[0:1], norm_gains[1:2]
    source = hidden_in.astype(F32)
    normed_one = (source * norm_scale(source) * gain_one).astype(BF)
    low_in = (dot(normed_one, a_in) * mask).astype(BF)
    h_one = (dot(normed_one, w_in) + dot(low_in, b_in)).astype(BF)
    low_sh = (dot(normed_one, a_sh) * mask).astype(BF)
    h_two = (dot(normed_one, w_shared) + dot(low_sh, b_sh)).astype(BF)
    dt_raw = dot(normed_one, w_dt)
    gate = h_one[:, :inner].astype(F32)
    xs = h_one[:, inner : 2 * inner]
    xs_f = xs.astype(F32)
    q = h_one[:, 2 * inner :]
    q_t = q.T
    bm, cm = h_two[:, :STATE], h_two[:, STATE : 2 * STATE]
    kv_group = tp_at // (QHEADS // KVH)
    key_col = 2 * STATE + kv_group * HD
    keys_mine = lax.dynamic_slice_in_dim(h_two, key_col, HD, 1)
    vals_mine = lax.dynamic_slice_in_dim(h_two, key_col + KVH * HD, HD, 1)

    pre = dt_raw + head_params[0]
    dt = soft_plus(pre)
    rate = jnp.exp(head_params[1])
    order = jnp.arange(rows)
    tri = (order[:, None] >= order[None, :]).astype(F32)
    decay = jnp.dot(tri, -dt * rate, precision=lax.Precision.HIGHEST)
    decay_t, dt_t = decay.T, dt.T
    allowed = (order[:, None] >= order[None, :]) & (doc_ids[:, None] == doc_ids[None, :])
    gap = jnp.where(allowed[None], decay_t[:, :, None] - decay_t[:, None, :], -1e30)
    fade = jnp.exp(gap)
    inter = dot_nt(cm, bm)
    pulls = inter[None] * fade
    mixing = (pulls * dt_t[:, None, :]).astype(BF)
    xs_h = by_head(xs)
    inner_y = flat_heads(
        lax.dot_general(mixing, xs_h, (((2,), (1,)), ((0,), (0,))), preferred_element_type=F32)
    )
    tail = jnp.where(
        (doc_ids == doc_ids[-1])[:, None], jnp.exp(decay[-1][None, :] - decay), 0.0
    )
    tail_dt = tail * dt
    state_out = dot_tn(bm, (spread(tail_dt) * xs_f).astype(BF))
    total_decay = jnp.exp(decay[-1]) * (doc_ids[-1] == doc_before).astype(F32)
    total_wide = jnp.repeat(total_decay, MHEAD)[None, :]
    entering, kv_all = front_exchange(
        state_out, total_wide, jnp.concatenate([keys_mine, vals_mine], axis=1)
    )
    entering_low = entering.reshape(STATE, inner)
    entering = entering_low.astype(F32)
    reach = spread(jnp.exp(decay) * (doc_ids == doc_before).astype(F32)[:, None])
    cross = dot(cm, entering_low) * reach
    skip = jnp.repeat(head_params[2], MHEAD)[None, :]
    ssd = inner_y + cross + skip * xs_f
    gate_sig = jax.nn.sigmoid(gate)
    gated = ssd * (gate * gate_sig)

    attn_t, lse = flash_forward(at, q_t, kv_all, starts_row, scale)
    merged = jnp.concatenate([gated, attn_t.T], axis=1).astype(BF)
    low_out_part = dot(merged, a_out) * mask
    mix_part = jnp.concatenate([dot(merged, w_out).astype(BF), low_out_part.astype(BF)], axis=1)
    shared_mix, resid = mixer_exchange(
        mix_part.reshape(tp_count, share, -1), rows_of(hidden_in), gain_two, b_out
    )
    shared_mix = shared_mix.reshape(rows, -1)
    normed_two, low_out = shared_mix[:, :width], shared_mix[:, width:]

    low_gu = (dot(normed_two, a_gu) * mask).astype(BF)
    h_gu = (dot(normed_two, w_gu) + dot(low_gu, b_gu)).astype(BF).astype(F32)
    gate_mlp, up = h_gu[:, :hidden], h_gu[:, hidden:]
    sig = jax.nn.sigmoid(gate_mlp)
    act = (gate_mlp * sig * up).astype(BF)
    low_dn_part = dot(act, a_dn) * mask
    mlp_part = dot(act, w_down)
    grad_low_dn = (dot_nt(out_grad, b_dn) * mask).astype(BF)
    grad_act = (dot_nt(out_grad, w_down) + dot_nt(grad_low_dn, a_dn)).astype(BF).astype(F32)
    grad_gu = jnp.concatenate(
        [grad_act * up * sig * (1.0 + gate_mlp * (1.0 - sig)), grad_act * (gate_mlp * sig)], axis=1
    ).astype(BF)
    grad_low_gu_part = dot_nt(grad_gu, b_gu)
    grad_two_part = dot_nt(grad_gu, w_gu)
    part = jnp.concatenate([grad_two_part.astype(BF), grad_low_gu_part.astype(BF)], axis=1)
    shared_mlp, grad_resid, gain_part_two, early = mlp_exchange(
        part.reshape(tp_count, share, -1),
        resid,
        gain_two,
        rows_of(out_grad),
        a_gu,
        mask_rows,
        normed_two,
        grad_gu,
        out_grad,
        act,
        low_gu,
        grad_low_dn,
    )
    early_rows = early.shape[1]
    early = lax.psum_scatter(
        early.reshape(16 * early_rows, -1), "ctx", scatter_dimension=0, tiled=True
    )
    shared_mlp = shared_mlp.reshape(rows, -1)
    grad_mixer, grad_low_gu = shared_mlp[:, :width], shared_mlp[:, width:]

    grad_low_out = (dot_nt(grad_mixer, b_out) * mask).astype(BF)
    grad_merged = (dot_nt(grad_mixer, w_out) + dot_nt(grad_low_out, a_out)).astype(BF)
    late = dot_tn(grad_mixer, merged).astype(BF)
    late = lax.psum_scatter(late, "ctx", scatter_dimension=0, tiled=True)
    grad_gated = grad_merged[:, :inner].astype(F32)
    grad_attn = grad_merged[:, inner:]
    grad_ssd = grad_gated * (gate * gate_sig)
    grad_gate = grad_gated * ssd * gate_sig * (1.0 + gate * (1.0 - gate_sig))
    grad_attn_t = grad_attn.T
    delta = jnp.sum(grad_attn_t.astype(F32) * attn_t, axis=0, keepdims=True)
    dq_t, dkv = flash_backward(
        at, q_t, q, kv_all, starts_row, lse, grad_attn_t, grad_attn, delta, scale
    )
    dy = grad_ssd.astype(BF)
    dy_h = by_head(dy)
    reached = (reach * grad_ssd).astype(BF)
    pull_state = dot_tn(cm, reached)
    mlp_rows = jnp.concatenate([mlp_part.astype(BF), low_dn_part.astype(BF)], axis=1)
    leaving, dkv_sum, mixed, low_dn = back_exchange(
        pull_state, total_wide, dkv, mlp_rows.reshape(tp_count, share, -1), resid, b_dn
    )
    mixed, low_dn = mixed.reshape(rows, -1), low_dn.reshape(rows, -1)
    leaving_low = leaving.reshape(STATE, inner)
    leaving = leaving_low.astype(F32)
    d_mix = lax.dot_general(dy_h, xs_h, (((2,), (2,)), ((0,), (0,))), preferred_element_type=F32)
    d_inter = jnp.sum(d_mix * (fade * dt_t[:, None, :]), axis=0).astype(BF)
    weighted = d_mix * pulls
    col = jnp.sum(weighted, axis=1).T
    row = jnp.sum(weighted * dt_t[:, None, :], axis=2).T
    dx_inner = flat_heads(
        lax.dot_general(mixing, dy_h, (((1,), (1,)), ((0,), (0,))), preferred_element_type=F32)
    )
    from_state = dot(bm, leaving_low)

    def head_sums(flat):
        return jnp.sum(flat.reshape(flat.shape[0], heads, MHEAD), axis=2)

    held = head_sums(from_state * xs_f) * tail
    d_cross = head_sums(cross * grad_ssd)
    d_decay = row - col * dt + d_cross - held * dt
    d_last = jnp.sum(held * dt, axis=0) + total_decay * head_sums(
        jnp.sum(leaving * entering, axis=0)[None]
    )[0]
    d_log = jnp.dot(tri.T, d_decay, precision=lax.Precision.HIGHEST) + d_last[None, :]
    grad_dt = (col + held - rate * d_log) * jax.nn.sigmoid(pre)
    grad_x = dx_inner + spread(tail_dt) * from_state + skip * grad_ssd
    grad_bm = dot_tn(d_inter, cm) + dot_nt((spread(tail_dt) * xs_f).astype(BF), leaving_low)
    grad_cm = dot(d_inter, bm) + dot_nt(reached, entering_low)
    grad_head = jnp.stack(
        [
            jnp.sum(grad_dt, axis=0),
            -jnp.sum(dt * rate * d_log, axis=0),
            jnp.sum(head_sums(grad_ssd * xs_f), axis=0),
        ]
    )
    grad_one = jnp.concatenate([grad_gate, grad_x, dq_t.T], axis=1).astype(BF)
    half = rows // 2
    dkv_rows = lax.dynamic_update_slice_in_dim(
        jnp.zeros((rows, 2 * HD), F32), dkv_sum, (tp_at % 2) * half, 0
    ).astype(BF)
    group = (jnp.arange(KVH) == kv_group).astype(BF)[None, :, None]
    grad_two = jnp.concatenate(
        [
            grad_bm.astype(BF),
            grad_cm.astype(BF),
            (dkv_rows[:, None, :HD] * group).reshape(rows, KVH * HD),
            (dkv_rows[:, None, HD:] * group).reshape(rows, KVH * HD),
        ],
        axis=1,
    )
    grad_dt_low = grad_dt.astype(BF)
    norm_part = dot_nt(grad_one, w_in) + dot_nt(grad_two, w_shared) + dot_nt(grad_dt_low, w_dt)
    part = jnp.concatenate(
        [
            norm_part.astype(BF),
            dot_nt(grad_one, b_in).astype(BF),
            dot_nt(grad_two, b_sh).astype(BF),
        ],
        axis=1,
    )
    two_blocks = grad_two.reshape(rows, tp_count, -1).transpose(1, 0, 2)
    pad_dt = jnp.concatenate([grad_one, grad_dt_low, jnp.zeros((rows, 128 - heads), BF)], axis=1)
    head_tile = jnp.pad(grad_head, ((0, 5), (0, 128 - heads)))
    input_grad, big_sum, small_sum, shared, head_sum = tail_exchange(
        part.reshape(tp_count, share, -1),
        two_blocks,
        rows_of(hidden_in),
        gain_one,
        grad_resid,
        a_in,
        a_sh,
        mask_rows,
        gain_part_two,
        normed_one,
        pad_dt,
        low_in,
        low_sh,
        merged,
        grad_low_out,
        normed_two,
        grad_low_gu,
        grad_mixer,
        low_out,
        out_grad,
        low_dn,
        head_tile,
    )
    deep = width // 16
    out_shared = shared[:, :deep].transpose(1, 0, 2).reshape(deep, -1)
    out_a_sh = shared[:, deep : deep + 16].reshape(deep, -1)
    out_b_sh = shared[:, deep + 16 : deep + 24].transpose(1, 0, 2).reshape(8, -1)
    spot_at = deep + 24
    out_gain = small_sum[spot_at : spot_at + 2]
    spot_at += 8
    out_a_out = small_sum[spot_at : spot_at + 32]
    spot_at += 32
    four = [small_sum[spot_at + 16 * k : spot_at + 16 * (k + 1)] for k in range(4)]
    early = early.astype(F32)
    return (
        mixed,
        input_grad.reshape(rows, width),
        out_gain,
        big_sum[:deep, : w_in.shape[1]].reshape(deep, 1, -1),
        out_shared,
        big_sum[:deep, w_in.shape[1] : w_in.shape[1] + heads],
        head_sum[:3, :heads],
        late.astype(F32).T[None],
        early[:deep, : 2 * hidden].reshape(deep, 2, hidden),
        early[:deep, 2 * hidden :].T,
        four[0],
        big_sum[deep : deep + 8, : w_in.shape[1]].reshape(8, 1, -1),
        out_a_sh,
        out_b_sh,
        out_a_out[None],
        four[2].T,
        four[1],
        early[deep : deep + 8, : 2 * hidden].reshape(8, 2, hidden),
        early[deep : deep + 8, 2 * hidden :].T,
        four[3].T,
    )
def solution(mesh):
    placed = (
        P("ctx", None),
        P(),
        P(None, "tp", None),
        P(),
        P(None, "tp"),
        P(None, "tp"),
        P("tp", None, None),
        P(None, None, "tp"),
        P("tp", None),
        P(),
        P(None, "tp", None),
        P(),
        P(),
        P("tp", None, None),
        P(),
        P(),
        P(None, None, "tp"),
        P("tp", None),
        P(),
        P(),
        P(),
        P("ctx", None),
    )
    return jax.shard_map(
        body,
        mesh=mesh,
        in_specs=placed,
        out_specs=(
            P("ctx", None),
            P("ctx", None),
            P(None, "ctx"),
            P("ctx", "tp", None),
            P("ctx", None),
            P("ctx", "tp"),
            P(None, "tp"),
            P("tp", None, "ctx"),
            P("ctx", None, "tp"),
            P("tp", "ctx"),
            P(("ctx", "tp"), None),
            P("ctx", "tp", None),
            P("ctx", None),
            P("ctx", None),
            P("tp", "ctx", None),
            P(None, ("ctx", "tp")),
            P(("ctx", "tp"), None),
            P("ctx", None, "tp"),
            P("tp", "ctx"),
            P(None, ("ctx", "tp")),
        ),
        check_vma=False,
    )
```

```python
import functools

import jax
import jax.numpy as jnp
from jax import lax
from jax.experimental import pallas as pl
from jax.experimental.pallas import tpu as pltpu
from jax.sharding import PartitionSpec as P

MHEAD = 64
STATE = 256
QHEADS = 8
KVH = 2
HD = 128
RANK = 16
NORM_EPSILON = 1e-06

MESH = pl.DeviceIdType.MESH
VM = pl.BlockSpec(memory_space=pltpu.VMEM)
SM = pl.BlockSpec(memory_space=pltpu.SMEM)
HB = pl.BlockSpec(memory_space=pl.ANY)
BF = jnp.bfloat16
F32 = jnp.float32
DMA = pltpu.SemaphoreType.DMA
OFFSETS = (2, 1, 3)


def call(kernel, outs, ins, scratch, cid, name, specs=None):
    return pl.pallas_call(
        kernel,
        out_shape=[jax.ShapeDtypeStruct(s, d) for s, d in outs],
        in_specs=specs or [VM] * len(ins),
        out_specs=[VM] * len(outs),
        scratch_shapes=scratch,
        compiler_params=pltpu.CompilerParams(
            collective_id=cid, has_side_effects=True, vmem_limit_bytes=56 << 20
        ),
        name=name,
    )(*ins)


def greet(peers):
    barrier = pltpu.get_barrier_semaphore()
    for peer in peers:
        pl.semaphore_signal(barrier, inc=1, device_id=peer, device_id_type=MESH)


def met(peers):
    pl.semaphore_wait(pltpu.get_barrier_semaphore(), len(peers))


def send(src, dst, sems, slot, peer):
    cp = pltpu.make_async_remote_copy(
        src_ref=src,
        dst_ref=dst,
        send_sem=sems[0].at[slot],
        recv_sem=sems[1].at[slot],
        device_id=peer,
        device_id_type=MESH,
    )
    cp.start()
    return cp


def pair(*shape):
    return [DMA(shape), DMA(shape)]


def tp_place():
    ctx = lax.axis_index("ctx")
    tp = lax.axis_index("tp")
    return ctx, tp, tp // 2, tp % 2


def tp_peers(ctx, tp, z, c):
    return [(ctx, ((z + d) % 4) * 2 + c) for d in (1, 2, 3)] + [(ctx, z * 2 + 1 - c)]


def reduce_bufs(rows, width):
    return [
        pltpu.VMEM((4, rows, width), BF),
        pltpu.VMEM((3, rows, width), BF),
        pltpu.VMEM((3, rows, width), BF),
        *pair(4),
        *pair(3),
    ]


def chips(place):
    ctx, tp, z, c = place
    return (z + 2) % 4, (z + 1 + 2 * c) % 4, (z + 3 - 2 * c) % 4, z


def reduce_pass(part, bufs, place, k):
    ctx, tp, z, c = place
    chip = chips(place)[(0, 2, 1, 3)[k]]
    return send(part.at[chip * 2 + 1 - c], bufs[0].at[k], bufs[3:5], k, (ctx, z * 2 + 1 - c))


def reduce_send(part, bufs, place, passed, k, relayed=None):
    sib, snd, rcv = bufs[:3]
    ctx, tp, z, c = place
    two, way, other, own = chips(place)
    passed.wait_recv()
    both = part[(two, way, other)[k] * 2 + c].astype(F32) + sib[k].astype(F32)
    if k == 1:
        relayed.wait_recv()
        both = both + rcv[0].astype(F32)
    snd[k] = both.astype(BF)
    to = other if k == 2 else way
    return send(snd.at[k], rcv.at[k], bufs[5:7], k, (ctx, to * 2 + c))


def reduce_start(part, bufs, place):
    return [reduce_pass(part, bufs, place, k) for k in range(4)]


def reduce_middle(part, bufs, place, first):
    two = reduce_send(part, bufs, place, first[0], 0)
    other = reduce_send(part, bufs, place, first[2], 2)
    return [two, None, other]


def reduce_relay(part, bufs, place, first, second):
    second[1] = reduce_send(part, bufs, place, first[1], 1, second[0])


def reduce_end(part, bufs, place, first, second):
    sib, snd, rcv = bufs[:3]
    first[3].wait_recv()
    total = part[place[1]].astype(F32) + sib[3].astype(F32)
    for k in (2, 1):
        second[k].wait_recv()
        total = total + rcv[k].astype(F32)
    for cp in first + second:
        cp.wait_send()
    return total


def share_sems():
    return [*pair(3), *pair(4)]


def share_start(out, sems, place):
    ctx, tp, z, c = place
    two, way, other, own = chips(place)
    return [
        send(out.at[tp], out.at[tp], sems[:2], 0, (ctx, way * 2 + c)),
        send(out.at[tp], out.at[tp], sems[:2], 1, (ctx, other * 2 + c)),
        send(out.at[tp], out.at[tp], sems[2:], 0, (ctx, z * 2 + 1 - c)),
    ]


def share_pass(out, sems, place, started, k):
    ctx, tp, z, c = place
    two, way, other, own = chips(place)
    mate = (ctx, z * 2 + 1 - c)
    at = (other, way, two)[k] * 2 + c
    if k == 2:
        started[3].wait_recv()
    else:
        started[k].wait_recv()
    if k == 0:
        started.append(send(out.at[at], out.at[at], sems[:2], 2, (ctx, way * 2 + c)))
    passed = send(out.at[at], out.at[at], sems[2:], k + 1, mate)
    return passed


def share_end(out, sems, place, started, passed=()):
    passed = list(passed)
    passed += [share_pass(out, sems, place, started, k) for k in range(len(passed), 3)]
    started[2].wait_recv()
    for cp in passed:
        cp.wait_recv()
    for cp in started + passed:
        cp.wait_send()


def norm_scale(v):
    return lax.rsqrt(jnp.mean(v * v, axis=-1, keepdims=True) + NORM_EPSILON)


def norm_back(v, gain, grad):
    r = norm_scale(v)
    pulled = grad * gain
    inner = jnp.mean(pulled * v, axis=-1, keepdims=True)
    grad_v = r * pulled - v * (r * r * r) * inner
    return grad_v, jnp.sum(grad * v * r, axis=0, keepdims=True)


def dot(a, b):
    return jnp.dot(a, b, preferred_element_type=F32)


def dot_nt(a, b):
    return lax.dot_general(a, b, (((1,), (1,)), ((), ())), preferred_element_type=F32)


def dot_tn(a, b):
    return lax.dot_general(a, b, (((0,), (0,)), ((), ())), preferred_element_type=F32)


def dot_f(a, b):
    return jnp.dot(a, b, precision=lax.Precision.HIGHEST, preferred_element_type=F32)


def cut_t(ref, j):
    return ref[:, pl.ds(pl.multiple_of(j * 128, 128), 128)].T


def eight(ref, j):
    rows = ref[pl.ds(pl.multiple_of(j * 8, 8), 8)]
    return jnp.concatenate([rows, jnp.zeros_like(rows)], axis=0)


def fetch(src, dst, sem):
    cp = pltpu.make_async_copy(src, dst, sem)
    cp.start()
    return cp


def soft_plus(values):
    return jnp.maximum(values, 0.0) + jnp.log1p(jnp.exp(-jnp.abs(values)))


def pick(t, lengths, values):
    one = lengths[0]
    two = one + lengths[1]
    three = two + lengths[2]
    return jnp.where(
        t >= three,
        values[3],
        jnp.where(t >= two, values[2], jnp.where(t >= one, values[1], values[0])),
    )


def doc_start(t, lengths):
    one = lengths[0]
    two = one + lengths[1]
    return pick(t, lengths, (0, one, two, two + lengths[2]))


def iota(shape, axis):
    return lax.broadcasted_iota(jnp.int32, shape, axis)


def expander(heads):
    shape = (128, heads * MHEAD)
    return (iota(shape, 1) // MHEAD == iota(shape, 0)).astype(F32)


def collector(heads):
    shape = (heads * MHEAD, 128)
    return (iota(shape, 0) // MHEAD == iota(shape, 1)).astype(F32)


def spread(per_head, heads):
    return dot_f(per_head, expander(heads))


def head_sums(flat):
    return dot_f(flat, collector(flat.shape[1] // MHEAD))


def one_head(pair, h):
    return jnp.where(iota(pair.shape, 1) // MHEAD == h % 2, pair, jnp.zeros_like(pair))


def running_sum(dst, src, rows, later):
    for i in range(rows // 128):
        shape = (128, rows)
        t, s = i * 128 + iota(shape, 0), iota(shape, 1)
        tri = jnp.where((s >= t) if later else (s <= t), 1.0, 0.0)
        dst[pl.ds(i * 128, 128)] = dot_f(tri, src[...])


def fades(i, base, lengths):
    wide = (i + 1) * 128
    t = base + i * 128 + iota((128, 128), 0)
    start = doc_start(t, lengths)[:, 0:1]
    shape = (128, wide)
    s = base + iota(shape, 1)
    return (s <= base + i * 128 + iota(shape, 0)) & (s >= start)


def mlp_kernel(
    part,
    gain,
    b_out,
    a_gu,
    b_gu,
    a_dn,
    b_dn,
    out_grad,
    mask,
    merged,
    hidden_far,
    w_gu_far,
    w_down_far,
    low_out,
    grad_mixer,
    grad_low_gu,
    resid,
    grad_resid,
    gain_part,
    early,
    late_part,
    normed_mine,
    grad_mine,
    mixer_mine,
    source,
    w_gu,
    w_down,
    shared,
    shared_two,
    part_two,
    grad_act,
    low_dn_grad,
    low_gu,
    act,
    grad_gu,
    turned,
    b_gu_sum,
    a_dn_sum,
    loads,
    *scratch,
):
    place = tp_place()
    tp = place[1]
    peers = tp_peers(*place)
    greet(peers)
    share, model = resid.shape
    hidden = w_down.shape[0]
    rows = out_grad.shape[0]
    each = 128 // share
    rows_mine = pl.ds(pl.multiple_of(tp * share, share), share)
    get_source = fetch(hidden_far.at[rows_mine], source, loads.at[0])
    get_down = fetch(w_down_far, w_down, loads.at[1])
    get_gu = fetch(w_gu_far, w_gu, loads.at[2])
    bufs, sems, more, sems_two = scratch[:7], scratch[7:11], scratch[11:18], scratch[18:]
    met(peers)
    first = reduce_start(part, bufs, place)
    second = reduce_middle(part, bufs, place, first)

    def span_of(i):
        return pl.ds(pl.multiple_of(i * 128, 128), 128)

    get_down.wait()

    def back_first(i, carry):
        at = span_of(i)
        g = out_grad[at]
        low = (dot_nt(g, b_dn[...]) * mask[at]).astype(BF)
        low_dn_grad[at] = low
        grad_act[at] = (dot_nt(g, w_down[...]) + dot_nt(low, a_dn[...])).astype(BF)
        return carry

    slot = pl.ds(pl.multiple_of(tp * 16, 16), 16)

    def weights_two(j, carry):
        turned[...] = cut_t(out_grad, j)
        grad_mine[j] = turned[slot]
        early[j, 0:128, 2 * hidden : 3 * hidden] = dot(turned[...], act[...]).astype(BF)
        return carry

    lax.fori_loop(0, rows // 128, back_first, 0)
    reduce_relay(part, bufs, place, first, second)
    get_source.wait()
    total = reduce_end(part, bufs, place, first, second)
    low = total[:, model:].astype(BF)
    residual = source[...].astype(F32) + total[:, :model] + dot(low, b_out[...])
    resid[...] = residual
    shared[tp, :, :model] = (residual * norm_scale(residual) * gain[...]).astype(BF)
    shared[tp, :, model:] = low
    started = share_start(shared, sems, place)
    get_gu.wait()

    def both_ways(i):
        at = span_of(i)
        block = shared[pl.ds(i * each, each)].reshape(128, -1)
        n = block[:, :model]
        low_out[at] = block[:, model:]
        low = (dot(n, a_gu[...]) * mask[at]).astype(BF)
        low_gu[at] = low
        h = (dot(n, w_gu[...]) + dot(low, b_gu[...])).astype(BF).astype(F32)
        gate, up = h[:, :hidden], h[:, hidden:]
        sig = jax.nn.sigmoid(gate)
        act[at] = (gate * sig * up).astype(BF)
        pulled = grad_act[at].astype(F32)
        grad = jnp.concatenate(
            [pulled * up * sig * (1.0 + gate * (1.0 - sig)), pulled * (gate * sig)], axis=1
        ).astype(BF)
        grad_gu[at] = grad
        full = dot_nt(grad, w_gu[...]).astype(BF)
        low = dot_nt(grad, b_gu[...]).astype(BF)
        for k in range(each):
            part_two[i * each + k, :, :model] = full[k * share : (k + 1) * share]
            part_two[i * each + k, :, model:] = low[k * share : (k + 1) * share]

    chip = chips(place)
    passed = [None] * 3
    started[2].wait_recv()
    both_ways(chip[3])
    third = reduce_pass(part_two, more, place, 3)
    passed[0] = share_pass(shared, sems, place, started, 0)
    passed[1] = share_pass(shared, sems, place, started, 1)
    passed[1].wait_recv()
    both_ways(chip[2])
    pass_one = reduce_pass(part_two, more, place, 1)
    passed[2] = share_pass(shared, sems, place, started, 2)
    passed[0].wait_recv()
    both_ways(chip[1])
    pass_two = reduce_pass(part_two, more, place, 2)
    send_two = reduce_send(part_two, more, place, pass_two, 2)
    passed[2].wait_recv()
    both_ways(chip[0])
    pass_none = reduce_pass(part_two, more, place, 0)
    for cp in started + passed:
        cp.wait_send()

    def forward_rest(i, carry):
        at = span_of(i)
        a = act[at]
        full = dot(a, w_down[...]).astype(BF)
        low = (dot(a, a_dn[...]) * mask[at]).astype(BF)
        for k in range(each):
            late_part[i * each + k, :, :model] = full[k * share : (k + 1) * share]
            late_part[i * each + k, :, model:] = low[k * share : (k + 1) * share]
        return carry

    wide = grad_gu.shape[1]

    def weights(j, carry):
        cols = pl.ds(pl.multiple_of(j * 128, 128), 128)
        turned[...] = shared[:, :, cols].reshape(rows, 128).T
        normed_mine[j] = turned[slot]
        early[j, 0:128, :wide] = dot(turned[...], grad_gu[...]).astype(BF)
        return carry

    send_none = reduce_send(part_two, more, place, pass_none, 0)
    lax.fori_loop(0, 8, weights, 0)
    send_one = reduce_send(part_two, more, place, pass_one, 1, send_none)
    lax.fori_loop(8, 16, weights, 0)
    total = reduce_end(
        part_two, more, place, [pass_none, pass_one, pass_two, third], [send_none, send_one, send_two]
    )
    low = (total[:, model:] * mask[rows_mine]).astype(BF)
    grad = total[:, :model] + dot_nt(low, a_gu[...])
    grad_v, grad_gain = norm_back(resid[...], gain[...], grad)
    grad_r = out_grad[rows_mine].astype(F32) + grad_v
    grad_resid[...] = grad_r
    gain_part[...] = grad_gain
    shared_two[tp, :, :model] = grad_r.astype(BF)
    shared_two[tp, :, model:] = low
    started = share_start(shared_two, sems_two, place)
    b_gu_sum[...] = dot_tn(low_gu[...], grad_gu[...])
    a_dn_sum[...] = dot_tn(low_dn_grad[...], act[...])
    for j in range(16):
        early[j, 128:144, :wide] = eight(b_gu_sum, j).astype(BF)
        early[j, 128:144, wide : 3 * hidden] = eight(a_dn_sum, j).astype(BF)
        early[j, 128:144, 3 * hidden :] = jnp.zeros((16, merged.shape[1]), BF)
    lax.fori_loop(0, rows // 128, forward_rest, 0)
    passed = [share_pass(shared_two, sems_two, place, started, k) for k in (0, 1)]
    lax.fori_loop(0, 16, weights_two, 0)
    share_end(shared_two, sems_two, place, started, passed)
    for k in range(8):
        to = pl.ds(k * share, share)
        grad_mixer[to] = shared_two[k, :, :model]
        grad_low_gu[to] = shared_two[k, :, model:]

    def weights_three(j, carry):
        turned[...] = cut_t(grad_mixer, j)
        mixer_mine[j] = turned[slot]
        early[j, 0:128, 3 * hidden :] = dot(turned[...], merged[...]).astype(BF)
        return carry

    lax.fori_loop(0, 16, weights_three, 0)


def mlp_exchange(
    part, gain, b_out, a_gu, b_gu, a_dn, b_dn, out_grad, mask, merged, hidden_in, w_gu, w_down
):
    _, share, wide = part.shape
    rows, model = out_grad.shape
    hidden = w_down.shape[0]
    rank = a_gu.shape[1]
    return call(
        mlp_kernel,
        [
            ((rows, rank), BF),
            ((rows, model), BF),
            ((rows, rank), BF),
            ((share, model), F32),
            ((share, model), F32),
            ((1, model), F32),
            ((16, 144, 3 * hidden + merged.shape[1]), BF),
            (part.shape, BF),
            ((16, 16, rows), BF),
            ((16, 16, rows), BF),
            ((16, 16, rows), BF),
        ],
        [part, gain, b_out, a_gu, b_gu, a_dn, b_dn, out_grad, mask, merged, hidden_in, w_gu, w_down],
        [
            pltpu.VMEM((share, model), BF),
            pltpu.VMEM(w_gu.shape, BF),
            pltpu.VMEM(w_down.shape, BF),
            pltpu.VMEM(part.shape, BF),
            pltpu.VMEM(part.shape, BF),
            pltpu.VMEM(part.shape, BF),
            pltpu.VMEM((rows, hidden), BF),
            pltpu.VMEM((rows, rank), BF),
            pltpu.VMEM((rows, rank), BF),
            pltpu.VMEM((rows, hidden), BF),
            pltpu.VMEM((rows, 2 * hidden), BF),
            pltpu.VMEM((128, rows), BF),
            pltpu.VMEM((128, 2 * hidden), F32),
            pltpu.VMEM((128, hidden), F32),
            DMA((3,)),
            *reduce_bufs(share, wide),
            *share_sems(),
            *reduce_bufs(share, wide),
            *share_sems(),
        ],
        2,
        "mlp_exchange",
        [VM] * 10 + [HB] * 3,
    )


def ctx_place():
    ctx = lax.axis_index("ctx")
    return ctx, lax.axis_index("tp"), ctx // 4, ctx % 4


def spot(h, fast, slow):
    return slow * 4 + fast if h == 0 else fast * 4 + slow


def scatter_bufs(rows, width):
    most = max(rows - rows // 32 * 16, rows // 32 * 16)
    return [
        pltpu.VMEM((2, 3, most, width), BF),
        pltpu.VMEM((2, 3, 4, most, width), BF),
        pltpu.VMEM((2, 3, most, width), BF),
        *pair(2, 3, 4),
        *pair(2, 3),
    ]


def spans_of(rows):
    half = rows // 32 * 16
    return ((0, half), (half, rows - half))


def scatter_start(part, bufs, place):
    mid, r1, r2, s1s, s1r, s2s, s2r = bufs
    ctx, tp, y, x = place
    spans = spans_of(part.shape[1])
    first = {}
    for j in OFFSETS + (0,):
        for off in OFFSETS:
            for h in (0, 1):
                fast, slow = ((x, y), (y, x))[h]
                lo, size = spans[h]
                to = (fast + off) % 4
                first[h, off, j] = send(
                    part.at[spot(h, to, (slow + j) % 4), pl.ds(lo, size)],
                    r1.at[h, off - 1, j, pl.ds(0, size)],
                    (s1s, s1r),
                    (h, off - 1, j),
                    (spot(h, to, slow), tp),
                )
    return first


def scatter_middle(part, out, bufs, place, first):
    mid, r1, r2, s1s, s1r, s2s, s2r = bufs
    ctx, tp, y, x = place
    spans = spans_of(part.shape[1])
    second = {}
    for j in OFFSETS + (0,):
        for h in (0, 1):
            fast, slow = ((x, y), (y, x))[h]
            lo, size = spans[h]
            for off in OFFSETS:
                first[h, off, j].wait_recv()
            total = part[spot(h, fast, (slow + j) % 4), pl.ds(lo, size)].astype(F32)
            for off in (1, 2, 3):
                total = total + r1[h, off - 1, j, pl.ds(0, size)].astype(F32)
            if j == 0:
                out[pl.ds(lo, size)] = total
            else:
                mid[h, j - 1, pl.ds(0, size)] = total.astype(BF)
                second[h, j] = send(
                    mid.at[h, j - 1, pl.ds(0, size)],
                    r2.at[h, j - 1, pl.ds(0, size)],
                    (s2s, s2r),
                    (h, j - 1),
                    (spot(h, fast, (slow + j) % 4), tp),
                )
    return second


def scatter_end(part, out, bufs, first, second):
    r2 = bufs[2]
    for h, (lo, size) in enumerate(spans_of(part.shape[1])):
        for j in OFFSETS:
            second[h, j].wait_recv()
        total = out[pl.ds(lo, size)]
        for j in (1, 2, 3):
            total = total + r2[h, j - 1, pl.ds(0, size)].astype(F32)
        out[pl.ds(lo, size)] = total
    for cp in list(first.values()) + list(second.values()):
        cp.wait_send()


def ctx_peers(ctx, tp):
    return [((ctx + d) % 16, tp) for d in range(1, 16)]


def swap_start(src, dst, sems, place):
    ctx, tp = place[:2]
    return [
        send(src.at[(ctx + d) % 16], dst.at[ctx], sems, d - 1, ((ctx + d) % 16, tp))
        for d in range(1, 16)
    ]


def pack_state(state, decay, msg):
    width = decay.shape[1]
    for j in range(16):
        msg[j, :, :width] = state[16 * j : 16 * (j + 1)].astype(BF)
    high = decay[0:1].astype(BF).astype(F32)
    low = decay[0:1] - high
    row = lax.broadcasted_iota(jnp.int32, (16, 128), 0)
    tile = jnp.zeros((16, 128), F32)
    count = width // 128
    for k in range(count):
        span = slice(128 * k, 128 * (k + 1))
        tile = jnp.where(row == k, high[:, span], tile)
        tile = jnp.where(row == count + k, low[:, span], tile)
    for j in range(16):
        msg[j, :, width:] = tile.astype(BF)


def prefix_into(order, got, ent):
    width = ent.shape[2]
    count = width // 128
    running = jnp.zeros(ent.shape[1:], F32)
    for i in order:
        ent[i] = running.astype(BF)
        tile = got[i, :, width:].astype(F32)
        decay = jnp.concatenate(
            [tile[k : k + 1] + tile[count + k : count + k + 1] for k in range(count)], axis=1
        )
        running = got[i, :, :width].astype(F32) + decay * running


def front_kernel(
    lengths,
    ids,
    hidden,
    gain,
    a_in,
    a_sh,
    w_dt,
    b_in,
    b_sh,
    params,
    w_in_far,
    w_sh_far,
    normed,
    low_in,
    low_sh,
    z_out,
    xs,
    q_out,
    bc,
    mask,
    decay,
    dt,
    pre,
    total,
    entering,
    ssd,
    gated,
    kv_all,
    w_in,
    w_sh,
    kv,
    work,
    row_decay,
    row_dt,
    x_one,
    inner,
    state,
    msg,
    got,
    ent,
    loads,
    *sems,
):
    place = ctx_place()
    ctx, tp, y, x = place
    c = tp % 2
    mate = (ctx, tp + 1 - 2 * c)
    peers = ctx_peers(ctx, tp) + [mate]
    greet(peers)
    get_sh = fetch(w_sh_far, w_sh, loads.at[0])
    get_in = fetch(w_in_far, w_in, loads.at[1])
    rows = hidden.shape[0]
    width = ssd.shape[1]
    heads = width // MHEAD
    base = ctx * rows
    blocks = rows // 128

    def span_of(i):
        return pl.ds(pl.multiple_of(i * 128, 128), 128)

    def norms(i, carry):
        at = span_of(i)
        v = hidden[at].astype(F32)
        normed[at] = (v * norm_scale(v) * gain[...]).astype(BF)
        t = base + i * 128 + iota((128, 128), 0)
        chosen = pick(t, lengths, [ids[k] for k in range(4)])
        mask[at] = (chosen == iota((128, 128), 1) // RANK).astype(F32)
        return carry

    lax.fori_loop(0, blocks, norms, 0)
    get_sh.wait()

    def shared(i, carry):
        at = span_of(i)
        n = normed[at]
        low = (dot(n, a_sh[...]) * mask[at]).astype(BF)
        low_sh[at] = low
        h = dot(n, w_sh[...]) + dot(low, b_sh[...])
        bc[at] = h[:, : 2 * STATE].astype(BF)
        lo = 2 * STATE
        group = tp // (QHEADS // KVH)
        for k in range(2):
            first = h[:, lo + 2 * k * HD : lo + (2 * k + 1) * HD]
            second = h[:, lo + (2 * k + 1) * HD : lo + (2 * k + 2) * HD]
            kv[at, HD * k : HD * (k + 1)] = jnp.where(group == 0, first, second).astype(BF)
        return carry

    lax.fori_loop(0, blocks, shared, 0)
    met(peers)
    s_one, s_two, s_kv1, s_kv2, s_m1, s_m2 = [sems[2 * k : 2 * k + 2] for k in range(6)]
    half = rows // 2
    part = half // 2
    mine = pl.multiple_of(c * half, half)
    span = [pl.ds(pl.multiple_of(mine + h * part, part), part) for h in (0, 1)]
    kv1 = {}
    for off in OFFSETS:
        for h in (0, 1):
            fast, slow = ((x, y), (y, x))[h]
            kv1[h, off] = send(
                kv.at[span[h]],
                kv_all.at[ctx, span[h]],
                s_kv1,
                (h, off - 1),
                (spot(h, (fast + off) % 4, slow), tp),
            )
    kv_all[ctx] = kv[...]
    get_in.wait()

    def project(i, carry):
        at = span_of(i)
        n = normed[at]
        low = (dot(n, a_in[...]) * mask[at]).astype(BF)
        low_in[at] = low
        h = (dot(n, w_in[...]) + dot(low, b_in[...])).astype(BF)
        z_out[at] = h[:, :width]
        xs[at] = h[:, width : 2 * width]
        q_out[at] = h[:, 2 * width :]
        v = dot_nt(n, w_dt[...]) + params[0:1]
        step = soft_plus(v)
        pre[at] = v
        dt[at] = step
        work[at] = -step * jnp.exp(params[1:2])
        return carry

    lax.fori_loop(0, blocks, project, 0)
    running_sum(decay, work, rows, False)
    row_decay[...] = decay[...].T
    row_dt[...] = dt[...].T
    for h in range(heads):
        x_one[h] = one_head(xs[:, (h // 2) * 128 : (h // 2 + 1) * 128], h)
    final = decay[rows - 1 : rows]
    last_start = doc_start(base + rows - 1, lengths)
    tail = jnp.where(
        base + iota((rows, 128), 0) >= last_start, jnp.exp(final - decay[...]) * dt[...], 0.0
    )
    scaled = (spread(tail, heads) * xs[...].astype(F32)).astype(BF)
    state[...] = dot_tn(bc[:, :STATE], scaled)
    through = jnp.where(last_start < base, 1.0, 0.0)
    whole = jnp.broadcast_to(jnp.exp(final) * through, (8, 128))
    total[...] = spread(whole, heads)
    pack_state(state, total, msg)
    one = swap_start(msg, got, s_one, place)
    got[ctx] = msg[ctx]
    kv2, to_mate = {}, []
    for off in OFFSETS:
        for h in (0, 1):
            kv1[h, off].wait_recv()
    for h in (0, 1):
        fast, slow = ((x, y), (y, x))[h]
        for off in OFFSETS:
            for k in range(4):
                at = spot(h, k, slow)
                kv2[h, off, k] = send(
                    kv_all.at[at, span[h]],
                    kv_all.at[at, span[h]],
                    s_kv2,
                    (h, off - 1, k),
                    (spot(h, fast, (slow + off) % 4), tp),
                )
    for off in OFFSETS:
        for h in (0, 1):
            fast, slow = ((x, y), (y, x))[h]
            at = spot(h, (fast + 4 - off) % 4, slow)
            to_mate.append(
                send(kv_all.at[at, span[h]], kv_all.at[at, span[h]], s_m1, (h, off - 1), mate)
            )
    for i in range(blocks):
        at = pl.ds(i * 128, 128)
        wide = (i + 1) * 128
        seen = fades(i, base, lengths)
        inter = dot_nt(bc[at, STATE:], bc[0:wide, :STATE])
        for pair_at in range(heads // 2):
            acc = jnp.zeros((128, 128), F32)
            for h in (2 * pair_at, 2 * pair_at + 1):
                gap = decay[at, h : h + 1] - row_decay[h : h + 1, 0:wide]
                fade = jnp.exp(jnp.where(seen, gap, -1e30))
                mixing = (inter * fade * row_dt[h : h + 1, 0:wide]).astype(BF)
                acc = acc + dot(mixing, x_one[h, 0:wide])
            inner[at, pair_at * 128 : (pair_at + 1) * 128] = acc
    for cp in one:
        cp.wait_recv()
    prefix_into(range(16), got, ent)
    two = swap_start(ent, entering, s_two, place)
    entering[ctx] = ent[ctx]
    for off in OFFSETS:
        for h in (0, 1):
            fast, slow = ((x, y), (y, x))[h]
            for k in range(4):
                kv2[h, off, k].wait_recv()
                at = spot(h, k, (slow + 4 - off) % 4)
                to_mate.append(
                    send(
                        kv_all.at[at, span[h]], kv_all.at[at, span[h]], s_m2, (h, off - 1, k), mate
                    )
                )
    for cp in two:
        cp.wait_recv()
    arrived = entering[...].reshape(STATE, width)

    def finish(i, carry):
        at = span_of(i)
        t = base + i * 128 + iota((128, 128), 0)
        reach = jnp.where(doc_start(t, lengths) < base, jnp.exp(decay[at]), 0.0)
        cross = dot(bc[at, STATE:], arrived) * spread(reach, heads)
        skip = spread(jnp.broadcast_to(params[2:3], (8, 128)), heads)[0:1]
        out = inner[at] + cross + skip * xs[at].astype(F32)
        ssd[at] = out
        z = z_out[at].astype(F32)
        gated[at] = (out * (z * jax.nn.sigmoid(z))).astype(BF)
        return carry

    lax.fori_loop(0, blocks, finish, 0)
    for cp in to_mate:
        cp.wait_recv()
    for cp in one + two + to_mate + list(kv1.values()) + list(kv2.values()):
        cp.wait_send()


def front_exchange(lengths, ids, hidden, gain, a_in, a_sh, w_dt, b_in, b_sh, params, w_in, w_sh, heads):
    rows, model = hidden.shape
    width = heads * MHEAD
    rank = a_in.shape[1]
    return call(
        front_kernel,
        [
            ((rows, model), BF),
            ((rows, rank), BF),
            ((rows, rank), BF),
            ((rows, width), BF),
            ((rows, width), BF),
            ((rows, HD), BF),
            ((rows, 2 * STATE), BF),
            ((rows, 128), F32),
            ((rows, 128), F32),
            ((rows, 128), F32),
            ((rows, 128), F32),
            ((8, width), F32),
            ((16, 16, width), BF),
            ((rows, width), F32),
            ((rows, width), BF),
            ((16, rows, 2 * HD), BF),
        ],
        [lengths, ids, hidden, gain, a_in, a_sh, w_dt, b_in, b_sh, params, w_in, w_sh],
        [
            pltpu.VMEM(w_in.shape, BF),
            pltpu.VMEM(w_sh.shape, BF),
            pltpu.VMEM((rows, 2 * HD), BF),
            pltpu.VMEM((rows, 128), F32),
            pltpu.VMEM((128, rows), F32),
            pltpu.VMEM((128, rows), F32),
            pltpu.VMEM((heads, rows, 128), BF),
            pltpu.VMEM((rows, width), F32),
            pltpu.VMEM((STATE, width), F32),
            pltpu.VMEM((16, 16, width + 128), BF),
            pltpu.VMEM((16, 16, width + 128), BF),
            pltpu.VMEM((16, 16, width), BF),
            DMA((2,)),
            *pair(15),
            *pair(15),
            *pair(2, 3),
            *pair(2, 3, 4),
            *pair(2, 3),
            *pair(2, 3, 4),
        ],
        4,
        "front_exchange",
        [SM, SM] + [VM] * 8 + [HB, HB],
    )


def back_kernel(
    lengths,
    state,
    total,
    dkv,
    part,
    resid,
    b_dn,
    bc,
    xs,
    decay,
    dt,
    pre,
    params,
    grad_ssd,
    grad_z,
    dq,
    entering,
    b_in,
    b_sh,
    w_dt,
    w_in_far,
    w_sh_far,
    gathered,
    part_out,
    two_out,
    grad_one,
    grad_head,
    w_in,
    w_sh,
    msg,
    got,
    ent,
    leaving,
    mate_buf,
    both,
    dkv_sum,
    kv_rows,
    grad_two,
    row_decay,
    row_dt,
    col_sum,
    row_sum,
    x_one,
    dy_one,
    dx,
    grad_b,
    grad_c,
    work,
    partial,
    loads,
    *scratch,
):
    place = ctx_place()
    ctx, tp, y, x = place
    tp_at = tp_place()
    c = tp % 2
    mate = (ctx, tp + 1 - 2 * c)
    peers = ctx_peers(ctx, tp) + tp_peers(*tp_at)
    greet(peers)
    get_in = fetch(w_in_far, w_in, loads.at[0])
    get_sh = fetch(w_sh_far, w_sh, loads.at[1])
    pack_state(state, total, msg)
    rows, width = xs.shape
    heads = width // MHEAD
    base = ctx * rows
    blocks = rows // 128
    met(peers)
    s_one, s_two, s_mate = scratch[0:2], scratch[2:4], scratch[4:6]
    bufs, more, sems = scratch[6:13], scratch[13:20], scratch[20:]
    one = swap_start(msg, got, s_one, place)
    half = rows // 2
    mine = pl.ds(pl.multiple_of(c * half, half), half)
    other = pl.ds(pl.multiple_of((1 - c) * half, half), half)
    cps = [
        send(dkv.at[pl.ds(4 * k, 4), other], mate_buf.at[pl.ds(4 * k, 4)], s_mate, k, mate)
        for k in range(4)
    ]
    first_z = reduce_start(part, more, tp_at)
    got[ctx] = msg[ctx]
    for k in range(4):
        cps[k].wait_recv()
        for i in range(4 * k, 4 * k + 4):
            both[i] = (dkv[i, mine].astype(F32) + mate_buf[i].astype(F32)).astype(BF)
    first = scatter_start(both, bufs, place)
    second_z = reduce_middle(part, more, tp_at, first_z)
    for cp in one:
        cp.wait_recv()
    reduce_relay(part, more, tp_at, first_z, second_z)
    prefix_into(range(15, -1, -1), got, ent)
    two = swap_start(ent, leaving, s_two, place)
    leaving[ctx] = ent[ctx]

    row_decay[...] = decay[...].T
    row_dt[...] = dt[...].T
    col_sum[...] = jnp.zeros(col_sum.shape, F32)
    for h in range(heads):
        cols = slice((h // 2) * 128, (h // 2 + 1) * 128)
        x_one[h] = one_head(xs[:, cols], h)
        dy_one[h] = one_head(grad_ssd[:, cols], h).astype(BF)
    grad_b[...] = jnp.zeros(grad_b.shape, F32)
    dx[...] = jnp.zeros(dx.shape, F32)
    for i in range(blocks):
        at = pl.ds(i * 128, 128)
        wide = (i + 1) * 128
        seen = fades(i, base, lengths)
        inter = dot_nt(bc[at, STATE:], bc[0:wide, :STATE])
        d_inter = jnp.zeros((128, wide), F32)
        sums = jnp.zeros((128, 128), F32)
        for pair_at in range(heads // 2):
            cols = slice(pair_at * 128, (pair_at + 1) * 128)
            for h in (2 * pair_at, 2 * pair_at + 1):
                step = row_dt[h : h + 1, 0:wide]
                gap = decay[at, h : h + 1] - row_decay[h : h + 1, 0:wide]
                fade = jnp.exp(jnp.where(seen, gap, -1e30))
                d_mix = dot_nt(dy_one[h, at], x_one[h, 0:wide])
                faded = fade * step
                d_inter = d_inter + d_mix * faded
                weighted = d_mix * inter * fade
                col_sum[h : h + 1, 0:wide] += jnp.sum(weighted, axis=0, keepdims=True)
                sums = jnp.where(
                    iota((128, 128), 1) == h,
                    jnp.sum(weighted * step, axis=1, keepdims=True),
                    sums,
                )
                dx[0:wide, cols] += dot_tn((inter * faded).astype(BF), dy_one[h, at])
        row_sum[at] = sums
        low = d_inter.astype(BF)
        grad_c[at] = dot(low, bc[0:wide, :STATE])
        grad_b[0:wide] += dot_tn(low, bc[at, STATE:])

    width_out = resid.shape[1]
    out = reduce_end(part, more, tp_at, first_z, second_z)
    low = out[:, width_out:].astype(BF)
    gathered[tp, :, :width_out] = (resid[...] + out[:, :width_out] + dot(low, b_dn[...])).astype(BF)
    gathered[tp, :, width_out:] = low
    started = share_start(gathered, sems, tp_at)
    second = scatter_middle(both, dkv_sum, bufs, place, first)

    for cp in two:
        cp.wait_recv()
    after = leaving[...].reshape(STATE, width)
    before = entering[...].reshape(STATE, width)
    final = decay[rows - 1 : rows]
    last_start = doc_start(base + rows - 1, lengths)
    cols_sum = col_sum[...].T
    crossing = head_sums(
        jnp.broadcast_to(
            jnp.sum(after.astype(F32) * before.astype(F32), axis=0, keepdims=True) * total[0:1],
            (8, width),
        )
    )[0:1]
    rate = jnp.exp(params[1:2])
    skip = spread(jnp.broadcast_to(params[2:3], (8, 128)), heads)[0:1]
    d_last = crossing
    skips = jnp.zeros((1, 128), F32)
    for i in range(blocks):
        at = pl.ds(i * 128, 128)
        t = base + i * 128 + iota((128, 128), 0)
        steps = dt[at]
        tail = jnp.where(t >= last_start, jnp.exp(final - decay[at]), 0.0)
        reach = jnp.where(doc_start(t, lengths) < base, jnp.exp(decay[at]), 0.0)
        x_f = xs[at].astype(F32)
        gs = grad_ssd[at]
        came = dot(bc[at, :STATE], after)
        held = head_sums(came * x_f) * tail
        reached = spread(reach, heads) * gs
        d_cross = head_sums(dot(bc[at, STATE:], before) * reached)
        cols_at = cols_sum[i * 128 : (i + 1) * 128]
        work[at] = row_sum[at] - cols_at * steps + d_cross - held * steps
        row_sum[at] = cols_at + held
        d_last = d_last + jnp.sum(held * steps, axis=0, keepdims=True)
        tails = spread(tail * steps, heads)
        grad_one[at, :width] = grad_z[at]
        grad_one[at, width : 2 * width] = (dx[at] + tails * came + skip * gs).astype(BF)
        grad_one[at, 2 * width : 2 * width + HD] = dq[at]
        skips = skips + jnp.sum(head_sums(gs * x_f), axis=0, keepdims=True)
        grad_two[at, :STATE] = (grad_b[at] + dot_nt((tails * x_f).astype(BF), after)).astype(BF)
        grad_two[at, STATE : 2 * STATE] = (grad_c[at] + dot_nt(reached.astype(BF), before)).astype(
            BF
        )
    passed = [share_pass(gathered, sems, tp_at, started, k) for k in (0, 1)]
    running_sum(dx.at[:, 0:128], work, rows, True)
    d_log = dx[:, 0:128] + d_last
    grad_dt = (row_sum[...] - rate * d_log) * jax.nn.sigmoid(pre[...])
    grad_one[:, 2 * width + HD :] = grad_dt.astype(BF)
    grad_head[0:1] = jnp.sum(grad_dt, axis=0, keepdims=True)
    grad_head[1:2] = -jnp.sum(dt[...] * rate * d_log, axis=0, keepdims=True)
    grad_head[2:3] = skips
    grad_head[3:8] = jnp.zeros((5, 128), F32)
    get_in.wait()
    get_sh.wait()
    narrow = 2 * width + HD

    def norm_part(i, carry):
        at = pl.ds(pl.multiple_of(i * 128, 128), 128)
        g = grad_one[at]
        partial[at] = (
            dot_nt(g[:, :narrow], w_in[...])
            + dot(g[:, narrow:], w_dt[...])
            + dot_nt(grad_two[at, : 2 * STATE], w_sh[:, : 2 * STATE])
        )
        return carry

    lax.fori_loop(0, blocks, norm_part, 0)
    passed.append(share_pass(gathered, sems, tp_at, started, 2))
    scatter_end(both, dkv_sum, bufs, first, second)
    kv_rows[...] = jnp.zeros(kv_rows.shape, F32)
    kv_rows[mine] = dkv_sum[...]
    group = tp // (QHEADS // KVH)
    for k in range(KVH):
        on = jnp.where(group == k, 1.0, 0.0)
        for v in range(2):
            lo = 2 * STATE + (v * KVH + k) * HD
            grad_two[:, lo : lo + HD] = (kv_rows[:, v * HD : (v + 1) * HD] * on).astype(BF)
    model = resid.shape[1]
    rank = b_in.shape[0]
    share = resid.shape[0]
    each = 128 // share

    def finish(i, carry):
        at = pl.ds(pl.multiple_of(i * 128, 128), 128)
        g = grad_one[at]
        full = (partial[at] + dot_nt(grad_two[at, 2 * STATE :], w_sh[:, 2 * STATE :])).astype(BF)
        low = dot_nt(g[:, :narrow], b_in[...]).astype(BF)
        low_two = dot_nt(grad_two[at], b_sh[...]).astype(BF)
        for k in range(each):
            some = slice(k * share, (k + 1) * share)
            part_out[i * each + k, :, :model] = full[some]
            part_out[i * each + k, :, model : model + rank] = low[some]
            part_out[i * each + k, :, model + rank :] = low_two[some]
        return carry

    lax.fori_loop(0, blocks, finish, 0)
    for k in range(8):
        two_out[k] = grad_two[:, k * 128 : (k + 1) * 128]
    share_end(gathered, sems, tp_at, started, passed)
    for cp in one + two + cps:
        cp.wait_send()


def back_exchange(*args):
    dkv, part, resid, xs, b_in, w_in, w_sh = args[3], args[4], args[5], args[8], args[17], args[20], args[21]
    rows, width = xs.shape
    heads = width // MHEAD
    _, tall, cols = dkv.shape
    _, share, wide = part.shape
    half = tall // 2
    model = resid.shape[1]
    rank = b_in.shape[0]
    return call(
        back_kernel,
        [
            (part.shape, BF),
            ((8, share, model + 2 * rank), BF),
            ((8, rows, w_sh.shape[1] // 8), BF),
            ((rows, 2 * width + HD + 128), BF),
            ((8, 128), F32),
        ],
        list(args),
        [
            pltpu.VMEM(w_in.shape, BF),
            pltpu.VMEM(w_sh.shape, BF),
            pltpu.VMEM((16, 16, width + 128), BF),
            pltpu.VMEM((16, 16, width + 128), BF),
            pltpu.VMEM((16, 16, width), BF),
            pltpu.VMEM((16, 16, width), BF),
            pltpu.VMEM((16, half, cols), BF),
            pltpu.VMEM((16, half, cols), BF),
            pltpu.VMEM((half, cols), F32),
            pltpu.VMEM((rows, cols), F32),
            pltpu.VMEM((rows, w_sh.shape[1]), BF),
            pltpu.VMEM((128, rows), F32),
            pltpu.VMEM((128, rows), F32),
            pltpu.VMEM((128, rows), F32),
            pltpu.VMEM((rows, 128), F32),
            pltpu.VMEM((heads, rows, 128), BF),
            pltpu.VMEM((heads, rows, 128), BF),
            pltpu.VMEM((rows, width), F32),
            pltpu.VMEM((rows, STATE), F32),
            pltpu.VMEM((rows, STATE), F32),
            pltpu.VMEM((rows, 128), F32),
            pltpu.VMEM((rows, model), F32),
            DMA((2,)),
            *pair(15),
            *pair(15),
            *pair(4),
            *scatter_bufs(half, cols),
            *reduce_bufs(share, wide),
            *share_sems(),
        ],
        5,
        "back_exchange",
        [SM] + [VM] * 19 + [HB] * 2,
    )


def tail_kernel(
    part,
    part_two,
    gain,
    grad_resid,
    a_in,
    a_sh,
    mask,
    gain_two,
    normed_one,
    grad_one,
    low_in,
    low_sh,
    merged,
    grad_low_out,
    normed_mine,
    grad_low_gu,
    mixer_mine,
    low_out,
    grad_mine,
    low_dn,
    head,
    hidden_far,
    gathered,
    big_out,
    small_out,
    shared,
    head_out,
    source,
    turned,
    mine,
    big,
    small,
    b_in_sum,
    heads,
    loads,
    *scratch,
):
    place = ctx_place()
    tp_at = tp_place()
    ctx, tp = place[:2]
    peers = ctx_peers(ctx, tp) + tp_peers(*tp_at)
    greet(peers)
    share, width = source.shape
    rank = a_in.shape[1]
    rows_mine = pl.ds(pl.multiple_of(tp * share, share), share)
    get_source = fetch(hidden_far.at[rows_mine], source, loads.at[0])
    bufs_z, more_z, sems = scratch[:7], scratch[7:14], scratch[14:18]
    bufs, more, s_head, sems_s = scratch[18:25], scratch[25:32], scratch[32:34], scratch[34:]
    met(peers)
    first_z = reduce_start(part, bufs_z, tp_at)
    first_two = reduce_start(part_two, more_z, tp_at)
    second_z = reduce_middle(part, bufs_z, tp_at, first_z)
    second_two = reduce_middle(part_two, more_z, tp_at, first_two)
    sent = [send(head, heads.at[ctx], s_head, d - 1, ((ctx + d) % 16, tp)) for d in range(1, 16)]
    heads[ctx] = head[...]
    slot = pl.ds(pl.multiple_of(tp * 16, 16), 16)
    b_in_sum[...] = dot_tn(low_in[...], grad_one[...])

    def weights(j, carry):
        turned[j] = cut_t(normed_one, j)
        mine[j] = turned[j, slot]
        big[j, 0:128] = dot(turned[j], grad_one[...]).astype(BF)
        big[j, 128:144] = eight(b_in_sum, j).astype(BF)
        return carry

    lax.fori_loop(0, 16, weights, 0)
    first = scatter_start(big, bufs, place)
    reduce_relay(part, bufs_z, tp_at, first_z, second_z)
    reduce_relay(part_two, more_z, tp_at, first_two, second_two)
    get_source.wait()
    total = reduce_end(part, bufs_z, tp_at, first_z, second_z)
    mask_mine = mask[rows_mine]
    low_one = (total[:, width : width + rank] * mask_mine).astype(BF)
    low_two = (total[:, width + rank :] * mask_mine).astype(BF)
    grad = total[:, :width] + dot_nt(low_one, a_in[...]) + dot_nt(low_two, a_sh[...])
    grad_v, grad_gain = norm_back(source[...].astype(F32), gain[...], grad)
    gathered[tp, :, :width] = (grad_resid[...] + grad_v).astype(BF)
    gathered[tp, :, width : width + rank] = low_one
    gathered[tp, :, width + rank :] = low_two
    started = share_start(gathered, sems, tp_at)

    a_out_sum = dot_tn(merged[...], grad_low_out[...])
    for j in range(16):
        small[j, 160:192] = a_out_sum[j * 32 : (j + 1) * 32].astype(BF)
    for row, low, tall in (
        (208, grad_low_gu, normed_mine),
        (224, low_out, mixer_mine),
    ):
        full = dot(tall[...].reshape(256, -1), low[...]).astype(BF)
        small[:, row : row + 16] = full.reshape(16, 16, rank)
    full = dot(grad_mine[...].reshape(256, -1), low_dn[...].reshape(-1, low_dn.shape[2])[:, width:])
    small[:, 240:256] = full.astype(BF).reshape(16, 16, rank)
    passed = [share_pass(gathered, sems, tp_at, started, k) for k in (0, 1)]
    two = reduce_end(part_two, more_z, tp_at, first_two, second_two).astype(BF)
    b_sh_sum = dot_tn(low_sh[...], two)

    def shared_maps(j, carry):
        small[j, 0:128] = dot(turned[j], two).astype(BF)
        return carry

    lax.fori_loop(0, 16, shared_maps, 0)
    gain_rows = jnp.concatenate([grad_gain, gain_two[...], jnp.zeros((6, width), F32)], axis=0)
    for j in range(16):
        small[j, 144:160] = jnp.concatenate(
            [b_sh_sum[8 * j : 8 * j + 8], gain_rows[:, 128 * j : 128 * (j + 1)]], axis=0
        ).astype(BF)
    share_end(gathered, sems, tp_at, started, passed)
    lows = gathered[:, :, width:].reshape(-1, 2 * rank)
    full = dot(mine[...].reshape(256, -1), lows).astype(BF)
    small[:, 192:208] = full[:, :rank].reshape(16, 16, rank)
    small[:, 128:144] = full[:, rank:].reshape(16, 16, rank)
    first_s = scatter_start(small, more, place)
    second = scatter_middle(big, big_out, bufs, place, first)
    second_s = scatter_middle(small, small_out, more, place, first_s)
    scatter_end(small, small_out, more, first_s, second_s)
    shared[tp] = small_out[pl.ds(0, shared.shape[1])].astype(BF)
    started_s = share_start(shared, sems_s, tp_at)
    scatter_end(big, big_out, bufs, first, second)
    for cp in sent:
        cp.wait_recv()
    head_out[...] = jnp.sum(heads[...], axis=0)
    share_end(shared, sems_s, tp_at, started_s)
    for cp in sent:
        cp.wait_send()


def tail_exchange(*args):
    part, part_two, grad_resid, grad_one, head = args[0], args[1], args[3], args[9], args[20]
    _, rows, wide = part.shape
    _, tall, cols = part_two.shape
    width = grad_resid.shape[1]
    deep = grad_one.shape[1]
    return call(
        tail_kernel,
        [
            (part.shape, BF),
            ((144, deep), F32),
            ((256, 128), F32),
            ((8, 160, 128), BF),
            (head.shape, F32),
        ],
        list(args),
        [
            pltpu.VMEM((rows, width), BF),
            pltpu.VMEM((16, 128, tall), BF),
            pltpu.VMEM((16, 16, tall), BF),
            pltpu.VMEM((16, 144, deep), BF),
            pltpu.VMEM((16, 256, 128), BF),
            pltpu.VMEM((128, deep), F32),
            pltpu.VMEM((16,) + head.shape, F32),
            DMA((1,)),
            *reduce_bufs(rows, wide),
            *reduce_bufs(tall, cols),
            *share_sems(),
            *scatter_bufs(144, deep),
            *scatter_bufs(256, 128),
            *pair(15),
            *share_sems(),
        ],
        6,
        "tail_exchange",
        [VM] * 21 + [HB],
    )


def finish_kernel(
    mixed_in,
    input_in,
    big,
    small,
    shared,
    head,
    early,
    mixed,
    input_grad,
    gains,
    w_in,
    w_sh,
    w_dt,
    params,
    w_out,
    w_gu,
    w_down,
    a_in,
    b_in,
    a_sh,
    b_sh,
    a_out,
    b_out,
    a_gu,
    b_gu,
    a_dn,
    b_dn,
):
    width = mixed.shape[1]
    mixed[...] = mixed_in[0, :, :width].astype(F32)
    input_grad[...] = input_in[0, :, :width].astype(F32)

    @pl.when(pl.program_id(0) == 0)
    def rest():
        narrow = w_in.shape[2]
        hidden = w_down.shape[0]
        heads = w_dt.shape[0]
        w_in[:, 0, :] = big[0:128, :narrow]
        b_in[:, 0, :] = big[128:136, :narrow]
        w_dt[...] = big[0:128, narrow : narrow + 128].T[0:heads]
        params[...] = head[0:3, 0:heads]
        total = jnp.zeros((8, 128), F32)
        for k in range(8):
            block = shared[k].astype(F32)
            cols = slice(128 * k, 128 * (k + 1))
            w_sh[:, cols] = block[0:128]
            a_sh[16 * k : 16 * (k + 1)] = block[128:144]
            b_sh[:, cols] = block[144:152]
            total = total + block[152:160]
        gains[...] = total[0:2]
        a_out[0] = small[160:192]
        a_in[...] = small[192:208]
        a_gu[...] = small[208:224]
        b_out[...] = small[224:240]
        b_dn[...] = small[240:256]
        w_out[0] = early[0:128, 3 * hidden :].astype(F32).T
        w_gu[:, 0, :] = early[0:128, :hidden].astype(F32)
        w_gu[:, 1, :] = early[0:128, hidden : 2 * hidden].astype(F32)
        w_down[...] = early[0:128, 2 * hidden : 3 * hidden].astype(F32).T
        rest_rows = early[128:144].astype(F32)
        b_gu[:, 0, :] = rest_rows[0:8, :hidden]
        b_gu[:, 1, :] = rest_rows[0:8, hidden : 2 * hidden]
        a_dn[...] = rest_rows[0:8, 2 * hidden : 3 * hidden]


def finish(mixed, input_grad, big, small, shared, head, early, narrow, heads):
    _, rows, wide = mixed.shape
    _, _, wide_two = input_grad.shape
    width = wide - 128
    hidden = early.shape[1] // 4
    outs = [
        (8 * rows, width),
        (8 * rows, width),
        (2, 128),
        (128, 1, narrow),
        (128, 1024),
        (heads, 128),
        (3, heads),
        (1, hidden, 128),
        (128, 2, hidden),
        (hidden, 128),
        (16, 128),
        (8, 1, narrow),
        (128, 128),
        (8, 1024),
        (1, 32, 128),
        (16, 128),
        (16, 128),
        (8, 2, hidden),
        (8, hidden),
        (16, 128),
    ]

    def whole(shape):
        return pl.BlockSpec(shape, lambda i: (0,) * len(shape))

    done = pl.pallas_call(
        finish_kernel,
        grid=(8,),
        out_shape=[jax.ShapeDtypeStruct(s, F32) for s in outs],
        in_specs=[
            pl.BlockSpec((1, rows, wide), lambda i: (i, 0, 0)),
            pl.BlockSpec((1, rows, wide_two), lambda i: (i, 0, 0)),
        ]
        + [whole(a.shape) for a in (big, small, shared, head, early)],
        out_specs=[pl.BlockSpec((rows, width), lambda i: (i, 0))] * 2 + [whole(s) for s in outs[2:]],
        compiler_params=pltpu.CompilerParams(vmem_limit_bytes=56 << 20),
        name="finish",
    )(mixed, input_grad, big, small, shared, head, early)
    return tuple(a.T if k in (5, 15, 18, 19) else a for k, a in enumerate(done))


def flash_kernel(
    scale, at, lengths, q, kv, gated, w_out, a_out, mask, part, attn_t, lse, merged
):
    ctx = at[0]
    block, size = kv.shape[1], q.shape[0]
    queries = q[...].T
    begin = doc_start(ctx * block + iota((8, size), 1), lengths)[0:1]
    first = doc_start(ctx * block, lengths) // block
    latest = doc_start(ctx * block + size - 1, lengths)

    def step(i, carry, masked, diagonal):
        top, total, acc = carry
        s = dot(kv[i, :, :HD], queries)
        if masked:
            key = i * block + iota(s.shape, 0)
            allowed = key >= begin
            if diagonal:
                allowed &= key <= ctx * block + iota(s.shape, 1)
            s = jnp.where(allowed, s, -1e30)
        new = jnp.maximum(top, jnp.max(s, axis=0, keepdims=True))
        p = jnp.exp((s - new) * scale)
        if masked:
            p = jnp.where(allowed, p, 0.0)
        fade = jnp.exp((top - new) * scale)
        total = total * fade + jnp.sum(p, axis=0, keepdims=True)
        acc = acc * fade + dot_tn(kv[i, :, HD:], p.astype(BF))
        return new, total, acc

    carry = (
        jnp.full((1, size), -1e30, F32),
        jnp.zeros((1, size), F32),
        jnp.zeros((HD, size), F32),
    )
    border = jnp.clip((latest + block - 1) // block, first, ctx)
    carry = lax.fori_loop(first, border, lambda i, k: step(i, k, True, False), carry)
    carry = lax.fori_loop(border, ctx, lambda i, k: step(i, k, False, False), carry)
    top, total, acc = step(ctx, carry, True, True)
    out = acc / total
    attn_t[...] = out
    lse[...] = top * scale + jnp.log(total)
    width = gated.shape[1]
    merged[:, :width] = gated[...]
    merged[:, width:] = out.T.astype(BF)
    model = w_out.shape[1]
    share = part.shape[1]

    def mix(i, carry):
        rows = pl.ds(pl.multiple_of(i * 128, 128), 128)
        m = merged[rows]
        full = dot(m, w_out[...]).astype(BF)
        low = (dot(m, a_out[...]) * mask[rows]).astype(BF)
        for k in range(128 // share):
            to = i * (128 // share) + k
            part[to, :, :model] = full[k * share : (k + 1) * share]
            part[to, :, model:] = low[k * share : (k + 1) * share]
        return carry

    lax.fori_loop(0, size // 128, mix, 0)


def plain_call(kernel, outs, ins, specs, name, scratch=()):
    return pl.pallas_call(
        kernel,
        out_shape=[jax.ShapeDtypeStruct(s, d) for s, d in outs],
        in_specs=specs,
        out_specs=[VM] * len(outs),
        scratch_shapes=list(scratch),
        compiler_params=pltpu.CompilerParams(vmem_limit_bytes=56 << 20),
        name=name,
    )(*ins)


def flash_forward(scale, at, lengths, q, kv, gated, w_out, a_out, mask, tps):
    rows = q.shape[0]
    wide = w_out.shape[1] + a_out.shape[1]
    return plain_call(
        functools.partial(flash_kernel, scale),
        [
            ((tps, rows // tps, wide), BF),
            ((HD, rows), F32),
            ((1, rows), F32),
            ((rows, gated.shape[1] + HD), BF),
        ],
        [at, lengths, q, kv, gated, w_out, a_out, mask],
        [SM, SM] + [VM] * 6,
        "flash_forward",
    )


def flash_back_kernel(
    scale,
    at,
    lengths,
    q,
    kv,
    lse,
    attn_t,
    grad_mixer,
    w_out,
    b_out,
    a_out,
    mask,
    z_in,
    ssd,
    bc,
    decay,
    dq,
    dkv,
    grad_z,
    grad_ssd,
    pull,
    grad_low,
    grad_attn,
    hold,
):
    ctx = at[0]
    block = kv.shape[1]
    rows = q.shape[0]
    width = z_in.shape[1]
    heads = width // MHEAD
    base = ctx * rows

    def merged_back(i, carry):
        span = pl.ds(pl.multiple_of(i * 128, 128), 128)
        g = grad_mixer[span]
        low = (dot_nt(g, b_out[...]) * mask[span]).astype(BF)
        grad_low[span] = low
        grad = (dot_nt(g, w_out[...]) + dot_nt(low, a_out[...])).astype(BF)
        grad_attn[span] = grad[:, width:]
        gg = grad[:, :width].astype(F32)
        z = z_in[span].astype(F32)
        sig = jax.nn.sigmoid(z)
        grad_z[span] = (gg * ssd[span] * sig * (1.0 + z * (1.0 - sig))).astype(BF)
        gs = gg * (z * sig)
        grad_ssd[span] = gs
        t = base + i * 128 + iota((128, 128), 0)
        reach = jnp.where(doc_start(t, lengths) < base, jnp.exp(decay[span]), 0.0)
        hold[span] = (spread(reach, heads) * gs).astype(BF)
        return carry

    lax.fori_loop(0, rows // 128, merged_back, 0)
    pull[...] = dot_tn(bc[:, STATE:], hold[...])

    dkv[...] = jnp.zeros(dkv.shape, BF)
    queries_t, queries = q[...].T, q[...]
    og = grad_attn[...]
    og_t = og.T
    low = jnp.sum(og_t.astype(F32) * attn_t[...], axis=0, keepdims=True)
    offset = lse[...]
    begin = doc_start(base + iota((8, rows), 1), lengths)[0:1]
    first = doc_start(base, lengths) // block
    latest = doc_start(base + rows - 1, lengths)

    def step(i, acc, masked, diagonal):
        keys = kv[i, :, :HD]
        s = dot(keys, queries_t) * scale - offset
        if masked:
            key = i * block + iota(s.shape, 0)
            allowed = key >= begin
            if diagonal:
                allowed &= key <= base + iota(s.shape, 1)
            s = jnp.where(allowed, s, -1e30)
        p = jnp.exp(s)
        dp = dot(kv[i, :, HD:], og_t)
        ds = (p * (dp - low)).astype(BF)
        dkv[i, :, :HD] = (dot(ds, queries) * scale).astype(BF)
        dkv[i, :, HD:] = dot(p.astype(BF), og).astype(BF)
        return acc + dot_tn(keys, ds)

    border = jnp.clip((latest + block - 1) // block, first, ctx)
    acc = jnp.zeros((HD, rows), F32)
    acc = lax.fori_loop(first, border, lambda i, k: step(i, k, True, False), acc)
    acc = lax.fori_loop(border, ctx, lambda i, k: step(i, k, False, False), acc)
    acc = step(ctx, acc, True, True) * scale
    dq[...] = acc.T.astype(BF)


def flash_backward(scale, at, *args):
    lengths, q, kv, lse, attn_t, grad_mixer, w_out, b_out, a_out, mask, z, ssd, bc, decay = args
    rows = q.shape[0]
    width = z.shape[1]
    return plain_call(
        functools.partial(flash_back_kernel, scale),
        [
            ((rows, HD), BF),
            (kv.shape, BF),
            ((rows, width), BF),
            ((rows, width), F32),
            ((STATE, width), F32),
            (mask.shape, BF),
        ],
        [at, *args],
        [SM, SM] + [VM] * 13,
        "flash_backward",
        [
            pltpu.VMEM((rows, HD), BF),
            pltpu.VMEM((rows, width), BF),
        ],
    )


def body(
    hidden_in,
    norm_gains,
    w_in,
    w_shared,
    w_dt,
    head_params,
    w_out,
    w_gu,
    w_down,
    a_in,
    b_in,
    a_sh,
    b_sh,
    a_out,
    b_out,
    a_gu,
    b_gu,
    a_dn,
    b_dn,
    adapter_ids,
    doc_lengths,
    out_grad,
):
    rows, width = hidden_in.shape
    heads = head_params.shape[1]
    tp_count = lax.axis_size("tp")
    at = jnp.stack([lax.axis_index("ctx"), lax.axis_index("tp")]).astype(jnp.int32)
    w_in = w_in.reshape(width, -1)
    b_in = b_in.reshape(b_in.shape[0], -1)
    w_out = w_out.reshape(-1, width)
    a_out = a_out.reshape(-1, a_out.shape[2])
    w_gu = w_gu.reshape(width, -1)
    b_gu = b_gu.reshape(b_gu.shape[0], -1)
    w_dt = jnp.pad(w_dt.T, ((0, 128 - heads), (0, 0)))
    params = jnp.pad(head_params, ((0, 5), (0, 128 - heads)))
    scale = HD ** (-0.5)
    gain_one, gain_two = norm_gains[0:1], norm_gains[1:2]
    (
        normed_one,
        low_in,
        low_sh,
        z,
        xs,
        q,
        bc,
        mask,
        decay,
        dt,
        pre,
        total,
        entering,
        ssd,
        gated,
        kv_all,
    ) = front_exchange(
        doc_lengths,
        adapter_ids,
        hidden_in,
        gain_one,
        a_in,
        a_sh,
        w_dt,
        b_in,
        b_sh,
        params,
        w_in,
        w_shared,
        heads,
    )
    mix_part, attn_t, lse, merged = flash_forward(
        scale, at, doc_lengths, q, kv_all, gated, w_out, a_out, mask, tp_count
    )
    (
        low_out,
        grad_mixer,
        grad_low_gu,
        resid,
        grad_resid,
        gain_part_two,
        early,
        mlp_part,
        normed_mine,
        grad_mine,
        mixer_mine,
    ) = mlp_exchange(
        mix_part,
        gain_two,
        b_out,
        a_gu,
        b_gu,
        a_dn,
        b_dn,
        out_grad,
        mask,
        merged,
        hidden_in,
        w_gu,
        w_down,
    )
    early = lax.psum_scatter(
        early.reshape(-1, early.shape[2]), "ctx", scatter_dimension=0, tiled=True
    )
    dq, dkv, grad_z, grad_ssd, pull, grad_low_out = flash_backward(
        scale,
        at,
        doc_lengths,
        q,
        kv_all,
        lse,
        attn_t,
        grad_mixer,
        w_out,
        b_out,
        a_out,
        mask,
        z,
        ssd,
        bc,
        decay,
    )
    mixed, part, two_blocks, grad_one, grad_head = back_exchange(
        doc_lengths,
        pull,
        total,
        dkv,
        mlp_part,
        resid,
        b_dn,
        bc,
        xs,
        decay,
        dt,
        pre,
        params,
        grad_ssd,
        grad_z,
        dq,
        entering,
        b_in,
        b_sh,
        w_dt,
        w_in,
        w_shared,
    )
    input_grad, big, small, shared, head = tail_exchange(
        part,
        two_blocks,
        gain_one,
        grad_resid,
        a_in,
        a_sh,
        mask,
        gain_part_two,
        normed_one,
        grad_one,
        low_in,
        low_sh,
        merged,
        grad_low_out,
        normed_mine,
        grad_low_gu,
        mixer_mine,
        low_out,
        grad_mine,
        mixed,
        grad_head,
        hidden_in,
    )
    return finish(mixed, input_grad, big, small, shared, head, early, w_in.shape[1], heads)


def solution(mesh):
    placed = (
        P("ctx", None),
        P(),
        P(None, "tp", None),
        P(),
        P(None, "tp"),
        P(None, "tp"),
        P("tp", None, None),
        P(None, None, "tp"),
        P("tp", None),
        P(),
        P(None, "tp", None),
        P(),
        P(),
        P("tp", None, None),
        P(),
        P(),
        P(None, None, "tp"),
        P("tp", None),
        P(),
        P(),
        P(),
        P("ctx", None),
    )
    return jax.shard_map(
        body,
        mesh=mesh,
        in_specs=placed,
        out_specs=(
            P("ctx", None),
            P("ctx", None),
            P(None, "ctx"),
            P("ctx", "tp", None),
            P("ctx", None),
            P("ctx", "tp"),
            P(None, "tp"),
            P("tp", None, "ctx"),
            P("ctx", None, "tp"),
            P("tp", "ctx"),
            P(("ctx", "tp"), None),
            P("ctx", "tp", None),
            P("ctx", None),
            P("ctx", None),
            P("tp", "ctx", None),
            P(None, ("ctx", "tp")),
            P(("ctx", "tp"), None),
            P("ctx", None, "tp"),
            P("tp", "ctx"),
            P(None, ("ctx", "tp")),
        ),
        check_vma=False,
    )
```

```python
import functools

import jax
import jax.numpy as jnp
from jax import lax
from jax.experimental import pallas as pl
from jax.experimental.pallas import tpu as pltpu
from jax.sharding import PartitionSpec as P

MHEAD = 64
STATE = 256
QHEADS = 8
KVH = 2
HD = 128
RANK = 16
NORM_EPSILON = 1e-06

MESH = pl.DeviceIdType.MESH
VM = pl.BlockSpec(memory_space=pltpu.VMEM)
SM = pl.BlockSpec(memory_space=pltpu.SMEM)
HB = pl.BlockSpec(memory_space=pl.ANY)
BF = jnp.bfloat16
F32 = jnp.float32
DMA = pltpu.SemaphoreType.DMA
OFFSETS = (2, 1, 3)
LOG2E = 1.4426950408889634
UNROLL = 3


def call(kernel, outs, ins, scratch, cid, name, specs=None, out_specs=None):
    return pl.pallas_call(
        kernel,
        out_shape=[jax.ShapeDtypeStruct(s, d) for s, d in outs],
        in_specs=specs or [VM] * len(ins),
        out_specs=out_specs or [VM] * len(outs),
        scratch_shapes=scratch,
        compiler_params=pltpu.CompilerParams(
            collective_id=cid, has_side_effects=True, vmem_limit_bytes=56 << 20
        ),
        name=name,
    )(*ins)


def greet(peers):
    barrier = pltpu.get_barrier_semaphore()
    for peer in peers:
        pl.semaphore_signal(barrier, inc=1, device_id=peer, device_id_type=MESH)


def met(peers):
    pl.semaphore_wait(pltpu.get_barrier_semaphore(), len(peers))


def send(src, dst, sems, slot, peer):
    cp = pltpu.make_async_remote_copy(
        src_ref=src,
        dst_ref=dst,
        send_sem=sems[0].at[slot],
        recv_sem=sems[1].at[slot],
        device_id=peer,
        device_id_type=MESH,
    )
    cp.start()
    return cp


def pair(*shape):
    return [DMA(shape), DMA(shape)]


def tp_place():
    ctx = lax.axis_index("ctx")
    tp = lax.axis_index("tp")
    return ctx, tp, tp // 2, tp % 2


def tp_peers(ctx, tp, z, c):
    return [(ctx, ((z + d) % 4) * 2 + c) for d in (1, 2, 3)] + [(ctx, z * 2 + 1 - c)]


def reduce_bufs(rows, width):
    return [
        pltpu.VMEM((4, rows, width), BF),
        pltpu.VMEM((3, rows, width), BF),
        pltpu.VMEM((3, rows, width), BF),
        *pair(4),
        *pair(3),
    ]


def chips(place):
    ctx, tp, z, c = place
    return (z + 2) % 4, (z + 1 + 2 * c) % 4, (z + 3 - 2 * c) % 4, z


def reduce_pass(part, bufs, place, k):
    ctx, tp, z, c = place
    chip = chips(place)[(0, 2, 1, 3)[k]]
    return send(part.at[chip * 2 + 1 - c], bufs[0].at[k], bufs[3:5], k, (ctx, z * 2 + 1 - c))


def reduce_send(part, bufs, place, passed, k, relayed=None):
    sib, snd, rcv = bufs[:3]
    ctx, tp, z, c = place
    two, way, other, own = chips(place)
    passed.wait_recv()
    both = part[(two, way, other)[k] * 2 + c].astype(F32) + sib[k].astype(F32)
    if k == 1:
        relayed.wait_recv()
        both = both + rcv[0].astype(F32)
    snd[k] = both.astype(BF)
    to = other if k == 2 else way
    return send(snd.at[k], rcv.at[k], bufs[5:7], k, (ctx, to * 2 + c))


def reduce_start(part, bufs, place):
    return [reduce_pass(part, bufs, place, k) for k in range(4)]


def reduce_middle(part, bufs, place, first):
    two = reduce_send(part, bufs, place, first[0], 0)
    other = reduce_send(part, bufs, place, first[2], 2)
    return [two, None, other]


def reduce_relay(part, bufs, place, first, second):
    second[1] = reduce_send(part, bufs, place, first[1], 1, second[0])


def reduce_end(part, bufs, place, first, second):
    sib, snd, rcv = bufs[:3]
    first[3].wait_recv()
    total = part[place[1]].astype(F32) + sib[3].astype(F32)
    for k in (2, 1):
        second[k].wait_recv()
        total = total + rcv[k].astype(F32)
    for cp in first + second:
        cp.wait_send()
    return total


def share_sems():
    return [*pair(3), *pair(4)]


def share_start(out, sems, place):
    ctx, tp, z, c = place
    two, way, other, own = chips(place)
    return [
        send(out.at[tp], out.at[tp], sems[:2], 0, (ctx, way * 2 + c)),
        send(out.at[tp], out.at[tp], sems[:2], 1, (ctx, other * 2 + c)),
        send(out.at[tp], out.at[tp], sems[2:], 0, (ctx, z * 2 + 1 - c)),
    ]


def share_pass(out, sems, place, started, k):
    ctx, tp, z, c = place
    two, way, other, own = chips(place)
    mate = (ctx, z * 2 + 1 - c)
    at = (other, way, two)[k] * 2 + c
    if k == 2:
        started[3].wait_recv()
    else:
        started[k].wait_recv()
    if k == 0:
        started.append(send(out.at[at], out.at[at], sems[:2], 2, (ctx, way * 2 + c)))
    passed = send(out.at[at], out.at[at], sems[2:], k + 1, mate)
    return passed


def share_end(out, sems, place, started, passed=()):
    passed = list(passed)
    passed += [share_pass(out, sems, place, started, k) for k in range(len(passed), 3)]
    started[2].wait_recv()
    for cp in passed:
        cp.wait_recv()
    for cp in started + passed:
        cp.wait_send()


def norm_scale(v):
    return lax.rsqrt(jnp.mean(v * v, axis=-1, keepdims=True) + NORM_EPSILON)


def norm_back(v, gain, grad):
    r = norm_scale(v)
    pulled = grad * gain
    inner = jnp.mean(pulled * v, axis=-1, keepdims=True)
    grad_v = r * pulled - v * (r * r * r) * inner
    return grad_v, jnp.sum(grad * v * r, axis=0, keepdims=True)


def dot(a, b):
    return jnp.dot(a, b, preferred_element_type=F32)


def dot_nt(a, b):
    return lax.dot_general(a, b, (((1,), (1,)), ((), ())), preferred_element_type=F32)


def dot_tn(a, b):
    return lax.dot_general(a, b, (((0,), (0,)), ((), ())), preferred_element_type=F32)


def dot_f(a, b):
    return jnp.dot(a, b, precision=lax.Precision.HIGHEST, preferred_element_type=F32)


def lanes(k, size):
    return pl.ds(pl.multiple_of(k * size, 128), size)


def split_out(dst, row, full, first):
    for k in range(full.shape[1] // 128):
        at = (first // 4, k) if len(dst.shape) == 4 else (first + k,)
        dst[(*at, slice(row, row + full.shape[0]))] = full[:, 128 * k : 128 * (k + 1)].astype(BF)


def eights(dst, row, full):
    for j in range(16):
        for k in range(0, full.shape[1] // 128, 2):
            two = [
                full[8 * j : 8 * j + 8, 128 * (k + i) : 128 * (k + i + 1)] for i in (0, 1)
            ]
            at = (j // 4, j % 4) if len(dst.shape) == 4 else (j,)
            dst[(*at, slice(row + 8 * k, row + 8 * k + 16))] = jnp.concatenate(two, axis=0).astype(
                BF
            )


def chooser(tp):
    r, c = iota((1024, 128), 0), iota((1024, 128), 1)
    return jnp.where((r // 128 == c // 16) & (r % 128 == tp * 16 + c % 16), 1.0, 0.0).astype(BF)


def fetch(src, dst, sem):
    cp = pltpu.make_async_copy(src, dst, sem)
    cp.start()
    return cp


def soft_plus(values):
    return jnp.maximum(values, 0.0) + jnp.log1p(jnp.exp(-jnp.abs(values)))


def pick(t, lengths, values):
    one = lengths[0]
    two = one + lengths[1]
    three = two + lengths[2]
    return jnp.where(
        t >= three,
        values[3],
        jnp.where(t >= two, values[2], jnp.where(t >= one, values[1], values[0])),
    )


def doc_start(t, lengths):
    one = lengths[0]
    two = one + lengths[1]
    return pick(t, lengths, (0, one, two, two + lengths[2]))


def iota(shape, axis):
    return lax.broadcasted_iota(jnp.int32, shape, axis)


def expander(heads):
    shape = (128, heads * MHEAD)
    return (iota(shape, 1) // MHEAD == iota(shape, 0)).astype(F32)


def collector(heads):
    shape = (heads * MHEAD, 128)
    return (iota(shape, 0) // MHEAD == iota(shape, 1)).astype(F32)


def spread(per_head, heads):
    return dot_f(per_head, expander(heads))


def head_sums(flat):
    return dot_f(flat, collector(flat.shape[1] // MHEAD))


def one_head(pair, h):
    return jnp.where(iota(pair.shape, 1) // MHEAD == h % 2, pair, jnp.zeros_like(pair))


def running_sum(dst, src, rows, later):
    for i in range(rows // 128):
        shape = (128, rows)
        t, s = i * 128 + iota(shape, 0), iota(shape, 1)
        tri = jnp.where((s >= t) if later else (s <= t), 1.0, 0.0)
        dst[pl.ds(i * 128, 128)] = dot_f(tri, src[...])


def fades(i, base, lengths):
    wide = (i + 1) * 128
    t = base + i * 128 + iota((128, 128), 0)
    start = doc_start(t, lengths)[:, 0:1]
    shape = (128, wide)
    s = base + iota(shape, 1)
    return (s <= base + i * 128 + iota(shape, 0)) & (s >= start)


FAR = -1e9


def doc_of(t, lengths):
    one = lengths[0]
    two = one + lengths[1]
    return (
        (t >= one).astype(jnp.int32)
        + (t >= two).astype(jnp.int32)
        + (t >= two + lengths[2]).astype(jnp.int32)
    )


def marked_keys(keys, base, lengths):
    shape = keys.shape
    mark = jnp.where(doc_of(base + iota(shape, 0), lengths) == iota(shape, 1), 1.0, 0.0)
    return jnp.concatenate([keys, mark.astype(BF)], axis=1)


def marked_queries(queries, base, lengths):
    shape = queries.shape
    row = iota(shape, 0)
    own = doc_of(base + iota(shape, 1), lengths) == row
    return jnp.concatenate([queries, jnp.where(own | (row > 3), 0.0, FAR).astype(BF)], axis=0)


def attend(scale, ctx, lengths, q, kv):
    block, size = kv.shape[2], q.shape[0]
    queries = marked_queries(q[...].T, ctx * block, lengths)
    factor = scale * LOG2E

    def step(blocks, carry, diagonal):
        top, total, acc = carry
        parts = []
        for i in blocks:
            keys = kv[i // 4, i % 4, :, :HD]
            s = dot(marked_keys(keys, i * block, lengths), queries) * factor
            if diagonal:
                s = jnp.where(iota(s.shape, 0) <= iota(s.shape, 1), s, FAR)
            parts.append(s)
        new = top
        for s in parts:
            new = jnp.maximum(new, jnp.max(s, axis=0, keepdims=True))
        fade = jnp.exp2(top - new)
        total = total * fade
        acc = acc * fade
        for i, s in zip(blocks, parts):
            p = jnp.exp2(s - new)
            total = total + jnp.sum(p, axis=0, keepdims=True)
            acc = acc + dot_tn(kv[i // 4, i % 4, :, HD:], p.astype(BF))
        return new, total, acc

    carry = (
        jnp.full((1, size), 2 * FAR, F32),
        jnp.zeros((1, size), F32),
        jnp.zeros((HD, size), F32),
    )
    some = ctx // UNROLL
    carry = lax.fori_loop(
        0, some, lambda i, k: step([UNROLL * i + n for n in range(UNROLL)], k, False), carry
    )
    carry = lax.fori_loop(UNROLL * some, ctx, lambda i, k: step([i], k, False), carry)
    top, total, acc = step([ctx], carry, True)
    return acc / total, top + jnp.log(total) * LOG2E


def attend_back(scale, ctx, lengths, q, kv, lse, low, grad_attn, dkv):
    block, size = kv.shape[2], q.shape[0]
    queries_t, queries = marked_queries(q[...].T, ctx * block, lengths), q[...]
    og = grad_attn[...]
    og_t = og.T
    factor = scale * LOG2E

    def step(blocks, acc, diagonal):
        for i in blocks:
            keys = kv[i // 4, i % 4, :, :HD]
            s = dot(marked_keys(keys, i * block, lengths), queries_t) * factor - lse
            if diagonal:
                s = jnp.where(iota(s.shape, 0) <= iota(s.shape, 1), s, FAR)
            p = jnp.exp2(s)
            dp = dot(kv[i // 4, i % 4, :, HD:], og_t)
            ds = (p * (dp - low)).astype(BF)
            dkv[i // 4, i % 4, :, :HD] = (dot(ds, queries) * scale).astype(BF)
            dkv[i // 4, i % 4, :, HD:] = dot(p.astype(BF), og).astype(BF)
            acc = acc + dot_tn(keys, ds)
        return acc

    some = ctx // 2
    acc = jnp.zeros((HD, size), F32)
    acc = lax.fori_loop(0, some, lambda i, k: step([2 * i, 2 * i + 1], k, False), acc)
    acc = lax.fori_loop(2 * some, ctx, lambda i, k: step([i], k, False), acc)
    return step([ctx], acc, True) * scale


def mlp_kernel(
    part,
    gain,
    b_out,
    a_gu,
    b_gu,
    a_dn,
    b_dn,
    mask,
    merged,
    hidden_far,
    w_gu_far,
    w_down_far,
    out_grad_far,
    low_out,
    grad_mixer_far,
    grad_low_gu,
    resid,
    grad_resid,
    gain_part,
    early_far,
    late_far,
    normed_mine,
    grad_mine,
    mixer_mine,
    source,
    w_gu,
    w_down,
    shared,
    shared_two,
    part_two,
    grad_act,
    low_dn_grad,
    low_gu,
    act,
    grad_gu,
    turned,
    picks,
    early,
    late_part,
    out_grad,
    loads,
    *scratch,
):
    place = tp_place()
    tp = place[1]
    peers = tp_peers(*place)
    greet(peers)
    share, model = resid.shape
    hidden = w_down.shape[0]
    rows = out_grad.shape[0]
    each = 128 // share
    rows_mine = pl.ds(pl.multiple_of(tp * share, share), share)
    get_source = fetch(hidden_far.at[rows_mine], source, loads.at[0])
    get_grad = fetch(out_grad_far, out_grad, loads.at[7])
    get_down = fetch(w_down_far, w_down, loads.at[1])
    get_gu = fetch(w_gu_far, w_gu, loads.at[2])
    bufs, sems, more, sems_two = scratch[:7], scratch[7:11], scratch[11:18], scratch[18:]
    met(peers)
    first = reduce_start(part, bufs, place)
    second = reduce_middle(part, bufs, place, first)

    def span_of(i):
        return pl.ds(pl.multiple_of(i * 128, 128), 128)

    get_grad.wait()
    get_down.wait()

    low_dn_grad[...] = (dot_nt(out_grad[...], b_dn[...]) * mask[...]).astype(BF)
    grad_act[...] = (dot_nt(out_grad[...], w_down[...]) + dot_nt(low_dn_grad[...], a_dn[...])).astype(
        BF
    )
    reduce_relay(part, bufs, place, first, second)
    get_source.wait()
    total = reduce_end(part, bufs, place, first, second)
    low = total[:, model:].astype(BF)
    residual = source[...].astype(F32) + total[:, :model] + dot(low, b_out[...])
    resid[...] = residual
    shared[tp, :, :model] = (residual * norm_scale(residual) * gain[...]).astype(BF)
    shared[tp, :, model:] = low
    started = share_start(shared, sems, place)
    get_gu.wait()

    def both_ways(*some):
        def rows_at(ref):
            return jnp.concatenate([ref[span_of(i)] for i in some], axis=0)

        def put(ref, value):
            for k, i in enumerate(some):
                ref[span_of(i)] = value[128 * k : 128 * (k + 1)]

        block = jnp.concatenate(
            [shared[pl.ds(i * each, each)].reshape(128, -1) for i in some], axis=0
        )
        n = block[:, :model]
        put(low_out, block[:, model:])
        low = (dot(n, a_gu[...]) * rows_at(mask)).astype(BF)
        put(low_gu, low)
        h = (dot(n, w_gu[...]) + dot(low, b_gu[...])).astype(BF).astype(F32)
        gate, up = h[:, :hidden], h[:, hidden:]
        sig = jax.nn.sigmoid(gate)
        put(act, (gate * sig * up).astype(BF))
        pulled = rows_at(grad_act).astype(F32)
        grad = jnp.concatenate(
            [pulled * up * sig * (1.0 + gate * (1.0 - sig)), pulled * (gate * sig)], axis=1
        ).astype(BF)
        put(grad_gu, grad)
        full = dot_nt(grad, w_gu[...]).astype(BF)
        low = dot_nt(grad, b_gu[...]).astype(BF)
        for n_th, i in enumerate(some):
            for k in range(each):
                part_of = slice(n_th * 128 + k * share, n_th * 128 + (k + 1) * share)
                part_two[i * each + k, :, :model] = full[part_of]
                part_two[i * each + k, :, model:] = low[part_of]

    chip = chips(place)
    started[2].wait_recv()
    both_ways(chip[3])
    third = reduce_pass(part_two, more, place, 3)
    passed = [share_pass(shared, sems, place, started, k) for k in (0, 1)]
    passed[1].wait_recv()
    passed[0].wait_recv()
    both_ways(chip[1], chip[2])
    pass_one = reduce_pass(part_two, more, place, 1)
    pass_two = reduce_pass(part_two, more, place, 2)
    passed.append(share_pass(shared, sems, place, started, 2))
    send_two = reduce_send(part_two, more, place, pass_two, 2)
    passed[2].wait_recv()
    both_ways(chip[0])
    pass_none = reduce_pass(part_two, more, place, 0)
    turned[...] = grad_gu[...].T
    wide = grad_gu.shape[1]
    send_none = reduce_send(part_two, more, place, pass_none, 0)

    def weights(j, carry):
        some = shared[:, :, lanes(j, 512)].reshape(rows, 512)
        split_out(early, 0, dot(turned[...], some), 4 * j)
        return carry

    lax.fori_loop(0, 2, weights, 0)
    send_one = reduce_send(part_two, more, place, pass_one, 1, send_none)
    lax.fori_loop(2, 4, weights, 0)
    total = reduce_end(
        part_two, more, place, [pass_none, pass_one, pass_two, third], [send_none, send_one, send_two]
    )
    low = (total[:, model:] * mask[rows_mine]).astype(BF)
    grad = total[:, :model] + dot_nt(low, a_gu[...])
    grad_v, grad_gain = norm_back(resid[...], gain[...], grad)
    grad_r = out_grad[rows_mine].astype(F32) + grad_v
    grad_resid[...] = grad_r
    gain_part[...] = grad_gain
    shared_two[tp, :, :model] = grad_r.astype(BF)
    shared_two[tp, :, model:] = low
    for cp in started + passed:
        cp.wait_send()
    started = share_start(shared_two, sems_two, place)
    eights(early, wide + 2 * hidden, dot_tn(low_gu[...], grad_gu[...]))
    eights(early, 2 * wide + 64, dot_tn(low_dn_grad[...], act[...]))
    picks[...] = chooser(tp)
    half = model // 2
    for k in range(2):
        cols = slice(half * k, half * (k + 1))
        to = slice(128 * k, 128 * (k + 1))
        normed_mine[:, to] = dot(shared[:, :, cols].reshape(rows, half), picks[...]).astype(BF)
        grad_mine[:, to] = dot(out_grad[:, cols], picks[...]).astype(BF)
    passed = [share_pass(shared_two, sems_two, place, started, k) for k in (0, 1)]
    turned[0:hidden] = act[...].T

    def weights_two(j, carry):
        split_out(early, wide, dot(turned[0:hidden], out_grad[:, lanes(j, 512)]), 4 * j)
        return carry

    lax.fori_loop(0, 4, weights_two, 0)
    passed.append(share_pass(shared_two, sems_two, place, started, 2))
    rows_in = (pl.ds(0, wide + hidden), pl.ds(wide + 2 * hidden, 96), pl.ds(wide + hidden, hidden))
    stores = [
        fetch(early.at[:, rows_in[k]], early_far.at[:, rows_in[k]], loads.at[3 + k]) for k in (0, 1)
    ]

    def forward_rest(i, carry):
        at = pl.ds(pl.multiple_of(i * 256, 256), 256)
        a = act[at]
        full = dot(a, w_down[...]).astype(BF)
        low = (dot(a, a_dn[...]) * mask[at]).astype(BF)
        for k in range(2 * each):
            late_part[i * 2 * each + k, :, :model] = full[k * share : (k + 1) * share]
            late_part[i * 2 * each + k, :, model:] = low[k * share : (k + 1) * share]
        return carry

    lax.fori_loop(0, rows // 256, forward_rest, 0)
    stores.append(fetch(late_part, late_far, loads.at[6]))
    turned[hidden:] = merged[...].T
    share_end(shared_two, sems_two, place, started, passed)
    for k in range(8):
        to = pl.ds(k * share, share)
        grad_low_gu[to] = shared_two[k, :, model:]
        stores.append(
            fetch(shared_two.at[k, :, pl.ds(0, model)], grad_mixer_far.at[to], loads.at[8 + k])
        )
    for k in range(2):
        cols = slice(half * k, half * (k + 1))
        some = shared_two[:, :, cols].reshape(rows, half)
        mixer_mine[:, 128 * k : 128 * (k + 1)] = dot(some, picks[...]).astype(BF)

    def weights_three(j, carry):
        some = shared_two[:, :, lanes(j, 512)].reshape(rows, 512)
        split_out(early, wide + hidden, dot(turned[hidden:], some), 4 * j)
        return carry

    lax.fori_loop(0, 4, weights_three, 0)
    stores.append(fetch(early.at[:, rows_in[2]], early_far.at[:, rows_in[2]], loads.at[5]))
    for cp in stores:
        cp.wait()


def mlp_exchange(
    part, gain, b_out, a_gu, b_gu, a_dn, b_dn, mask, merged, hidden_in, w_gu, w_down, out_grad
):
    _, share, wide = part.shape
    rows, model = out_grad.shape
    hidden = w_down.shape[0]
    rank = a_gu.shape[1]
    return call(
        mlp_kernel,
        [
            ((rows, rank), BF),
            ((rows, model), BF),
            ((rows, rank), BF),
            ((share, model), F32),
            ((share, model), F32),
            ((1, model), F32),
            ((16, 4 * hidden + 96, 128), BF),
            (part.shape, BF),
            ((rows, 256), BF),
            ((rows, 256), BF),
            ((rows, 256), BF),
        ],
        [part, gain, b_out, a_gu, b_gu, a_dn, b_dn, mask, merged, hidden_in, w_gu, w_down, out_grad],
        [
            pltpu.VMEM((share, model), BF),
            pltpu.VMEM(w_gu.shape, BF),
            pltpu.VMEM(w_down.shape, BF),
            pltpu.VMEM(part.shape, BF),
            pltpu.VMEM(part.shape, BF),
            pltpu.VMEM(part.shape, BF),
            pltpu.VMEM((rows, hidden), BF),
            pltpu.VMEM((rows, rank), BF),
            pltpu.VMEM((rows, rank), BF),
            pltpu.VMEM((rows, hidden), BF),
            pltpu.VMEM((rows, 2 * hidden), BF),
            pltpu.VMEM((2 * hidden, rows), BF),
            pltpu.VMEM((1024, 128), BF),
            pltpu.VMEM((16, 4 * hidden + 96, 128), BF),
            pltpu.VMEM(part.shape, BF),
            pltpu.VMEM(out_grad.shape, BF),
            DMA((16,)),
            *reduce_bufs(share, wide),
            *share_sems(),
            *reduce_bufs(share, wide),
            *share_sems(),
        ],
        2,
        "mlp_exchange",
        [VM] * 9 + [HB] * 4,
        [VM, HB] + [VM] * 4 + [HB] * 2 + [VM] * 3,
    )


def ctx_place():
    ctx = lax.axis_index("ctx")
    return ctx, lax.axis_index("tp"), ctx // 4, ctx % 4


def spot(h, fast, slow):
    return slow * 4 + fast if h == 0 else fast * 4 + slow


def scatter_bufs(rows, width):
    most = max(rows - rows // 32 * 16, rows // 32 * 16)
    return [
        pltpu.VMEM((2, 3, most, width), BF),
        pltpu.VMEM((2, 3, 4, most, width), BF),
        pltpu.VMEM((2, 3, most, width), BF),
        *pair(2, 3, 4),
        *pair(2, 3),
    ]


def spans_of(rows):
    half = rows // 32 * 16
    return ((0, half), (half, rows - half))


def block_of(ref, h, fast, slow):
    return ref.at[slow, fast] if h == 0 else ref.at[fast, slow]


def scatter_start(part, bufs, place, at_once=False):
    mid, r1, r2, s1s, s1r, s2s, s2r = bufs
    ctx, tp, y, x = place
    spans = spans_of(part.shape[2])
    first = {}
    for j in (0,) if at_once else OFFSETS + (0,):
        for off in OFFSETS:
            for h in (0, 1):
                fast, slow = ((x, y), (y, x))[h]
                lo, size = spans[h]
                to = (fast + off) % 4
                if at_once:
                    src = part.at[:, to] if h == 0 else part.at[to]
                    src = src.at[:, pl.ds(lo, size)]
                    dst = r1.at[h, off - 1, :, pl.ds(0, size)]
                else:
                    other = (slow + j) % 4
                    src = block_of(part, h, to, other).at[pl.ds(lo, size)]
                    dst = r1.at[h, off - 1, other, pl.ds(0, size)]
                first[h, off, j] = send(
                    src, dst, (s1s, s1r), (h, off - 1, j), (spot(h, to, slow), tp)
                )
    return first


def scatter_middle(part, out, bufs, place, first):
    mid, r1, r2, s1s, s1r, s2s, s2r = bufs
    ctx, tp, y, x = place
    spans = spans_of(part.shape[2])
    at_once = len(first) == 6
    second = {}
    for j in OFFSETS + (0,):
        for h in (0, 1):
            fast, slow = ((x, y), (y, x))[h]
            lo, size = spans[h]
            if not at_once or j == OFFSETS[0]:
                for off in OFFSETS:
                    first[h, off, 0 if at_once else j].wait_recv()
            other = (slow + j) % 4
            total = block_of(part, h, fast, other)[pl.ds(lo, size)].astype(F32)
            for off in (1, 2, 3):
                total = total + r1[h, off - 1, other, pl.ds(0, size)].astype(F32)
            if j == 0:
                out[pl.ds(lo, size)] = total
            else:
                mid[h, j - 1, pl.ds(0, size)] = total.astype(BF)
                second[h, j] = send(
                    mid.at[h, j - 1, pl.ds(0, size)],
                    r2.at[h, j - 1, pl.ds(0, size)],
                    (s2s, s2r),
                    (h, j - 1),
                    (spot(h, fast, other), tp),
                )
    return second


def scatter_end(part, out, bufs, first, second):
    r2 = bufs[2]
    for h, (lo, size) in enumerate(spans_of(part.shape[2])):
        for j in OFFSETS:
            second[h, j].wait_recv()
        total = out[pl.ds(lo, size)]
        for j in (1, 2, 3):
            total = total + r2[h, j - 1, pl.ds(0, size)].astype(F32)
        out[pl.ds(lo, size)] = total
    for cp in list(first.values()) + list(second.values()):
        cp.wait_send()


def ctx_peers(ctx, tp):
    return [((ctx + d) % 16, tp) for d in range(1, 16)]


def swap_start(src, dst, sems, place):
    ctx, tp = place[:2]
    return [
        send(src.at[(ctx + d) % 16], dst.at[ctx], sems, d - 1, ((ctx + d) % 16, tp))
        for d in range(1, 16)
    ]


def pack_state(state, decay, msg):
    width = decay.shape[1]
    for j in range(16):
        msg[j, :, :width] = state[16 * j : 16 * (j + 1)].astype(BF)
    high = decay[0:1].astype(BF).astype(F32)
    low = decay[0:1] - high
    row = lax.broadcasted_iota(jnp.int32, (16, 128), 0)
    tile = jnp.zeros((16, 128), F32)
    count = width // 128
    for k in range(count):
        span = slice(128 * k, 128 * (k + 1))
        tile = jnp.where(row == k, high[:, span], tile)
        tile = jnp.where(row == count + k, low[:, span], tile)
    for j in range(16):
        msg[j, :, width:] = tile.astype(BF)


def prefix_into(order, got, ent):
    width = ent.shape[2]
    count = width // 128
    running = jnp.zeros(ent.shape[1:], F32)
    for i in order:
        ent[i] = running.astype(BF)
        tile = got[i, :, width:].astype(F32)
        decay = jnp.concatenate(
            [tile[k : k + 1] + tile[count + k : count + k + 1] for k in range(count)], axis=1
        )
        running = got[i, :, :width].astype(F32) + decay * running


def front_kernel(
    scale,
    lengths,
    ids,
    hidden,
    gain,
    a_in,
    a_sh,
    w_dt,
    b_in,
    b_sh,
    params,
    a_out,
    w_in_far,
    w_sh_far,
    w_out_far,
    normed_far,
    low_in,
    low_sh,
    z_out,
    xs,
    q_out,
    bc,
    mask,
    decay,
    dt,
    pre,
    total,
    entering,
    ssd,
    kv_far,
    part_out,
    attn_t,
    lse,
    merged,
    normed,
    gated,
    kv_all,
    w_in,
    w_sh,
    w_out,
    kv,
    work,
    row_decay,
    row_dt,
    x_one,
    inner,
    state,
    msg,
    got,
    ent,
    loads,
    *sems,
):
    place = ctx_place()
    ctx, tp, y, x = place
    c = tp % 2
    mate = (ctx, tp + 1 - 2 * c)
    peers = ctx_peers(ctx, tp) + [mate]
    greet(peers)
    get_sh = fetch(w_sh_far, w_sh, loads.at[0])
    get_in = fetch(w_in_far, w_in, loads.at[1])
    get_out = fetch(w_out_far, w_out, loads.at[2])
    rows = hidden.shape[0]
    width = ssd.shape[1]
    heads = width // MHEAD
    base = ctx * rows
    blocks = rows // 128

    def span_of(i):
        return pl.ds(pl.multiple_of(i * 128, 128), 128)

    def norms(i, carry):
        at = span_of(i)
        v = hidden[at].astype(F32)
        normed[at] = (v * norm_scale(v) * gain[...]).astype(BF)
        t = base + i * 128 + iota((128, 128), 0)
        chosen = pick(t, lengths, [ids[k] for k in range(4)])
        mask[at] = (chosen == iota((128, 128), 1) // RANK).astype(F32)
        return carry

    lax.fori_loop(0, blocks, norms, 0)
    get_sh.wait()

    low_sh[...] = (dot(normed[...], a_sh[...]) * mask[...]).astype(BF)
    lo = 2 * STATE
    h = dot(normed[...], w_sh[:, lo:]) + dot(low_sh[...], b_sh[:, lo:])
    group = tp // (QHEADS // KVH)
    for k in range(2):
        one = h[:, 2 * k * HD : (2 * k + 1) * HD]
        two = h[:, (2 * k + 1) * HD : (2 * k + 2) * HD]
        kv[:, HD * k : HD * (k + 1)] = jnp.where(group == 0, one, two).astype(BF)
    met(peers)
    s_one, s_two, s_kv1, s_kv2, s_m1, s_m2 = [sems[2 * k : 2 * k + 2] for k in range(6)]
    half = rows // 2
    part = half // 2
    mine = pl.multiple_of(c * half, half)
    span = [pl.ds(pl.multiple_of(mine + h * part, part), part) for h in (0, 1)]
    kv1 = {}
    for off in OFFSETS:
        for h in (0, 1):
            fast, slow = ((x, y), (y, x))[h]
            kv1[h, off] = send(
                kv.at[span[h]],
                kv_all.at[y, x, span[h]],
                s_kv1,
                (h, off - 1),
                (spot(h, (fast + off) % 4, slow), tp),
            )
    kv_all[y, x] = kv[...]
    keep_normed = fetch(normed, normed_far, loads.at[3])
    bc[...] = (dot(normed[...], w_sh[:, :lo]) + dot(low_sh[...], b_sh[:, :lo])).astype(BF)
    get_in.wait()
    low_in[...] = (dot(normed[...], a_in[...]) * mask[...]).astype(BF)
    h = (dot(normed[...], w_in[...]) + dot(low_in[...], b_in[...])).astype(BF)
    z_out[...] = h[:, :width]
    xs[...] = h[:, width : 2 * width]
    q_out[...] = h[:, 2 * width :]
    v = dot_nt(normed[...], w_dt[...]) + params[0:1]
    pre[...] = v
    v = soft_plus(v)
    dt[...] = v
    work[...] = -v * jnp.exp(params[1:2])
    running_sum(decay, work, rows, False)
    row_decay[...] = decay[...].T
    row_dt[...] = dt[...].T
    for h in range(heads):
        x_one[h] = one_head(xs[:, (h // 2) * 128 : (h // 2 + 1) * 128], h)
    final = decay[rows - 1 : rows]
    last_start = doc_start(base + rows - 1, lengths)
    tail = jnp.where(
        base + iota((rows, 128), 0) >= last_start, jnp.exp(final - decay[...]) * dt[...], 0.0
    )
    scaled = (spread(tail, heads) * xs[...].astype(F32)).astype(BF)
    state[...] = dot_tn(bc[:, :STATE], scaled)
    through = jnp.where(last_start < base, 1.0, 0.0)
    whole = jnp.broadcast_to(jnp.exp(final) * through, (8, 128))
    total[...] = spread(whole, heads)
    pack_state(state, total, msg)
    one = swap_start(msg, got, s_one, place)
    got[ctx] = msg[ctx]
    kv2, to_mate = {}, []
    for off in OFFSETS:
        for h in (0, 1):
            kv1[h, off].wait_recv()

    def line(h, at):
        return (kv_all.at[at] if h == 0 else kv_all.at[:, at]).at[:, span[h]]

    for off in OFFSETS:
        for h in (0, 1):
            fast, slow = ((x, y), (y, x))[h]
            kv2[h, off] = send(
                line(h, slow),
                line(h, slow),
                s_kv2,
                (h, off - 1),
                (spot(h, fast, (slow + off) % 4), tp),
            )
    for off in OFFSETS:
        for h in (0, 1):
            fast, slow = ((x, y), (y, x))[h]
            block = block_of(kv_all, h, (fast + 4 - off) % 4, slow).at[span[h]]
            to_mate.append(send(block, block, s_m1, (h, off - 1), mate))
    for i in range(blocks):
        at = pl.ds(i * 128, 128)
        wide = (i + 1) * 128
        seen = fades(i, base, lengths)
        inter = dot_nt(bc[at, STATE:], bc[0:wide, :STATE])
        for pair_at in range(heads // 2):
            acc = jnp.zeros((128, 128), F32)
            for h in (2 * pair_at, 2 * pair_at + 1):
                gap = decay[at, h : h + 1] - row_decay[h : h + 1, 0:wide]
                fade = jnp.exp(jnp.where(seen, gap, -1e30))
                mixing = (inter * fade * row_dt[h : h + 1, 0:wide]).astype(BF)
                acc = acc + dot(mixing, x_one[h, 0:wide])
            inner[at, pair_at * 128 : (pair_at + 1) * 128] = acc
    for cp in one:
        cp.wait_recv()
    prefix_into(range(16), got, ent)
    two = swap_start(ent, entering, s_two, place)
    entering[ctx] = ent[ctx]
    for off in OFFSETS:
        for h in (0, 1):
            fast, slow = ((x, y), (y, x))[h]
            kv2[h, off].wait_recv()
            came = line(h, (slow + 4 - off) % 4)
            to_mate.append(send(came, came, s_m2, (h, off - 1), mate))
    for cp in two:
        cp.wait_recv()
    arrived = entering[...].reshape(STATE, width)

    def finish(i, carry):
        at = span_of(i)
        t = base + i * 128 + iota((128, 128), 0)
        reach = jnp.where(doc_start(t, lengths) < base, jnp.exp(decay[at]), 0.0)
        cross = dot(bc[at, STATE:], arrived) * spread(reach, heads)
        skip = spread(jnp.broadcast_to(params[2:3], (8, 128)), heads)[0:1]
        out = inner[at] + cross + skip * xs[at].astype(F32)
        ssd[at] = out
        z = z_out[at].astype(F32)
        gated[at] = (out * (z * jax.nn.sigmoid(z))).astype(BF)
        return carry

    lax.fori_loop(0, blocks, finish, 0)
    for cp in to_mate:
        cp.wait_recv()
    keep_kv = fetch(kv_all, kv_far, loads.at[4])
    out, lse[...] = attend(scale, ctx, lengths, q_out, kv_all)
    attn_t[...] = out
    merged[:, :width] = gated[...]
    merged[:, width:] = out.T.astype(BF)
    get_out.wait()
    model = w_out.shape[1]
    share = part_out.shape[1]
    low = (dot(merged[...], a_out[...]) * mask[...]).astype(BF)
    for k in range(8):
        part_out[k, :, model:] = low[k * share : (k + 1) * share]

    def mix(j, carry):
        cols = lanes(j, 512)
        full = dot(merged[...], w_out[:, cols]).astype(BF)
        for k in range(8):
            part_out[k, :, cols] = full[k * share : (k + 1) * share]
        return carry

    lax.fori_loop(0, model // 512, mix, 0)
    for cp in one + two + to_mate + list(kv1.values()) + list(kv2.values()):
        cp.wait_send()
    keep_normed.wait()
    keep_kv.wait()


def front_exchange(scale, *args):
    hidden, a_in, a_out, w_in, w_sh, w_out = (args[k] for k in (2, 4, 10, 11, 12, 13))
    rows, model = hidden.shape
    width = (w_in.shape[1] - HD) // 2
    heads = width // MHEAD
    rank = a_in.shape[1]
    return call(
        functools.partial(front_kernel, scale),
        [
            ((rows, model), BF),
            ((rows, rank), BF),
            ((rows, rank), BF),
            ((rows, width), BF),
            ((rows, width), BF),
            ((rows, HD), BF),
            ((rows, 2 * STATE), BF),
            ((rows, 128), F32),
            ((rows, 128), F32),
            ((rows, 128), F32),
            ((rows, 128), F32),
            ((8, width), F32),
            ((16, 16, width), BF),
            ((rows, width), F32),
            ((4, 4, rows, 2 * HD), BF),
            ((8, rows // 8, model + rank), BF),
            ((HD, rows), F32),
            ((1, rows), F32),
            ((rows, width + HD), BF),
        ],
        list(args),
        [
            pltpu.VMEM((rows, model), BF),
            pltpu.VMEM((rows, width), BF),
            pltpu.VMEM((4, 4, rows, 2 * HD), BF),
            pltpu.VMEM(w_in.shape, BF),
            pltpu.VMEM(w_sh.shape, BF),
            pltpu.VMEM(w_out.shape, BF),
            pltpu.VMEM((rows, 2 * HD), BF),
            pltpu.VMEM((rows, 128), F32),
            pltpu.VMEM((128, rows), F32),
            pltpu.VMEM((128, rows), F32),
            pltpu.VMEM((heads, rows, 128), BF),
            pltpu.VMEM((rows, width), F32),
            pltpu.VMEM((STATE, width), F32),
            pltpu.VMEM((16, 16, width + 128), BF),
            pltpu.VMEM((16, 16, width + 128), BF),
            pltpu.VMEM((16, 16, width), BF),
            DMA((5,)),
            *pair(15),
            *pair(15),
            *pair(2, 3),
            *pair(2, 3),
            *pair(2, 3),
            *pair(2, 3),
        ],
        4,
        "front_exchange",
        [SM, SM] + [VM] * 9 + [HB] * 3,
        [HB] + [VM] * 13 + [HB] + [VM] * 4,
    )


def back_kernel(
    scale,
    lengths,
    total,
    resid,
    b_dn,
    bc,
    xs,
    decay,
    dt,
    pre,
    params,
    entering,
    b_in,
    b_sh,
    w_dt,
    q,
    lse,
    attn_t,
    grad_mixer,
    w_out,
    b_out,
    a_out,
    mask,
    z_in,
    ssd,
    kv_far,
    part_far,
    w_in_far,
    w_sh_far,
    gathered,
    part_out,
    two_out,
    grad_one,
    grad_head,
    grad_low,
    kv,
    part,
    w_in,
    w_sh,
    dkv,
    grad_attn,
    grad_ssd,
    grad_z,
    hold,
    msg,
    got,
    ent,
    leaving,
    both,
    dkv_sum,
    kv_rows,
    grad_two,
    row_decay,
    row_dt,
    col_sum,
    row_sum,
    x_one,
    dy_one,
    dx,
    grad_b,
    grad_c,
    work,
    loads,
    *scratch,
):
    place = ctx_place()
    ctx, tp, y, x = place
    tp_at = tp_place()
    c = tp % 2
    mate = (ctx, tp + 1 - 2 * c)
    peers = ctx_peers(ctx, tp) + tp_peers(*tp_at)
    greet(peers)
    get_kv = fetch(kv_far, kv, loads.at[0])
    get_part = fetch(part_far, part, loads.at[1])
    get_in = fetch(w_in_far, w_in, loads.at[2])
    get_sh = fetch(w_sh_far, w_sh, loads.at[3])
    rows, width = xs.shape
    heads = width // MHEAD
    base = ctx * rows
    blocks = rows // 128
    s_one, s_two, s_mate = scratch[0:2], scratch[2:4], scratch[4:6]
    bufs, more, sems = scratch[6:13], scratch[13:20], scratch[20:]

    grad_low[...] = (dot_nt(grad_mixer[...], b_out[...]) * mask[...]).astype(BF)
    grad = (dot_nt(grad_mixer[...], w_out[...]) + dot_nt(grad_low[...], a_out[...])).astype(BF)
    grad_attn[...] = grad[:, width:]
    gated = grad[:, :width].astype(F32)
    z = z_in[...].astype(F32)
    sig = jax.nn.sigmoid(z)
    grad_z[...] = (gated * ssd[...] * sig * (1.0 + z * (1.0 - sig))).astype(BF)
    gated = gated * (z * sig)
    grad_ssd[...] = gated
    reach = jnp.where(
        doc_start(base + iota((rows, 128), 0), lengths) < base, jnp.exp(decay[...]), 0.0
    )
    hold[...] = (spread(reach, heads) * gated).astype(BF)
    pack_state(dot_tn(bc[:, STATE:], hold[...]), total, msg)
    met(peers)
    one = swap_start(msg, got, s_one, place)
    got[ctx] = msg[ctx]
    get_part.wait()
    first_z = reduce_start(part, more, tp_at)
    low = jnp.sum(grad_attn[...].T.astype(F32) * attn_t[...], axis=0, keepdims=True)
    dkv[...] = jnp.zeros(dkv.shape, BF)
    get_kv.wait()
    second_z = reduce_middle(part, more, tp_at, first_z)
    dq = attend_back(scale, ctx, lengths, q, kv, lse[...], low, grad_attn, dkv)
    grad_one[:, 2 * width : 2 * width + HD] = dq.T.astype(BF)
    half = rows // 2
    mine = pl.ds(pl.multiple_of(c * half, half), half)
    other = pl.ds(pl.multiple_of((1 - c) * half, half), half)
    cps = [send(dkv.at[k, :, other], both.at[k], s_mate, k, mate) for k in range(4)]
    reduce_relay(part, more, tp_at, first_z, second_z)
    for cp in one:
        cp.wait_recv()
    prefix_into(range(15, -1, -1), got, ent)
    two = swap_start(ent, leaving, s_two, place)
    leaving[ctx] = ent[ctx]
    for k in range(4):
        cps[k].wait_recv()
        for i in range(4):
            both[k, i] = (dkv[k, i, mine].astype(F32) + both[k, i].astype(F32)).astype(BF)
    first = scatter_start(both, bufs, place)

    row_decay[...] = decay[...].T
    row_dt[...] = dt[...].T
    col_sum[...] = jnp.zeros(col_sum.shape, F32)
    for h in range(heads):
        cols = slice((h // 2) * 128, (h // 2 + 1) * 128)
        x_one[h] = one_head(xs[:, cols], h)
        dy_one[h] = one_head(grad_ssd[:, cols], h).astype(BF)
    grad_b[...] = jnp.zeros(grad_b.shape, F32)
    dx[...] = jnp.zeros(dx.shape, F32)
    for i in range(blocks):
        at = pl.ds(i * 128, 128)
        wide = (i + 1) * 128
        seen = fades(i, base, lengths)
        inter = dot_nt(bc[at, STATE:], bc[0:wide, :STATE])
        d_inter = jnp.zeros((128, wide), F32)
        sums = jnp.zeros((128, 128), F32)
        for pair_at in range(heads // 2):
            cols = slice(pair_at * 128, (pair_at + 1) * 128)
            for h in (2 * pair_at, 2 * pair_at + 1):
                step = row_dt[h : h + 1, 0:wide]
                gap = decay[at, h : h + 1] - row_decay[h : h + 1, 0:wide]
                fade = jnp.exp(jnp.where(seen, gap, -1e30))
                d_mix = dot_nt(dy_one[h, at], x_one[h, 0:wide])
                faded = fade * step
                d_inter = d_inter + d_mix * faded
                weighted = d_mix * inter * fade
                col_sum[h : h + 1, 0:wide] += jnp.sum(weighted, axis=0, keepdims=True)
                sums = jnp.where(
                    iota((128, 128), 1) == h,
                    jnp.sum(weighted * step, axis=1, keepdims=True),
                    sums,
                )
                dx[0:wide, cols] += dot_tn((inter * faded).astype(BF), dy_one[h, at])
        row_sum[at] = sums
        low = d_inter.astype(BF)
        grad_c[at] = dot(low, bc[0:wide, :STATE])
        grad_b[0:wide] += dot_tn(low, bc[at, STATE:])

    width_out = resid.shape[1]
    out = reduce_end(part, more, tp_at, first_z, second_z)
    low = out[:, width_out:].astype(BF)
    gathered[tp, :, :width_out] = (resid[...] + out[:, :width_out] + dot(low, b_dn[...])).astype(BF)
    gathered[tp, :, width_out:] = low
    started = share_start(gathered, sems, tp_at)
    second = scatter_middle(both, dkv_sum, bufs, place, first)

    for cp in two:
        cp.wait_recv()
    after = leaving[...].reshape(STATE, width)
    before = entering[...].reshape(STATE, width)
    final = decay[rows - 1 : rows]
    last_start = doc_start(base + rows - 1, lengths)
    cols_sum = col_sum[...].T
    crossing = head_sums(
        jnp.broadcast_to(
            jnp.sum(after.astype(F32) * before.astype(F32), axis=0, keepdims=True) * total[0:1],
            (8, width),
        )
    )[0:1]
    rate = jnp.exp(params[1:2])
    skip = spread(jnp.broadcast_to(params[2:3], (8, 128)), heads)[0:1]
    d_last = crossing
    skips = jnp.zeros((1, 128), F32)
    for i in range(blocks):
        at = pl.ds(i * 128, 128)
        t = base + i * 128 + iota((128, 128), 0)
        steps = dt[at]
        tail = jnp.where(t >= last_start, jnp.exp(final - decay[at]), 0.0)
        reach = jnp.where(doc_start(t, lengths) < base, jnp.exp(decay[at]), 0.0)
        x_f = xs[at].astype(F32)
        gs = grad_ssd[at]
        came = dot(bc[at, :STATE], after)
        held = head_sums(came * x_f) * tail
        reached = spread(reach, heads) * gs
        d_cross = head_sums(dot(bc[at, STATE:], before) * reached)
        cols_at = cols_sum[i * 128 : (i + 1) * 128]
        work[at] = row_sum[at] - cols_at * steps + d_cross - held * steps
        row_sum[at] = cols_at + held
        d_last = d_last + jnp.sum(held * steps, axis=0, keepdims=True)
        tails = spread(tail * steps, heads)
        grad_one[at, :width] = grad_z[at]
        grad_one[at, width : 2 * width] = (dx[at] + tails * came + skip * gs).astype(BF)
        skips = skips + jnp.sum(head_sums(gs * x_f), axis=0, keepdims=True)
        grad_two[at, :STATE] = (grad_b[at] + dot_nt((tails * x_f).astype(BF), after)).astype(BF)
        grad_two[at, STATE : 2 * STATE] = (grad_c[at] + dot_nt(reached.astype(BF), before)).astype(
            BF
        )
    passed = [share_pass(gathered, sems, tp_at, started, k) for k in (0, 1)]
    running_sum(dx.at[:, 0:128], work, rows, True)
    d_log = dx[:, 0:128] + d_last
    grad_dt = (row_sum[...] - rate * d_log) * jax.nn.sigmoid(pre[...])
    grad_one[:, 2 * width + HD :] = grad_dt.astype(BF)
    grad_head[0:1] = jnp.sum(grad_dt, axis=0, keepdims=True)
    grad_head[1:2] = -jnp.sum(dt[...] * rate * d_log, axis=0, keepdims=True)
    grad_head[2:3] = skips
    grad_head[3:8] = jnp.zeros((5, 128), F32)
    get_in.wait()
    get_sh.wait()
    narrow = 2 * width + HD

    model = resid.shape[1]
    rank = b_in.shape[0]
    share = resid.shape[0]

    def norm_part(j, carry):
        cols = lanes(j, 512)
        full = (
            dot_nt(grad_one[:, :narrow], w_in[cols])
            + dot(grad_one[:, narrow:], w_dt[:, cols])
            + dot_nt(grad_two[:, : 2 * STATE], w_sh[cols, : 2 * STATE])
        ).astype(BF)
        for k in range(8):
            part_out[k, :, cols] = full[k * share : (k + 1) * share]
        return carry

    lax.fori_loop(0, resid.shape[1] // 512, norm_part, 0)
    passed.append(share_pass(gathered, sems, tp_at, started, 2))
    low_one = dot_nt(grad_one[:, :narrow], b_in[...]).astype(BF)
    for k in range(8):
        part_out[k, :, model : model + rank] = low_one[k * share : (k + 1) * share]
    scatter_end(both, dkv_sum, bufs, first, second)
    kv_rows[...] = jnp.zeros(kv_rows.shape, F32)
    kv_rows[mine] = dkv_sum[...]
    group = tp // (QHEADS // KVH)
    for k in range(KVH):
        on = jnp.where(group == k, 1.0, 0.0)
        for v in range(2):
            lo = 2 * STATE + (v * KVH + k) * HD
            grad_two[:, lo : lo + HD] = (kv_rows[:, v * HD : (v + 1) * HD] * on).astype(BF)

    def finish(j, carry):
        cols = lanes(j, 512)
        full = dot_nt(grad_two[:, 2 * STATE :], w_sh[cols, 2 * STATE :])
        for k in range(8):
            some = part_out[k, :, cols].astype(F32) + full[k * share : (k + 1) * share]
            part_out[k, :, cols] = some.astype(BF)
        return carry

    lax.fori_loop(0, model // 512, finish, 0)
    low_two = dot_nt(grad_two[...], b_sh[...]).astype(BF)
    for k in range(8):
        part_out[k, :, model + rank :] = low_two[k * share : (k + 1) * share]
    for k in range(8):
        two_out[k] = grad_two[:, k * 128 : (k + 1) * 128]
    share_end(gathered, sems, tp_at, started, passed)
    for cp in one + two + cps:
        cp.wait_send()


def back_exchange(scale, *args):
    resid, bc, xs, b_in, b_sh, kv, part, w_in, w_sh = (
        args[k] for k in (2, 4, 5, 11, 12, 24, 25, 26, 27)
    )
    rows, width = xs.shape
    heads = width // MHEAD
    half = rows // 2
    cols = 2 * HD
    _, share, wide = part.shape
    model = resid.shape[1]
    rank = b_in.shape[0]
    return call(
        functools.partial(back_kernel, scale),
        [
            (part.shape, BF),
            ((8, share, model + 2 * rank), BF),
            ((8, rows, w_sh.shape[1] // 8), BF),
            ((rows, 2 * width + HD + 128), BF),
            ((8, 128), F32),
            ((rows, rank), BF),
        ],
        list(args),
        [
            pltpu.VMEM(kv.shape, BF),
            pltpu.VMEM(part.shape, BF),
            pltpu.VMEM(w_in.shape, BF),
            pltpu.VMEM(w_sh.shape, BF),
            pltpu.VMEM(kv.shape, BF),
            pltpu.VMEM((rows, HD), BF),
            pltpu.VMEM((rows, width), F32),
            pltpu.VMEM((rows, width), BF),
            pltpu.VMEM((rows, width), BF),
            pltpu.VMEM((16, 16, width + 128), BF),
            pltpu.VMEM((16, 16, width + 128), BF),
            pltpu.VMEM((16, 16, width), BF),
            pltpu.VMEM((16, 16, width), BF),
            pltpu.VMEM((4, 4, half, cols), BF),
            pltpu.VMEM((half, cols), F32),
            pltpu.VMEM((rows, cols), F32),
            pltpu.VMEM((rows, w_sh.shape[1]), BF),
            pltpu.VMEM((128, rows), F32),
            pltpu.VMEM((128, rows), F32),
            pltpu.VMEM((128, rows), F32),
            pltpu.VMEM((rows, 128), F32),
            pltpu.VMEM((heads, rows, 128), BF),
            pltpu.VMEM((heads, rows, 128), BF),
            pltpu.VMEM((rows, width), F32),
            pltpu.VMEM((rows, STATE), F32),
            pltpu.VMEM((rows, STATE), F32),
            pltpu.VMEM((rows, 128), F32),
            DMA((4,)),
            *pair(15),
            *pair(15),
            *pair(4),
            *scatter_bufs(half, cols),
            *reduce_bufs(share, wide),
            *share_sems(),
        ],
        5,
        "back_exchange",
        [SM] + [VM] * 23 + [HB] * 4,
    )


def tail_kernel(
    part,
    part_two,
    gain,
    mask,
    gain_two,
    grad_resid,
    low_in,
    low_sh,
    grad_low_out,
    grad_low_gu,
    low_out,
    head,
    a_in,
    a_sh,
    hidden_far,
    normed_far,
    grad_one_far,
    merged_far,
    normed_mine_far,
    mixer_mine_far,
    grad_mine_far,
    rows_far,
    gathered,
    big_out,
    small_out,
    shared,
    head_out,
    source,
    normed_one,
    grad_one,
    merged,
    normed_mine,
    mixer_mine,
    grad_mine,
    low_dn,
    lows,
    turned,
    mine,
    big,
    small,
    two,
    two_t,
    picks,
    heads,
    loads,
    *scratch,
):
    place = ctx_place()
    tp_at = tp_place()
    ctx, tp = place[:2]
    peers = ctx_peers(ctx, tp) + tp_peers(*tp_at)
    greet(peers)
    share, width = source.shape
    rank = a_in.shape[1]
    rows = normed_one.shape[0]
    rows_mine = pl.ds(pl.multiple_of(tp * share, share), share)
    get = [
        fetch(src, dst, loads.at[k])
        for k, (src, dst) in enumerate(
            (
                (grad_one_far, grad_one),
                (normed_far, normed_one),
                (hidden_far.at[rows_mine], source),
                (merged_far, merged),
                (normed_mine_far, normed_mine),
                (mixer_mine_far, mixer_mine),
                (grad_mine_far, grad_mine),
                (rows_far.at[:, :, pl.ds(width, rank)], low_dn),
            )
        )
    ]
    bufs_z, more_z, sems, sems_l = scratch[:7], scratch[7:14], scratch[14:18], scratch[18:22]
    bufs, more, s_head, sems_s = scratch[22:29], scratch[29:36], scratch[36:38], scratch[38:]
    met(peers)
    first_z = reduce_start(part, bufs_z, tp_at)
    first_two = reduce_start(part_two, more_z, tp_at)
    second_z = reduce_middle(part, bufs_z, tp_at, first_z)
    second_two = reduce_middle(part_two, more_z, tp_at, first_two)
    get[0].wait()
    turned[...] = grad_one[...].T
    deep = grad_one.shape[1]
    get[1].wait()

    def weights(j, carry):
        split_out(big, 0, dot(turned[...], normed_one[:, lanes(j, 512)]), 4 * j)
        return carry

    lax.fori_loop(0, 2, weights, 0)
    reduce_relay(part, bufs_z, tp_at, first_z, second_z)
    lax.fori_loop(2, 4, weights, 0)
    eights(big, deep, dot_tn(low_in[...], grad_one[...]))
    first = scatter_start(big, bufs, place)
    reduce_relay(part_two, more_z, tp_at, first_two, second_two)
    get[2].wait()
    total = reduce_end(part, bufs_z, tp_at, first_z, second_z)
    mask_mine = mask[rows_mine]
    low_one = (total[:, width : width + rank] * mask_mine).astype(BF)
    low_two = (total[:, width + rank :] * mask_mine).astype(BF)
    lows[tp, :, :rank] = low_one
    lows[tp, :, rank:] = low_two
    started_l = share_start(lows, sems_l, tp_at)
    grad = total[:, :width] + dot_nt(low_one, a_in[...]) + dot_nt(low_two, a_sh[...])
    grad_v, grad_gain = norm_back(source[...].astype(F32), gain[...], grad)
    gathered[tp] = (grad_resid[...] + grad_v).astype(BF)
    started = share_start(gathered, sems, tp_at)
    passed_l = [share_pass(lows, sems_l, tp_at, started_l, k) for k in (0, 1)]

    for k in range(3, 8):
        get[k].wait()
    a_out_sum = dot_tn(merged[...], grad_low_out[...])
    for j in range(16):
        small[j // 4, j % 4, 160:192] = a_out_sum[j * 32 : (j + 1) * 32].astype(BF)

    def put(row, full):
        small[:, :, row : row + 16] = full.astype(BF).reshape(4, 4, 16, rank)

    put(208, dot_tn(normed_mine[...], grad_low_gu[...]))
    put(224, dot_tn(mixer_mine[...], low_out[...]))
    put(240, dot_tn(grad_mine[...], low_dn[...].reshape(rows, rank)))
    picks[...] = chooser(tp)
    half = width // 2
    for k in range(2):
        cols = slice(half * k, half * (k + 1))
        mine[:, 128 * k : 128 * (k + 1)] = dot(normed_one[:, cols], picks[...]).astype(BF)
    passed_l.append(share_pass(lows, sems_l, tp_at, started_l, 2))
    two[...] = reduce_end(part_two, more_z, tp_at, first_two, second_two).astype(BF)
    b_sh_sum = dot_tn(low_sh[...], two[...])
    two_t[...] = two[...].T

    def shared_maps(j, carry):
        split_out(small, 0, dot(two_t[...], normed_one[:, lanes(j, 512)]), 4 * j)
        return carry

    lax.fori_loop(0, 4, shared_maps, 0)
    gain_rows = jnp.concatenate([grad_gain, gain_two[...], jnp.zeros((6, width), F32)], axis=0)
    for j in range(16):
        small[j // 4, j % 4, 144:160] = jnp.concatenate(
            [b_sh_sum[8 * j : 8 * j + 8], gain_rows[:, 128 * j : 128 * (j + 1)]], axis=0
        ).astype(BF)
    passed = [share_pass(gathered, sems, tp_at, started, k) for k in (0, 1)]
    share_end(lows, sems_l, tp_at, started_l, passed_l)
    full = dot_tn(mine[...], lows[...].reshape(rows, 2 * rank))
    put(192, full[:, :rank])
    put(128, full[:, rank:])
    first_s = scatter_start(small, more, place, True)
    sent = [send(head, heads.at[ctx], s_head, d - 1, ((ctx + d) % 16, tp)) for d in range(1, 16)]
    heads[ctx] = head[...]
    second = scatter_middle(big, big_out, bufs, place, first)
    passed.append(share_pass(gathered, sems, tp_at, started, 2))
    second_s = scatter_middle(small, small_out, more, place, first_s)
    scatter_end(small, small_out, more, first_s, second_s)
    shared[tp] = small_out[pl.ds(0, shared.shape[1])].astype(BF)
    started_s = share_start(shared, sems_s, tp_at)
    scatter_end(big, big_out, bufs, first, second)
    share_end(gathered, sems, tp_at, started, passed)
    for cp in sent:
        cp.wait_recv()
    head_out[...] = jnp.sum(heads[...], axis=0)
    share_end(shared, sems_s, tp_at, started_s)
    for cp in sent:
        cp.wait_send()


def tail_exchange(*args):
    part, part_two, grad_resid, head, grad_one, merged, rows_in = (
        args[k] for k in (0, 1, 5, 11, 16, 17, 21)
    )
    _, share, wide = part.shape
    _, rows, cols = part_two.shape
    width = grad_resid.shape[1]
    rank = (wide - width) // 2
    deep = grad_one.shape[1]
    return call(
        tail_kernel,
        [
            ((8, share, width), BF),
            ((deep + 64, 128), F32),
            ((256, 128), F32),
            ((8, 160, 128), BF),
            (head.shape, F32),
        ],
        list(args),
        [
            pltpu.VMEM((share, width), BF),
            pltpu.VMEM((rows, width), BF),
            pltpu.VMEM(grad_one.shape, BF),
            pltpu.VMEM(merged.shape, BF),
            pltpu.VMEM((rows, 256), BF),
            pltpu.VMEM((rows, 256), BF),
            pltpu.VMEM((rows, 256), BF),
            pltpu.VMEM((8, share, rank), BF),
            pltpu.VMEM((8, share, 2 * rank), BF),
            pltpu.VMEM((deep, rows), BF),
            pltpu.VMEM((rows, 256), BF),
            pltpu.VMEM((4, 4, deep + 64, 128), BF),
            pltpu.VMEM((4, 4, 256, 128), BF),
            pltpu.VMEM((rows, 128), BF),
            pltpu.VMEM((128, rows), BF),
            pltpu.VMEM((1024, 128), BF),
            pltpu.VMEM((16,) + head.shape, F32),
            DMA((8,)),
            *reduce_bufs(share, wide),
            *reduce_bufs(rows, cols),
            *share_sems(),
            *share_sems(),
            *scatter_bufs(deep + 64, 128),
            *scatter_bufs(256, 128),
            *pair(15),
            *share_sems(),
        ],
        6,
        "tail_exchange",
        [VM] * 14 + [HB] * 8,
    )


def finish_kernel(
    mixed_in,
    input_in,
    big,
    small,
    shared,
    head,
    early,
    mixed,
    input_grad,
    gains,
    w_in,
    w_sh,
    w_dt,
    params,
    w_out,
    w_gu,
    w_down,
    a_in,
    b_in,
    a_sh,
    b_sh,
    a_out,
    b_out,
    a_gu,
    b_gu,
    a_dn,
    b_dn,
):
    width = mixed.shape[1]
    mixed[...] = mixed_in[0, :, :width].astype(F32)
    input_grad[...] = input_in[0, :, :width].astype(F32)

    @pl.when(pl.program_id(0) == 0)
    def rest():
        narrow = w_in.shape[2]
        hidden = w_down.shape[0]
        heads = w_dt.shape[0]
        w_in[:, 0, :] = big[0:narrow].T
        w_dt[...] = big[narrow : narrow + heads]
        deep = narrow + 128
        for k in range(narrow // 128):
            cols = slice(128 * k, 128 * (k + 1))
            b_in[:, 0, cols] = big[deep + 8 * k : deep + 8 * (k + 1)]
        params[...] = head[0:3, 0:heads]
        total = jnp.zeros((8, 128), F32)
        for k in range(8):
            block = shared[k].astype(F32)
            cols = slice(128 * k, 128 * (k + 1))
            w_sh[:, cols] = block[0:128].T
            a_sh[16 * k : 16 * (k + 1)] = block[128:144]
            b_sh[:, cols] = block[144:152]
            total = total + block[152:160]
        gains[...] = total[0:2]
        a_out[0] = small[160:192]
        a_in[...] = small[192:208]
        a_gu[...] = small[208:224]
        b_out[...] = small[224:240]
        b_dn[...] = small[240:256]
        w_gu[:, 0, :] = early[0:hidden].astype(F32).T
        w_gu[:, 1, :] = early[hidden : 2 * hidden].astype(F32).T
        w_down[...] = early[2 * hidden : 3 * hidden].astype(F32)
        w_out[0] = early[3 * hidden : 4 * hidden].astype(F32)
        maps = early[4 * hidden :].astype(F32)
        for k in range(hidden // 128):
            cols = slice(128 * k, 128 * (k + 1))
            b_gu[:, 0, cols] = maps[8 * k : 8 * (k + 1)]
            b_gu[:, 1, cols] = maps[32 + 8 * k : 32 + 8 * (k + 1)]
            a_dn[:, cols] = maps[64 + 8 * k : 64 + 8 * (k + 1)]


def finish(mixed, input_grad, big, small, shared, head, early, narrow, heads):
    _, rows, wide = mixed.shape
    _, _, wide_two = input_grad.shape
    width = wide - 128
    hidden = early.shape[0] // 4 // 128 * 128
    outs = [
        (8 * rows, width),
        (8 * rows, width),
        (2, 128),
        (128, 1, narrow),
        (128, 1024),
        (heads, 128),
        (3, heads),
        (1, hidden, 128),
        (128, 2, hidden),
        (hidden, 128),
        (16, 128),
        (8, 1, narrow),
        (128, 128),
        (8, 1024),
        (1, 32, 128),
        (16, 128),
        (16, 128),
        (8, 2, hidden),
        (8, hidden),
        (16, 128),
    ]

    def whole(shape):
        return pl.BlockSpec(shape, lambda i: (0,) * len(shape))

    done = pl.pallas_call(
        finish_kernel,
        grid=(8,),
        out_shape=[jax.ShapeDtypeStruct(s, F32) for s in outs],
        in_specs=[
            pl.BlockSpec((1, rows, wide), lambda i: (i, 0, 0)),
            pl.BlockSpec((1, rows, wide_two), lambda i: (i, 0, 0)),
        ]
        + [whole(a.shape) for a in (big, small, shared, head, early)],
        out_specs=[pl.BlockSpec((rows, width), lambda i: (i, 0))] * 2 + [whole(s) for s in outs[2:]],
        compiler_params=pltpu.CompilerParams(vmem_limit_bytes=56 << 20),
        name="finish",
    )(mixed, input_grad, big, small, shared, head, early)
    return tuple(a.T if k in (5, 15, 18, 19) else a for k, a in enumerate(done))


def body(
    hidden_in,
    norm_gains,
    w_in,
    w_shared,
    w_dt,
    head_params,
    w_out,
    w_gu,
    w_down,
    a_in,
    b_in,
    a_sh,
    b_sh,
    a_out,
    b_out,
    a_gu,
    b_gu,
    a_dn,
    b_dn,
    adapter_ids,
    doc_lengths,
    out_grad,
):
    rows, width = hidden_in.shape
    heads = head_params.shape[1]
    w_in = w_in.reshape(width, -1)
    b_in = b_in.reshape(b_in.shape[0], -1)
    w_out = w_out.reshape(-1, width)
    a_out = a_out.reshape(-1, a_out.shape[2])
    w_gu = w_gu.reshape(width, -1)
    b_gu = b_gu.reshape(b_gu.shape[0], -1)
    w_dt = jnp.pad(w_dt.T, ((0, 128 - heads), (0, 0)))
    params = jnp.pad(head_params, ((0, 5), (0, 128 - heads)))
    scale = HD ** (-0.5)
    gain_one, gain_two = norm_gains[0:1], norm_gains[1:2]
    (
        normed_one,
        low_in,
        low_sh,
        z,
        xs,
        q,
        bc,
        mask,
        decay,
        dt,
        pre,
        total,
        entering,
        ssd,
        kv_all,
        mix_part,
        attn_t,
        lse,
        merged,
    ) = front_exchange(
        scale,
        doc_lengths,
        adapter_ids,
        hidden_in,
        gain_one,
        a_in,
        a_sh,
        w_dt,
        b_in,
        b_sh,
        params,
        a_out,
        w_in,
        w_shared,
        w_out,
    )
    (
        low_out,
        grad_mixer,
        grad_low_gu,
        resid,
        grad_resid,
        gain_part_two,
        early,
        mlp_part,
        normed_mine,
        grad_mine,
        mixer_mine,
    ) = mlp_exchange(
        mix_part,
        gain_two,
        b_out,
        a_gu,
        b_gu,
        a_dn,
        b_dn,
        mask,
        merged,
        hidden_in,
        w_gu,
        w_down,
        out_grad,
    )
    early = lax.psum_scatter(
        early.reshape(-1, early.shape[2]), "ctx", scatter_dimension=0, tiled=True
    )
    mixed, part, two_blocks, grad_one, grad_head, grad_low_out = back_exchange(
        scale,
        doc_lengths,
        total,
        resid,
        b_dn,
        bc,
        xs,
        decay,
        dt,
        pre,
        params,
        entering,
        b_in,
        b_sh,
        w_dt,
        q,
        lse,
        attn_t,
        grad_mixer,
        w_out,
        b_out,
        a_out,
        mask,
        z,
        ssd,
        kv_all,
        mlp_part,
        w_in,
        w_shared,
    )
    input_grad, big, small, shared, head = tail_exchange(
        part,
        two_blocks,
        gain_one,
        mask,
        gain_part_two,
        grad_resid,
        low_in,
        low_sh,
        grad_low_out,
        grad_low_gu,
        low_out,
        grad_head,
        a_in,
        a_sh,
        hidden_in,
        normed_one,
        grad_one,
        merged,
        normed_mine,
        mixer_mine,
        grad_mine,
        mixed,
    )
    return finish(mixed, input_grad, big, small, shared, head, early, w_in.shape[1], heads)


def solution(mesh):
    placed = (
        P("ctx", None),
        P(),
        P(None, "tp", None),
        P(),
        P(None, "tp"),
        P(None, "tp"),
        P("tp", None, None),
        P(None, None, "tp"),
        P("tp", None),
        P(),
        P(None, "tp", None),
        P(),
        P(),
        P("tp", None, None),
        P(),
        P(),
        P(None, None, "tp"),
        P("tp", None),
        P(),
        P(),
        P(),
        P("ctx", None),
    )
    return jax.shard_map(
        body,
        mesh=mesh,
        in_specs=placed,
        out_specs=(
            P("ctx", None),
            P("ctx", None),
            P(None, "ctx"),
            P("ctx", "tp", None),
            P("ctx", None),
            P("ctx", "tp"),
            P(None, "tp"),
            P("tp", None, "ctx"),
            P("ctx", None, "tp"),
            P("tp", "ctx"),
            P(("ctx", "tp"), None),
            P("ctx", "tp", None),
            P("ctx", None),
            P("ctx", None),
            P("tp", "ctx", None),
            P(None, ("ctx", "tp")),
            P(("ctx", "tp"), None),
            P("ctx", None, "tp"),
            P("tp", "ctx"),
            P(None, ("ctx", "tp")),
        ),
        check_vma=False,
    )
```

```python
import functools

import jax
import jax.numpy as jnp
from jax import lax
from jax.experimental import pallas as pl
from jax.experimental.pallas import tpu as pltpu
from jax.sharding import PartitionSpec as P

MHEAD = 64
STATE = 256
QHEADS = 8
KVH = 2
HD = 128
RANK = 16
NORM_EPSILON = 1e-06

MESH = pl.DeviceIdType.MESH
VM = pl.BlockSpec(memory_space=pltpu.VMEM)
SM = pl.BlockSpec(memory_space=pltpu.SMEM)
HB = pl.BlockSpec(memory_space=pl.ANY)
BF = jnp.bfloat16
F32 = jnp.float32
DMA = pltpu.SemaphoreType.DMA
OFFSETS = (2, 1, 3)
LOG2E = 1.4426950408889634
UNROLL = 3


def call(kernel, outs, ins, scratch, cid, name, specs=None, out_specs=None):
    return pl.pallas_call(
        kernel,
        out_shape=[jax.ShapeDtypeStruct(s, d) for s, d in outs],
        in_specs=specs or [VM] * len(ins),
        out_specs=out_specs or [VM] * len(outs),
        scratch_shapes=scratch,
        compiler_params=pltpu.CompilerParams(
            collective_id=cid, has_side_effects=True, vmem_limit_bytes=61 << 20
        ),
        name=name,
    )(*ins)


def greet(peers):
    barrier = pltpu.get_barrier_semaphore()
    for peer in peers:
        pl.semaphore_signal(barrier, inc=1, device_id=peer, device_id_type=MESH)


def met(peers):
    pl.semaphore_wait(pltpu.get_barrier_semaphore(), len(peers))


def send(src, dst, sems, slot, peer):
    cp = pltpu.make_async_remote_copy(
        src_ref=src,
        dst_ref=dst,
        send_sem=sems[0].at[slot],
        recv_sem=sems[1].at[slot],
        device_id=peer,
        device_id_type=MESH,
    )
    cp.start()
    return cp


def pair(*shape):
    return [DMA(shape), DMA(shape)]


def tp_place():
    ctx = lax.axis_index("ctx")
    tp = lax.axis_index("tp")
    return ctx, tp, tp // 2, tp % 2


def tp_peers(ctx, tp, z, c):
    return [(ctx, ((z + d) % 4) * 2 + c) for d in (1, 2, 3)] + [(ctx, z * 2 + 1 - c)]


def reduce_bufs(rows, width):
    return [
        pltpu.VMEM((4, rows, width), BF),
        pltpu.VMEM((3, rows, width), BF),
        pltpu.VMEM((3, rows, width), BF),
        *pair(4),
        *pair(3),
    ]


def chips(place):
    ctx, tp, z, c = place
    return (z + 2) % 4, (z + 1 + 2 * c) % 4, (z + 3 - 2 * c) % 4, z


def reduce_pass(part, bufs, place, k):
    ctx, tp, z, c = place
    chip = chips(place)[(0, 2, 1, 3)[k]]
    return send(part.at[chip * 2 + 1 - c], bufs[0].at[k], bufs[3:5], k, (ctx, z * 2 + 1 - c))


def reduce_send(part, bufs, place, passed, k, relayed=None):
    sib, snd, rcv = bufs[:3]
    ctx, tp, z, c = place
    two, way, other, own = chips(place)
    passed.wait_recv()
    both = part[(two, way, other)[k] * 2 + c].astype(F32) + sib[k].astype(F32)
    if k == 1:
        relayed.wait_recv()
        both = both + rcv[0].astype(F32)
    snd[k] = both.astype(BF)
    to = other if k == 2 else way
    return send(snd.at[k], rcv.at[k], bufs[5:7], k, (ctx, to * 2 + c))


def reduce_start(part, bufs, place):
    return [reduce_pass(part, bufs, place, k) for k in range(4)]


def reduce_middle(part, bufs, place, first):
    two = reduce_send(part, bufs, place, first[0], 0)
    other = reduce_send(part, bufs, place, first[2], 2)
    return [two, None, other]


def reduce_relay(part, bufs, place, first, second):
    second[1] = reduce_send(part, bufs, place, first[1], 1, second[0])


def reduce_end(part, bufs, place, first, second):
    sib, snd, rcv = bufs[:3]
    first[3].wait_recv()
    total = part[place[1]].astype(F32) + sib[3].astype(F32)
    for k in (2, 1):
        second[k].wait_recv()
        total = total + rcv[k].astype(F32)
    for cp in first + second:
        cp.wait_send()
    return total


def share_sems():
    return [*pair(3), *pair(4)]


def share_start(out, sems, place):
    ctx, tp, z, c = place
    two, way, other, own = chips(place)
    return [
        send(out.at[tp], out.at[tp], sems[:2], 0, (ctx, way * 2 + c)),
        send(out.at[tp], out.at[tp], sems[:2], 1, (ctx, other * 2 + c)),
        send(out.at[tp], out.at[tp], sems[2:], 0, (ctx, z * 2 + 1 - c)),
    ]


def share_pass(out, sems, place, started, k):
    ctx, tp, z, c = place
    two, way, other, own = chips(place)
    mate = (ctx, z * 2 + 1 - c)
    at = (other, way, two)[k] * 2 + c
    if k == 2:
        started[3].wait_recv()
    else:
        started[k].wait_recv()
    if k == 0:
        started.append(send(out.at[at], out.at[at], sems[:2], 2, (ctx, way * 2 + c)))
    passed = send(out.at[at], out.at[at], sems[2:], k + 1, mate)
    return passed


def share_end(out, sems, place, started, passed=()):
    passed = list(passed)
    passed += [share_pass(out, sems, place, started, k) for k in range(len(passed), 3)]
    started[2].wait_recv()
    for cp in passed:
        cp.wait_recv()
    for cp in started + passed:
        cp.wait_send()


def share_direct(out, sems, place):
    ctx, tp = place[:2]
    return [
        send(out.at[tp], out.at[tp], sems, d - 1, (ctx, (tp + d) % 8)) for d in range(1, 8)
    ]


def all_tp(ctx, tp, z, c):
    return [(ctx, (tp + d) % 8) for d in range(1, 8)]


def norm_scale(v):
    return lax.rsqrt(jnp.mean(v * v, axis=-1, keepdims=True) + NORM_EPSILON)


def norm_back(v, gain, grad):
    r = norm_scale(v)
    pulled = grad * gain
    inner = jnp.mean(pulled * v, axis=-1, keepdims=True)
    grad_v = r * pulled - v * (r * r * r) * inner
    return grad_v, jnp.sum(grad * v * r, axis=0, keepdims=True)


def dot(a, b):
    return jnp.dot(a, b, preferred_element_type=F32)


def dot_nt(a, b):
    return lax.dot_general(a, b, (((1,), (1,)), ((), ())), preferred_element_type=F32)


def dot_tn(a, b):
    return lax.dot_general(a, b, (((0,), (0,)), ((), ())), preferred_element_type=F32)


def dot_f(a, b):
    return jnp.dot(a, b, precision=lax.Precision.HIGHEST, preferred_element_type=F32)


def lanes(k, size):
    return pl.ds(pl.multiple_of(k * size, 128), size)


def split_out(dst, row, full, first):
    for k in range(full.shape[1] // 128):
        at = (first // 4, k) if len(dst.shape) == 4 else (first + k,)
        dst[(*at, slice(row, row + full.shape[0]))] = full[:, 128 * k : 128 * (k + 1)].astype(BF)


def eights(dst, row, full):
    for j in range(16):
        for k in range(0, full.shape[1] // 128, 2):
            two = [
                full[8 * j : 8 * j + 8, 128 * (k + i) : 128 * (k + i + 1)] for i in (0, 1)
            ]
            at = (j // 4, j % 4) if len(dst.shape) == 4 else (j,)
            dst[(*at, slice(row + 8 * k, row + 8 * k + 16))] = jnp.concatenate(two, axis=0).astype(
                BF
            )


def chooser(tp):
    r, c = iota((1024, 128), 0), iota((1024, 128), 1)
    return jnp.where((r // 128 == c // 16) & (r % 128 == tp * 16 + c % 16), 1.0, 0.0).astype(BF)


def fetch(src, dst, sem):
    cp = pltpu.make_async_copy(src, dst, sem)
    cp.start()
    return cp


def soft_plus(values):
    return jnp.maximum(values, 0.0) + jnp.log1p(jnp.exp(-jnp.abs(values)))


def pick(t, lengths, values):
    one = lengths[0]
    two = one + lengths[1]
    three = two + lengths[2]
    return jnp.where(
        t >= three,
        values[3],
        jnp.where(t >= two, values[2], jnp.where(t >= one, values[1], values[0])),
    )


def doc_start(t, lengths):
    one = lengths[0]
    two = one + lengths[1]
    return pick(t, lengths, (0, one, two, two + lengths[2]))


def iota(shape, axis):
    return lax.broadcasted_iota(jnp.int32, shape, axis)


def expander(heads):
    shape = (128, heads * MHEAD)
    return (iota(shape, 1) // MHEAD == iota(shape, 0)).astype(F32)


def collector(heads):
    shape = (heads * MHEAD, 128)
    return (iota(shape, 0) // MHEAD == iota(shape, 1)).astype(F32)


def spread(per_head, heads):
    return dot_f(per_head, expander(heads))


def head_sums(flat):
    return dot_f(flat, collector(flat.shape[1] // MHEAD))


def one_head(pair, h):
    return jnp.where(iota(pair.shape, 1) // MHEAD == h % 2, pair, jnp.zeros_like(pair))


def running_sum(dst, src, rows, later):
    for i in range(rows // 128):
        shape = (128, rows)
        t, s = i * 128 + iota(shape, 0), iota(shape, 1)
        tri = jnp.where((s >= t) if later else (s <= t), 1.0, 0.0)
        dst[pl.ds(i * 128, 128)] = dot_f(tri, src[...])


def fades(i, base, lengths):
    wide = (i + 1) * 128
    t = base + i * 128 + iota((128, 128), 0)
    start = doc_start(t, lengths)[:, 0:1]
    shape = (128, wide)
    s = base + iota(shape, 1)
    return (s <= base + i * 128 + iota(shape, 0)) & (s >= start)


FAR = -1e9


def doc_of(t, lengths):
    one = lengths[0]
    two = one + lengths[1]
    return (
        (t >= one).astype(jnp.int32)
        + (t >= two).astype(jnp.int32)
        + (t >= two + lengths[2]).astype(jnp.int32)
    )


def marked_keys(keys, base, lengths):
    shape = keys.shape
    mark = jnp.where(doc_of(base + iota(shape, 0), lengths) == iota(shape, 1), 1.0, 0.0)
    return jnp.concatenate([keys, mark.astype(BF)], axis=1)


def marked_queries(queries, base, lengths):
    shape = queries.shape
    row = iota(shape, 0)
    own = doc_of(base + iota(shape, 1), lengths) == row
    return jnp.concatenate([queries, jnp.where(own | (row > 3), 0.0, FAR).astype(BF)], axis=0)


def attend(scale, ctx, lengths, q, kv):
    block, size = kv.shape[2], q.shape[0]
    queries = marked_queries(q[...].T, ctx * block, lengths)
    factor = scale * LOG2E

    def step(blocks, carry, diagonal):
        top, total, acc = carry
        parts = []
        for i in blocks:
            keys = kv[i // 4, i % 4, :, :HD]
            s = dot(marked_keys(keys, i * block, lengths), queries) * factor
            if diagonal:
                s = jnp.where(iota(s.shape, 0) <= iota(s.shape, 1), s, FAR)
            parts.append(s)
        new = top
        for s in parts:
            new = jnp.maximum(new, jnp.max(s, axis=0, keepdims=True))
        fade = jnp.exp2(top - new)
        total = total * fade
        acc = acc * fade
        for i, s in zip(blocks, parts):
            p = jnp.exp2(s - new)
            total = total + jnp.sum(p, axis=0, keepdims=True)
            acc = acc + dot_tn(kv[i // 4, i % 4, :, HD:], p.astype(BF))
        return new, total, acc

    carry = (
        jnp.full((1, size), 2 * FAR, F32),
        jnp.zeros((1, size), F32),
        jnp.zeros((HD, size), F32),
    )
    some = ctx // UNROLL
    carry = lax.fori_loop(
        0, some, lambda i, k: step([UNROLL * i + n for n in range(UNROLL)], k, False), carry
    )
    carry = lax.fori_loop(UNROLL * some, ctx, lambda i, k: step([i], k, False), carry)
    top, total, acc = step([ctx], carry, True)
    return acc / total, top + jnp.log(total) * LOG2E


def attend_back(scale, ctx, lengths, q, kv, lse, low, grad_attn, dkv, midway):
    block, size = kv.shape[2], q.shape[0]
    queries_t, queries = marked_queries(q[...].T, ctx * block, lengths), q[...]
    og = grad_attn[...]
    og_t = og.T
    factor = scale * LOG2E

    def step(blocks, acc, diagonal):
        for i in blocks:
            keys = kv[i // 4, i % 4, :, :HD]
            s = dot(marked_keys(keys, i * block, lengths), queries_t) * factor - lse
            if diagonal:
                s = jnp.where(iota(s.shape, 0) <= iota(s.shape, 1), s, FAR)
            p = jnp.exp2(s)
            dp = dot(kv[i // 4, i % 4, :, HD:], og_t)
            ds = (p * (dp - low)).astype(BF)
            dkv[i // 4, i % 4, :, :HD] = (dot(ds, queries) * scale).astype(BF)
            dkv[i // 4, i % 4, :, HD:] = dot(p.astype(BF), og).astype(BF)
            acc = acc + dot_tn(keys, ds)
        return acc

    some = ctx // 2
    acc = jnp.zeros((HD, size), F32)

    def pairs(i, k):
        return step([2 * i, 2 * i + 1], k, False)

    acc = lax.fori_loop(0, some // 2, pairs, acc)
    midway()
    acc = lax.fori_loop(some // 2, some, pairs, acc)
    acc = lax.fori_loop(2 * some, ctx, lambda i, k: step([i], k, False), acc)
    return step([ctx], acc, True) * scale


def mlp_kernel(
    part,
    gain,
    b_out,
    a_gu,
    b_gu,
    a_dn,
    b_dn,
    mask,
    merged,
    hidden_far,
    w_gu_far,
    w_down_far,
    out_grad_far,
    low_out,
    grad_mixer_far,
    grad_low_gu,
    resid,
    grad_resid,
    gain_part,
    early_sum,
    rest_far,
    late_far,
    normed_mine,
    grad_mine,
    mixer_mine,
    source,
    w_gu,
    w_down,
    shared,
    shared_two,
    part_two,
    grad_act,
    low_dn_grad,
    low_gu,
    act,
    grad_gu,
    turned,
    picks,
    early,
    rest,
    late_part,
    out_grad,
    loads,
    *scratch,
):
    place = tp_place()
    tp = place[1]
    on_ctx = ctx_place()
    peers = tp_peers(*place) + line_peers(*on_ctx)
    greet(peers)
    share, model = resid.shape
    hidden = w_down.shape[0]
    rows = out_grad.shape[0]
    each = 128 // share
    rows_mine = pl.ds(pl.multiple_of(tp * share, share), share)
    get_source = fetch(hidden_far.at[rows_mine], source, loads.at[0])
    get_grad = fetch(out_grad_far, out_grad, loads.at[7])
    get_down = fetch(w_down_far, w_down, loads.at[1])
    get_gu = fetch(w_gu_far, w_gu, loads.at[2])
    bufs, sems, more, sems_two = scratch[:7], scratch[7:11], scratch[11:18], scratch[18:22]
    wide_bufs = scratch[22:]
    met(peers)
    first = reduce_start(part, bufs, place)
    second = reduce_middle(part, bufs, place, first)

    def span_of(i):
        return pl.ds(pl.multiple_of(i * 128, 128), 128)

    get_grad.wait()
    get_down.wait()

    low_dn_grad[...] = (dot_nt(out_grad[...], b_dn[...]) * mask[...]).astype(BF)
    grad_act[...] = (dot_nt(out_grad[...], w_down[...]) + dot_nt(low_dn_grad[...], a_dn[...])).astype(
        BF
    )
    reduce_relay(part, bufs, place, first, second)
    get_source.wait()
    total = reduce_end(part, bufs, place, first, second)
    low = total[:, model:].astype(BF)
    residual = source[...].astype(F32) + total[:, :model] + dot(low, b_out[...])
    resid[...] = residual
    shared[tp, :, :model] = (residual * norm_scale(residual) * gain[1:2]).astype(BF)
    shared[tp, :, model:] = low
    started = share_start(shared, sems, place)
    get_gu.wait()

    def both_ways(*some):
        def rows_at(ref):
            return jnp.concatenate([ref[span_of(i)] for i in some], axis=0)

        def put(ref, value):
            for k, i in enumerate(some):
                ref[span_of(i)] = value[128 * k : 128 * (k + 1)]

        block = jnp.concatenate(
            [shared[pl.ds(i * each, each)].reshape(128, -1) for i in some], axis=0
        )
        n = block[:, :model]
        put(low_out, block[:, model:])
        low = (dot(n, a_gu[...]) * rows_at(mask)).astype(BF)
        put(low_gu, low)
        h = (dot(n, w_gu[...]) + dot(low, b_gu[...])).astype(BF).astype(F32)
        gate, up = h[:, :hidden], h[:, hidden:]
        sig = jax.nn.sigmoid(gate)
        put(act, (gate * sig * up).astype(BF))
        pulled = rows_at(grad_act).astype(F32)
        grad = jnp.concatenate(
            [pulled * up * sig * (1.0 + gate * (1.0 - sig)), pulled * (gate * sig)], axis=1
        ).astype(BF)
        put(grad_gu, grad)
        full = dot_nt(grad, w_gu[...]).astype(BF)
        low = dot_nt(grad, b_gu[...]).astype(BF)
        for n_th, i in enumerate(some):
            for k in range(each):
                part_of = slice(n_th * 128 + k * share, n_th * 128 + (k + 1) * share)
                part_two[i * each + k, :, :model] = full[part_of]
                part_two[i * each + k, :, model:] = low[part_of]

    chip = chips(place)
    started[2].wait_recv()
    both_ways(chip[3])
    third = reduce_pass(part_two, more, place, 3)
    passed = [share_pass(shared, sems, place, started, k) for k in (0, 1)]
    passed[1].wait_recv()
    passed[0].wait_recv()
    both_ways(chip[1], chip[2])
    pass_one = reduce_pass(part_two, more, place, 1)
    pass_two = reduce_pass(part_two, more, place, 2)
    passed.append(share_pass(shared, sems, place, started, 2))
    send_two = reduce_send(part_two, more, place, pass_two, 2)
    passed[2].wait_recv()
    both_ways(chip[0])
    pass_none = reduce_pass(part_two, more, place, 0)
    turned[...] = grad_gu[...].T
    wide = grad_gu.shape[1]
    send_none = reduce_send(part_two, more, place, pass_none, 0)

    def weights(j, carry):
        some = shared[:, :, lanes(j, 512)].reshape(rows, 512)
        split_out(early, 0, dot(turned[...], some), 4 * j)
        return carry

    lax.fori_loop(0, 4, weights, 0)
    eights(early, wide, dot_tn(low_gu[...], grad_gu[...]))
    first_w = scatter_start(early, wide_bufs, on_ctx)
    send_one = reduce_send(part_two, more, place, pass_one, 1, send_none)
    turned[0:hidden] = act[...].T

    def weights_two(j, carry):
        split_out(rest, 0, dot(turned[0:hidden], out_grad[:, lanes(j, 512)]), 4 * j)
        return carry

    lax.fori_loop(0, 4, weights_two, 0)
    total = reduce_end(
        part_two, more, place, [pass_none, pass_one, pass_two, third], [send_none, send_one, send_two]
    )
    low = (total[:, model:] * mask[rows_mine]).astype(BF)
    grad = total[:, :model] + dot_nt(low, a_gu[...])
    grad_v, grad_gain = norm_back(resid[...], gain[1:2], grad)
    grad_r = out_grad[rows_mine].astype(F32) + grad_v
    grad_resid[...] = grad_r
    gain_part[...] = grad_gain
    shared_two[tp, :, :model] = grad_r.astype(BF)
    shared_two[tp, :, model:] = low
    for cp in started + passed:
        cp.wait_send()
    started = share_start(shared_two, sems_two, place)
    scatter_relay(early, wide_bufs, on_ctx, first_w)
    eights(rest, 2 * hidden, dot_tn(low_dn_grad[...], act[...]))
    picks[...] = chooser(tp)
    half = model // 2
    for k in range(2):
        cols = slice(half * k, half * (k + 1))
        to = slice(128 * k, 128 * (k + 1))
        normed_mine[:, to] = dot(shared[:, :, cols].reshape(rows, half), picks[...]).astype(BF)
        grad_mine[:, to] = dot(out_grad[:, cols], picks[...]).astype(BF)
    passed = [share_pass(shared_two, sems_two, place, started, k) for k in (0, 1)]
    passed.append(share_pass(shared_two, sems_two, place, started, 2))

    def forward_rest(i, carry):
        at = pl.ds(pl.multiple_of(i * 256, 256), 256)
        a = act[at]
        full = dot(a, w_down[...]).astype(BF)
        low = (dot(a, a_dn[...]) * mask[at]).astype(BF)
        for k in range(2 * each):
            late_part[i * 2 * each + k, :, :model] = full[k * share : (k + 1) * share]
            late_part[i * 2 * each + k, :, model:] = low[k * share : (k + 1) * share]
        return carry

    lax.fori_loop(0, rows // 256, forward_rest, 0)
    stores = [fetch(late_part, late_far, loads.at[6])]
    turned[hidden:] = merged[...].T
    second_w = scatter_middle(early, early_sum, wide_bufs, on_ctx, first_w)
    share_end(shared_two, sems_two, place, started, passed)
    for k in range(8):
        to = pl.ds(k * share, share)
        grad_low_gu[to] = shared_two[k, :, model:]
        stores.append(
            fetch(shared_two.at[k, :, pl.ds(0, model)], grad_mixer_far.at[to], loads.at[8 + k])
        )
    for k in range(2):
        cols = slice(half * k, half * (k + 1))
        some = shared_two[:, :, cols].reshape(rows, half)
        mixer_mine[:, 128 * k : 128 * (k + 1)] = dot(some, picks[...]).astype(BF)

    def weights_three(j, carry):
        some = shared_two[:, :, lanes(j, 512)].reshape(rows, 512)
        split_out(rest, hidden, dot(turned[hidden:], some), 4 * j)
        return carry

    lax.fori_loop(0, 4, weights_three, 0)
    stores.append(fetch(rest, rest_far, loads.at[5]))
    scatter_end(early, early_sum, wide_bufs, first_w, second_w)
    for cp in stores:
        cp.wait()


def mlp_exchange(
    part, gain, b_out, a_gu, b_gu, a_dn, b_dn, mask, merged, hidden_in, w_gu, w_down, out_grad
):
    _, share, wide = part.shape
    rows, model = out_grad.shape
    hidden = w_down.shape[0]
    rank = a_gu.shape[1]
    return call(
        mlp_kernel,
        [
            ((rows, rank), BF),
            ((rows, model), BF),
            ((rows, rank), BF),
            ((share, model), F32),
            ((share, model), F32),
            ((1, model), F32),
            ((2 * hidden + 64, 128), F32),
            ((4, 4, 2 * hidden + 32, 128), BF),
            (part.shape, BF),
            ((rows, 256), BF),
            ((rows, 256), BF),
            ((rows, 256), BF),
        ],
        [part, gain, b_out, a_gu, b_gu, a_dn, b_dn, mask, merged, hidden_in, w_gu, w_down, out_grad],
        [
            pltpu.VMEM((share, model), BF),
            pltpu.VMEM(w_gu.shape, BF),
            pltpu.VMEM(w_down.shape, BF),
            pltpu.VMEM(part.shape, BF),
            pltpu.VMEM(part.shape, BF),
            pltpu.VMEM(part.shape, BF),
            pltpu.VMEM((rows, hidden), BF),
            pltpu.VMEM((rows, rank), BF),
            pltpu.VMEM((rows, rank), BF),
            pltpu.VMEM((rows, hidden), BF),
            pltpu.VMEM((rows, 2 * hidden), BF),
            pltpu.VMEM((2 * hidden, rows), BF),
            pltpu.VMEM((1024, 128), BF),
            pltpu.VMEM((4, 4, 2 * hidden + 64, 128), BF),
            pltpu.VMEM((4, 4, 2 * hidden + 32, 128), BF),
            pltpu.VMEM(part.shape, BF),
            pltpu.VMEM(out_grad.shape, BF),
            DMA((16,)),
            *reduce_bufs(share, wide),
            *share_sems(),
            *reduce_bufs(share, wide),
            *share_sems(),
            *scatter_bufs(2 * hidden + 64, 128),
        ],
        2,
        "mlp_exchange",
        [VM] * 9 + [HB] * 4,
        [VM, HB] + [VM] * 5 + [HB] * 2 + [VM] * 3,
    )


def ctx_place():
    ctx = lax.axis_index("ctx")
    return ctx, lax.axis_index("tp"), ctx // 4, ctx % 4


def spot(h, fast, slow):
    return slow * 4 + fast if h == 0 else fast * 4 + slow


def scatter_bufs(rows, width):
    most = max(rows - rows // 32 * 16, rows // 32 * 16)
    return [
        pltpu.VMEM((2, 3, most, width), BF),
        pltpu.VMEM((2, 3, 4, most, width), BF),
        pltpu.VMEM((2, 3, most, width), BF),
        pltpu.VMEM((2, 4, most, width), BF),
        *pair(2, 3, 4),
        *pair(2, 3),
    ]


def spans_of(rows):
    half = rows // 32 * 16
    return ((0, half), (half, rows - half))


def block_of(ref, h, fast, slow):
    return ref.at[slow, fast] if h == 0 else ref.at[fast, slow]


def block_of(ref, h, fast, slow):
    return ref.at[slow, fast] if h == 0 else ref.at[fast, slow]


def line_of(ref, h, fast):
    return ref.at[:, fast] if h == 0 else ref.at[fast]


def ways(place, h):
    ctx, tp, y, x = place
    fast, slow = ((x, y), (y, x))[h]
    c = tp % 2
    return (fast + 2) % 4, (fast + 1 + 2 * c) % 4, (fast + 3 - 2 * c) % 4, fast, slow


def scatter_send(part, bufs, place, h, k, j):
    ctx, tp = place[:2]
    two, way, other, fast, slow = ways(place, h)
    lo, size = spans_of(part.shape[2])[h]
    block, to = (two, way) if k == 0 else (other, other)
    line = (slow + j) % 4
    return send(
        block_of(part, h, block, line).at[pl.ds(lo, size)],
        bufs[1].at[h, k, line, pl.ds(0, size)],
        bufs[4:6],
        (h, k, j),
        (spot(h, to, slow), tp),
    )


def scatter_start(part, bufs, place):
    return {
        (h, 0, j): scatter_send(part, bufs, place, h, 0, j)
        for j in OFFSETS + (0,)
        for h in (0, 1)
    }


def scatter_direct(part, bufs, place):
    ctx, tp = place[:2]
    first = {}
    for off in OFFSETS:
        for h in (0, 1):
            two, way, other, fast, slow = ways(place, h)
            lo, size = spans_of(part.shape[2])[h]
            to = (fast + off) % 4
            first[h, off - 1, 0] = send(
                line_of(part, h, to).at[:, pl.ds(lo, size)],
                bufs[1].at[h, off - 1, :, pl.ds(0, size)],
                bufs[4:6],
                (h, off - 1, 0),
                (spot(h, to, slow), tp),
            )
    return first


def scatter_relay(part, bufs, place, first):
    r1, passing = bufs[1], bufs[3]
    ctx, tp = place[:2]
    for j in OFFSETS + (0,):
        for h in (0, 1):
            two, way, other, fast, slow = ways(place, h)
            lo, size = spans_of(part.shape[2])[h]
            line = (slow + j) % 4
            span = pl.ds(0, size)
            first[h, 0, j].wait_recv()
            mine = block_of(part, h, way, line)[pl.ds(lo, size)].astype(F32)
            passing[h, line, span] = (mine + r1[h, 0, line, span].astype(F32)).astype(BF)
            first[h, 1, j] = send(
                passing.at[h, line, span],
                r1.at[h, 1, line, span],
                bufs[4:6],
                (h, 1, j),
                (spot(h, way, slow), tp),
            )
            first[h, 2, j] = scatter_send(part, bufs, place, h, 2, j)


def scatter_middle(part, out, bufs, place, first):
    mid, r1, r2 = bufs[:3]
    ctx, tp = place[:2]
    direct = len(first) == 6
    second = {}
    for j in OFFSETS + (0,):
        for h in (0, 1):
            two, way, other, fast, slow = ways(place, h)
            lo, size = spans_of(part.shape[2])[h]
            line = (slow + j) % 4
            span = pl.ds(0, size)
            came = (0, 1, 2) if direct else (2, 1)
            if not direct or j == OFFSETS[0]:
                for k in came:
                    first[h, k, 0 if direct else j].wait_recv()
            total = block_of(part, h, fast, line)[pl.ds(lo, size)].astype(F32)
            for k in came:
                total = total + r1[h, k, line, span].astype(F32)
            if j == 0:
                out[pl.ds(lo, size)] = total
            else:
                mid[h, j - 1, span] = total.astype(BF)
                second[h, j] = send(
                    mid.at[h, j - 1, span],
                    r2.at[h, j - 1, span],
                    bufs[6:8],
                    (h, j - 1),
                    (spot(h, fast, line), tp),
                )
    return second


def scatter_end(part, out, bufs, first, second):
    r2 = bufs[2]
    for h, (lo, size) in enumerate(spans_of(part.shape[2])):
        for j in OFFSETS:
            second[h, j].wait_recv()
        total = out[pl.ds(lo, size)]
        for j in (1, 2, 3):
            total = total + r2[h, j - 1, pl.ds(0, size)].astype(F32)
        out[pl.ds(lo, size)] = total
    for cp in list(first.values()) + list(second.values()):
        cp.wait_send()


def line_peers(ctx, tp, y, x):
    return [(y * 4 + (x + d) % 4, tp) for d in (1, 2, 3)] + [
        (((y + d) % 4) * 4 + x, tp) for d in (1, 2, 3)
    ]


def ctx_peers(ctx, tp):
    return [((ctx + d) % 16, tp) for d in range(1, 16)]


def swap_start(src, dst, sems, place):
    ctx, tp = place[:2]
    return [
        send(src.at[(ctx + d) % 16], dst.at[ctx], sems, d - 1, ((ctx + d) % 16, tp))
        for d in range(1, 16)
    ]


def pack_state(state, decay, msg):
    width = decay.shape[1]
    for j in range(16):
        msg[j, :, :width] = state[16 * j : 16 * (j + 1)].astype(BF)
    high = decay[0:1].astype(BF).astype(F32)
    low = decay[0:1] - high
    row = lax.broadcasted_iota(jnp.int32, (16, 128), 0)
    tile = jnp.zeros((16, 128), F32)
    count = width // 128
    for k in range(count):
        span = slice(128 * k, 128 * (k + 1))
        tile = jnp.where(row == k, high[:, span], tile)
        tile = jnp.where(row == count + k, low[:, span], tile)
    for j in range(16):
        msg[j, :, width:] = tile.astype(BF)


def prefix_into(order, got, ent):
    width = ent.shape[2]
    count = width // 128
    running = jnp.zeros(ent.shape[1:], F32)
    for i in order:
        ent[i] = running.astype(BF)
        tile = got[i, :, width:].astype(F32)
        decay = jnp.concatenate(
            [tile[k : k + 1] + tile[count + k : count + k + 1] for k in range(count)], axis=1
        )
        running = got[i, :, :width].astype(F32) + decay * running


def front_kernel(
    scale,
    lengths,
    ids,
    hidden,
    gain,
    w_dt,
    b_in,
    b_sh,
    head_params,
    a_out,
    a_in_far,
    a_sh_far,
    w_in_far,
    w_sh_far,
    w_out_far,
    normed_far,
    low_in,
    low_sh,
    z_out,
    xs,
    q_out,
    bc,
    mask,
    decay,
    dt,
    pre,
    total,
    entering,
    ssd,
    kv_far,
    part_out,
    attn_t,
    lse,
    merged,
    params,
    normed,
    gated,
    kv_all,
    maps,
    w_in,
    w_sh,
    w_out,
    kv,
    work,
    row_decay,
    row_dt,
    x_one,
    inner,
    state,
    msg,
    got,
    ent,
    loads,
    *sems,
):
    place = ctx_place()
    ctx, tp, y, x = place
    c = tp % 2
    mate = (ctx, tp + 1 - 2 * c)
    peers = ctx_peers(ctx, tp) + [mate]
    greet(peers)
    rank = mask.shape[1]
    get_maps = [
        fetch(a_sh_far, maps.at[:, pl.ds(0, rank)], loads.at[5]),
        fetch(a_in_far, maps.at[:, pl.ds(rank, rank)], loads.at[6]),
    ]
    get_sh = fetch(w_sh_far, w_sh, loads.at[0])
    get_in = fetch(w_in_far, w_in, loads.at[1])
    get_out = fetch(w_out_far, w_out, loads.at[2])
    rows = hidden.shape[0]
    width = ssd.shape[1]
    heads = width // MHEAD
    base = ctx * rows
    blocks = rows // 128

    def span_of(i):
        return pl.ds(pl.multiple_of(i * 128, 128), 128)

    def norms(i, carry):
        at = span_of(i)
        v = hidden[at].astype(F32)
        normed[at] = (v * norm_scale(v) * gain[0:1]).astype(BF)
        t = base + i * 128 + iota((128, 128), 0)
        chosen = pick(t, lengths, [ids[k] for k in range(4)])
        mask[at] = (chosen == iota((128, 128), 1) // RANK).astype(F32)
        return carry

    lax.fori_loop(0, blocks, norms, 0)
    params[...] = jnp.zeros(params.shape, F32)
    params[0:3, 0:heads] = head_params[...]
    maps[:, 2 * rank :] = w_dt[...].T
    for cp in get_maps:
        cp.wait()
    h = dot(normed[...], maps[...])
    low_sh[...] = (h[:, :rank] * mask[...]).astype(BF)
    low_in[...] = (h[:, rank : 2 * rank] * mask[...]).astype(BF)
    v = h[:, 2 * rank :] + params[0:1]
    pre[...] = v
    v = soft_plus(v)
    dt[...] = v
    work[...] = -v * jnp.exp(params[1:2])
    get_sh.wait()
    lo = 2 * STATE
    h = dot(normed[...], w_sh[...]) + dot(low_sh[...], b_sh[...])
    bc[...] = h[:, :lo].astype(BF)
    group = tp // (QHEADS // KVH)
    for k in range(2):
        one = h[:, lo + 2 * k * HD : lo + (2 * k + 1) * HD]
        two = h[:, lo + (2 * k + 1) * HD : lo + (2 * k + 2) * HD]
        kv[:, HD * k : HD * (k + 1)] = jnp.where(group == 0, one, two).astype(BF)
    met(peers)
    s_one, s_two, s_kv1, s_kv2, s_m1, s_m2 = [sems[2 * k : 2 * k + 2] for k in range(6)]
    half = rows // 2
    part = half // 2
    mine = pl.multiple_of(c * half, half)
    span = [pl.ds(pl.multiple_of(mine + h * part, part), part) for h in (0, 1)]
    kv1 = {}
    for off in OFFSETS:
        for h in (0, 1):
            fast, slow = ((x, y), (y, x))[h]
            kv1[h, off] = send(
                kv.at[span[h]],
                kv_all.at[y, x, span[h]],
                s_kv1,
                (h, off - 1),
                (spot(h, (fast + off) % 4, slow), tp),
            )
    kv_all[y, x] = kv[...]
    keep_normed = fetch(normed, normed_far, loads.at[3])
    get_in.wait()
    h = (dot(normed[...], w_in[...]) + dot(low_in[...], b_in[...])).astype(BF)
    z_out[...] = h[:, :width]
    xs[...] = h[:, width : 2 * width]
    q_out[...] = h[:, 2 * width :]
    kv2, to_mate = {}, []
    for off in OFFSETS:
        for h in (0, 1):
            kv1[h, off].wait_recv()

    def line(h, at):
        return (kv_all.at[at] if h == 0 else kv_all.at[:, at]).at[:, span[h]]

    for off in OFFSETS:
        for h in (0, 1):
            fast, slow = ((x, y), (y, x))[h]
            kv2[h, off] = send(
                line(h, slow),
                line(h, slow),
                s_kv2,
                (h, off - 1),
                (spot(h, fast, (slow + off) % 4), tp),
            )
    for off in OFFSETS:
        for h in (0, 1):
            fast, slow = ((x, y), (y, x))[h]
            block = block_of(kv_all, h, (fast + 4 - off) % 4, slow).at[span[h]]
            to_mate.append(send(block, block, s_m1, (h, off - 1), mate))
    running_sum(decay, work, rows, False)
    row_decay[...] = decay[...].T
    row_dt[...] = dt[...].T
    for h in range(heads):
        x_one[h] = one_head(xs[:, (h // 2) * 128 : (h // 2 + 1) * 128], h)
    final = decay[rows - 1 : rows]
    last_start = doc_start(base + rows - 1, lengths)
    tail = jnp.where(
        base + iota((rows, 128), 0) >= last_start, jnp.exp(final - decay[...]) * dt[...], 0.0
    )
    scaled = (spread(tail, heads) * xs[...].astype(F32)).astype(BF)
    state[...] = dot_tn(bc[:, :STATE], scaled)
    through = jnp.where(last_start < base, 1.0, 0.0)
    whole = jnp.broadcast_to(jnp.exp(final) * through, (8, 128))
    total[...] = spread(whole, heads)
    pack_state(state, total, msg)
    one = swap_start(msg, got, s_one, place)
    got[ctx] = msg[ctx]
    for i in range(blocks):
        at = pl.ds(i * 128, 128)
        wide = (i + 1) * 128
        seen = fades(i, base, lengths)
        inter = dot_nt(bc[at, STATE:], bc[0:wide, :STATE])
        for pair_at in range(heads // 2):
            acc = jnp.zeros((128, 128), F32)
            for h in (2 * pair_at, 2 * pair_at + 1):
                gap = decay[at, h : h + 1] - row_decay[h : h + 1, 0:wide]
                fade = jnp.exp(jnp.where(seen, gap, -1e30))
                mixing = (inter * fade * row_dt[h : h + 1, 0:wide]).astype(BF)
                acc = acc + dot(mixing, x_one[h, 0:wide])
            inner[at, pair_at * 128 : (pair_at + 1) * 128] = acc
    for cp in one:
        cp.wait_recv()
    prefix_into(range(16), got, ent)
    two = swap_start(ent, entering, s_two, place)
    entering[ctx] = ent[ctx]
    for off in OFFSETS:
        for h in (0, 1):
            fast, slow = ((x, y), (y, x))[h]
            kv2[h, off].wait_recv()
            came = line(h, (slow + 4 - off) % 4)
            to_mate.append(send(came, came, s_m2, (h, off - 1), mate))
    for cp in two:
        cp.wait_recv()
    arrived = entering[...].reshape(STATE, width)

    def finish(i, carry):
        at = span_of(i)
        t = base + i * 128 + iota((128, 128), 0)
        reach = jnp.where(doc_start(t, lengths) < base, jnp.exp(decay[at]), 0.0)
        cross = dot(bc[at, STATE:], arrived) * spread(reach, heads)
        skip = spread(jnp.broadcast_to(params[2:3], (8, 128)), heads)[0:1]
        out = inner[at] + cross + skip * xs[at].astype(F32)
        ssd[at] = out
        z = z_out[at].astype(F32)
        gated[at] = (out * (z * jax.nn.sigmoid(z))).astype(BF)
        return carry

    lax.fori_loop(0, blocks, finish, 0)
    for cp in to_mate:
        cp.wait_recv()
    keep_kv = fetch(kv_all, kv_far, loads.at[4])
    out, lse[...] = attend(scale, ctx, lengths, q_out, kv_all)
    attn_t[...] = out
    merged[:, :width] = gated[...]
    merged[:, width:] = out.T.astype(BF)
    get_out.wait()
    model = w_out.shape[1]
    share = part_out.shape[1]
    low = (dot(merged[...], a_out[...]) * mask[...]).astype(BF)
    for k in range(8):
        part_out[k, :, model:] = low[k * share : (k + 1) * share]

    def mix(j, carry):
        cols = lanes(j, 512)
        full = dot(merged[...], w_out[:, cols]).astype(BF)
        for k in range(8):
            part_out[k, :, cols] = full[k * share : (k + 1) * share]
        return carry

    lax.fori_loop(0, model // 512, mix, 0)
    for cp in one + two + to_mate + list(kv1.values()) + list(kv2.values()):
        cp.wait_send()
    keep_normed.wait()
    keep_kv.wait()


def front_exchange(scale, *args):
    hidden, a_in, w_in, w_sh, w_out = (args[k] for k in (2, 9, 11, 12, 13))
    rows, model = hidden.shape
    width = (w_in.shape[1] - HD) // 2
    heads = width // MHEAD
    rank = a_in.shape[1]
    return call(
        functools.partial(front_kernel, scale),
        [
            ((rows, model), BF),
            ((rows, rank), BF),
            ((rows, rank), BF),
            ((rows, width), BF),
            ((rows, width), BF),
            ((rows, HD), BF),
            ((rows, 2 * STATE), BF),
            ((rows, 128), F32),
            ((rows, 128), F32),
            ((rows, 128), F32),
            ((rows, 128), F32),
            ((8, width), F32),
            ((16, 16, width), BF),
            ((rows, width), F32),
            ((4, 4, rows, 2 * HD), BF),
            ((8, rows // 8, model + rank), BF),
            ((HD, rows), F32),
            ((1, rows), F32),
            ((rows, width + HD), BF),
            ((8, 128), F32),
        ],
        list(args),
        [
            pltpu.VMEM((rows, model), BF),
            pltpu.VMEM((rows, width), BF),
            pltpu.VMEM((4, 4, rows, 2 * HD), BF),
            pltpu.VMEM((model, 2 * rank + 128), BF),
            pltpu.VMEM(w_in.shape, BF),
            pltpu.VMEM(w_sh.shape, BF),
            pltpu.VMEM(w_out.shape, BF),
            pltpu.VMEM((rows, 2 * HD), BF),
            pltpu.VMEM((rows, 128), F32),
            pltpu.VMEM((128, rows), F32),
            pltpu.VMEM((128, rows), F32),
            pltpu.VMEM((heads, rows, 128), BF),
            pltpu.VMEM((rows, width), F32),
            pltpu.VMEM((STATE, width), F32),
            pltpu.VMEM((16, 16, width + 128), BF),
            pltpu.VMEM((16, 16, width + 128), BF),
            pltpu.VMEM((16, 16, width), BF),
            DMA((7,)),
            *pair(15),
            *pair(15),
            *pair(2, 3),
            *pair(2, 3),
            *pair(2, 3),
            *pair(2, 3),
        ],
        4,
        "front_exchange",
        [SM, SM] + [VM] * 7 + [HB] * 5,
        [HB] + [VM] * 13 + [HB] + [VM] * 5,
    )


def back_kernel(
    scale,
    lengths,
    total,
    resid,
    b_dn,
    bc,
    xs,
    decay,
    dt,
    pre,
    params,
    entering,
    b_in,
    b_sh,
    w_dt,
    q,
    lse,
    attn_t,
    grad_mixer,
    w_out,
    b_out,
    a_out,
    mask,
    z_in,
    ssd,
    kv_far,
    part_far,
    w_in_far,
    w_sh_far,
    rest_far,
    gathered_far,
    part_out,
    two_out,
    grad_one_far,
    grad_head,
    grad_low,
    rest_sum,
    gathered,
    grad_one,
    kv,
    part,
    rest,
    dkv,
    grad_attn,
    grad_ssd,
    grad_z,
    hold,
    msg,
    got,
    ent,
    leaving,
    both,
    dkv_sum,
    kv_rows,
    grad_two,
    row_decay,
    row_dt,
    col_sum,
    row_sum,
    x_one,
    dy_one,
    dx,
    grad_b,
    grad_c,
    work,
    loads,
    *scratch,
):
    place = ctx_place()
    ctx, tp, y, x = place
    tp_at = tp_place()
    c = tp % 2
    mate = (ctx, tp + 1 - 2 * c)
    peers = ctx_peers(ctx, tp) + tp_peers(*tp_at)
    greet(peers)
    get_kv = fetch(kv_far, kv, loads.at[0])
    get_part = fetch(part_far, part, loads.at[1])
    get_rest = fetch(rest_far, rest, loads.at[2])
    rows, width = xs.shape
    heads = width // MHEAD
    base = ctx * rows
    blocks = rows // 128
    s_one, s_two, s_mate = scratch[0:2], scratch[2:4], scratch[4:6]
    bufs, more, sems, wide_bufs = scratch[6:14], scratch[14:21], scratch[21:25], scratch[25:]

    grad_low[...] = (dot_nt(grad_mixer[...], b_out[...]) * mask[...]).astype(BF)
    grad = (dot_nt(grad_mixer[...], w_out[...]) + dot_nt(grad_low[...], a_out[...])).astype(BF)
    grad_attn[...] = grad[:, width:]
    gated = grad[:, :width].astype(F32)
    z = z_in[...].astype(F32)
    sig = jax.nn.sigmoid(z)
    grad_z[...] = (gated * ssd[...] * sig * (1.0 + z * (1.0 - sig))).astype(BF)
    gated = gated * (z * sig)
    grad_ssd[...] = gated
    reach = jnp.where(
        doc_start(base + iota((rows, 128), 0), lengths) < base, jnp.exp(decay[...]), 0.0
    )
    hold[...] = (spread(reach, heads) * gated).astype(BF)
    pack_state(dot_tn(bc[:, STATE:], hold[...]), total, msg)
    met(peers)
    one = swap_start(msg, got, s_one, place)
    got[ctx] = msg[ctx]
    get_part.wait()
    first_z = reduce_start(part, more, tp_at)
    get_rest.wait()
    first_w = scatter_start(rest, wide_bufs, place)
    low = jnp.sum(grad_attn[...].T.astype(F32) * attn_t[...], axis=0, keepdims=True)
    dkv[...] = jnp.zeros(dkv.shape, BF)
    get_kv.wait()
    second_z = reduce_middle(part, more, tp_at, first_z)

    def midway():
        scatter_relay(rest, wide_bufs, place, first_w)
        reduce_relay(part, more, tp_at, first_z, second_z)

    dq = attend_back(scale, ctx, lengths, q, kv, lse[...], low, grad_attn, dkv, midway)
    grad_one[:, 2 * width : 2 * width + HD] = dq.T.astype(BF)
    half = rows // 2
    mine = pl.ds(pl.multiple_of(c * half, half), half)
    other = pl.ds(pl.multiple_of((1 - c) * half, half), half)
    cps = [send(dkv.at[k, :, other], both.at[k], s_mate, k, mate) for k in range(4)]
    for cp in one:
        cp.wait_recv()
    prefix_into(range(15, -1, -1), got, ent)
    two = swap_start(ent, leaving, s_two, place)
    leaving[ctx] = ent[ctx]
    for k in range(4):
        cps[k].wait_recv()
        for i in range(4):
            both[k, i] = (dkv[k, i, mine].astype(F32) + both[k, i].astype(F32)).astype(BF)
    first = scatter_start(both, bufs, place)
    loaded = []
    for i in range(4):
        for k in range(4):
            rows_at = pl.ds(512 * i, 512)
            loaded.append(
                fetch(w_sh_far.at[rows_at, pl.ds(256 * k, 256)], kv.at[i, k], loads.at[4 + 4 * i + k])
            )
    for cp in cps:
        cp.wait_send()
    for i in range(4):
        for k in range(4):
            size = min(256, w_in_far.shape[1] - 256 * k)
            loaded.append(
                fetch(
                    w_in_far.at[pl.ds(512 * i, 512), pl.ds(256 * k, size)],
                    dkv.at[i, k, :, pl.ds(0, size)],
                    loads.at[20 + 4 * i + k],
                )
            )

    row_decay[...] = decay[...].T
    row_dt[...] = dt[...].T
    col_sum[...] = jnp.zeros(col_sum.shape, F32)
    for h in range(heads):
        cols = slice((h // 2) * 128, (h // 2 + 1) * 128)
        x_one[h] = one_head(xs[:, cols], h)
        dy_one[h] = one_head(grad_ssd[:, cols], h).astype(BF)
    grad_b[...] = jnp.zeros(grad_b.shape, F32)
    dx[...] = jnp.zeros(dx.shape, F32)
    for i in range(blocks):
        at = pl.ds(i * 128, 128)
        wide = (i + 1) * 128
        seen = fades(i, base, lengths)
        inter = dot_nt(bc[at, STATE:], bc[0:wide, :STATE])
        d_inter = jnp.zeros((128, wide), F32)
        sums = jnp.zeros((128, 128), F32)
        for pair_at in range(heads // 2):
            cols = slice(pair_at * 128, (pair_at + 1) * 128)
            for h in (2 * pair_at, 2 * pair_at + 1):
                step = row_dt[h : h + 1, 0:wide]
                gap = decay[at, h : h + 1] - row_decay[h : h + 1, 0:wide]
                fade = jnp.exp(jnp.where(seen, gap, -1e30))
                d_mix = dot_nt(dy_one[h, at], x_one[h, 0:wide])
                faded = fade * step
                d_inter = d_inter + d_mix * faded
                weighted = d_mix * inter * fade
                col_sum[h : h + 1, 0:wide] += jnp.sum(weighted, axis=0, keepdims=True)
                sums = jnp.where(
                    iota((128, 128), 1) == h,
                    jnp.sum(weighted * step, axis=1, keepdims=True),
                    sums,
                )
                dx[0:wide, cols] += dot_tn((inter * faded).astype(BF), dy_one[h, at])
        if i == blocks // 2:
            scatter_relay(both, bufs, place, first)
        row_sum[at] = sums
        low = d_inter.astype(BF)
        grad_c[at] = dot(low, bc[0:wide, :STATE])
        grad_b[0:wide] += dot_tn(low, bc[at, STATE:])

    width_out = resid.shape[1]
    out = reduce_end(part, more, tp_at, first_z, second_z)
    low = out[:, width_out:].astype(BF)
    gathered[tp, :, :width_out] = (resid[...] + out[:, :width_out] + dot(low, b_dn[...])).astype(BF)
    gathered[tp, :, width_out:] = low
    started = share_start(gathered, sems, tp_at)
    second_w = scatter_middle(rest, rest_sum, wide_bufs, place, first_w)

    for cp in two:
        cp.wait_recv()
    after = leaving[...].reshape(STATE, width)
    before = entering[...].reshape(STATE, width)
    final = decay[rows - 1 : rows]
    last_start = doc_start(base + rows - 1, lengths)
    cols_sum = col_sum[...].T
    crossing = head_sums(
        jnp.broadcast_to(
            jnp.sum(after.astype(F32) * before.astype(F32), axis=0, keepdims=True) * total[0:1],
            (8, width),
        )
    )[0:1]
    rate = jnp.exp(params[1:2])
    skip = spread(jnp.broadcast_to(params[2:3], (8, 128)), heads)[0:1]
    d_last = crossing
    skips = jnp.zeros((1, 128), F32)
    for i in range(blocks):
        at = pl.ds(i * 128, 128)
        t = base + i * 128 + iota((128, 128), 0)
        steps = dt[at]
        tail = jnp.where(t >= last_start, jnp.exp(final - decay[at]), 0.0)
        reach = jnp.where(doc_start(t, lengths) < base, jnp.exp(decay[at]), 0.0)
        x_f = xs[at].astype(F32)
        gs = grad_ssd[at]
        came = dot(bc[at, :STATE], after)
        held = head_sums(came * x_f) * tail
        reached = spread(reach, heads) * gs
        d_cross = head_sums(dot(bc[at, STATE:], before) * reached)
        cols_at = cols_sum[i * 128 : (i + 1) * 128]
        work[at] = row_sum[at] - cols_at * steps + d_cross - held * steps
        row_sum[at] = cols_at + held
        d_last = d_last + jnp.sum(held * steps, axis=0, keepdims=True)
        tails = spread(tail * steps, heads)
        grad_one[at, :width] = grad_z[at]
        grad_one[at, width : 2 * width] = (dx[at] + tails * came + skip * gs).astype(BF)
        skips = skips + jnp.sum(head_sums(gs * x_f), axis=0, keepdims=True)
        grad_two[at, :STATE] = (grad_b[at] + dot_nt((tails * x_f).astype(BF), after)).astype(BF)
        grad_two[at, STATE : 2 * STATE] = (grad_c[at] + dot_nt(reached.astype(BF), before)).astype(
            BF
        )
    second = scatter_middle(both, dkv_sum, bufs, place, first)
    passed = [share_pass(gathered, sems, tp_at, started, k) for k in (0, 1)]
    running_sum(dx.at[:, 0:128], work, rows, True)
    d_log = dx[:, 0:128] + d_last
    grad_dt = (row_sum[...] - rate * d_log) * jax.nn.sigmoid(pre[...])
    grad_one[:, 2 * width + HD :] = grad_dt.astype(BF)
    grad_head[0:1] = jnp.sum(grad_dt, axis=0, keepdims=True)
    grad_head[1:2] = -jnp.sum(dt[...] * rate * d_log, axis=0, keepdims=True)
    grad_head[2:3] = skips
    grad_head[3:8] = jnp.zeros((5, 128), F32)
    for cp in loaded:
        cp.wait()
    narrow = 2 * width + HD

    model = resid.shape[1]
    rank = b_in.shape[0]
    share = resid.shape[0]

    def norm_part(j, carry):
        cols = lanes(j, 512)
        full = dot(grad_one[:, narrow:], w_dt[:, cols])
        for k in range(0, narrow, 256):
            size = min(256, narrow - k)
            full = full + dot_nt(grad_one[:, k : k + size], dkv[j, k // 256, :, 0:size])
        for k in range(2):
            full = full + dot_nt(grad_two[:, 256 * k : 256 * (k + 1)], kv[j, k])
        full = full.astype(BF)
        for k in range(8):
            part_out[k, :, cols] = full[k * share : (k + 1) * share]
        return carry

    lax.fori_loop(0, resid.shape[1] // 512, norm_part, 0)
    stores = [fetch(grad_one, grad_one_far, loads.at[36])]
    share_end(gathered, sems, tp_at, started, passed)
    stores.append(fetch(gathered, gathered_far, loads.at[37]))
    low_one = dot_nt(grad_one[:, :narrow], b_in[...]).astype(BF)
    for k in range(8):
        part_out[k, :, model : model + rank] = low_one[k * share : (k + 1) * share]
    scatter_end(both, dkv_sum, bufs, first, second)
    kv_rows[...] = jnp.zeros(kv_rows.shape, F32)
    kv_rows[mine] = dkv_sum[...]
    group = tp // (QHEADS // KVH)
    for k in range(KVH):
        on = jnp.where(group == k, 1.0, 0.0)
        for v in range(2):
            lo = 2 * STATE + (v * KVH + k) * HD
            grad_two[:, lo : lo + HD] = (kv_rows[:, v * HD : (v + 1) * HD] * on).astype(BF)

    def finish(j, carry):
        cols = lanes(j, 512)
        full = dot_nt(grad_two[:, 512:768], kv[j, 2]) + dot_nt(grad_two[:, 768:], kv[j, 3])
        for k in range(8):
            some = part_out[k, :, cols].astype(F32) + full[k * share : (k + 1) * share]
            part_out[k, :, cols] = some.astype(BF)
        return carry

    lax.fori_loop(0, model // 512, finish, 0)
    low_two = dot_nt(grad_two[...], b_sh[...]).astype(BF)
    for k in range(8):
        part_out[k, :, model + rank :] = low_two[k * share : (k + 1) * share]
    for k in range(8):
        two_out[k] = grad_two[:, k * 128 : (k + 1) * 128]
    scatter_end(rest, rest_sum, wide_bufs, first_w, second_w)
    for cp in one + two:
        cp.wait_send()
    for cp in stores:
        cp.wait()


def back_exchange(scale, *args):
    resid, bc, xs, b_in, kv, part, w_sh, rest = (args[k] for k in (2, 4, 5, 11, 24, 25, 27, 28))
    rows, width = xs.shape
    heads = width // MHEAD
    half = rows // 2
    cols = 2 * HD
    _, share, wide = part.shape
    model = resid.shape[1]
    rank = b_in.shape[0]
    return call(
        functools.partial(back_kernel, scale),
        [
            (part.shape, BF),
            ((8, share, model + 2 * rank), BF),
            ((8, rows, w_sh.shape[1] // 8), BF),
            ((rows, 2 * width + HD + 128), BF),
            ((8, 128), F32),
            ((rows, rank), BF),
            (rest.shape[2:], F32),
        ],
        list(args),
        [
            pltpu.VMEM(part.shape, BF),
            pltpu.VMEM((rows, 2 * width + HD + 128), BF),
            pltpu.VMEM(kv.shape, BF),
            pltpu.VMEM(part.shape, BF),
            pltpu.VMEM(rest.shape, BF),
            pltpu.VMEM(kv.shape, BF),
            pltpu.VMEM((rows, HD), BF),
            pltpu.VMEM((rows, width), F32),
            pltpu.VMEM((rows, width), BF),
            pltpu.VMEM((rows, width), BF),
            pltpu.VMEM((16, 16, width + 128), BF),
            pltpu.VMEM((16, 16, width + 128), BF),
            pltpu.VMEM((16, 16, width), BF),
            pltpu.VMEM((16, 16, width), BF),
            pltpu.VMEM((4, 4, half, cols), BF),
            pltpu.VMEM((half, cols), F32),
            pltpu.VMEM((rows, cols), F32),
            pltpu.VMEM((rows, w_sh.shape[1]), BF),
            pltpu.VMEM((128, rows), F32),
            pltpu.VMEM((128, rows), F32),
            pltpu.VMEM((128, rows), F32),
            pltpu.VMEM((rows, 128), F32),
            pltpu.VMEM((heads, rows, 128), BF),
            pltpu.VMEM((heads, rows, 128), BF),
            pltpu.VMEM((rows, width), F32),
            pltpu.VMEM((rows, STATE), F32),
            pltpu.VMEM((rows, STATE), F32),
            pltpu.VMEM((rows, 128), F32),
            DMA((38,)),
            *pair(15),
            *pair(15),
            *pair(4),
            *scatter_bufs(half, cols),
            *reduce_bufs(share, wide),
            *share_sems(),
            *scatter_bufs(rest.shape[2], 128),
        ],
        5,
        "back_exchange",
        [SM] + [VM] * 23 + [HB] * 5,
        [HB, VM, VM, HB, VM, VM, VM],
    )


def tail_kernel(
    part,
    part_two,
    gain,
    mask,
    gain_two,
    grad_resid,
    low_in,
    low_sh,
    grad_low_out,
    grad_low_gu,
    low_out,
    head,
    a_in,
    a_sh,
    hidden_far,
    normed_far,
    grad_one_far,
    merged_far,
    normed_mine_far,
    mixer_mine_far,
    grad_mine_far,
    rows_far,
    gathered,
    big_out,
    small_out,
    shared,
    head_out,
    source,
    normed_one,
    grad_one,
    merged,
    normed_mine,
    mixer_mine,
    grad_mine,
    low_dn,
    lows,
    turned,
    mine,
    big,
    small,
    two,
    two_t,
    picks,
    heads,
    loads,
    *scratch,
):
    place = ctx_place()
    tp_at = tp_place()
    ctx, tp = place[:2]
    peers = ctx_peers(ctx, tp) + all_tp(*tp_at)
    greet(peers)
    share, width = source.shape
    rank = a_in.shape[1]
    rows = normed_one.shape[0]
    rows_mine = pl.ds(pl.multiple_of(tp * share, share), share)
    get = [
        fetch(src, dst, loads.at[k])
        for k, (src, dst) in enumerate(
            (
                (grad_one_far, grad_one),
                (normed_far, normed_one),
                (merged_far, merged),
                (normed_mine_far, normed_mine),
                (mixer_mine_far, mixer_mine),
                (grad_mine_far, grad_mine),
                (rows_far.at[:, :, pl.ds(width, rank)], low_dn),
                (hidden_far.at[rows_mine], source),
            )
        )
    ]
    bufs_z, more_z, sems, sems_l = scratch[:7], scratch[7:14], scratch[14:18], scratch[18:20]
    bufs, more, s_head, sems_s = scratch[20:28], scratch[28:36], scratch[36:38], scratch[38:]
    get[0].wait()
    turned[...] = grad_one[...].T
    deep = grad_one.shape[1]
    get[1].wait()

    def weights(j, carry):
        split_out(big, 0, dot(turned[...], normed_one[:, lanes(j, 512)]), 4 * j)
        return carry

    lax.fori_loop(0, 4, weights, 0)
    eights(big, deep, dot_tn(low_in[...], grad_one[...]))
    for k in range(2, 8):
        get[k].wait()
    row = deep + 64
    a_out_sum = dot_tn(merged[...], grad_low_out[...])
    for j in range(16):
        big[j // 4, j % 4, row : row + 32] = a_out_sum[j * 32 : (j + 1) * 32].astype(BF)
    for k, full in enumerate(
        (
            dot_tn(normed_mine[...], grad_low_gu[...]),
            dot_tn(mixer_mine[...], low_out[...]),
            dot_tn(grad_mine[...], low_dn[...].reshape(rows, rank)),
        )
    ):
        at = row + 32 + 16 * k
        big[:, :, at : at + 16] = full.astype(BF).reshape(4, 4, 16, rank)
    met(peers)
    first_z = reduce_start(part, bufs_z, tp_at)
    first = scatter_start(big, bufs, place)
    second_z = reduce_middle(part, bufs_z, tp_at, first_z)
    first_two = reduce_start(part_two, more_z, tp_at)
    picks[...] = chooser(tp)
    half = width // 2
    for k in range(2):
        cols = slice(half * k, half * (k + 1))
        mine[:, 128 * k : 128 * (k + 1)] = dot(normed_one[:, cols], picks[...]).astype(BF)
    reduce_relay(part, bufs_z, tp_at, first_z, second_z)
    second_two = reduce_middle(part_two, more_z, tp_at, first_two)
    scatter_relay(big, bufs, place, first)
    total = reduce_end(part, bufs_z, tp_at, first_z, second_z)
    mask_mine = mask[rows_mine]
    low_one = (total[:, width : width + rank] * mask_mine).astype(BF)
    low_two = (total[:, width + rank :] * mask_mine).astype(BF)
    lows[tp, :, :rank] = low_one
    lows[tp, :, rank:] = low_two
    started_l = share_direct(lows, sems_l, tp_at)
    grad = total[:, :width] + dot_nt(low_one, a_in[...]) + dot_nt(low_two, a_sh[...])
    grad_v, grad_gain = norm_back(source[...].astype(F32), gain[0:1], grad)
    gathered[tp] = (grad_resid[...] + grad_v).astype(BF)
    reduce_relay(part_two, more_z, tp_at, first_two, second_two)
    started = share_start(gathered, sems, tp_at)
    two[...] = reduce_end(part_two, more_z, tp_at, first_two, second_two).astype(BF)
    b_sh_sum = dot_tn(low_sh[...], two[...])
    two_t[...] = two[...].T

    def shared_maps(j, carry):
        split_out(small, 0, dot(two_t[...], normed_one[:, lanes(j, 512)]), 4 * j)
        return carry

    lax.fori_loop(0, 4, shared_maps, 0)
    gain_rows = jnp.concatenate([grad_gain, gain_two[...], jnp.zeros((6, width), F32)], axis=0)
    for j in range(16):
        small[j // 4, j % 4, 144:160] = jnp.concatenate(
            [b_sh_sum[8 * j : 8 * j + 8], gain_rows[:, 128 * j : 128 * (j + 1)]], axis=0
        ).astype(BF)
    passed = [share_pass(gathered, sems, tp_at, started, k) for k in (0, 1)]
    for cp in started_l:
        cp.wait_recv()
    full = dot_tn(mine[...], lows[...].reshape(rows, 2 * rank)).astype(BF)
    small[:, :, 160:176] = full[:, :rank].reshape(4, 4, 16, rank)
    small[:, :, 128:144] = full[:, rank:].reshape(4, 4, 16, rank)
    first_s = scatter_direct(small, more, place)
    sent = [send(head, heads.at[ctx], s_head, d - 1, ((ctx + d) % 16, tp)) for d in range(1, 16)]
    heads[ctx] = head[...]
    second = scatter_middle(big, big_out, bufs, place, first)
    passed.append(share_pass(gathered, sems, tp_at, started, 2))
    second_s = scatter_middle(small, small_out, more, place, first_s)
    scatter_end(small, small_out, more, first_s, second_s)
    shared[tp] = small_out[pl.ds(0, shared.shape[1])].astype(BF)
    started_s = share_direct(shared, sems_s, tp_at)
    scatter_end(big, big_out, bufs, first, second)
    share_end(gathered, sems, tp_at, started, passed)
    for cp in sent:
        cp.wait_recv()
    head_out[...] = jnp.sum(heads[...], axis=0)
    for cp in started_s:
        cp.wait_recv()
    for cp in sent + started_l + started_s:
        cp.wait_send()


def tail_exchange(*args):
    part, part_two, grad_resid, head, grad_one, merged, rows_in = (
        args[k] for k in (0, 1, 5, 11, 16, 17, 21)
    )
    _, share, wide = part.shape
    _, rows, cols = part_two.shape
    width = grad_resid.shape[1]
    rank = (wide - width) // 2
    deep = grad_one.shape[1]
    return call(
        tail_kernel,
        [
            ((8, share, width), BF),
            ((deep + 144, 128), F32),
            ((176, 128), F32),
            ((8, 160, 128), BF),
            (head.shape, F32),
        ],
        list(args),
        [
            pltpu.VMEM((share, width), BF),
            pltpu.VMEM((rows, width), BF),
            pltpu.VMEM(grad_one.shape, BF),
            pltpu.VMEM(merged.shape, BF),
            pltpu.VMEM((rows, 256), BF),
            pltpu.VMEM((rows, 256), BF),
            pltpu.VMEM((rows, 256), BF),
            pltpu.VMEM((8, share, rank), BF),
            pltpu.VMEM((8, share, 2 * rank), BF),
            pltpu.VMEM((deep, rows), BF),
            pltpu.VMEM((rows, 256), BF),
            pltpu.VMEM((4, 4, deep + 144, 128), BF),
            pltpu.VMEM((4, 4, 176, 128), BF),
            pltpu.VMEM((rows, 128), BF),
            pltpu.VMEM((128, rows), BF),
            pltpu.VMEM((1024, 128), BF),
            pltpu.VMEM((16,) + head.shape, F32),
            DMA((8,)),
            *reduce_bufs(share, wide),
            *reduce_bufs(rows, cols),
            *share_sems(),
            *pair(7),
            *scatter_bufs(deep + 144, 128),
            *scatter_bufs(176, 128),
            *pair(15),
            *pair(7),
        ],
        6,
        "tail_exchange",
        [VM] * 14 + [HB] * 8,
    )


def finish_kernel(
    mixed_in,
    input_in,
    big,
    small,
    shared,
    head,
    early,
    rest_in,
    mixed,
    input_grad,
    gains,
    w_in,
    w_sh,
    w_dt,
    params,
    w_out,
    w_gu,
    w_down,
    a_in,
    b_in,
    a_sh,
    b_sh,
    a_out,
    b_out,
    a_gu,
    b_gu,
    a_dn,
    b_dn,
):
    width = mixed.shape[1]
    mixed[...] = mixed_in[0, :, :width].astype(F32)
    input_grad[...] = input_in[0, :, :width].astype(F32)

    @pl.when(pl.program_id(0) == 0)
    def rest():
        narrow = w_in.shape[2]
        hidden = w_down.shape[0]
        heads = w_dt.shape[0]
        w_in[:, 0, :] = big[0:narrow].T
        w_dt[...] = big[narrow : narrow + heads]
        deep = narrow + 128
        for k in range(narrow // 128):
            cols = slice(128 * k, 128 * (k + 1))
            b_in[:, 0, cols] = big[deep + 8 * k : deep + 8 * (k + 1)]
        params[...] = head[0:3, 0:heads]
        total = jnp.zeros((8, 128), F32)
        for k in range(8):
            block = shared[k].astype(F32)
            cols = slice(128 * k, 128 * (k + 1))
            w_sh[:, cols] = block[0:128].T
            a_sh[16 * k : 16 * (k + 1)] = block[128:144]
            b_sh[:, cols] = block[144:152]
            total = total + block[152:160]
        gains[...] = total[0:2]
        maps = deep + 64
        a_out[0] = big[maps : maps + 32]
        a_gu[...] = big[maps + 32 : maps + 48]
        b_out[...] = big[maps + 48 : maps + 64]
        b_dn[...] = big[maps + 64 : maps + 80]
        a_in[...] = small[160:176]
        w_gu[:, 0, :] = early[0:hidden].T
        w_gu[:, 1, :] = early[hidden : 2 * hidden].T
        w_down[...] = rest_in[0:hidden]
        w_out[0] = rest_in[hidden : 2 * hidden]
        for k in range(hidden // 128):
            cols = slice(128 * k, 128 * (k + 1))
            row = 2 * hidden + 8 * k
            b_gu[:, 0, cols] = early[row : row + 8]
            b_gu[:, 1, cols] = early[row + 32 : row + 40]
            a_dn[:, cols] = rest_in[row : row + 8]


def finish(mixed, input_grad, big, small, shared, head, early, rest, narrow, heads):
    _, rows, wide = mixed.shape
    _, _, wide_two = input_grad.shape
    width = wide - 128
    hidden = early.shape[0] // 2 // 128 * 128
    outs = [
        (8 * rows, width),
        (8 * rows, width),
        (2, 128),
        (128, 1, narrow),
        (128, 1024),
        (heads, 128),
        (3, heads),
        (1, hidden, 128),
        (128, 2, hidden),
        (hidden, 128),
        (16, 128),
        (8, 1, narrow),
        (128, 128),
        (8, 1024),
        (1, 32, 128),
        (16, 128),
        (16, 128),
        (8, 2, hidden),
        (8, hidden),
        (16, 128),
    ]

    def whole(shape):
        return pl.BlockSpec(shape, lambda i: (0,) * len(shape))

    done = pl.pallas_call(
        finish_kernel,
        grid=(8,),
        out_shape=[jax.ShapeDtypeStruct(s, F32) for s in outs],
        in_specs=[
            pl.BlockSpec((1, rows, wide), lambda i: (i, 0, 0)),
            pl.BlockSpec((1, rows, wide_two), lambda i: (i, 0, 0)),
        ]
        + [whole(a.shape) for a in (big, small, shared, head, early, rest)],
        out_specs=[pl.BlockSpec((rows, width), lambda i: (i, 0))] * 2 + [whole(s) for s in outs[2:]],
        compiler_params=pltpu.CompilerParams(vmem_limit_bytes=61 << 20),
        name="finish",
    )(mixed, input_grad, big, small, shared, head, early, rest)
    return tuple(a.T if k in (5, 15, 18, 19) else a for k, a in enumerate(done))


def body(
    hidden_in,
    norm_gains,
    w_in,
    w_shared,
    w_dt,
    head_params,
    w_out,
    w_gu,
    w_down,
    a_in,
    b_in,
    a_sh,
    b_sh,
    a_out,
    b_out,
    a_gu,
    b_gu,
    a_dn,
    b_dn,
    adapter_ids,
    doc_lengths,
    out_grad,
):
    rows, width = hidden_in.shape
    heads = head_params.shape[1]
    w_in = w_in.reshape(width, -1)
    b_in = b_in.reshape(b_in.shape[0], -1)
    w_out = w_out.reshape(-1, width)
    a_out = a_out.reshape(-1, a_out.shape[2])
    w_gu = w_gu.reshape(width, -1)
    b_gu = b_gu.reshape(b_gu.shape[0], -1)
    w_dt = jnp.pad(w_dt.T, ((0, 128 - heads), (0, 0)))
    scale = HD ** (-0.5)
    (
        normed_one,
        low_in,
        low_sh,
        z,
        xs,
        q,
        bc,
        mask,
        decay,
        dt,
        pre,
        total,
        entering,
        ssd,
        kv_all,
        mix_part,
        attn_t,
        lse,
        merged,
        params,
    ) = front_exchange(
        scale,
        doc_lengths,
        adapter_ids,
        hidden_in,
        norm_gains,
        w_dt,
        b_in,
        b_sh,
        head_params,
        a_out,
        a_in,
        a_sh,
        w_in,
        w_shared,
        w_out,
    )
    (
        low_out,
        grad_mixer,
        grad_low_gu,
        resid,
        grad_resid,
        gain_part_two,
        early,
        rest,
        mlp_part,
        normed_mine,
        grad_mine,
        mixer_mine,
    ) = mlp_exchange(
        mix_part,
        norm_gains,
        b_out,
        a_gu,
        b_gu,
        a_dn,
        b_dn,
        mask,
        merged,
        hidden_in,
        w_gu,
        w_down,
        out_grad,
    )
    mixed, part, two_blocks, grad_one, grad_head, grad_low_out, rest = back_exchange(
        scale,
        doc_lengths,
        total,
        resid,
        b_dn,
        bc,
        xs,
        decay,
        dt,
        pre,
        params,
        entering,
        b_in,
        b_sh,
        w_dt,
        q,
        lse,
        attn_t,
        grad_mixer,
        w_out,
        b_out,
        a_out,
        mask,
        z,
        ssd,
        kv_all,
        mlp_part,
        w_in,
        w_shared,
        rest,
    )
    input_grad, big, small, shared, head = tail_exchange(
        part,
        two_blocks,
        norm_gains,
        mask,
        gain_part_two,
        grad_resid,
        low_in,
        low_sh,
        grad_low_out,
        grad_low_gu,
        low_out,
        grad_head,
        a_in,
        a_sh,
        hidden_in,
        normed_one,
        grad_one,
        merged,
        normed_mine,
        mixer_mine,
        grad_mine,
        mixed,
    )
    return finish(mixed, input_grad, big, small, shared, head, early, rest, w_in.shape[1], heads)


def solution(mesh):
    placed = (
        P("ctx", None),
        P(),
        P(None, "tp", None),
        P(),
        P(None, "tp"),
        P(None, "tp"),
        P("tp", None, None),
        P(None, None, "tp"),
        P("tp", None),
        P(),
        P(None, "tp", None),
        P(),
        P(),
        P("tp", None, None),
        P(),
        P(),
        P(None, None, "tp"),
        P("tp", None),
        P(),
        P(),
        P(),
        P("ctx", None),
    )
    return jax.shard_map(
        body,
        mesh=mesh,
        in_specs=placed,
        out_specs=(
            P("ctx", None),
            P("ctx", None),
            P(None, "ctx"),
            P("ctx", "tp", None),
            P("ctx", None),
            P("ctx", "tp"),
            P(None, "tp"),
            P("tp", None, "ctx"),
            P("ctx", None, "tp"),
            P("tp", "ctx"),
            P(("ctx", "tp"), None),
            P("ctx", "tp", None),
            P("ctx", None),
            P("ctx", None),
            P("tp", "ctx", None),
            P(None, ("ctx", "tp")),
            P(("ctx", "tp"), None),
            P("ctx", None, "tp"),
            P("tp", "ctx"),
            P(None, ("ctx", "tp")),
        ),
        check_vma=False,
    )
```

```python
import functools

import jax
import jax.numpy as jnp
from jax import lax
from jax.experimental import pallas as pl
from jax.experimental.pallas import tpu as pltpu
from jax.sharding import PartitionSpec as P

MHEAD = 64
STATE = 256
QHEADS = 8
KVH = 2
HD = 128
RANK = 16
NORM_EPSILON = 1e-06

MESH = pl.DeviceIdType.MESH
VM = pl.BlockSpec(memory_space=pltpu.VMEM)
SM = pl.BlockSpec(memory_space=pltpu.SMEM)
HB = pl.BlockSpec(memory_space=pl.ANY)
BF = jnp.bfloat16
F32 = jnp.float32
DMA = pltpu.SemaphoreType.DMA
OFFSETS = (2, 1, 3)
LOG2E = 1.4426950408889634
UNROLL = 2


def call(kernel, outs, ins, scratch, cid, name, specs=None, out_specs=None):
    return pl.pallas_call(
        kernel,
        out_shape=[jax.ShapeDtypeStruct(s, d) for s, d in outs],
        in_specs=specs or [VM] * len(ins),
        out_specs=out_specs or [VM] * len(outs),
        scratch_shapes=scratch,
        compiler_params=pltpu.CompilerParams(
            collective_id=cid, has_side_effects=True, vmem_limit_bytes=61 << 20
        ),
        name=name,
    )(*ins)


def greet(peers):
    barrier = pltpu.get_barrier_semaphore()
    for peer in peers:
        pl.semaphore_signal(barrier, inc=1, device_id=peer, device_id_type=MESH)


def met(peers):
    pl.semaphore_wait(pltpu.get_barrier_semaphore(), len(peers))


def send(src, dst, sems, slot, peer):
    cp = pltpu.make_async_remote_copy(
        src_ref=src,
        dst_ref=dst,
        send_sem=sems[0].at[slot],
        recv_sem=sems[1].at[slot],
        device_id=peer,
        device_id_type=MESH,
    )
    cp.start()
    return cp


def pair(*shape):
    return [DMA(shape), DMA(shape)]


def tp_place():
    ctx = lax.axis_index("ctx")
    tp = lax.axis_index("tp")
    return ctx, tp, tp // 2, tp % 2


def tp_peers(ctx, tp, z, c):
    return [(ctx, ((z + d) % 4) * 2 + c) for d in (1, 2, 3)] + [(ctx, z * 2 + 1 - c)]


def reduce_bufs(rows, width):
    return [
        pltpu.VMEM((4, rows, width), BF),
        pltpu.VMEM((3, rows, width), BF),
        pltpu.VMEM((3, rows, width), BF),
        *pair(4),
        *pair(3),
    ]


def chips(place):
    ctx, tp, z, c = place
    return (z + 2) % 4, (z + 1 + 2 * c) % 4, (z + 3 - 2 * c) % 4, z


def reduce_pass(part, bufs, place, k):
    ctx, tp, z, c = place
    chip = chips(place)[(0, 2, 1, 3)[k]]
    return send(part.at[chip * 2 + 1 - c], bufs[0].at[k], bufs[3:5], k, (ctx, z * 2 + 1 - c))


def reduce_send(part, bufs, place, passed, k, relayed=None):
    sib, snd, rcv = bufs[:3]
    ctx, tp, z, c = place
    two, way, other, own = chips(place)
    passed.wait_recv()
    both = part[(two, way, other)[k] * 2 + c].astype(F32) + sib[k].astype(F32)
    if k == 1:
        relayed.wait_recv()
        both = both + rcv[0].astype(F32)
    snd[k] = both.astype(BF)
    to = other if k == 2 else way
    return send(snd.at[k], rcv.at[k], bufs[5:7], k, (ctx, to * 2 + c))


def reduce_start(part, bufs, place):
    return [reduce_pass(part, bufs, place, k) for k in range(4)]


def reduce_middle(part, bufs, place, first):
    return [reduce_send(part, bufs, place, first[0], 0), None, None]


def reduce_relay(part, bufs, place, first, second):
    second[1] = reduce_send(part, bufs, place, first[1], 1, second[0])
    second[2] = reduce_send(part, bufs, place, first[2], 2)


def reduce_end(part, bufs, place, first, second):
    sib, snd, rcv = bufs[:3]
    first[3].wait_recv()
    total = part[place[1]].astype(F32) + sib[3].astype(F32)
    for k in (2, 1):
        second[k].wait_recv()
        total = total + rcv[k].astype(F32)
    for cp in first + second:
        cp.wait_send()
    return total


def share_sems():
    return [*pair(3), *pair(4)]


def share_start(out, sems, place):
    ctx, tp, z, c = place
    two, way, other, own = chips(place)
    return [
        send(out.at[tp], out.at[tp], sems[:2], 0, (ctx, way * 2 + c)),
        send(out.at[tp], out.at[tp], sems[:2], 1, (ctx, other * 2 + c)),
        send(out.at[tp], out.at[tp], sems[2:], 0, (ctx, z * 2 + 1 - c)),
    ]


def share_pass(out, sems, place, started, k):
    ctx, tp, z, c = place
    two, way, other, own = chips(place)
    mate = (ctx, z * 2 + 1 - c)
    at = (other, way, two)[k] * 2 + c
    if k == 2:
        started[3].wait_recv()
    else:
        started[k].wait_recv()
    if k == 0:
        started.append(send(out.at[at], out.at[at], sems[:2], 2, (ctx, way * 2 + c)))
    passed = send(out.at[at], out.at[at], sems[2:], k + 1, mate)
    return passed


def share_end(out, sems, place, started, passed=()):
    passed = list(passed)
    passed += [share_pass(out, sems, place, started, k) for k in range(len(passed), 3)]
    started[2].wait_recv()
    for cp in passed:
        cp.wait_recv()
    for cp in started + passed:
        cp.wait_send()


def share_direct(out, sems, place):
    ctx, tp = place[:2]
    return [
        send(out.at[tp], out.at[tp], sems, d - 1, (ctx, (tp + d) % 8)) for d in range(1, 8)
    ]


def all_tp(ctx, tp, z, c):
    return [(ctx, (tp + d) % 8) for d in range(1, 8)]


def norm_scale(v):
    return lax.rsqrt(jnp.mean(v * v, axis=-1, keepdims=True) + NORM_EPSILON)


def norm_back(v, gain, grad):
    r = norm_scale(v)
    pulled = grad * gain
    inner = jnp.mean(pulled * v, axis=-1, keepdims=True)
    grad_v = r * pulled - v * (r * r * r) * inner
    return grad_v, jnp.sum(grad * v * r, axis=0, keepdims=True)


def dot(a, b):
    return jnp.dot(a, b, preferred_element_type=F32)


def dot_nt(a, b):
    return lax.dot_general(a, b, (((1,), (1,)), ((), ())), preferred_element_type=F32)


def dot_tn(a, b):
    return lax.dot_general(a, b, (((0,), (0,)), ((), ())), preferred_element_type=F32)


def two_terms(a):
    high = a.astype(BF)
    return high, (a - high.astype(F32)).astype(BF)


def dot_ones(a, ones):
    high, low = two_terms(a)
    return dot(high, ones) + dot(low, ones)


def lanes(k, size):
    return pl.ds(pl.multiple_of(k * size, 128), size)


def split_out(dst, row, full, first):
    for k in range(full.shape[1] // 128):
        at = ((first + k) // 4, (first + k) % 4) if len(dst.shape) == 4 else (first + k,)
        dst[(*at, slice(row, row + full.shape[0]))] = full[:, 128 * k : 128 * (k + 1)].astype(BF)


def eights(dst, row, full):
    for j in range(16):
        for k in range(0, full.shape[1] // 128, 2):
            two = [
                full[8 * j : 8 * j + 8, 128 * (k + i) : 128 * (k + i + 1)] for i in (0, 1)
            ]
            at = (j // 4, j % 4) if len(dst.shape) == 4 else (j,)
            dst[(*at, slice(row + 8 * k, row + 8 * k + 16))] = jnp.concatenate(two, axis=0).astype(
                BF
            )


def chooser(tp):
    r, c = iota((1024, 128), 0), iota((1024, 128), 1)
    return jnp.where((r // 128 == c // 16) & (r % 128 == tp * 16 + c % 16), 1.0, 0.0).astype(BF)


def fetch(src, dst, sem):
    cp = pltpu.make_async_copy(src, dst, sem)
    cp.start()
    return cp


def soft_plus(values):
    return jnp.maximum(values, 0.0) + jnp.log1p(jnp.exp(-jnp.abs(values)))


def pick(t, lengths, values):
    one = lengths[0]
    two = one + lengths[1]
    three = two + lengths[2]
    return jnp.where(
        t >= three,
        values[3],
        jnp.where(t >= two, values[2], jnp.where(t >= one, values[1], values[0])),
    )


def doc_start(t, lengths):
    one = lengths[0]
    two = one + lengths[1]
    return pick(t, lengths, (0, one, two, two + lengths[2]))


def iota(shape, axis):
    return lax.broadcasted_iota(jnp.int32, shape, axis)


def expander(heads):
    shape = (128, heads * MHEAD)
    return (iota(shape, 1) // MHEAD == iota(shape, 0)).astype(F32).astype(BF)


def collector(heads):
    shape = (heads * MHEAD, 128)
    return (iota(shape, 0) // MHEAD == iota(shape, 1)).astype(F32).astype(BF)


def spread(per_head, heads):
    return dot_ones(per_head, expander(heads))


def head_sums(flat):
    return dot_ones(flat, collector(flat.shape[1] // MHEAD))


def one_head(pair, h):
    return jnp.where(iota(pair.shape, 1) // MHEAD == h % 2, pair, jnp.zeros_like(pair))


def running_sum(dst, src, rows, later):
    high, low = two_terms(src[...])
    t, s = iota((rows, rows), 0), iota((rows, rows), 1)
    tri = jnp.where((s >= t) if later else (s <= t), 1.0, 0.0).astype(BF)
    dst[...] = dot(tri, high) + dot(tri, low)


def fades(i, base, lengths):
    wide = (i + 1) * 128
    t = base + i * 128 + iota((128, 128), 0)
    start = doc_start(t, lengths)[:, 0:1]
    shape = (128, wide)
    s = base + iota(shape, 1)
    return (s <= base + i * 128 + iota(shape, 0)) & (s >= start)


FAR = -1e9


def doc_of(t, lengths):
    one = lengths[0]
    two = one + lengths[1]
    return (
        (t >= one).astype(jnp.int32)
        + (t >= two).astype(jnp.int32)
        + (t >= two + lengths[2]).astype(jnp.int32)
    )


def marked_keys(keys, base, lengths):
    shape = keys.shape
    mark = jnp.where(doc_of(base + iota(shape, 0), lengths) == iota(shape, 1), 1.0, 0.0)
    return jnp.concatenate([keys, mark.astype(BF)], axis=1)


def marked_queries(queries, base, lengths):
    shape = queries.shape
    row = iota(shape, 0)
    own = doc_of(base + iota(shape, 1), lengths) == row
    return jnp.concatenate([queries, jnp.where(own | (row > 3), 0.0, FAR).astype(BF)], axis=0)


def attend(scale, ctx, lengths, q, kv, midway):
    block, size = kv.shape[2], q.shape[0]
    queries = marked_queries(q[...].T, ctx * block, lengths)
    factor = scale * LOG2E

    def step(blocks, carry, diagonal):
        top, total, acc = carry
        parts = []
        for i in blocks:
            keys = kv[i // 4, i % 4, :, :HD]
            s = dot(marked_keys(keys, i * block, lengths), queries) * factor
            if diagonal:
                s = jnp.where(iota(s.shape, 0) <= iota(s.shape, 1), s, FAR)
            parts.append(s)
        new = top
        for s in parts:
            new = jnp.maximum(new, jnp.max(s, axis=0, keepdims=True))
        fade = jnp.exp2(top - new)
        total = total * fade
        acc = acc * fade
        for i, s in zip(blocks, parts):
            p = jnp.exp2(s - new)
            total = total + jnp.sum(p, axis=0, keepdims=True)
            acc = acc + dot_tn(kv[i // 4, i % 4, :, HD:], p.astype(BF))
        return new, total, acc

    carry = (
        jnp.full((1, size), 2 * FAR, F32),
        jnp.zeros((1, size), F32),
        jnp.zeros((HD, size), F32),
    )
    some = ctx // UNROLL

    def several(i, k):
        return step([UNROLL * i + n for n in range(UNROLL)], k, False)

    carry = lax.fori_loop(0, some // 2, several, carry)
    midway()
    carry = lax.fori_loop(some // 2, some, several, carry)
    carry = lax.fori_loop(UNROLL * some, ctx, lambda i, k: step([i], k, False), carry)
    top, total, acc = step([ctx], carry, True)
    return acc / total, top + jnp.log(total) * LOG2E


def attend_back(scale, ctx, lengths, q, kv, lse, low, grad_attn, dkv, after):
    block, size = kv.shape[2], q.shape[0]
    queries_t, queries = marked_queries(q[...].T, ctx * block, lengths), q[...]
    og = grad_attn[...]
    og_t = og.T
    factor = scale * LOG2E

    def step(blocks, acc, diagonal):
        for i in blocks:
            keys = kv[i // 4, i % 4, :, :HD]
            s = dot(marked_keys(keys, i * block, lengths), queries_t) * factor - lse
            if diagonal:
                s = jnp.where(iota(s.shape, 0) <= iota(s.shape, 1), s, FAR)
            p = jnp.exp2(s)
            dp = dot(kv[i // 4, i % 4, :, HD:], og_t)
            ds = (p * (dp - low)).astype(BF)
            dkv[i // 4, i % 4, :, :HD] = (dot(ds, queries) * scale).astype(BF)
            dkv[i // 4, i % 4, :, HD:] = dot(p.astype(BF), og).astype(BF)
            acc = acc + dot_tn(keys, ds)
        return acc

    acc = step([ctx], jnp.zeros((HD, size), F32), True)
    for k in range(4):
        last = jnp.clip(ctx, 4 * k, 4 * k + 4)
        acc = lax.fori_loop(4 * k, last, lambda i, t: step([i], t, False), acc)
        after(k)
    return acc * scale


def mlp_kernel(
    part,
    gain,
    b_out_far,
    a_gu_far,
    b_gu_far,
    a_dn_far,
    b_dn_far,
    mask_far,
    merged_far,
    hidden_far,
    w_gu_far,
    w_down_far,
    out_grad_far,
    low_out,
    grad_mixer_far,
    grad_low_gu,
    resid,
    grad_resid,
    gain_part,
    early_sum,
    rest_far,
    late_far,
    normed_mine,
    grad_mine,
    mixer_mine,
    b_out,
    a_gu,
    b_gu,
    a_dn,
    b_dn,
    mask,
    merged,
    far,
    source,
    w_gu,
    w_down,
    shared,
    shared_two,
    part_two,
    grad_act,
    low_dn_grad,
    low_gu,
    act,
    grad_gu,
    turned,
    picks,
    early,
    rest,
    late_part,
    out_grad,
    loads,
    *scratch,
):
    place = tp_place()
    tp = place[1]
    on_ctx = ctx_place()
    peers = tp_peers(*place) + line_peers(*on_ctx)
    greet(peers)
    bring = [
        fetch(src, dst, far.at[k])
        for k, (src, dst) in enumerate(
            (
                (b_out_far, b_out),
                (a_gu_far, a_gu),
                (b_gu_far, b_gu),
                (a_dn_far, a_dn),
                (b_dn_far, b_dn),
                (mask_far, mask),
                (merged_far, merged),
            )
        )
    ]
    share, model = resid.shape
    hidden = w_down.shape[0]
    rows = out_grad.shape[0]
    each = 128 // share
    rows_mine = pl.ds(pl.multiple_of(tp * share, share), share)
    get_source = fetch(hidden_far.at[rows_mine], source, loads.at[0])
    get_grad = fetch(out_grad_far, out_grad, loads.at[7])
    get_down = fetch(w_down_far, w_down, loads.at[1])
    get_gu = fetch(w_gu_far, w_gu, loads.at[2])
    bufs, sems, more, sems_two = scratch[:7], scratch[7:11], scratch[11:18], scratch[18:22]
    wide_bufs = scratch[22:]
    met(peers)
    first = reduce_start(part, bufs, place)
    second = reduce_middle(part, bufs, place, first)

    def span_of(i):
        return pl.ds(pl.multiple_of(i * 128, 128), 128)

    for cp in bring:
        cp.wait()
    get_grad.wait()
    get_down.wait()

    low_dn_grad[...] = (dot_nt(out_grad[...], b_dn[...]) * mask[...]).astype(BF)
    grad_act[...] = (dot_nt(out_grad[...], w_down[...]) + dot_nt(low_dn_grad[...], a_dn[...])).astype(
        BF
    )
    reduce_relay(part, bufs, place, first, second)
    get_source.wait()
    total = reduce_end(part, bufs, place, first, second)
    low = total[:, model:].astype(BF)
    residual = source[...].astype(F32) + total[:, :model] + dot(low, b_out[...])
    resid[...] = residual
    shared[tp, :, :model] = (residual * norm_scale(residual) * gain[1:2]).astype(BF)
    shared[tp, :, model:] = low
    started = share_start(shared, sems, place)
    get_gu.wait()

    def both_ways(*some):
        def rows_at(ref):
            return jnp.concatenate([ref[span_of(i)] for i in some], axis=0)

        def put(ref, value):
            for k, i in enumerate(some):
                ref[span_of(i)] = value[128 * k : 128 * (k + 1)]

        block = jnp.concatenate(
            [shared[pl.ds(i * each, each)].reshape(128, -1) for i in some], axis=0
        )
        n = block[:, :model]
        put(low_out, block[:, model:])
        low = (dot(n, a_gu[...]) * rows_at(mask)).astype(BF)
        put(low_gu, low)
        h = (dot(n, w_gu[...]) + dot(low, b_gu[...])).astype(BF).astype(F32)
        gate, up = h[:, :hidden], h[:, hidden:]
        sig = jax.nn.sigmoid(gate)
        put(act, (gate * sig * up).astype(BF))
        pulled = rows_at(grad_act).astype(F32)
        grad = jnp.concatenate(
            [pulled * up * sig * (1.0 + gate * (1.0 - sig)), pulled * (gate * sig)], axis=1
        ).astype(BF)
        put(grad_gu, grad)
        full = dot_nt(grad, w_gu[...]).astype(BF)
        low = dot_nt(grad, b_gu[...]).astype(BF)
        for n_th, i in enumerate(some):
            for k in range(each):
                part_of = slice(n_th * 128 + k * share, n_th * 128 + (k + 1) * share)
                part_two[i * each + k, :, :model] = full[part_of]
                part_two[i * each + k, :, model:] = low[part_of]

    chip = chips(place)
    started[2].wait_recv()
    both_ways(chip[3])
    third = reduce_pass(part_two, more, place, 3)
    passed = [share_pass(shared, sems, place, started, k) for k in (0, 1)]
    passed[1].wait_recv()
    passed[0].wait_recv()
    both_ways(chip[1], chip[2])
    pass_one = reduce_pass(part_two, more, place, 1)
    pass_two = reduce_pass(part_two, more, place, 2)
    passed.append(share_pass(shared, sems, place, started, 2))
    send_two = reduce_send(part_two, more, place, pass_two, 2)
    passed[2].wait_recv()
    both_ways(chip[0])
    pass_none = reduce_pass(part_two, more, place, 0)
    turned[...] = grad_gu[...].T
    wide = grad_gu.shape[1]
    send_none = reduce_send(part_two, more, place, pass_none, 0)

    def weights(j, carry):
        some = shared[:, :, lanes(j, 256)].reshape(rows, 256)
        split_out(early, 0, dot(turned[...], some), 2 * j)
        return carry

    lax.fori_loop(0, 8, weights, 0)
    eights(early, wide, dot_tn(low_gu[...], grad_gu[...]))
    first_w = scatter_start(early, wide_bufs, on_ctx, True)
    send_one = reduce_send(part_two, more, place, pass_one, 1, send_none)
    turned[0:hidden] = act[...].T

    def weights_two(j, carry):
        split_out(rest, 0, dot(turned[0:hidden], out_grad[:, lanes(j, 512)]), 4 * j)
        return carry

    lax.fori_loop(0, 4, weights_two, 0)
    total = reduce_end(
        part_two, more, place, [pass_none, pass_one, pass_two, third], [send_none, send_one, send_two]
    )
    low = (total[:, model:] * mask[rows_mine]).astype(BF)
    grad = total[:, :model] + dot_nt(low, a_gu[...])
    grad_v, grad_gain = norm_back(resid[...], gain[1:2], grad)
    grad_r = out_grad[rows_mine].astype(F32) + grad_v
    grad_resid[...] = grad_r
    gain_part[...] = grad_gain
    shared_two[tp, :, :model] = grad_r.astype(BF)
    shared_two[tp, :, model:] = low
    for cp in started + passed:
        cp.wait_send()
    started = share_start(shared_two, sems_two, place)
    eights(rest, 2 * hidden, dot_tn(low_dn_grad[...], act[...]))
    picks[...] = chooser(tp)
    half = model // 2
    for k in range(2):
        cols = slice(half * k, half * (k + 1))
        to = slice(128 * k, 128 * (k + 1))
        normed_mine[:, to] = dot(shared[:, :, cols].reshape(rows, half), picks[...]).astype(BF)
        grad_mine[:, to] = dot(out_grad[:, cols], picks[...]).astype(BF)
    def forward_rest(i, carry):
        at = pl.ds(pl.multiple_of(i * 256, 256), 256)
        a = act[at]
        full = dot(a, w_down[...]).astype(BF)
        low = (dot(a, a_dn[...]) * mask[at]).astype(BF)
        for k in range(2 * each):
            late_part[i * 2 * each + k, :, :model] = full[k * share : (k + 1) * share]
            late_part[i * 2 * each + k, :, model:] = low[k * share : (k + 1) * share]
        return carry

    lax.fori_loop(0, rows // 256, forward_rest, 0)
    stores = [fetch(late_part, late_far, loads.at[6])]
    scatter_relay(early, wide_bufs, on_ctx, first_w)
    passed = [share_pass(shared_two, sems_two, place, started, k) for k in (0, 1)]
    passed.append(share_pass(shared_two, sems_two, place, started, 2))
    turned[hidden:] = merged[...].T
    second_w = scatter_middle(early, early_sum, wide_bufs, on_ctx, first_w)
    share_end(shared_two, sems_two, place, started, passed)
    for k in range(8):
        to = pl.ds(k * share, share)
        grad_low_gu[to] = shared_two[k, :, model:]
        stores.append(
            fetch(shared_two.at[k, :, pl.ds(0, model)], grad_mixer_far.at[to], loads.at[8 + k])
        )
    for k in range(2):
        cols = slice(half * k, half * (k + 1))
        some = shared_two[:, :, cols].reshape(rows, half)
        mixer_mine[:, 128 * k : 128 * (k + 1)] = dot(some, picks[...]).astype(BF)

    def weights_three(j, carry):
        some = shared_two[:, :, lanes(j, 512)].reshape(rows, 512)
        split_out(rest, hidden, dot(turned[hidden:], some), 4 * j)
        return carry

    lax.fori_loop(0, 4, weights_three, 0)
    stores.append(fetch(rest, rest_far, loads.at[5]))
    scatter_end(early, early_sum, wide_bufs, first_w, second_w)
    for cp in stores:
        cp.wait()


def mlp_exchange(
    part, gain, b_out, a_gu, b_gu, a_dn, b_dn, mask, merged, hidden_in, w_gu, w_down, out_grad
):
    _, share, wide = part.shape
    rows, model = out_grad.shape
    hidden = w_down.shape[0]
    rank = a_gu.shape[1]
    return call(
        mlp_kernel,
        [
            ((rows, rank), BF),
            ((rows, model), BF),
            ((rows, rank), BF),
            ((share, model), F32),
            ((share, model), F32),
            ((1, model), F32),
            ((2 * hidden + 64, 128), F32),
            ((4, 4, 2 * hidden + 32, 128), BF),
            (part.shape, BF),
            ((rows, 256), BF),
            ((rows, 256), BF),
            ((rows, 256), BF),
        ],
        [part, gain, b_out, a_gu, b_gu, a_dn, b_dn, mask, merged, hidden_in, w_gu, w_down, out_grad],
        [
            pltpu.VMEM(b_out.shape, b_out.dtype),
            pltpu.VMEM(a_gu.shape, a_gu.dtype),
            pltpu.VMEM(b_gu.shape, b_gu.dtype),
            pltpu.VMEM(a_dn.shape, a_dn.dtype),
            pltpu.VMEM(b_dn.shape, b_dn.dtype),
            pltpu.VMEM(mask.shape, mask.dtype),
            pltpu.VMEM(merged.shape, merged.dtype),
            DMA((7,)),
            pltpu.VMEM((share, model), BF),
            pltpu.VMEM(w_gu.shape, BF),
            pltpu.VMEM(w_down.shape, BF),
            pltpu.VMEM(part.shape, BF),
            pltpu.VMEM(part.shape, BF),
            pltpu.VMEM(part.shape, BF),
            pltpu.VMEM((rows, hidden), BF),
            pltpu.VMEM((rows, rank), BF),
            pltpu.VMEM((rows, rank), BF),
            pltpu.VMEM((rows, hidden), BF),
            pltpu.VMEM((rows, 2 * hidden), BF),
            pltpu.VMEM((2 * hidden, rows), BF),
            pltpu.VMEM((1024, 128), BF),
            pltpu.VMEM((4, 4, 2 * hidden + 64, 128), BF),
            pltpu.VMEM((4, 4, 2 * hidden + 32, 128), BF),
            pltpu.VMEM(part.shape, BF),
            pltpu.VMEM(out_grad.shape, BF),
            DMA((16,)),
            *reduce_bufs(share, wide),
            *share_sems(),
            *reduce_bufs(share, wide),
            *share_sems(),
            *scatter_bufs(2 * hidden + 64, 128),
        ],
        2,
        "mlp_exchange",
        [VM, VM, HB, HB, HB, HB, HB, HB, HB, HB, HB, HB, HB],
        [VM, HB] + [VM] * 5 + [HB] * 2 + [VM] * 3,
    )


def ctx_place():
    ctx = lax.axis_index("ctx")
    return ctx, lax.axis_index("tp"), ctx // 4, ctx % 4


def spot(h, fast, slow):
    return slow * 4 + fast if h == 0 else fast * 4 + slow


def scatter_bufs(rows, width):
    most = max(rows - rows // 32 * 16, rows // 32 * 16)
    return [
        pltpu.VMEM((2, 3, most, width), BF),
        pltpu.VMEM((2, 3, 4, most, width), BF),
        pltpu.VMEM((2, 3, most, width), BF),
        pltpu.VMEM((2, 4, most, width), BF),
        *pair(2, 3, 4),
        *pair(2, 3),
    ]


def spans_of(rows):
    half = rows // 32 * 16
    return ((0, half), (half, rows - half))


def block_of(ref, h, fast, slow):
    return ref.at[slow, fast] if h == 0 else ref.at[fast, slow]


def block_of(ref, h, fast, slow):
    return ref.at[slow, fast] if h == 0 else ref.at[fast, slow]


def line_of(ref, h, fast):
    return ref.at[:, fast] if h == 0 else ref.at[fast]


def ways(place, h):
    ctx, tp, y, x = place
    fast, slow = ((x, y), (y, x))[h]
    c = tp % 2
    return (fast + 2) % 4, (fast + 1 + 2 * c) % 4, (fast + 3 - 2 * c) % 4, fast, slow


def scatter_send(part, bufs, place, h, k, j):
    ctx, tp = place[:2]
    two, way, other, fast, slow = ways(place, h)
    lo, size = spans_of(part.shape[2])[h]
    block, to = (two, way) if k == 0 else (other, other)
    line = (slow + j) % 4
    return send(
        block_of(part, h, block, line).at[pl.ds(lo, size)],
        bufs[1].at[h, k, line, pl.ds(0, size)],
        bufs[4:6],
        (h, k, j),
        (spot(h, to, slow), tp),
    )


def scatter_start(part, bufs, place, both=False):
    return {
        (h, k, j): scatter_send(part, bufs, place, h, k, j)
        for k in ((0, 2) if both else (0,))
        for j in OFFSETS + (0,)
        for h in (0, 1)
    }


def scatter_direct(part, bufs, place):
    ctx, tp = place[:2]
    first = {}
    for off in OFFSETS:
        for h in (0, 1):
            two, way, other, fast, slow = ways(place, h)
            lo, size = spans_of(part.shape[2])[h]
            to = (fast + off) % 4
            first[h, off - 1, 0] = send(
                line_of(part, h, to).at[:, pl.ds(lo, size)],
                bufs[1].at[h, off - 1, :, pl.ds(0, size)],
                bufs[4:6],
                (h, off - 1, 0),
                (spot(h, to, slow), tp),
            )
    return first


def scatter_relay(part, bufs, place, first, hold=False):
    r1, passing = bufs[1], bufs[3]
    ctx, tp = place[:2]
    for j in OFFSETS + (0,):
        for h in (0, 1):
            two, way, other, fast, slow = ways(place, h)
            lo, size = spans_of(part.shape[2])[h]
            line = (slow + j) % 4
            span = pl.ds(0, size)
            first[h, 0, j].wait_recv()
            mine = block_of(part, h, way, line)[pl.ds(lo, size)].astype(F32)
            passing[h, line, span] = (mine + r1[h, 0, line, span].astype(F32)).astype(BF)
            first[h, 1, j] = send(
                passing.at[h, line, span],
                r1.at[h, 1, line, span],
                bufs[4:6],
                (h, 1, j),
                (spot(h, way, slow), tp),
            )
            if not hold and (h, 2, j) not in first:
                first[h, 2, j] = scatter_send(part, bufs, place, h, 2, j)


def scatter_others(part, bufs, place, first):
    for j in OFFSETS + (0,):
        for h in (0, 1):
            first[h, 2, j] = scatter_send(part, bufs, place, h, 2, j)


def scatter_middle(part, out, bufs, place, first):
    mid, r1, r2 = bufs[:3]
    ctx, tp = place[:2]
    direct = len(first) == 6
    second = {}
    for j in OFFSETS + (0,):
        for h in (0, 1):
            two, way, other, fast, slow = ways(place, h)
            lo, size = spans_of(part.shape[2])[h]
            line = (slow + j) % 4
            span = pl.ds(0, size)
            came = (0, 1, 2) if direct else (2, 1)
            if not direct or j == OFFSETS[0]:
                for k in came:
                    first[h, k, 0 if direct else j].wait_recv()
            total = block_of(part, h, fast, line)[pl.ds(lo, size)].astype(F32)
            for k in came:
                total = total + r1[h, k, line, span].astype(F32)
            if j == 0:
                out[pl.ds(lo, size)] = total
            else:
                mid[h, j - 1, span] = total.astype(BF)
                second[h, j] = send(
                    mid.at[h, j - 1, span],
                    r2.at[h, j - 1, span],
                    bufs[6:8],
                    (h, j - 1),
                    (spot(h, fast, line), tp),
                )
    return second


def scatter_end(part, out, bufs, first, second):
    r2 = bufs[2]
    for h, (lo, size) in enumerate(spans_of(part.shape[2])):
        for j in OFFSETS:
            second[h, j].wait_recv()
        total = out[pl.ds(lo, size)]
        for j in (1, 2, 3):
            total = total + r2[h, j - 1, pl.ds(0, size)].astype(F32)
        out[pl.ds(lo, size)] = total
    for cp in list(first.values()) + list(second.values()):
        cp.wait_send()


def line_peers(ctx, tp, y, x):
    return [(y * 4 + (x + d) % 4, tp) for d in (1, 2, 3)] + [
        (((y + d) % 4) * 4 + x, tp) for d in (1, 2, 3)
    ]


def ctx_peers(ctx, tp):
    return [((ctx + d) % 16, tp) for d in range(1, 16)]


def swap_start(src, dst, sems, place):
    ctx, tp = place[:2]
    return [
        send(src.at[(ctx + d) % 16], dst.at[ctx], sems, d - 1, ((ctx + d) % 16, tp))
        for d in range(1, 16)
    ]


def pack_state(state, decay, msg):
    width = decay.shape[1]
    for j in range(16):
        msg[j, :, :width] = state[16 * j : 16 * (j + 1)].astype(BF)
    high = decay[0:1].astype(BF).astype(F32)
    low = decay[0:1] - high
    row = lax.broadcasted_iota(jnp.int32, (16, 128), 0)
    tile = jnp.zeros((16, 128), F32)
    count = width // 128
    for k in range(count):
        span = slice(128 * k, 128 * (k + 1))
        tile = jnp.where(row == k, high[:, span], tile)
        tile = jnp.where(row == count + k, low[:, span], tile)
    for j in range(16):
        msg[j, :, width:] = tile.astype(BF)


def prefix_into(order, got, ent):
    width = ent.shape[2]
    count = width // 128
    running = jnp.zeros(ent.shape[1:], F32)
    for i in order:
        ent[i] = running.astype(BF)
        tile = got[i, :, width:].astype(F32)
        decay = jnp.concatenate(
            [tile[k : k + 1] + tile[count + k : count + k + 1] for k in range(count)], axis=1
        )
        running = got[i, :, :width].astype(F32) + decay * running


def front_kernel(
    scale,
    lengths,
    ids,
    hidden,
    gain,
    w_dt,
    b_in,
    b_sh,
    head_params,
    a_out,
    a_in_far,
    a_sh_far,
    w_in_far,
    w_sh_far,
    w_out_far,
    normed_far,
    low_in_far,
    low_sh_far,
    z_out_far,
    xs_far,
    q_out_far,
    bc_far,
    mask_far,
    decay_far,
    dt_far,
    pre_far,
    total,
    entering,
    ssd,
    kv_far,
    part_out,
    attn_t,
    lse,
    merged,
    params,
    low_in,
    low_sh,
    z_out,
    xs,
    q_out,
    bc,
    mask,
    decay,
    dt,
    pre,
    gone,
    normed,
    gated,
    kv_all,
    maps,
    w_in,
    w_sh,
    w_out,
    kv,
    work,
    row_decay,
    row_dt,
    x_one,
    inner,
    state,
    msg,
    got,
    ent,
    loads,
    *sems,
):
    place = ctx_place()
    ctx, tp, y, x = place
    c = tp % 2
    mate = (ctx, tp + 1 - 2 * c)
    peers = ctx_peers(ctx, tp) + [mate]
    greet(peers)
    rank = mask.shape[1]
    get_maps = [
        fetch(a_sh_far, maps.at[:, pl.ds(0, rank)], loads.at[5]),
        fetch(a_in_far, maps.at[:, pl.ds(rank, rank)], loads.at[6]),
    ]
    get_sh = fetch(w_sh_far, w_sh, loads.at[0])
    get_in = fetch(w_in_far, w_in, loads.at[1])
    get_out = fetch(w_out_far, w_out, loads.at[2])
    rows = hidden.shape[0]
    width = ssd.shape[1]
    heads = width // MHEAD
    base = ctx * rows
    blocks = rows // 128

    def span_of(i):
        return pl.ds(pl.multiple_of(i * 128, 128), 128)

    def norms(i, carry):
        at = span_of(i)
        v = hidden[at].astype(F32)
        normed[at] = (v * norm_scale(v) * gain[0:1]).astype(BF)
        t = base + i * 128 + iota((128, 128), 0)
        chosen = pick(t, lengths, [ids[k] for k in range(4)])
        mask[at] = (chosen == iota((128, 128), 1) // RANK).astype(F32)
        return carry

    lax.fori_loop(0, blocks, norms, 0)
    params[...] = jnp.zeros(params.shape, F32)
    params[0:3, 0:heads] = head_params[...]
    maps[:, 2 * rank :] = w_dt[...].T
    for cp in get_maps:
        cp.wait()
    h = dot(normed[...], maps[...])
    low_sh[...] = (h[:, :rank] * mask[...]).astype(BF)
    low_in[...] = (h[:, rank : 2 * rank] * mask[...]).astype(BF)
    v = h[:, 2 * rank :] + params[0:1]
    pre[...] = v
    v = soft_plus(v)
    dt[...] = v
    work[...] = -v * jnp.exp(params[1:2])
    get_sh.wait()
    lo = 2 * STATE
    h = dot(normed[...], w_sh[...]) + dot(low_sh[...], b_sh[...])
    bc[...] = h[:, :lo].astype(BF)
    group = tp // (QHEADS // KVH)
    for k in range(2):
        one = h[:, lo + 2 * k * HD : lo + (2 * k + 1) * HD]
        two = h[:, lo + (2 * k + 1) * HD : lo + (2 * k + 2) * HD]
        kv[:, HD * k : HD * (k + 1)] = jnp.where(group == 0, one, two).astype(BF)
    met(peers)
    s_one, s_two, s_kv1, s_kv2, s_m1, s_m2 = [sems[2 * k : 2 * k + 2] for k in range(6)]
    half = rows // 2
    part = half // 2
    mine = pl.multiple_of(c * half, half)
    span = [pl.ds(pl.multiple_of(mine + h * part, part), part) for h in (0, 1)]
    kv1 = {}
    for off in OFFSETS:
        for h in (0, 1):
            fast, slow = ((x, y), (y, x))[h]
            kv1[h, off] = send(
                kv.at[span[h]],
                kv_all.at[y, x, span[h]],
                s_kv1,
                (h, off - 1),
                (spot(h, (fast + off) % 4, slow), tp),
            )
    kv_all[y, x] = kv[...]
    keep_normed = fetch(normed, normed_far, loads.at[3])
    get_in.wait()
    h = (dot(normed[...], w_in[...]) + dot(low_in[...], b_in[...])).astype(BF)
    z_out[...] = h[:, :width]
    xs[...] = h[:, width : 2 * width]
    q_out[...] = h[:, 2 * width :]
    kv2, to_mate = {}, []
    for off in OFFSETS:
        for h in (0, 1):
            kv1[h, off].wait_recv()

    def line(h, at):
        return (kv_all.at[at] if h == 0 else kv_all.at[:, at]).at[:, span[h]]

    for off in OFFSETS:
        for h in (0, 1):
            fast, slow = ((x, y), (y, x))[h]
            kv2[h, off] = send(
                line(h, slow),
                line(h, slow),
                s_kv2,
                (h, off - 1),
                (spot(h, fast, (slow + off) % 4), tp),
            )
    for off in OFFSETS:
        for h in (0, 1):
            fast, slow = ((x, y), (y, x))[h]
            block = block_of(kv_all, h, (fast + 4 - off) % 4, slow).at[span[h]]
            to_mate.append(send(block, block, s_m1, (h, off - 1), mate))
    running_sum(decay, work, rows, False)
    row_decay[...] = decay[...].T
    row_dt[...] = dt[...].T
    for h in range(heads):
        x_one[h] = one_head(xs[:, (h // 2) * 128 : (h // 2 + 1) * 128], h)
    final = decay[rows - 1 : rows]
    last_start = doc_start(base + rows - 1, lengths)
    tail = jnp.where(
        base + iota((rows, 128), 0) >= last_start, jnp.exp(final - decay[...]) * dt[...], 0.0
    )
    scaled = (spread(tail, heads) * xs[...].astype(F32)).astype(BF)
    state[...] = dot_tn(bc[:, :STATE], scaled)
    through = jnp.where(last_start < base, 1.0, 0.0)
    whole = jnp.broadcast_to(jnp.exp(final) * through, (8, 128))
    total[...] = spread(whole, heads)
    pack_state(state, total, msg)
    one = swap_start(msg, got, s_one, place)
    got[ctx] = msg[ctx]
    leave = [
        fetch(src, dst, gone.at[k])
        for k, (src, dst) in enumerate(
            (
                (low_in, low_in_far),
                (low_sh, low_sh_far),
                (z_out, z_out_far),
                (xs, xs_far),
                (q_out, q_out_far),
                (bc, bc_far),
                (mask, mask_far),
                (decay, decay_far),
                (dt, dt_far),
                (pre, pre_far),
            )
        )
    ]
    for i in range(blocks):
        at = pl.ds(i * 128, 128)
        wide = (i + 1) * 128
        seen = fades(i, base, lengths)
        inter = dot_nt(bc[at, STATE:], bc[0:wide, :STATE])
        for pair_at in range(heads // 2):
            acc = jnp.zeros((128, 128), F32)
            for h in (2 * pair_at, 2 * pair_at + 1):
                gap = decay[at, h : h + 1] - row_decay[h : h + 1, 0:wide]
                fade = jnp.exp(jnp.where(seen, gap, -1e30))
                mixing = (inter * fade * row_dt[h : h + 1, 0:wide]).astype(BF)
                acc = acc + dot(mixing, x_one[h, 0:wide])
            inner[at, pair_at * 128 : (pair_at + 1) * 128] = acc
    for off in OFFSETS:
        for h in (0, 1):
            fast, slow = ((x, y), (y, x))[h]
            kv2[h, off].wait_recv()
            came = line(h, (slow + 4 - off) % 4)
            to_mate.append(send(came, came, s_m2, (h, off - 1), mate))
    for cp in to_mate:
        cp.wait_recv()
    keep_kv = fetch(kv_all, kv_far, loads.at[4])
    two = []

    def midway():
        for cp in one:
            cp.wait_recv()
        prefix_into(range(16), got, ent)
        two.extend(swap_start(ent, entering, s_two, place))
        entering[ctx] = ent[ctx]

    out, lse[...] = attend(scale, ctx, lengths, q_out, kv_all, midway)
    attn_t[...] = out
    for cp in two:
        cp.wait_recv()
    arrived = entering[...].reshape(STATE, width)

    def finish(i, carry):
        at = span_of(i)
        t = base + i * 128 + iota((128, 128), 0)
        reach = jnp.where(doc_start(t, lengths) < base, jnp.exp(decay[at]), 0.0)
        cross = dot(bc[at, STATE:], arrived) * spread(reach, heads)
        skip = spread(jnp.broadcast_to(params[2:3], (8, 128)), heads)[0:1]
        out = inner[at] + cross + skip * xs[at].astype(F32)
        ssd[at] = out
        z = z_out[at].astype(F32)
        gated[at] = (out * (z * jax.nn.sigmoid(z))).astype(BF)
        return carry

    lax.fori_loop(0, blocks, finish, 0)
    merged[:, :width] = gated[...]
    merged[:, width:] = out.T.astype(BF)
    get_out.wait()
    model = w_out.shape[1]
    share = part_out.shape[1]
    low = (dot(merged[...], a_out[...]) * mask[...]).astype(BF)
    for k in range(8):
        part_out[k, :, model:] = low[k * share : (k + 1) * share]

    def mix(j, carry):
        cols = lanes(j, 512)
        full = dot(merged[...], w_out[:, cols]).astype(BF)
        for k in range(8):
            part_out[k, :, cols] = full[k * share : (k + 1) * share]
        return carry

    lax.fori_loop(0, model // 512, mix, 0)
    for cp in one + two + to_mate + list(kv1.values()) + list(kv2.values()):
        cp.wait_send()
    for cp in leave:
        cp.wait()
    keep_normed.wait()
    keep_kv.wait()


def front_exchange(scale, *args):
    hidden, a_in, w_in, w_sh, w_out = (args[k] for k in (2, 9, 11, 12, 13))
    rows, model = hidden.shape
    width = (w_in.shape[1] - HD) // 2
    heads = width // MHEAD
    rank = a_in.shape[1]
    return call(
        functools.partial(front_kernel, scale),
        [
            ((rows, model), BF),
            ((rows, rank), BF),
            ((rows, rank), BF),
            ((rows, width), BF),
            ((rows, width), BF),
            ((rows, HD), BF),
            ((rows, 2 * STATE), BF),
            ((rows, 128), F32),
            ((rows, 128), F32),
            ((rows, 128), F32),
            ((rows, 128), F32),
            ((8, width), F32),
            ((16, 16, width), BF),
            ((rows, width), F32),
            ((4, 4, rows, 2 * HD), BF),
            ((8, rows // 8, model + rank), BF),
            ((HD, rows), F32),
            ((1, rows), F32),
            ((rows, width + HD), BF),
            ((8, 128), F32),
        ],
        list(args),
        [
            pltpu.VMEM((rows, rank), BF),
            pltpu.VMEM((rows, rank), BF),
            pltpu.VMEM((rows, width), BF),
            pltpu.VMEM((rows, width), BF),
            pltpu.VMEM((rows, HD), BF),
            pltpu.VMEM((rows, 2 * STATE), BF),
            pltpu.VMEM((rows, 128), F32),
            pltpu.VMEM((rows, 128), F32),
            pltpu.VMEM((rows, 128), F32),
            pltpu.VMEM((rows, 128), F32),
            DMA((10,)),
            pltpu.VMEM((rows, model), BF),
            pltpu.VMEM((rows, width), BF),
            pltpu.VMEM((4, 4, rows, 2 * HD), BF),
            pltpu.VMEM((model, 2 * rank + 128), BF),
            pltpu.VMEM(w_in.shape, BF),
            pltpu.VMEM(w_sh.shape, BF),
            pltpu.VMEM(w_out.shape, BF),
            pltpu.VMEM((rows, 2 * HD), BF),
            pltpu.VMEM((rows, 128), F32),
            pltpu.VMEM((128, rows), F32),
            pltpu.VMEM((128, rows), F32),
            pltpu.VMEM((heads, rows, 128), BF),
            pltpu.VMEM((rows, width), F32),
            pltpu.VMEM((STATE, width), F32),
            pltpu.VMEM((16, 16, width + 128), BF),
            pltpu.VMEM((16, 16, width + 128), BF),
            pltpu.VMEM((16, 16, width), BF),
            DMA((7,)),
            *pair(15),
            *pair(15),
            *pair(2, 3),
            *pair(2, 3),
            *pair(2, 3),
            *pair(2, 3),
        ],
        4,
        "front_exchange",
        [SM, SM] + [VM] * 7 + [HB] * 5,
        [HB] * 11 + [VM] * 3 + [HB] + [VM] * 5,
    )


def back_kernel(
    scale,
    lengths,
    total,
    resid_far,
    b_dn_far,
    bc,
    xs_far,
    decay_far,
    dt_far,
    pre_far,
    params,
    entering_far,
    b_in_far,
    b_sh_far,
    w_dt_far,
    q_far,
    lse,
    attn_t_far,
    grad_mixer,
    w_out_far,
    b_out,
    a_out_far,
    mask,
    z_in_far,
    ssd_far,
    kv_far,
    part_far,
    w_in_far,
    w_sh_far,
    rest_far,
    gathered_far,
    part_out_far,
    two_out,
    grad_one_far,
    grad_head,
    grad_low,
    rest_sum,
    w_out,
    a_out,
    z_in,
    ssd,
    decay,
    attn_t,
    q,
    far_two,
    resid,
    b_dn,
    xs,
    dt,
    pre,
    entering,
    b_in,
    b_sh,
    w_dt,
    far,
    gathered,
    part_out,
    grad_one,
    kv,
    part,
    rest,
    dkv,
    grad_attn,
    grad_ssd,
    grad_z,
    hold,
    msg,
    got,
    ent,
    leaving,
    both,
    dkv_sum,
    kv_rows,
    grad_two,
    row_decay,
    row_dt,
    col_sum,
    row_sum,
    x_one,
    dy_one,
    dx,
    grad_b,
    grad_c,
    work,
    loads,
    *scratch,
):
    place = ctx_place()
    ctx, tp, y, x = place
    tp_at = tp_place()
    c = tp % 2
    mate = (ctx, tp + 1 - 2 * c)
    peers = ctx_peers(ctx, tp) + tp_peers(*tp_at)
    greet(peers)
    bring_two = [
        fetch(src, dst, far_two.at[k])
        for k, (src, dst) in enumerate(
            (
                (w_out_far, w_out),
                (a_out_far, a_out),
                (z_in_far, z_in),
                (ssd_far, ssd),
                (decay_far, decay),
                (attn_t_far, attn_t),
                (q_far, q),
            )
        )
    ]
    bring = [
        fetch(src, dst, far.at[k])
        for k, (src, dst) in enumerate(
            (
                (resid_far, resid),
                (b_dn_far, b_dn),
                (xs_far, xs),
                (dt_far, dt),
                (pre_far, pre),
                (entering_far, entering),
                (b_in_far, b_in),
                (b_sh_far, b_sh),
                (w_dt_far, w_dt),
            )
        )
    ]
    get_kv = fetch(kv_far, kv, loads.at[0])
    get_part = fetch(part_far, part, loads.at[1])
    get_rest = fetch(rest_far, rest, loads.at[2])
    rows, width = xs.shape
    heads = width // MHEAD
    base = ctx * rows
    blocks = rows // 128
    s_one, s_two, s_mate = scratch[0:2], scratch[2:4], scratch[4:6]
    bufs, more, sems, wide_bufs = scratch[6:14], scratch[14:21], scratch[21:25], scratch[25:]

    grad_low[...] = (dot_nt(grad_mixer[...], b_out[...]) * mask[...]).astype(BF)
    for cp in bring_two:
        cp.wait()
    grad = (dot_nt(grad_mixer[...], w_out[...]) + dot_nt(grad_low[...], a_out[...])).astype(BF)
    grad_attn[...] = grad[:, width:]
    gated = grad[:, :width].astype(F32)
    z = z_in[...].astype(F32)
    sig = jax.nn.sigmoid(z)
    grad_z[...] = (gated * ssd[...] * sig * (1.0 + z * (1.0 - sig))).astype(BF)
    gated = gated * (z * sig)
    grad_ssd[...] = gated
    reach = jnp.where(
        doc_start(base + iota((rows, 128), 0), lengths) < base, jnp.exp(decay[...]), 0.0
    )
    hold[...] = (spread(reach, heads) * gated).astype(BF)
    pack_state(dot_tn(bc[:, STATE:], hold[...]), total, msg)
    met(peers)
    one = swap_start(msg, got, s_one, place)
    got[ctx] = msg[ctx]
    get_part.wait()
    first_z = reduce_start(part, more, tp_at)
    get_rest.wait()
    first_w = scatter_start(rest, wide_bufs, place)
    low = jnp.sum(grad_attn[...].T.astype(F32) * attn_t[...], axis=0, keepdims=True)
    dkv[...] = jnp.zeros(dkv.shape, BF)
    get_kv.wait()
    second_z = reduce_middle(part, more, tp_at, first_z)

    half = rows // 2
    mine = pl.ds(pl.multiple_of(c * half, half), half)
    other = pl.ds(pl.multiple_of((1 - c) * half, half), half)
    cps = []

    def after(k):
        cps.append(send(dkv.at[k, :, other], both.at[k], s_mate, k, mate))
        if k == 1:
            scatter_relay(rest, wide_bufs, place, first_w, True)
            reduce_relay(part, more, tp_at, first_z, second_z)

    dq = attend_back(scale, ctx, lengths, q, kv, lse[...], low, grad_attn, dkv, after)
    grad_one[:, 2 * width : 2 * width + HD] = dq.T.astype(BF)
    for cp in bring:
        cp.wait()
    for cp in one:
        cp.wait_recv()
    prefix_into(range(15, -1, -1), got, ent)
    two = swap_start(ent, leaving, s_two, place)
    leaving[ctx] = ent[ctx]
    for k in range(4):
        cps[k].wait_recv()
        for i in range(4):
            both[k, i] = (dkv[k, i, mine].astype(F32) + both[k, i].astype(F32)).astype(BF)
    first = scatter_start(both, bufs, place)
    loaded = []
    for i in range(4):
        for k in range(4):
            rows_at = pl.ds(512 * i, 512)
            loaded.append(
                fetch(w_sh_far.at[rows_at, pl.ds(256 * k, 256)], kv.at[i, k], loads.at[4 + 4 * i + k])
            )
    for cp in cps:
        cp.wait_send()
    for i in range(4):
        for k in range(4):
            size = min(256, w_in_far.shape[1] - 256 * k)
            loaded.append(
                fetch(
                    w_in_far.at[pl.ds(512 * i, 512), pl.ds(256 * k, size)],
                    dkv.at[i, k, :, pl.ds(0, size)],
                    loads.at[20 + 4 * i + k],
                )
            )

    width_out = resid.shape[1]
    out = reduce_end(part, more, tp_at, first_z, second_z)
    low = out[:, width_out:].astype(BF)
    gathered[tp, :, :width_out] = (resid[...] + out[:, :width_out] + dot(low, b_dn[...])).astype(BF)
    gathered[tp, :, width_out:] = low
    started = share_start(gathered, sems, tp_at)
    row_decay[...] = decay[...].T
    row_dt[...] = dt[...].T
    col_sum[...] = jnp.zeros(col_sum.shape, F32)
    for h in range(heads):
        cols = slice((h // 2) * 128, (h // 2 + 1) * 128)
        x_one[h] = one_head(xs[:, cols], h)
        dy_one[h] = one_head(grad_ssd[:, cols], h).astype(BF)
    grad_b[...] = jnp.zeros(grad_b.shape, F32)
    dx[...] = jnp.zeros(dx.shape, F32)
    for i in range(blocks):
        at = pl.ds(i * 128, 128)
        wide = (i + 1) * 128
        seen = fades(i, base, lengths)
        inter = dot_nt(bc[at, STATE:], bc[0:wide, :STATE])
        d_inter = jnp.zeros((128, wide), F32)
        sums = jnp.zeros((128, 128), F32)
        for pair_at in range(heads // 2):
            cols = slice(pair_at * 128, (pair_at + 1) * 128)
            for h in (2 * pair_at, 2 * pair_at + 1):
                step = row_dt[h : h + 1, 0:wide]
                gap = decay[at, h : h + 1] - row_decay[h : h + 1, 0:wide]
                fade = jnp.exp(jnp.where(seen, gap, -1e30))
                d_mix = dot_nt(dy_one[h, at], x_one[h, 0:wide])
                faded = fade * step
                d_inter = d_inter + d_mix * faded
                weighted = d_mix * inter * fade
                col_sum[h : h + 1, 0:wide] += jnp.sum(weighted, axis=0, keepdims=True)
                sums = jnp.where(
                    iota((128, 128), 1) == h,
                    jnp.sum(weighted * step, axis=1, keepdims=True),
                    sums,
                )
                dx[0:wide, cols] += dot_tn((inter * faded).astype(BF), dy_one[h, at])
        if i == blocks // 2:
            scatter_relay(both, bufs, place, first)
            scatter_others(rest, wide_bufs, place, first_w)
        row_sum[at] = sums
        low = d_inter.astype(BF)
        grad_c[at] = dot(low, bc[0:wide, :STATE])
        grad_b[0:wide] += dot_tn(low, bc[at, STATE:])


    for cp in two:
        cp.wait_recv()
    after = leaving[...].reshape(STATE, width)
    before = entering[...].reshape(STATE, width)
    final = decay[rows - 1 : rows]
    last_start = doc_start(base + rows - 1, lengths)
    cols_sum = col_sum[...].T
    crossing = head_sums(
        jnp.broadcast_to(
            jnp.sum(after.astype(F32) * before.astype(F32), axis=0, keepdims=True) * total[0:1],
            (8, width),
        )
    )[0:1]
    rate = jnp.exp(params[1:2])
    skip = spread(jnp.broadcast_to(params[2:3], (8, 128)), heads)[0:1]
    d_last = crossing
    skips = jnp.zeros((1, 128), F32)
    for i in range(blocks):
        at = pl.ds(i * 128, 128)
        t = base + i * 128 + iota((128, 128), 0)
        steps = dt[at]
        tail = jnp.where(t >= last_start, jnp.exp(final - decay[at]), 0.0)
        reach = jnp.where(doc_start(t, lengths) < base, jnp.exp(decay[at]), 0.0)
        x_f = xs[at].astype(F32)
        gs = grad_ssd[at]
        came = dot(bc[at, :STATE], after)
        held = head_sums(came * x_f) * tail
        reached = spread(reach, heads) * gs
        d_cross = head_sums(dot(bc[at, STATE:], before) * reached)
        cols_at = cols_sum[i * 128 : (i + 1) * 128]
        work[at] = row_sum[at] - cols_at * steps + d_cross - held * steps
        row_sum[at] = cols_at + held
        d_last = d_last + jnp.sum(held * steps, axis=0, keepdims=True)
        tails = spread(tail * steps, heads)
        grad_one[at, :width] = grad_z[at]
        grad_one[at, width : 2 * width] = (dx[at] + tails * came + skip * gs).astype(BF)
        skips = skips + jnp.sum(head_sums(gs * x_f), axis=0, keepdims=True)
        grad_two[at, :STATE] = (grad_b[at] + dot_nt((tails * x_f).astype(BF), after)).astype(BF)
        grad_two[at, STATE : 2 * STATE] = (grad_c[at] + dot_nt(reached.astype(BF), before)).astype(
            BF
        )
    second = scatter_middle(both, dkv_sum, bufs, place, first)
    passed = [share_pass(gathered, sems, tp_at, started, k) for k in (0, 1)]
    running_sum(dx.at[:, 0:128], work, rows, True)
    d_log = dx[:, 0:128] + d_last
    grad_dt = (row_sum[...] - rate * d_log) * jax.nn.sigmoid(pre[...])
    grad_one[:, 2 * width + HD :] = grad_dt.astype(BF)
    grad_head[0:1] = jnp.sum(grad_dt, axis=0, keepdims=True)
    grad_head[1:2] = -jnp.sum(dt[...] * rate * d_log, axis=0, keepdims=True)
    grad_head[2:3] = skips
    grad_head[3:8] = jnp.zeros((5, 128), F32)
    for cp in loaded:
        cp.wait()
    narrow = 2 * width + HD

    model = resid.shape[1]
    rank = b_in.shape[0]
    share = resid.shape[0]

    def norm_part(j, carry):
        cols = lanes(j, 512)
        full = dot(grad_one[:, narrow:], w_dt[:, cols])
        for k in range(0, narrow, 256):
            size = min(256, narrow - k)
            full = full + dot_nt(grad_one[:, k : k + size], dkv[j, k // 256, :, 0:size])
        for k in range(2):
            full = full + dot_nt(grad_two[:, 256 * k : 256 * (k + 1)], kv[j, k])
        full = full.astype(BF)
        for k in range(8):
            part_out[k, :, cols] = full[k * share : (k + 1) * share]
        return carry

    lax.fori_loop(0, resid.shape[1] // 512, norm_part, 0)
    second_w = scatter_middle(rest, rest_sum, wide_bufs, place, first_w)
    stores = [fetch(grad_one, grad_one_far, loads.at[36])]
    share_end(gathered, sems, tp_at, started, passed)
    stores.append(fetch(gathered, gathered_far, loads.at[37]))
    low_one = dot_nt(grad_one[:, :narrow], b_in[...]).astype(BF)
    for k in range(8):
        part_out[k, :, model : model + rank] = low_one[k * share : (k + 1) * share]
    scatter_end(both, dkv_sum, bufs, first, second)
    kv_rows[...] = jnp.zeros(kv_rows.shape, F32)
    kv_rows[mine] = dkv_sum[...]
    group = tp // (QHEADS // KVH)
    for k in range(KVH):
        on = jnp.where(group == k, 1.0, 0.0)
        for v in range(2):
            lo = 2 * STATE + (v * KVH + k) * HD
            grad_two[:, lo : lo + HD] = (kv_rows[:, v * HD : (v + 1) * HD] * on).astype(BF)

    def finish(j):
        cols = pl.ds(512 * j, 512)
        full = dot_nt(grad_two[:, 512:768], kv[j, 2]) + dot_nt(grad_two[:, 768:], kv[j, 3])
        for k in range(8):
            some = part_out[k, :, cols].astype(F32) + full[k * share : (k + 1) * share]
            part_out[k, :, cols] = some.astype(BF)
        return fetch(part_out.at[:, :, cols], part_out_far.at[:, :, cols], loads.at[38 + j])

    low_two = dot_nt(grad_two[...], b_sh[...]).astype(BF)
    for k in range(8):
        part_out[k, :, model + rank :] = low_two[k * share : (k + 1) * share]
    cols = pl.ds(model, 2 * rank)
    stores.append(fetch(part_out.at[:, :, cols], part_out_far.at[:, :, cols], loads.at[42]))
    stores += [finish(j) for j in range(model // 512)]
    for k in range(8):
        two_out[k] = grad_two[:, k * 128 : (k + 1) * 128]
    scatter_end(rest, rest_sum, wide_bufs, first_w, second_w)
    for cp in one + two:
        cp.wait_send()
    for cp in stores:
        cp.wait()


def back_exchange(scale, *args):
    resid, bc, xs, b_in, kv, part, w_sh, rest = (args[k] for k in (2, 4, 5, 11, 24, 25, 27, 28))
    rows, width = xs.shape
    heads = width // MHEAD
    half = rows // 2
    cols = 2 * HD
    _, share, wide = part.shape
    model = resid.shape[1]
    rank = b_in.shape[0]
    return call(
        functools.partial(back_kernel, scale),
        [
            (part.shape, BF),
            ((8, share, model + 2 * rank), BF),
            ((8, rows, w_sh.shape[1] // 8), BF),
            ((rows, 2 * width + HD + 128), BF),
            ((8, 128), F32),
            ((rows, rank), BF),
            (rest.shape[2:], F32),
        ],
        list(args),
        [
            pltpu.VMEM(args[18].shape, args[18].dtype),
            pltpu.VMEM(args[20].shape, args[20].dtype),
            pltpu.VMEM(args[22].shape, args[22].dtype),
            pltpu.VMEM(args[23].shape, args[23].dtype),
            pltpu.VMEM(args[6].shape, args[6].dtype),
            pltpu.VMEM(args[16].shape, args[16].dtype),
            pltpu.VMEM(args[14].shape, args[14].dtype),
            DMA((7,)),
            pltpu.VMEM(args[2].shape, args[2].dtype),
            pltpu.VMEM(args[3].shape, args[3].dtype),
            pltpu.VMEM(args[5].shape, args[5].dtype),
            pltpu.VMEM(args[7].shape, args[7].dtype),
            pltpu.VMEM(args[8].shape, args[8].dtype),
            pltpu.VMEM(args[10].shape, args[10].dtype),
            pltpu.VMEM(args[11].shape, args[11].dtype),
            pltpu.VMEM(args[12].shape, args[12].dtype),
            pltpu.VMEM(args[13].shape, args[13].dtype),
            DMA((9,)),
            pltpu.VMEM(part.shape, BF),
            pltpu.VMEM((8, share, model + 2 * rank), BF),
            pltpu.VMEM((rows, 2 * width + HD + 128), BF),
            pltpu.VMEM(kv.shape, BF),
            pltpu.VMEM(part.shape, BF),
            pltpu.VMEM(rest.shape, BF),
            pltpu.VMEM(kv.shape, BF),
            pltpu.VMEM((rows, HD), BF),
            pltpu.VMEM((rows, width), F32),
            pltpu.VMEM((rows, width), BF),
            pltpu.VMEM((rows, width), BF),
            pltpu.VMEM((16, 16, width + 128), BF),
            pltpu.VMEM((16, 16, width + 128), BF),
            pltpu.VMEM((16, 16, width), BF),
            pltpu.VMEM((16, 16, width), BF),
            pltpu.VMEM((4, 4, half, cols), BF),
            pltpu.VMEM((half, cols), F32),
            pltpu.VMEM((rows, cols), F32),
            pltpu.VMEM((rows, w_sh.shape[1]), BF),
            pltpu.VMEM((128, rows), F32),
            pltpu.VMEM((128, rows), F32),
            pltpu.VMEM((128, rows), F32),
            pltpu.VMEM((rows, 128), F32),
            pltpu.VMEM((heads, rows, 128), BF),
            pltpu.VMEM((heads, rows, 128), BF),
            pltpu.VMEM((rows, width), F32),
            pltpu.VMEM((rows, STATE), F32),
            pltpu.VMEM((rows, STATE), F32),
            pltpu.VMEM((rows, 128), F32),
            DMA((43,)),
            *pair(15),
            *pair(15),
            *pair(4),
            *scatter_bufs(half, cols),
            *reduce_bufs(share, wide),
            *share_sems(),
            *scatter_bufs(rest.shape[2], 128),
        ],
        5,
        "back_exchange",
        [SM, VM, HB, HB, VM, HB, HB, HB, HB, VM, HB, HB, HB, HB, HB, VM, HB, VM, HB, VM, HB, VM, HB, HB, HB, HB, HB, HB, HB],
        [HB, HB, VM, HB, VM, VM, VM],
    )


def tail_kernel(
    part_far,
    part_two_far,
    gain,
    mask_far,
    gain_two,
    grad_resid_far,
    low_in,
    low_sh,
    grad_low_out,
    grad_low_gu,
    low_out,
    head,
    a_in_far,
    a_sh_far,
    hidden_far,
    normed_far,
    grad_one_far,
    merged_far,
    normed_mine_far,
    mixer_mine_far,
    grad_mine_far,
    rows_far,
    gathered_far,
    big_out,
    small_out,
    shared,
    head_out,
    part,
    part_two,
    a_in,
    a_sh,
    mask,
    grad_resid,
    far,
    gathered,
    source,
    normed_one,
    grad_one,
    merged,
    normed_mine,
    mixer_mine,
    grad_mine,
    low_dn,
    lows,
    turned,
    mine,
    big,
    small,
    two,
    two_t,
    picks,
    heads,
    loads,
    *scratch,
):
    place = ctx_place()
    tp_at = tp_place()
    ctx, tp = place[:2]
    peers = ctx_peers(ctx, tp) + all_tp(*tp_at)
    greet(peers)
    share, width = source.shape
    rank = a_in.shape[1]
    rows = normed_one.shape[0]
    rows_mine = pl.ds(pl.multiple_of(tp * share, share), share)
    get = [
        fetch(src, dst, loads.at[k])
        for k, (src, dst) in enumerate(
            (
                (grad_one_far, grad_one),
                (normed_far, normed_one),
                (merged_far, merged),
                (normed_mine_far, normed_mine),
                (mixer_mine_far, mixer_mine),
                (grad_mine_far, grad_mine),
                (rows_far.at[:, :, pl.ds(width, rank)], low_dn),
                (hidden_far.at[rows_mine], source),
            )
        )
    ]
    bring = [
        fetch(src, dst, far.at[k])
        for k, (src, dst) in enumerate(
            (
                (part_far, part),
                (part_two_far, part_two),
                (a_in_far, a_in),
                (a_sh_far, a_sh),
                (mask_far, mask),
                (grad_resid_far, grad_resid),
            )
        )
    ]
    bufs_z, more_z, sems, sems_l = scratch[:7], scratch[7:14], scratch[14:18], scratch[18:20]
    bufs, more, s_head, sems_s = scratch[20:28], scratch[28:36], scratch[36:38], scratch[38:]
    get[0].wait()
    turned[...] = grad_one[...].T
    deep = grad_one.shape[1]
    get[1].wait()

    def weights(j, carry):
        split_out(big, 0, dot(turned[...], normed_one[:, lanes(j, 256)]), 2 * j)
        return carry

    lax.fori_loop(0, 8, weights, 0)
    eights(big, deep, dot_tn(low_in[...], grad_one[...]))
    for k in range(2, 8):
        get[k].wait()
    row = deep + 64
    a_out_sum = dot_tn(merged[...], grad_low_out[...])
    for j in range(16):
        big[j // 4, j % 4, row : row + 32] = a_out_sum[j * 32 : (j + 1) * 32].astype(BF)
    for k, full in enumerate(
        (
            dot_tn(normed_mine[...], grad_low_gu[...]),
            dot_tn(mixer_mine[...], low_out[...]),
            dot_tn(grad_mine[...], low_dn[...].reshape(rows, rank)),
        )
    ):
        at = row + 32 + 16 * k
        big[:, :, at : at + 16] = full.astype(BF).reshape(4, 4, 16, rank)
    for cp in bring:
        cp.wait()
    met(peers)
    first_z = reduce_start(part, bufs_z, tp_at)
    first_two = reduce_start(part_two, more_z, tp_at)
    first = scatter_start(big, bufs, place)
    second_z = reduce_middle(part, bufs_z, tp_at, first_z)
    second_two = reduce_middle(part_two, more_z, tp_at, first_two)
    picks[...] = chooser(tp)
    half = width // 2
    for k in range(2):
        cols = slice(half * k, half * (k + 1))
        mine[:, 128 * k : 128 * (k + 1)] = dot(normed_one[:, cols], picks[...]).astype(BF)
    reduce_relay(part, bufs_z, tp_at, first_z, second_z)
    reduce_relay(part_two, more_z, tp_at, first_two, second_two)
    scatter_relay(big, bufs, place, first)
    total = reduce_end(part, bufs_z, tp_at, first_z, second_z)
    mask_mine = mask[rows_mine]
    low_one = (total[:, width : width + rank] * mask_mine).astype(BF)
    low_two = (total[:, width + rank :] * mask_mine).astype(BF)
    lows[tp, :, :rank] = low_one
    lows[tp, :, rank:] = low_two
    started_l = share_direct(lows, sems_l, tp_at)
    grad = total[:, :width] + dot_nt(low_one, a_in[...]) + dot_nt(low_two, a_sh[...])
    grad_v, grad_gain = norm_back(source[...].astype(F32), gain[0:1], grad)
    gathered[tp] = (grad_resid[...] + grad_v).astype(BF)
    started = share_start(gathered, sems, tp_at)
    two[...] = reduce_end(part_two, more_z, tp_at, first_two, second_two).astype(BF)
    b_sh_sum = dot_tn(low_sh[...], two[...])
    two_t[...] = two[...].T

    def shared_maps(j, carry):
        split_out(small, 0, dot(two_t[...], normed_one[:, lanes(j, 512)]), 4 * j)
        return carry

    lax.fori_loop(0, 4, shared_maps, 0)
    gain_rows = jnp.concatenate([grad_gain, gain_two[...], jnp.zeros((6, width), F32)], axis=0)
    for j in range(16):
        small[j // 4, j % 4, 144:160] = jnp.concatenate(
            [b_sh_sum[8 * j : 8 * j + 8], gain_rows[:, 128 * j : 128 * (j + 1)]], axis=0
        ).astype(BF)
    for cp in started_l:
        cp.wait_recv()
    full = dot_tn(mine[...], lows[...].reshape(rows, 2 * rank)).astype(BF)
    small[:, :, 160:176] = full[:, :rank].reshape(4, 4, 16, rank)
    small[:, :, 128:144] = full[:, rank:].reshape(4, 4, 16, rank)
    first_s = scatter_direct(small, more, place)
    sent = [send(head, heads.at[ctx], s_head, d - 1, ((ctx + d) % 16, tp)) for d in range(1, 16)]
    heads[ctx] = head[...]
    passed = [share_pass(gathered, sems, tp_at, started, k) for k in (0, 1)]
    second_s = scatter_middle(small, small_out, more, place, first_s)
    second = scatter_middle(big, big_out, bufs, place, first)
    passed.append(share_pass(gathered, sems, tp_at, started, 2))
    scatter_end(small, small_out, more, first_s, second_s)
    shared[tp] = small_out[pl.ds(0, shared.shape[1])].astype(BF)
    started_s = share_direct(shared, sems_s, tp_at)
    share_end(gathered, sems, tp_at, started, passed)
    store = fetch(gathered, gathered_far, loads.at[8])
    scatter_end(big, big_out, bufs, first, second)
    for cp in sent:
        cp.wait_recv()
    head_out[...] = jnp.sum(heads[...], axis=0)
    for cp in started_s:
        cp.wait_recv()
    for cp in sent + started_l + started_s:
        cp.wait_send()
    store.wait()


def tail_exchange(*args):
    part, part_two, grad_resid, head, grad_one, merged, rows_in = (
        args[k] for k in (0, 1, 5, 11, 16, 17, 21)
    )
    _, share, wide = part.shape
    _, rows, cols = part_two.shape
    width = grad_resid.shape[1]
    rank = (wide - width) // 2
    deep = grad_one.shape[1]
    return call(
        tail_kernel,
        [
            ((8, share, width), BF),
            ((deep + 144, 128), F32),
            ((176, 128), F32),
            ((8, 160, 128), BF),
            (head.shape, F32),
        ],
        list(args),
        [
            pltpu.VMEM(args[0].shape, args[0].dtype),
            pltpu.VMEM(args[1].shape, args[1].dtype),
            pltpu.VMEM(args[12].shape, args[12].dtype),
            pltpu.VMEM(args[13].shape, args[13].dtype),
            pltpu.VMEM(args[3].shape, args[3].dtype),
            pltpu.VMEM(args[5].shape, args[5].dtype),
            DMA((6,)),
            pltpu.VMEM((8, share, width), BF),
            pltpu.VMEM((share, width), BF),
            pltpu.VMEM((rows, width), BF),
            pltpu.VMEM(grad_one.shape, BF),
            pltpu.VMEM(merged.shape, BF),
            pltpu.VMEM((rows, 256), BF),
            pltpu.VMEM((rows, 256), BF),
            pltpu.VMEM((rows, 256), BF),
            pltpu.VMEM((8, share, rank), BF),
            pltpu.VMEM((8, share, 2 * rank), BF),
            pltpu.VMEM((deep, rows), BF),
            pltpu.VMEM((rows, 256), BF),
            pltpu.VMEM((4, 4, deep + 144, 128), BF),
            pltpu.VMEM((4, 4, 176, 128), BF),
            pltpu.VMEM((rows, 128), BF),
            pltpu.VMEM((128, rows), BF),
            pltpu.VMEM((1024, 128), BF),
            pltpu.VMEM((16,) + head.shape, F32),
            DMA((9,)),
            *reduce_bufs(share, wide),
            *reduce_bufs(rows, cols),
            *share_sems(),
            *pair(7),
            *scatter_bufs(deep + 144, 128),
            *scatter_bufs(176, 128),
            *pair(15),
            *pair(7),
        ],
        6,
        "tail_exchange",
        [HB, HB, VM, HB, VM, HB, VM, VM, VM, VM, VM, VM, HB, HB, HB, HB, HB, HB, HB, HB, HB, HB],
        [HB] + [VM] * 4,
    )


def finish_kernel(
    mixed_in,
    input_in,
    big,
    small,
    shared,
    head,
    early,
    rest_in,
    mixed,
    input_grad,
    gains,
    w_in,
    w_sh,
    w_dt,
    params,
    w_out,
    w_gu,
    w_down,
    a_in,
    b_in,
    a_sh,
    b_sh,
    a_out,
    b_out,
    a_gu,
    b_gu,
    a_dn,
    b_dn,
):
    width = mixed.shape[1]
    mixed[...] = mixed_in[0, :, :width].astype(F32)
    input_grad[...] = input_in[0, :, :width].astype(F32)

    @pl.when(pl.program_id(0) == 0)
    def rest():
        narrow = w_in.shape[2]
        hidden = w_down.shape[0]
        heads = w_dt.shape[0]
        w_in[:, 0, :] = big[0:narrow].T
        w_dt[...] = big[narrow : narrow + heads]
        deep = narrow + 128
        for k in range(narrow // 128):
            cols = slice(128 * k, 128 * (k + 1))
            b_in[:, 0, cols] = big[deep + 8 * k : deep + 8 * (k + 1)]
        params[...] = head[0:3, 0:heads]
        total = jnp.zeros((8, 128), F32)
        for k in range(8):
            block = shared[k].astype(F32)
            cols = slice(128 * k, 128 * (k + 1))
            w_sh[:, cols] = block[0:128].T
            a_sh[16 * k : 16 * (k + 1)] = block[128:144]
            b_sh[:, cols] = block[144:152]
            total = total + block[152:160]
        gains[...] = total[0:2]
        maps = deep + 64
        a_out[0] = big[maps : maps + 32]
        a_gu[...] = big[maps + 32 : maps + 48]
        b_out[...] = big[maps + 48 : maps + 64]
        b_dn[...] = big[maps + 64 : maps + 80]
        a_in[...] = small[160:176]
        w_gu[:, 0, :] = early[0:hidden].T
        w_gu[:, 1, :] = early[hidden : 2 * hidden].T
        w_down[...] = rest_in[0:hidden]
        w_out[0] = rest_in[hidden : 2 * hidden]
        for k in range(hidden // 128):
            cols = slice(128 * k, 128 * (k + 1))
            row = 2 * hidden + 8 * k
            b_gu[:, 0, cols] = early[row : row + 8]
            b_gu[:, 1, cols] = early[row + 32 : row + 40]
            a_dn[:, cols] = rest_in[row : row + 8]


def finish(mixed, input_grad, big, small, shared, head, early, rest, narrow, heads):
    _, rows, wide = mixed.shape
    _, _, wide_two = input_grad.shape
    width = wide - 128
    hidden = early.shape[0] // 2 // 128 * 128
    outs = [
        (8 * rows, width),
        (8 * rows, width),
        (2, 128),
        (128, 1, narrow),
        (128, 1024),
        (heads, 128),
        (3, heads),
        (1, hidden, 128),
        (128, 2, hidden),
        (hidden, 128),
        (16, 128),
        (8, 1, narrow),
        (128, 128),
        (8, 1024),
        (1, 32, 128),
        (16, 128),
        (16, 128),
        (8, 2, hidden),
        (8, hidden),
        (16, 128),
    ]

    def whole(shape):
        return pl.BlockSpec(shape, lambda i: (0,) * len(shape))

    done = pl.pallas_call(
        finish_kernel,
        grid=(8,),
        out_shape=[jax.ShapeDtypeStruct(s, F32) for s in outs],
        in_specs=[
            pl.BlockSpec((1, rows, wide), lambda i: (i, 0, 0)),
            pl.BlockSpec((1, rows, wide_two), lambda i: (i, 0, 0)),
        ]
        + [whole(a.shape) for a in (big, small, shared, head, early, rest)],
        out_specs=[pl.BlockSpec((rows, width), lambda i: (i, 0))] * 2 + [whole(s) for s in outs[2:]],
        compiler_params=pltpu.CompilerParams(vmem_limit_bytes=61 << 20),
        name="finish",
    )(mixed, input_grad, big, small, shared, head, early, rest)
    return tuple(a.T if k in (5, 15, 18, 19) else a for k, a in enumerate(done))


def body(
    hidden_in,
    norm_gains,
    w_in,
    w_shared,
    w_dt,
    head_params,
    w_out,
    w_gu,
    w_down,
    a_in,
    b_in,
    a_sh,
    b_sh,
    a_out,
    b_out,
    a_gu,
    b_gu,
    a_dn,
    b_dn,
    adapter_ids,
    doc_lengths,
    out_grad,
):
    rows, width = hidden_in.shape
    heads = head_params.shape[1]
    w_in = w_in.reshape(width, -1)
    b_in = b_in.reshape(b_in.shape[0], -1)
    w_out = w_out.reshape(-1, width)
    a_out = a_out.reshape(-1, a_out.shape[2])
    w_gu = w_gu.reshape(width, -1)
    b_gu = b_gu.reshape(b_gu.shape[0], -1)
    w_dt = jnp.pad(w_dt.T, ((0, 128 - heads), (0, 0)))
    scale = HD ** (-0.5)
    (
        normed_one,
        low_in,
        low_sh,
        z,
        xs,
        q,
        bc,
        mask,
        decay,
        dt,
        pre,
        total,
        entering,
        ssd,
        kv_all,
        mix_part,
        attn_t,
        lse,
        merged,
        params,
    ) = front_exchange(
        scale,
        doc_lengths,
        adapter_ids,
        hidden_in,
        norm_gains,
        w_dt,
        b_in,
        b_sh,
        head_params,
        a_out,
        a_in,
        a_sh,
        w_in,
        w_shared,
        w_out,
    )
    (
        low_out,
        grad_mixer,
        grad_low_gu,
        resid,
        grad_resid,
        gain_part_two,
        early,
        rest,
        mlp_part,
        normed_mine,
        grad_mine,
        mixer_mine,
    ) = mlp_exchange(
        mix_part,
        norm_gains,
        b_out,
        a_gu,
        b_gu,
        a_dn,
        b_dn,
        mask,
        merged,
        hidden_in,
        w_gu,
        w_down,
        out_grad,
    )
    mixed, part, two_blocks, grad_one, grad_head, grad_low_out, rest = back_exchange(
        scale,
        doc_lengths,
        total,
        resid,
        b_dn,
        bc,
        xs,
        decay,
        dt,
        pre,
        params,
        entering,
        b_in,
        b_sh,
        w_dt,
        q,
        lse,
        attn_t,
        grad_mixer,
        w_out,
        b_out,
        a_out,
        mask,
        z,
        ssd,
        kv_all,
        mlp_part,
        w_in,
        w_shared,
        rest,
    )
    input_grad, big, small, shared, head = tail_exchange(
        part,
        two_blocks,
        norm_gains,
        mask,
        gain_part_two,
        grad_resid,
        low_in,
        low_sh,
        grad_low_out,
        grad_low_gu,
        low_out,
        grad_head,
        a_in,
        a_sh,
        hidden_in,
        normed_one,
        grad_one,
        merged,
        normed_mine,
        mixer_mine,
        grad_mine,
        mixed,
    )
    return finish(mixed, input_grad, big, small, shared, head, early, rest, w_in.shape[1], heads)


def solution(mesh):
    placed = (
        P("ctx", None),
        P(),
        P(None, "tp", None),
        P(),
        P(None, "tp"),
        P(None, "tp"),
        P("tp", None, None),
        P(None, None, "tp"),
        P("tp", None),
        P(),
        P(None, "tp", None),
        P(),
        P(),
        P("tp", None, None),
        P(),
        P(),
        P(None, None, "tp"),
        P("tp", None),
        P(),
        P(),
        P(),
        P("ctx", None),
    )
    return jax.shard_map(
        body,
        mesh=mesh,
        in_specs=placed,
        out_specs=(
            P("ctx", None),
            P("ctx", None),
            P(None, "ctx"),
            P("ctx", "tp", None),
            P("ctx", None),
            P("ctx", "tp"),
            P(None, "tp"),
            P("tp", None, "ctx"),
            P("ctx", None, "tp"),
            P("tp", "ctx"),
            P(("ctx", "tp"), None),
            P("ctx", "tp", None),
            P("ctx", None),
            P("ctx", None),
            P("tp", "ctx", None),
            P(None, ("ctx", "tp")),
            P(("ctx", "tp"), None),
            P("ctx", None, "tp"),
            P("tp", "ctx"),
            P(None, ("ctx", "tp")),
        ),
        check_vma=False,
    )
```

```python
import functools

import jax
import jax.numpy as jnp
from jax import lax
from jax.experimental import pallas as pl
from jax.experimental.pallas import tpu as pltpu
from jax.sharding import PartitionSpec as P

MHEAD = 64
STATE = 256
QHEADS = 8
KVH = 2
HD = 128
RANK = 16
NORM_EPSILON = 1e-06

MESH = pl.DeviceIdType.MESH
VM = pl.BlockSpec(memory_space=pltpu.VMEM)
SM = pl.BlockSpec(memory_space=pltpu.SMEM)
HB = pl.BlockSpec(memory_space=pl.ANY)
BF = jnp.bfloat16
F32 = jnp.float32
DMA = pltpu.SemaphoreType.DMA
OFFSETS = (2, 1, 3)
LOG2E = 1.4426950408889634
UNROLL = 2


def call(kernel, outs, ins, scratch, cid, name, specs=None, out_specs=None):
    return pl.pallas_call(
        kernel,
        out_shape=[jax.ShapeDtypeStruct(s, d) for s, d in outs],
        in_specs=specs or [VM] * len(ins),
        out_specs=out_specs or [VM] * len(outs),
        scratch_shapes=scratch,
        compiler_params=pltpu.CompilerParams(
            collective_id=cid, has_side_effects=True, vmem_limit_bytes=61 << 20
        ),
        name=name,
    )(*ins)


def greet(peers):
    barrier = pltpu.get_barrier_semaphore()
    for peer in peers:
        pl.semaphore_signal(barrier, inc=1, device_id=peer, device_id_type=MESH)


def met(peers):
    pl.semaphore_wait(pltpu.get_barrier_semaphore(), len(peers))


def send(src, dst, sems, slot, peer):
    cp = pltpu.make_async_remote_copy(
        src_ref=src,
        dst_ref=dst,
        send_sem=sems[0].at[slot],
        recv_sem=sems[1].at[slot],
        device_id=peer,
        device_id_type=MESH,
    )
    cp.start()
    return cp


def pair(*shape):
    return [DMA(shape), DMA(shape)]


def tp_place():
    ctx = lax.axis_index("ctx")
    tp = lax.axis_index("tp")
    return ctx, tp, tp // 2, tp % 2


def tp_peers(ctx, tp, z, c):
    return [(ctx, ((z + d) % 4) * 2 + c) for d in (1, 2, 3)] + [(ctx, z * 2 + 1 - c)]


def reduce_bufs(rows, width):
    return [
        pltpu.VMEM((4, rows, width), BF),
        pltpu.VMEM((3, rows, width), BF),
        pltpu.VMEM((3, rows, width), BF),
        *pair(4),
        *pair(3),
    ]


def chips(place):
    ctx, tp, z, c = place
    return (z + 2) % 4, (z + 1 + 2 * c) % 4, (z + 3 - 2 * c) % 4, z


def reduce_pass(part, bufs, place, k):
    ctx, tp, z, c = place
    chip = chips(place)[(0, 2, 1, 3)[k]]
    return send(part.at[chip * 2 + 1 - c], bufs[0].at[k], bufs[3:5], k, (ctx, z * 2 + 1 - c))


def reduce_send(part, bufs, place, passed, k, relayed=None):
    sib, snd, rcv = bufs[:3]
    ctx, tp, z, c = place
    two, way, other, own = chips(place)
    passed.wait_recv()
    both = part[(two, way, other)[k] * 2 + c].astype(F32) + sib[k].astype(F32)
    if k == 1:
        relayed.wait_recv()
        both = both + rcv[0].astype(F32)
    snd[k] = both.astype(BF)
    to = other if k == 2 else way
    return send(snd.at[k], rcv.at[k], bufs[5:7], k, (ctx, to * 2 + c))


def reduce_start(part, bufs, place):
    return [reduce_pass(part, bufs, place, k) for k in range(4)]


def reduce_middle(part, bufs, place, first):
    return [reduce_send(part, bufs, place, first[0], 0), None, None]


def reduce_relay(part, bufs, place, first, second):
    second[1] = reduce_send(part, bufs, place, first[1], 1, second[0])
    second[2] = reduce_send(part, bufs, place, first[2], 2)


def reduce_end(part, bufs, place, first, second):
    sib, snd, rcv = bufs[:3]
    first[3].wait_recv()
    total = part[place[1]].astype(F32) + sib[3].astype(F32)
    for k in (2, 1):
        second[k].wait_recv()
        total = total + rcv[k].astype(F32)
    for cp in first + second:
        cp.wait_send()
    return total


def share_sems():
    return [*pair(3), *pair(4)]


def share_start(out, sems, place):
    ctx, tp, z, c = place
    two, way, other, own = chips(place)
    return [
        send(out.at[tp], out.at[tp], sems[:2], 0, (ctx, way * 2 + c)),
        send(out.at[tp], out.at[tp], sems[:2], 1, (ctx, other * 2 + c)),
        send(out.at[tp], out.at[tp], sems[2:], 0, (ctx, z * 2 + 1 - c)),
    ]


def share_pass(out, sems, place, started, k):
    ctx, tp, z, c = place
    two, way, other, own = chips(place)
    mate = (ctx, z * 2 + 1 - c)
    at = (other, way, two)[k] * 2 + c
    if k == 2:
        started[3].wait_recv()
    else:
        started[k].wait_recv()
    if k == 0:
        started.append(send(out.at[at], out.at[at], sems[:2], 2, (ctx, way * 2 + c)))
    passed = send(out.at[at], out.at[at], sems[2:], k + 1, mate)
    return passed


def share_end(out, sems, place, started, passed=()):
    passed = list(passed)
    passed += [share_pass(out, sems, place, started, k) for k in range(len(passed), 3)]
    started[2].wait_recv()
    for cp in passed:
        cp.wait_recv()
    for cp in started + passed:
        cp.wait_send()


def share_direct(out, sems, place):
    ctx, tp = place[:2]
    return [
        send(out.at[tp], out.at[tp], sems, d - 1, (ctx, (tp + d) % 8)) for d in range(1, 8)
    ]


def all_tp(ctx, tp, z, c):
    return [(ctx, (tp + d) % 8) for d in range(1, 8)]


def norm_scale(v):
    return lax.rsqrt(jnp.mean(v * v, axis=-1, keepdims=True) + NORM_EPSILON)


def norm_back(v, gain, grad):
    r = norm_scale(v)
    pulled = grad * gain
    inner = jnp.mean(pulled * v, axis=-1, keepdims=True)
    grad_v = r * pulled - v * (r * r * r) * inner
    return grad_v, jnp.sum(grad * v * r, axis=0, keepdims=True)


def dot(a, b):
    return jnp.dot(a, b, preferred_element_type=F32)


def dot_nt(a, b):
    return lax.dot_general(a, b, (((1,), (1,)), ((), ())), preferred_element_type=F32)


def dot_tn(a, b):
    return lax.dot_general(a, b, (((0,), (0,)), ((), ())), preferred_element_type=F32)


def two_terms(a):
    high = a.astype(BF)
    return high, (a - high.astype(F32)).astype(BF)


def dot_ones(a, ones):
    high, low = two_terms(a)
    return dot(high, ones) + dot(low, ones)


def lanes(k, size):
    return pl.ds(pl.multiple_of(k * size, 128), size)


def split_out(dst, row, full, first):
    for k in range(full.shape[1] // 128):
        at = ((first + k) // 4, (first + k) % 4) if len(dst.shape) == 4 else (first + k,)
        dst[(*at, slice(row, row + full.shape[0]))] = full[:, 128 * k : 128 * (k + 1)].astype(BF)


def eights(dst, row, full):
    for j in range(16):
        for k in range(0, full.shape[1] // 128, 2):
            two = [
                full[8 * j : 8 * j + 8, 128 * (k + i) : 128 * (k + i + 1)] for i in (0, 1)
            ]
            at = (j // 4, j % 4) if len(dst.shape) == 4 else (j,)
            dst[(*at, slice(row + 8 * k, row + 8 * k + 16))] = jnp.concatenate(two, axis=0).astype(
                BF
            )


def chooser(tp):
    r, c = iota((1024, 128), 0), iota((1024, 128), 1)
    return jnp.where((r // 128 == c // 16) & (r % 128 == tp * 16 + c % 16), 1.0, 0.0).astype(BF)


def fetch(src, dst, sem):
    cp = pltpu.make_async_copy(src, dst, sem)
    cp.start()
    return cp


def soft_plus(values):
    return jnp.maximum(values, 0.0) + jnp.log1p(jnp.exp(-jnp.abs(values)))


def pick(t, lengths, values):
    one = lengths[0]
    two = one + lengths[1]
    three = two + lengths[2]
    return jnp.where(
        t >= three,
        values[3],
        jnp.where(t >= two, values[2], jnp.where(t >= one, values[1], values[0])),
    )


def doc_start(t, lengths):
    one = lengths[0]
    two = one + lengths[1]
    return pick(t, lengths, (0, one, two, two + lengths[2]))


def iota(shape, axis):
    return lax.broadcasted_iota(jnp.int32, shape, axis)


def expander(heads):
    shape = (128, heads * MHEAD)
    return (iota(shape, 1) // MHEAD == iota(shape, 0)).astype(F32).astype(BF)


def collector(heads):
    shape = (heads * MHEAD, 128)
    return (iota(shape, 0) // MHEAD == iota(shape, 1)).astype(F32).astype(BF)


def spread(per_head, heads):
    return dot_ones(per_head, expander(heads))


def head_sums(flat):
    return dot_ones(flat, collector(flat.shape[1] // MHEAD))


def one_head(pair, h):
    return jnp.where(iota(pair.shape, 1) // MHEAD == h % 2, pair, jnp.zeros_like(pair))


def running_sum(dst, src, rows, later):
    high, low = two_terms(src[...])
    t, s = iota((rows, rows), 0), iota((rows, rows), 1)
    tri = jnp.where((s >= t) if later else (s <= t), 1.0, 0.0).astype(BF)
    dst[...] = dot(tri, high) + dot(tri, low)


def fades(i, base, lengths):
    wide = (i + 1) * 128
    t = base + i * 128 + iota((128, 128), 0)
    start = doc_start(t, lengths)[:, 0:1]
    shape = (128, wide)
    s = base + iota(shape, 1)
    return (s <= base + i * 128 + iota(shape, 0)) & (s >= start)


FAR = -1e9


def doc_of(t, lengths):
    one = lengths[0]
    two = one + lengths[1]
    return (
        (t >= one).astype(jnp.int32)
        + (t >= two).astype(jnp.int32)
        + (t >= two + lengths[2]).astype(jnp.int32)
    )


def marked_keys(keys, base, lengths):
    shape = keys.shape
    mark = jnp.where(doc_of(base + iota(shape, 0), lengths) == iota(shape, 1), 1.0, 0.0)
    return jnp.concatenate([keys, mark.astype(BF)], axis=1)


def marked_queries(queries, base, lengths):
    shape = queries.shape
    row = iota(shape, 0)
    own = doc_of(base + iota(shape, 1), lengths) == row
    return jnp.concatenate([queries, jnp.where(own | (row > 3), 0.0, FAR).astype(BF)], axis=0)


def attend(scale, ctx, lengths, q, kv, midway):
    block, size = kv.shape[2], q.shape[0]
    queries = marked_queries(q[...].T, ctx * block, lengths)
    factor = scale * LOG2E

    def step(blocks, carry, diagonal):
        top, total, acc = carry
        parts = []
        for i in blocks:
            keys = kv[i // 4, i % 4, :, :HD]
            s = dot(marked_keys(keys, i * block, lengths), queries) * factor
            if diagonal:
                s = jnp.where(iota(s.shape, 0) <= iota(s.shape, 1), s, FAR)
            parts.append(s)
        new = top
        for s in parts:
            new = jnp.maximum(new, jnp.max(s, axis=0, keepdims=True))
        fade = jnp.exp2(top - new)
        total = total * fade
        acc = acc * fade
        for i, s in zip(blocks, parts):
            p = jnp.exp2(s - new)
            total = total + jnp.sum(p, axis=0, keepdims=True)
            acc = acc + dot_tn(kv[i // 4, i % 4, :, HD:], p.astype(BF))
        return new, total, acc

    carry = (
        jnp.full((1, size), 2 * FAR, F32),
        jnp.zeros((1, size), F32),
        jnp.zeros((HD, size), F32),
    )
    some = ctx // UNROLL

    def several(i, k):
        return step([UNROLL * i + n for n in range(UNROLL)], k, False)

    carry = lax.fori_loop(0, some // 2, several, carry)
    midway()
    carry = lax.fori_loop(some // 2, some, several, carry)
    carry = lax.fori_loop(UNROLL * some, ctx, lambda i, k: step([i], k, False), carry)
    top, total, acc = step([ctx], carry, True)
    return acc / total, top + jnp.log(total) * LOG2E


def attend_back(scale, ctx, lengths, q, kv, lse, low, grad_attn, dkv, after):
    block, size = kv.shape[2], q.shape[0]
    queries_t, queries = marked_queries(q[...].T, ctx * block, lengths), q[...]
    og = grad_attn[...]
    og_t = og.T
    factor = scale * LOG2E

    def step(blocks, acc, diagonal):
        for i in blocks:
            keys = kv[i // 4, i % 4, :, :HD]
            s = dot(marked_keys(keys, i * block, lengths), queries_t) * factor - lse
            if diagonal:
                s = jnp.where(iota(s.shape, 0) <= iota(s.shape, 1), s, FAR)
            p = jnp.exp2(s)
            dp = dot(kv[i // 4, i % 4, :, HD:], og_t)
            ds = (p * (dp - low)).astype(BF)
            dkv[i // 4, i % 4, :, :HD] = (dot(ds, queries) * scale).astype(BF)
            dkv[i // 4, i % 4, :, HD:] = dot(p.astype(BF), og).astype(BF)
            acc = acc + dot_tn(keys, ds)
        return acc

    acc = step([ctx], jnp.zeros((HD, size), F32), True)
    for k in range(4):
        last = jnp.clip(ctx, 4 * k, 4 * k + 4)
        acc = lax.fori_loop(4 * k, last, lambda i, t: step([i], t, False), acc)
        after(k)
    return acc * scale


def mlp_kernel(
    part,
    gain,
    b_out_far,
    a_gu_far,
    b_gu_far,
    a_dn_far,
    b_dn_far,
    mask_far,
    merged_far,
    hidden_far,
    w_gu_far,
    w_down_far,
    out_grad_far,
    low_out,
    grad_mixer_far,
    grad_low_gu,
    resid,
    grad_resid,
    gain_part,
    early_sum,
    rest_far,
    late_far,
    normed_mine,
    grad_mine,
    mixer_mine,
    b_out,
    a_gu,
    b_gu,
    a_dn,
    b_dn,
    mask,
    merged,
    far,
    source,
    w_gu,
    w_down,
    shared,
    shared_two,
    part_two,
    grad_act,
    low_dn_grad,
    low_gu,
    act,
    grad_gu,
    turned,
    picks,
    early,
    rest,
    late_part,
    out_grad,
    loads,
    *scratch,
):
    place = tp_place()
    tp = place[1]
    on_ctx = ctx_place()
    peers = tp_peers(*place) + line_peers(*on_ctx)
    greet(peers)
    bring = [
        fetch(src, dst, far.at[k])
        for k, (src, dst) in enumerate(
            (
                (b_out_far, b_out),
                (a_gu_far, a_gu),
                (b_gu_far, b_gu),
                (a_dn_far, a_dn),
                (b_dn_far, b_dn),
                (mask_far, mask),
                (merged_far, merged),
            )
        )
    ]
    share, model = resid.shape
    hidden = w_down.shape[0]
    rows = out_grad.shape[0]
    each = 128 // share
    rows_mine = pl.ds(pl.multiple_of(tp * share, share), share)
    get_source = fetch(hidden_far.at[rows_mine], source, loads.at[0])
    get_grad = fetch(out_grad_far, out_grad, loads.at[7])
    get_down = fetch(w_down_far, w_down, loads.at[1])
    get_gu = fetch(w_gu_far, w_gu, loads.at[2])
    bufs, sems, more, sems_two = scratch[:7], scratch[7:11], scratch[11:18], scratch[18:22]
    wide_bufs = scratch[22:]
    met(peers)
    first = reduce_start(part, bufs, place)
    second = reduce_middle(part, bufs, place, first)

    def span_of(i):
        return pl.ds(pl.multiple_of(i * 128, 128), 128)

    for cp in bring:
        cp.wait()
    get_grad.wait()
    get_down.wait()

    low_dn_grad[...] = (dot_nt(out_grad[...], b_dn[...]) * mask[...]).astype(BF)
    grad_act[...] = (dot_nt(out_grad[...], w_down[...]) + dot_nt(low_dn_grad[...], a_dn[...])).astype(
        BF
    )
    reduce_relay(part, bufs, place, first, second)
    get_source.wait()
    total = reduce_end(part, bufs, place, first, second)
    low = total[:, model:].astype(BF)
    residual = source[...].astype(F32) + total[:, :model] + dot(low, b_out[...])
    resid[...] = residual
    shared[tp, :, :model] = (residual * norm_scale(residual) * gain[1:2]).astype(BF)
    shared[tp, :, model:] = low
    started = share_start(shared, sems, place)
    get_gu.wait()

    def both_ways(*some):
        def rows_at(ref):
            return jnp.concatenate([ref[span_of(i)] for i in some], axis=0)

        def put(ref, value):
            for k, i in enumerate(some):
                ref[span_of(i)] = value[128 * k : 128 * (k + 1)]

        block = jnp.concatenate(
            [shared[pl.ds(i * each, each)].reshape(128, -1) for i in some], axis=0
        )
        n = block[:, :model]
        put(low_out, block[:, model:])
        low = (dot(n, a_gu[...]) * rows_at(mask)).astype(BF)
        put(low_gu, low)
        h = (dot(n, w_gu[...]) + dot(low, b_gu[...])).astype(BF).astype(F32)
        gate, up = h[:, :hidden], h[:, hidden:]
        sig = jax.nn.sigmoid(gate)
        put(act, (gate * sig * up).astype(BF))
        pulled = rows_at(grad_act).astype(F32)
        grad = jnp.concatenate(
            [pulled * up * sig * (1.0 + gate * (1.0 - sig)), pulled * (gate * sig)], axis=1
        ).astype(BF)
        put(grad_gu, grad)
        full = dot_nt(grad, w_gu[...]).astype(BF)
        low = dot_nt(grad, b_gu[...]).astype(BF)
        for n_th, i in enumerate(some):
            for k in range(each):
                part_of = slice(n_th * 128 + k * share, n_th * 128 + (k + 1) * share)
                part_two[i * each + k, :, :model] = full[part_of]
                part_two[i * each + k, :, model:] = low[part_of]

    chip = chips(place)
    started[2].wait_recv()
    both_ways(chip[3])
    third = reduce_pass(part_two, more, place, 3)
    passed = [share_pass(shared, sems, place, started, k) for k in (0, 1)]
    passed[1].wait_recv()
    passed[0].wait_recv()
    both_ways(chip[1], chip[2])
    pass_one = reduce_pass(part_two, more, place, 1)
    pass_two = reduce_pass(part_two, more, place, 2)
    passed.append(share_pass(shared, sems, place, started, 2))
    send_two = reduce_send(part_two, more, place, pass_two, 2)
    passed[2].wait_recv()
    both_ways(chip[0])
    pass_none = reduce_pass(part_two, more, place, 0)
    wide = grad_gu.shape[1]
    send_none = reduce_send(part_two, more, place, pass_none, 0)
    turned[...] = grad_gu[...].T

    def weights(j, carry):
        for m in range(2):
            at = pl.ds(m * hidden, hidden)
            full = dot(turned[at], shared[:, :, lanes(j, 256)].reshape(rows, 256)).astype(BF)
            for k in range(2):
                early[j // 2, 2 * (j % 2) + k, at] = full[:, 128 * k : 128 * (k + 1)]
        return carry

    lax.fori_loop(0, 8, weights, 0)
    eights(early, wide, dot_tn(low_gu[...], grad_gu[...]))
    first_w = scatter_start(early, wide_bufs, on_ctx, True)
    send_one = reduce_send(part_two, more, place, pass_one, 1, send_none)
    turned[0:hidden] = act[...].T

    def weights_two(j, carry):
        split_out(rest, 0, dot(turned[0:hidden], out_grad[:, lanes(j, 512)]), 4 * j)
        return carry

    lax.fori_loop(0, 4, weights_two, 0)
    total = reduce_end(
        part_two, more, place, [pass_none, pass_one, pass_two, third], [send_none, send_one, send_two]
    )
    low = (total[:, model:] * mask[rows_mine]).astype(BF)
    grad = total[:, :model] + dot_nt(low, a_gu[...])
    grad_v, grad_gain = norm_back(resid[...], gain[1:2], grad)
    grad_r = out_grad[rows_mine].astype(F32) + grad_v
    grad_resid[...] = grad_r
    gain_part[...] = grad_gain
    shared_two[tp, :, :model] = grad_r.astype(BF)
    shared_two[tp, :, model:] = low
    for cp in started + passed:
        cp.wait_send()
    started = share_start(shared_two, sems_two, place)
    eights(rest, 2 * hidden, dot_tn(low_dn_grad[...], act[...]))
    picks[...] = chooser(tp)
    half = model // 2
    for k in range(2):
        cols = slice(half * k, half * (k + 1))
        to = slice(128 * k, 128 * (k + 1))
        normed_mine[:, to] = dot(shared[:, :, cols].reshape(rows, half), picks[...]).astype(BF)
        grad_mine[:, to] = dot(out_grad[:, cols], picks[...]).astype(BF)
    def forward_rest(i, carry):
        at = pl.ds(pl.multiple_of(i * 256, 256), 256)
        a = act[at]
        full = dot(a, w_down[...]).astype(BF)
        low = (dot(a, a_dn[...]) * mask[at]).astype(BF)
        for k in range(2 * each):
            late_part[i * 2 * each + k, :, :model] = full[k * share : (k + 1) * share]
            late_part[i * 2 * each + k, :, model:] = low[k * share : (k + 1) * share]
        return carry

    lax.fori_loop(0, rows // 256, forward_rest, 0)
    stores = [fetch(late_part, late_far, loads.at[6])]
    scatter_relay(early, wide_bufs, on_ctx, first_w)
    passed = [share_pass(shared_two, sems_two, place, started, k) for k in (0, 1)]
    passed.append(share_pass(shared_two, sems_two, place, started, 2))
    turned[hidden:] = merged[...].T
    second_w = scatter_middle(early, early_sum, wide_bufs, on_ctx, first_w)
    share_end(shared_two, sems_two, place, started, passed)
    for k in range(8):
        to = pl.ds(k * share, share)
        grad_low_gu[to] = shared_two[k, :, model:]
        stores.append(
            fetch(shared_two.at[k, :, pl.ds(0, model)], grad_mixer_far.at[to], loads.at[8 + k])
        )
    for k in range(2):
        cols = slice(half * k, half * (k + 1))
        some = shared_two[:, :, cols].reshape(rows, half)
        mixer_mine[:, 128 * k : 128 * (k + 1)] = dot(some, picks[...]).astype(BF)

    def weights_three(j, carry):
        some = shared_two[:, :, lanes(j, 512)].reshape(rows, 512)
        split_out(rest, hidden, dot(turned[hidden:], some), 4 * j)
        return carry

    lax.fori_loop(0, 4, weights_three, 0)
    stores.append(fetch(rest, rest_far, loads.at[5]))
    scatter_end(early, early_sum, wide_bufs, first_w, second_w)
    for cp in stores:
        cp.wait()


def mlp_exchange(
    part, gain, b_out, a_gu, b_gu, a_dn, b_dn, mask, merged, hidden_in, w_gu, w_down, out_grad
):
    _, share, wide = part.shape
    rows, model = out_grad.shape
    hidden = w_down.shape[0]
    rank = a_gu.shape[1]
    return call(
        mlp_kernel,
        [
            ((rows, rank), BF),
            ((rows, model), BF),
            ((rows, rank), BF),
            ((share, model), F32),
            ((share, model), F32),
            ((1, model), F32),
            ((2 * hidden + 64, 128), F32),
            ((4, 4, 2 * hidden + 32, 128), BF),
            (part.shape, BF),
            ((rows, 256), BF),
            ((rows, 256), BF),
            ((rows, 256), BF),
        ],
        [part, gain, b_out, a_gu, b_gu, a_dn, b_dn, mask, merged, hidden_in, w_gu, w_down, out_grad],
        [
            pltpu.VMEM(b_out.shape, b_out.dtype),
            pltpu.VMEM(a_gu.shape, a_gu.dtype),
            pltpu.VMEM(b_gu.shape, b_gu.dtype),
            pltpu.VMEM(a_dn.shape, a_dn.dtype),
            pltpu.VMEM(b_dn.shape, b_dn.dtype),
            pltpu.VMEM(mask.shape, mask.dtype),
            pltpu.VMEM(merged.shape, merged.dtype),
            DMA((7,)),
            pltpu.VMEM((share, model), BF),
            pltpu.VMEM(w_gu.shape, BF),
            pltpu.VMEM(w_down.shape, BF),
            pltpu.VMEM(part.shape, BF),
            pltpu.VMEM(part.shape, BF),
            pltpu.VMEM(part.shape, BF),
            pltpu.VMEM((rows, hidden), BF),
            pltpu.VMEM((rows, rank), BF),
            pltpu.VMEM((rows, rank), BF),
            pltpu.VMEM((rows, hidden), BF),
            pltpu.VMEM((rows, 2 * hidden), BF),
            pltpu.VMEM((2 * hidden, rows), BF),
            pltpu.VMEM((1024, 128), BF),
            pltpu.VMEM((4, 4, 2 * hidden + 64, 128), BF),
            pltpu.VMEM((4, 4, 2 * hidden + 32, 128), BF),
            pltpu.VMEM(part.shape, BF),
            pltpu.VMEM(out_grad.shape, BF),
            DMA((16,)),
            *reduce_bufs(share, wide),
            *share_sems(),
            *reduce_bufs(share, wide),
            *share_sems(),
            *scatter_bufs(2 * hidden + 64, 128),
        ],
        2,
        "mlp_exchange",
        [VM, VM, HB, HB, HB, HB, HB, HB, HB, HB, HB, HB, HB],
        [VM, HB] + [VM] * 5 + [HB] * 2 + [VM] * 3,
    )


def ctx_place():
    ctx = lax.axis_index("ctx")
    return ctx, lax.axis_index("tp"), ctx // 4, ctx % 4


def spot(h, fast, slow):
    return slow * 4 + fast if h == 0 else fast * 4 + slow


def scatter_bufs(rows, width):
    most = max(rows - rows // 32 * 16, rows // 32 * 16)
    return [
        pltpu.VMEM((2, 3, most, width), BF),
        pltpu.VMEM((2, 3, 4, most, width), BF),
        pltpu.VMEM((2, 3, most, width), BF),
        pltpu.VMEM((2, 4, most, width), BF),
        *pair(2, 3, 4),
        *pair(2, 3),
    ]


def spans_of(rows):
    half = rows // 32 * 16
    return ((0, half), (half, rows - half))


def block_of(ref, h, fast, slow):
    return ref.at[slow, fast] if h == 0 else ref.at[fast, slow]


def block_of(ref, h, fast, slow):
    return ref.at[slow, fast] if h == 0 else ref.at[fast, slow]


def line_of(ref, h, fast):
    return ref.at[:, fast] if h == 0 else ref.at[fast]


def ways(place, h):
    ctx, tp, y, x = place
    fast, slow = ((x, y), (y, x))[h]
    c = tp % 2
    return (fast + 2) % 4, (fast + 1 + 2 * c) % 4, (fast + 3 - 2 * c) % 4, fast, slow


def scatter_send(part, bufs, place, h, k, j):
    ctx, tp = place[:2]
    two, way, other, fast, slow = ways(place, h)
    lo, size = spans_of(part.shape[2])[h]
    block, to = (two, way) if k == 0 else (other, other)
    line = (slow + j) % 4
    return send(
        block_of(part, h, block, line).at[pl.ds(lo, size)],
        bufs[1].at[h, k, line, pl.ds(0, size)],
        bufs[4:6],
        (h, k, j),
        (spot(h, to, slow), tp),
    )


def scatter_start(part, bufs, place, both=False):
    return {
        (h, k, j): scatter_send(part, bufs, place, h, k, j)
        for k in ((0, 2) if both else (0,))
        for j in OFFSETS + (0,)
        for h in (0, 1)
    }


def scatter_direct(part, bufs, place):
    ctx, tp = place[:2]
    first = {}
    for off in OFFSETS:
        for h in (0, 1):
            two, way, other, fast, slow = ways(place, h)
            lo, size = spans_of(part.shape[2])[h]
            to = (fast + off) % 4
            first[h, off - 1, 0] = send(
                line_of(part, h, to).at[:, pl.ds(lo, size)],
                bufs[1].at[h, off - 1, :, pl.ds(0, size)],
                bufs[4:6],
                (h, off - 1, 0),
                (spot(h, to, slow), tp),
            )
    return first


def scatter_relay(part, bufs, place, first, hold=False):
    r1, passing = bufs[1], bufs[3]
    ctx, tp = place[:2]
    for j in OFFSETS + (0,):
        for h in (0, 1):
            two, way, other, fast, slow = ways(place, h)
            lo, size = spans_of(part.shape[2])[h]
            line = (slow + j) % 4
            span = pl.ds(0, size)
            first[h, 0, j].wait_recv()
            mine = block_of(part, h, way, line)[pl.ds(lo, size)].astype(F32)
            passing[h, line, span] = (mine + r1[h, 0, line, span].astype(F32)).astype(BF)
            first[h, 1, j] = send(
                passing.at[h, line, span],
                r1.at[h, 1, line, span],
                bufs[4:6],
                (h, 1, j),
                (spot(h, way, slow), tp),
            )
            if not hold and (h, 2, j) not in first:
                first[h, 2, j] = scatter_send(part, bufs, place, h, 2, j)


def scatter_others(part, bufs, place, first):
    for j in OFFSETS + (0,):
        for h in (0, 1):
            first[h, 2, j] = scatter_send(part, bufs, place, h, 2, j)


def scatter_middle(part, out, bufs, place, first):
    mid, r1, r2 = bufs[:3]
    ctx, tp = place[:2]
    direct = len(first) == 6
    second = {}
    for j in OFFSETS + (0,):
        for h in (0, 1):
            two, way, other, fast, slow = ways(place, h)
            lo, size = spans_of(part.shape[2])[h]
            line = (slow + j) % 4
            span = pl.ds(0, size)
            came = (0, 1, 2) if direct else (2, 1)
            if not direct or j == OFFSETS[0]:
                for k in came:
                    first[h, k, 0 if direct else j].wait_recv()
            total = block_of(part, h, fast, line)[pl.ds(lo, size)].astype(F32)
            for k in came:
                total = total + r1[h, k, line, span].astype(F32)
            if j == 0:
                out[pl.ds(lo, size)] = total
            else:
                mid[h, j - 1, span] = total.astype(BF)
                second[h, j] = send(
                    mid.at[h, j - 1, span],
                    r2.at[h, j - 1, span],
                    bufs[6:8],
                    (h, j - 1),
                    (spot(h, fast, line), tp),
                )
    return second


def scatter_end(part, out, bufs, first, second):
    r2 = bufs[2]
    for h, (lo, size) in enumerate(spans_of(part.shape[2])):
        for j in OFFSETS:
            second[h, j].wait_recv()
        total = out[pl.ds(lo, size)]
        for j in (1, 2, 3):
            total = total + r2[h, j - 1, pl.ds(0, size)].astype(F32)
        out[pl.ds(lo, size)] = total
    for cp in list(first.values()) + list(second.values()):
        cp.wait_send()


def line_peers(ctx, tp, y, x):
    return [(y * 4 + (x + d) % 4, tp) for d in (1, 2, 3)] + [
        (((y + d) % 4) * 4 + x, tp) for d in (1, 2, 3)
    ]


def ctx_peers(ctx, tp):
    return [((ctx + d) % 16, tp) for d in range(1, 16)]


def swap_start(src, dst, sems, place):
    ctx, tp = place[:2]
    return [
        send(src.at[(ctx + d) % 16], dst.at[ctx], sems, d - 1, ((ctx + d) % 16, tp))
        for d in range(1, 16)
    ]


def pack_state(state, decay, msg):
    width = decay.shape[1]
    for j in range(16):
        msg[j, :, :width] = state[16 * j : 16 * (j + 1)].astype(BF)
    high = decay[0:1].astype(BF).astype(F32)
    low = decay[0:1] - high
    row = lax.broadcasted_iota(jnp.int32, (16, 128), 0)
    tile = jnp.zeros((16, 128), F32)
    count = width // 128
    for k in range(count):
        span = slice(128 * k, 128 * (k + 1))
        tile = jnp.where(row == k, high[:, span], tile)
        tile = jnp.where(row == count + k, low[:, span], tile)
    for j in range(16):
        msg[j, :, width:] = tile.astype(BF)


def prefix_into(order, got, ent):
    width = ent.shape[2]
    count = width // 128
    running = jnp.zeros(ent.shape[1:], F32)
    for i in order:
        ent[i] = running.astype(BF)
        tile = got[i, :, width:].astype(F32)
        decay = jnp.concatenate(
            [tile[k : k + 1] + tile[count + k : count + k + 1] for k in range(count)], axis=1
        )
        running = got[i, :, :width].astype(F32) + decay * running


def front_kernel(
    scale,
    lengths,
    ids,
    hidden,
    gain,
    w_dt,
    b_in,
    b_sh,
    head_params,
    a_out,
    a_in_far,
    a_sh_far,
    w_in_far,
    w_sh_far,
    w_out_far,
    normed_far,
    low_in_far,
    low_sh_far,
    z_out_far,
    xs_far,
    q_out_far,
    bc_far,
    mask_far,
    decay_far,
    dt_far,
    pre_far,
    total,
    entering,
    ssd,
    kv_far,
    part_out,
    attn_t,
    lse,
    merged,
    params,
    low_in,
    low_sh,
    z_out,
    xs,
    q_out,
    bc,
    mask,
    decay,
    dt,
    pre,
    gone,
    normed,
    gated,
    kv_all,
    maps,
    w_in,
    w_sh,
    w_out,
    kv,
    work,
    row_decay,
    row_dt,
    x_one,
    inner,
    state,
    msg,
    got,
    ent,
    loads,
    *sems,
):
    place = ctx_place()
    ctx, tp, y, x = place
    c = tp % 2
    mate = (ctx, tp + 1 - 2 * c)
    peers = ctx_peers(ctx, tp) + [mate]
    greet(peers)
    rank = mask.shape[1]
    get_maps = [
        fetch(a_sh_far, maps.at[:, pl.ds(0, rank)], loads.at[5]),
        fetch(a_in_far, maps.at[:, pl.ds(rank, rank)], loads.at[6]),
    ]
    get_sh = fetch(w_sh_far, w_sh, loads.at[0])
    get_in = fetch(w_in_far, w_in, loads.at[1])
    get_out = fetch(w_out_far, w_out, loads.at[2])
    rows = hidden.shape[0]
    width = ssd.shape[1]
    heads = width // MHEAD
    base = ctx * rows
    blocks = rows // 128

    def span_of(i):
        return pl.ds(pl.multiple_of(i * 128, 128), 128)

    def norms(i, carry):
        at = span_of(i)
        v = hidden[at].astype(F32)
        normed[at] = (v * norm_scale(v) * gain[0:1]).astype(BF)
        t = base + i * 128 + iota((128, 128), 0)
        chosen = pick(t, lengths, [ids[k] for k in range(4)])
        mask[at] = (chosen == iota((128, 128), 1) // RANK).astype(F32)
        return carry

    lax.fori_loop(0, blocks, norms, 0)
    params[...] = jnp.zeros(params.shape, F32)
    params[0:3, 0:heads] = head_params[...]
    maps[:, 2 * rank :] = w_dt[...].T
    for cp in get_maps:
        cp.wait()
    h = dot(normed[...], maps[...])
    low_sh[...] = (h[:, :rank] * mask[...]).astype(BF)
    low_in[...] = (h[:, rank : 2 * rank] * mask[...]).astype(BF)
    v = h[:, 2 * rank :] + params[0:1]
    pre[...] = v
    v = soft_plus(v)
    dt[...] = v
    work[...] = -v * jnp.exp(params[1:2])
    get_sh.wait()
    lo = 2 * STATE
    h = dot(normed[...], w_sh[...]) + dot(low_sh[...], b_sh[...])
    bc[...] = h[:, :lo].astype(BF)
    group = tp // (QHEADS // KVH)
    for k in range(2):
        one = h[:, lo + 2 * k * HD : lo + (2 * k + 1) * HD]
        two = h[:, lo + (2 * k + 1) * HD : lo + (2 * k + 2) * HD]
        kv[:, HD * k : HD * (k + 1)] = jnp.where(group == 0, one, two).astype(BF)
    met(peers)
    s_one, s_two, s_kv1, s_kv2, s_m1, s_m2 = [sems[2 * k : 2 * k + 2] for k in range(6)]
    half = rows // 2
    part = half // 2
    mine = pl.multiple_of(c * half, half)
    span = [pl.ds(pl.multiple_of(mine + h * part, part), part) for h in (0, 1)]
    kv1 = {}
    for off in OFFSETS:
        for h in (0, 1):
            fast, slow = ((x, y), (y, x))[h]
            kv1[h, off] = send(
                kv.at[span[h]],
                kv_all.at[y, x, span[h]],
                s_kv1,
                (h, off - 1),
                (spot(h, (fast + off) % 4, slow), tp),
            )
    kv_all[y, x] = kv[...]
    keep_normed = fetch(normed, normed_far, loads.at[3])
    get_in.wait()
    h = (dot(normed[...], w_in[...]) + dot(low_in[...], b_in[...])).astype(BF)
    z_out[...] = h[:, :width]
    xs[...] = h[:, width : 2 * width]
    q_out[...] = h[:, 2 * width :]
    kv2, to_mate = {}, []
    for off in OFFSETS:
        for h in (0, 1):
            kv1[h, off].wait_recv()

    def line(h, at):
        return (kv_all.at[at] if h == 0 else kv_all.at[:, at]).at[:, span[h]]

    for off in OFFSETS:
        for h in (0, 1):
            fast, slow = ((x, y), (y, x))[h]
            kv2[h, off] = send(
                line(h, slow),
                line(h, slow),
                s_kv2,
                (h, off - 1),
                (spot(h, fast, (slow + off) % 4), tp),
            )
    for off in OFFSETS:
        for h in (0, 1):
            fast, slow = ((x, y), (y, x))[h]
            block = block_of(kv_all, h, (fast + 4 - off) % 4, slow).at[span[h]]
            to_mate.append(send(block, block, s_m1, (h, off - 1), mate))
    running_sum(decay, work, rows, False)
    row_decay[...] = decay[...].T
    row_dt[...] = dt[...].T
    for h in range(heads):
        x_one[h] = one_head(xs[:, (h // 2) * 128 : (h // 2 + 1) * 128], h)
    final = decay[rows - 1 : rows]
    last_start = doc_start(base + rows - 1, lengths)
    tail = jnp.where(
        base + iota((rows, 128), 0) >= last_start, jnp.exp(final - decay[...]) * dt[...], 0.0
    )
    scaled = (spread(tail, heads) * xs[...].astype(F32)).astype(BF)
    state[...] = dot_tn(bc[:, :STATE], scaled)
    through = jnp.where(last_start < base, 1.0, 0.0)
    whole = jnp.broadcast_to(jnp.exp(final) * through, (8, 128))
    total[...] = spread(whole, heads)
    pack_state(state, total, msg)
    one = swap_start(msg, got, s_one, place)
    got[ctx] = msg[ctx]
    leave = [
        fetch(src, dst, gone.at[k])
        for k, (src, dst) in enumerate(
            (
                (low_in, low_in_far),
                (low_sh, low_sh_far),
                (z_out, z_out_far),
                (xs, xs_far),
                (q_out, q_out_far),
                (bc, bc_far),
                (mask, mask_far),
                (decay, decay_far),
                (dt, dt_far),
                (pre, pre_far),
            )
        )
    ]
    for i in range(blocks):
        at = pl.ds(i * 128, 128)
        wide = (i + 1) * 128
        seen = fades(i, base, lengths)
        inter = dot_nt(bc[at, STATE:], bc[0:wide, :STATE])
        for pair_at in range(heads // 2):
            acc = jnp.zeros((128, 128), F32)
            for h in (2 * pair_at, 2 * pair_at + 1):
                gap = decay[at, h : h + 1] - row_decay[h : h + 1, 0:wide]
                fade = jnp.exp(jnp.where(seen, gap, -1e30))
                mixing = (inter * fade * row_dt[h : h + 1, 0:wide]).astype(BF)
                acc = acc + dot(mixing, x_one[h, 0:wide])
            inner[at, pair_at * 128 : (pair_at + 1) * 128] = acc
    for off in OFFSETS:
        for h in (0, 1):
            fast, slow = ((x, y), (y, x))[h]
            kv2[h, off].wait_recv()
            came = line(h, (slow + 4 - off) % 4)
            to_mate.append(send(came, came, s_m2, (h, off - 1), mate))
    for cp in to_mate:
        cp.wait_recv()
    keep_kv = fetch(kv_all, kv_far, loads.at[4])
    two = []

    def midway():
        for cp in one:
            cp.wait_recv()
        prefix_into(range(16), got, ent)
        two.extend(swap_start(ent, entering, s_two, place))
        entering[ctx] = ent[ctx]

    out, lse[...] = attend(scale, ctx, lengths, q_out, kv_all, midway)
    attn_t[...] = out
    for cp in two:
        cp.wait_recv()
    arrived = entering[...].reshape(STATE, width)

    def finish(i, carry):
        at = span_of(i)
        t = base + i * 128 + iota((128, 128), 0)
        reach = jnp.where(doc_start(t, lengths) < base, jnp.exp(decay[at]), 0.0)
        cross = dot(bc[at, STATE:], arrived) * spread(reach, heads)
        skip = spread(jnp.broadcast_to(params[2:3], (8, 128)), heads)[0:1]
        out = inner[at] + cross + skip * xs[at].astype(F32)
        ssd[at] = out
        z = z_out[at].astype(F32)
        gated[at] = (out * (z * jax.nn.sigmoid(z))).astype(BF)
        return carry

    lax.fori_loop(0, blocks, finish, 0)
    merged[:, :width] = gated[...]
    merged[:, width:] = out.T.astype(BF)
    get_out.wait()
    model = w_out.shape[1]
    share = part_out.shape[1]
    low = (dot(merged[...], a_out[...]) * mask[...]).astype(BF)
    for k in range(8):
        part_out[k, :, model:] = low[k * share : (k + 1) * share]

    def mix(j, carry):
        cols = lanes(j, 512)
        full = dot(merged[...], w_out[:, cols]).astype(BF)
        for k in range(8):
            part_out[k, :, cols] = full[k * share : (k + 1) * share]
        return carry

    lax.fori_loop(0, model // 512, mix, 0)
    for cp in one + two + to_mate + list(kv1.values()) + list(kv2.values()):
        cp.wait_send()
    for cp in leave:
        cp.wait()
    keep_normed.wait()
    keep_kv.wait()


def front_exchange(scale, *args):
    hidden, a_in, w_in, w_sh, w_out = (args[k] for k in (2, 9, 11, 12, 13))
    rows, model = hidden.shape
    width = (w_in.shape[1] - HD) // 2
    heads = width // MHEAD
    rank = a_in.shape[1]
    return call(
        functools.partial(front_kernel, scale),
        [
            ((rows, model), BF),
            ((rows, rank), BF),
            ((rows, rank), BF),
            ((rows, width), BF),
            ((rows, width), BF),
            ((rows, HD), BF),
            ((rows, 2 * STATE), BF),
            ((rows, 128), F32),
            ((rows, 128), F32),
            ((rows, 128), F32),
            ((rows, 128), F32),
            ((8, width), F32),
            ((16, 16, width), BF),
            ((rows, width), F32),
            ((4, 4, rows, 2 * HD), BF),
            ((8, rows // 8, model + rank), BF),
            ((HD, rows), F32),
            ((1, rows), F32),
            ((rows, width + HD), BF),
            ((8, 128), F32),
        ],
        list(args),
        [
            pltpu.VMEM((rows, rank), BF),
            pltpu.VMEM((rows, rank), BF),
            pltpu.VMEM((rows, width), BF),
            pltpu.VMEM((rows, width), BF),
            pltpu.VMEM((rows, HD), BF),
            pltpu.VMEM((rows, 2 * STATE), BF),
            pltpu.VMEM((rows, 128), F32),
            pltpu.VMEM((rows, 128), F32),
            pltpu.VMEM((rows, 128), F32),
            pltpu.VMEM((rows, 128), F32),
            DMA((10,)),
            pltpu.VMEM((rows, model), BF),
            pltpu.VMEM((rows, width), BF),
            pltpu.VMEM((4, 4, rows, 2 * HD), BF),
            pltpu.VMEM((model, 2 * rank + 128), BF),
            pltpu.VMEM(w_in.shape, BF),
            pltpu.VMEM(w_sh.shape, BF),
            pltpu.VMEM(w_out.shape, BF),
            pltpu.VMEM((rows, 2 * HD), BF),
            pltpu.VMEM((rows, 128), F32),
            pltpu.VMEM((128, rows), F32),
            pltpu.VMEM((128, rows), F32),
            pltpu.VMEM((heads, rows, 128), BF),
            pltpu.VMEM((rows, width), F32),
            pltpu.VMEM((STATE, width), F32),
            pltpu.VMEM((16, 16, width + 128), BF),
            pltpu.VMEM((16, 16, width + 128), BF),
            pltpu.VMEM((16, 16, width), BF),
            DMA((7,)),
            *pair(15),
            *pair(15),
            *pair(2, 3),
            *pair(2, 3),
            *pair(2, 3),
            *pair(2, 3),
        ],
        4,
        "front_exchange",
        [SM, SM] + [VM] * 7 + [HB] * 5,
        [HB] * 11 + [VM] * 3 + [HB] + [VM] * 5,
    )


def back_kernel(
    scale,
    lengths,
    total,
    resid_far,
    b_dn_far,
    bc,
    xs_far,
    decay_far,
    dt_far,
    pre_far,
    params,
    entering_far,
    b_in_far,
    b_sh_far,
    w_dt_far,
    q_far,
    lse,
    attn_t_far,
    grad_mixer,
    w_out_far,
    b_out,
    a_out_far,
    mask,
    z_in_far,
    ssd_far,
    kv_far,
    part_far,
    w_in_far,
    w_sh_far,
    rest_far,
    gathered_far,
    part_out_far,
    two_out_far,
    grad_one_far,
    grad_head,
    grad_low,
    rest_sum,
    w_out,
    a_out,
    z_in,
    ssd,
    decay,
    attn_t,
    q,
    far_two,
    resid,
    b_dn,
    xs,
    dt,
    pre,
    entering,
    b_in,
    b_sh,
    w_dt,
    far,
    gathered,
    part_out,
    grad_one,
    kv,
    part,
    rest,
    dkv,
    grad_attn,
    grad_ssd,
    grad_z,
    hold,
    msg,
    got,
    ent,
    leaving,
    both,
    dkv_sum,
    kv_rows,
    grad_two,
    row_decay,
    row_dt,
    col_sum,
    row_sum,
    x_one,
    dy_one,
    dx,
    grad_b,
    grad_c,
    work,
    loads,
    *scratch,
):
    place = ctx_place()
    ctx, tp, y, x = place
    tp_at = tp_place()
    c = tp % 2
    mate = (ctx, tp + 1 - 2 * c)
    peers = ctx_peers(ctx, tp) + tp_peers(*tp_at)
    greet(peers)
    bring_two = [
        fetch(src, dst, far_two.at[k])
        for k, (src, dst) in enumerate(
            (
                (w_out_far, w_out),
                (a_out_far, a_out),
                (z_in_far, z_in),
                (ssd_far, ssd),
                (decay_far, decay),
                (attn_t_far, attn_t),
                (q_far, q),
            )
        )
    ]
    bring = [
        fetch(src, dst, far.at[k])
        for k, (src, dst) in enumerate(
            (
                (resid_far, resid),
                (b_dn_far, b_dn),
                (xs_far, xs),
                (dt_far, dt),
                (pre_far, pre),
                (entering_far, entering),
                (b_in_far, b_in),
                (b_sh_far, b_sh),
                (w_dt_far, w_dt),
            )
        )
    ]
    get_kv = fetch(kv_far, kv, loads.at[0])
    get_part = fetch(part_far, part, loads.at[1])
    get_rest = fetch(rest_far, rest, loads.at[2])
    rows, width = xs.shape
    heads = width // MHEAD
    base = ctx * rows
    blocks = rows // 128
    s_one, s_two, s_mate = scratch[0:2], scratch[2:4], scratch[4:6]
    bufs, more, sems, wide_bufs = scratch[6:14], scratch[14:21], scratch[21:25], scratch[25:]

    grad_low[...] = (dot_nt(grad_mixer[...], b_out[...]) * mask[...]).astype(BF)
    for cp in bring_two:
        cp.wait()
    grad = (dot_nt(grad_mixer[...], w_out[...]) + dot_nt(grad_low[...], a_out[...])).astype(BF)
    grad_attn[...] = grad[:, width:]
    gated = grad[:, :width].astype(F32)
    z = z_in[...].astype(F32)
    sig = jax.nn.sigmoid(z)
    grad_z[...] = (gated * ssd[...] * sig * (1.0 + z * (1.0 - sig))).astype(BF)
    gated = gated * (z * sig)
    grad_ssd[...] = gated
    reach = jnp.where(
        doc_start(base + iota((rows, 128), 0), lengths) < base, jnp.exp(decay[...]), 0.0
    )
    hold[...] = (spread(reach, heads) * gated).astype(BF)
    pack_state(dot_tn(bc[:, STATE:], hold[...]), total, msg)
    met(peers)
    one = swap_start(msg, got, s_one, place)
    got[ctx] = msg[ctx]
    get_part.wait()
    first_z = reduce_start(part, more, tp_at)
    get_rest.wait()
    first_w = scatter_start(rest, wide_bufs, place)
    low = jnp.sum(grad_attn[...].T.astype(F32) * attn_t[...], axis=0, keepdims=True)
    dkv[...] = jnp.zeros(dkv.shape, BF)
    get_kv.wait()
    second_z = reduce_middle(part, more, tp_at, first_z)

    half = rows // 2
    mine = pl.ds(pl.multiple_of(c * half, half), half)
    other = pl.ds(pl.multiple_of((1 - c) * half, half), half)
    cps = []

    def after(k):
        cps.append(send(dkv.at[k, :, other], both.at[k], s_mate, k, mate))
        if k == 1:
            scatter_relay(rest, wide_bufs, place, first_w, True)
            reduce_relay(part, more, tp_at, first_z, second_z)

    dq = attend_back(scale, ctx, lengths, q, kv, lse[...], low, grad_attn, dkv, after)
    grad_one[:, 2 * width : 2 * width + HD] = dq.T.astype(BF)
    for cp in bring:
        cp.wait()
    for cp in one:
        cp.wait_recv()
    prefix_into(range(15, -1, -1), got, ent)
    two = swap_start(ent, leaving, s_two, place)
    leaving[ctx] = ent[ctx]
    for k in range(4):
        cps[k].wait_recv()
        for i in range(4):
            both[k, i] = (dkv[k, i, mine].astype(F32) + both[k, i].astype(F32)).astype(BF)
    first = scatter_start(both, bufs, place)
    loaded = []
    for i in range(4):
        for k in range(4):
            rows_at = pl.ds(512 * i, 512)
            loaded.append(
                fetch(w_sh_far.at[rows_at, pl.ds(256 * k, 256)], kv.at[i, k], loads.at[4 + 4 * i + k])
            )
    for cp in cps:
        cp.wait_send()
    for i in range(4):
        for k in range(4):
            size = min(256, w_in_far.shape[1] - 256 * k)
            loaded.append(
                fetch(
                    w_in_far.at[pl.ds(512 * i, 512), pl.ds(256 * k, size)],
                    dkv.at[i, k, :, pl.ds(0, size)],
                    loads.at[20 + 4 * i + k],
                )
            )

    width_out = resid.shape[1]
    out = reduce_end(part, more, tp_at, first_z, second_z)
    low = out[:, width_out:].astype(BF)
    gathered[tp, :, :width_out] = (resid[...] + out[:, :width_out] + dot(low, b_dn[...])).astype(BF)
    gathered[tp, :, width_out:] = low
    started = share_start(gathered, sems, tp_at)
    row_decay[...] = decay[...].T
    row_dt[...] = dt[...].T
    col_sum[...] = jnp.zeros(col_sum.shape, F32)
    for h in range(heads):
        cols = slice((h // 2) * 128, (h // 2 + 1) * 128)
        x_one[h] = one_head(xs[:, cols], h)
        dy_one[h] = one_head(grad_ssd[:, cols], h).astype(BF)
    grad_b[...] = jnp.zeros(grad_b.shape, F32)
    dx[...] = jnp.zeros(dx.shape, F32)
    for i in range(blocks):
        at = pl.ds(i * 128, 128)
        wide = (i + 1) * 128
        seen = fades(i, base, lengths)
        inter = dot_nt(bc[at, STATE:], bc[0:wide, :STATE])
        d_inter = jnp.zeros((128, wide), F32)
        sums = jnp.zeros((128, 128), F32)
        for pair_at in range(heads // 2):
            cols = slice(pair_at * 128, (pair_at + 1) * 128)
            for h in (2 * pair_at, 2 * pair_at + 1):
                step = row_dt[h : h + 1, 0:wide]
                gap = decay[at, h : h + 1] - row_decay[h : h + 1, 0:wide]
                fade = jnp.exp(jnp.where(seen, gap, -1e30))
                d_mix = dot_nt(dy_one[h, at], x_one[h, 0:wide])
                faded = fade * step
                d_inter = d_inter + d_mix * faded
                weighted = d_mix * inter * fade
                col_sum[h : h + 1, 0:wide] += jnp.sum(weighted, axis=0, keepdims=True)
                sums = jnp.where(
                    iota((128, 128), 1) == h,
                    jnp.sum(weighted * step, axis=1, keepdims=True),
                    sums,
                )
                dx[0:wide, cols] += dot_tn((inter * faded).astype(BF), dy_one[h, at])
        if i == blocks // 2:
            scatter_relay(both, bufs, place, first)
            scatter_others(rest, wide_bufs, place, first_w)
        row_sum[at] = sums
        low = d_inter.astype(BF)
        grad_c[at] = dot(low, bc[0:wide, :STATE])
        grad_b[0:wide] += dot_tn(low, bc[at, STATE:])


    for cp in two:
        cp.wait_recv()
    after = leaving[...].reshape(STATE, width)
    before = entering[...].reshape(STATE, width)
    final = decay[rows - 1 : rows]
    last_start = doc_start(base + rows - 1, lengths)
    cols_sum = col_sum[...].T
    crossing = head_sums(
        jnp.broadcast_to(
            jnp.sum(after.astype(F32) * before.astype(F32), axis=0, keepdims=True) * total[0:1],
            (8, width),
        )
    )[0:1]
    rate = jnp.exp(params[1:2])
    skip = spread(jnp.broadcast_to(params[2:3], (8, 128)), heads)[0:1]
    d_last = crossing
    skips = jnp.zeros((1, 128), F32)
    for i in range(blocks):
        at = pl.ds(i * 128, 128)
        t = base + i * 128 + iota((128, 128), 0)
        steps = dt[at]
        tail = jnp.where(t >= last_start, jnp.exp(final - decay[at]), 0.0)
        reach = jnp.where(doc_start(t, lengths) < base, jnp.exp(decay[at]), 0.0)
        x_f = xs[at].astype(F32)
        gs = grad_ssd[at]
        came = dot(bc[at, :STATE], after)
        held = head_sums(came * x_f) * tail
        reached = spread(reach, heads) * gs
        d_cross = head_sums(dot(bc[at, STATE:], before) * reached)
        cols_at = cols_sum[i * 128 : (i + 1) * 128]
        work[at] = row_sum[at] - cols_at * steps + d_cross - held * steps
        row_sum[at] = cols_at + held
        d_last = d_last + jnp.sum(held * steps, axis=0, keepdims=True)
        tails = spread(tail * steps, heads)
        grad_one[at, :width] = grad_z[at]
        grad_one[at, width : 2 * width] = (dx[at] + tails * came + skip * gs).astype(BF)
        skips = skips + jnp.sum(head_sums(gs * x_f), axis=0, keepdims=True)
        grad_two[at, :STATE] = (grad_b[at] + dot_nt((tails * x_f).astype(BF), after)).astype(BF)
        grad_two[at, STATE : 2 * STATE] = (grad_c[at] + dot_nt(reached.astype(BF), before)).astype(
            BF
        )
    second = scatter_middle(both, dkv_sum, bufs, place, first)
    passed = [share_pass(gathered, sems, tp_at, started, k) for k in (0, 1)]
    running_sum(dx.at[:, 0:128], work, rows, True)
    d_log = dx[:, 0:128] + d_last
    grad_dt = (row_sum[...] - rate * d_log) * jax.nn.sigmoid(pre[...])
    grad_one[:, 2 * width + HD :] = grad_dt.astype(BF)
    grad_head[0:1] = jnp.sum(grad_dt, axis=0, keepdims=True)
    grad_head[1:2] = -jnp.sum(dt[...] * rate * d_log, axis=0, keepdims=True)
    grad_head[2:3] = skips
    grad_head[3:8] = jnp.zeros((5, 128), F32)
    for cp in loaded:
        cp.wait()
    narrow = 2 * width + HD

    model = resid.shape[1]
    rank = b_in.shape[0]
    share = resid.shape[0]

    def norm_part(j, carry):
        cols = lanes(j, 512)
        full = dot(grad_one[:, narrow:], w_dt[:, cols])
        for k in range(0, narrow, 256):
            size = min(256, narrow - k)
            full = full + dot_nt(grad_one[:, k : k + size], dkv[j, k // 256, :, 0:size])
        for k in range(2):
            full = full + dot_nt(grad_two[:, 256 * k : 256 * (k + 1)], kv[j, k])
        full = full.astype(BF)
        for k in range(8):
            part_out[k, :, cols] = full[k * share : (k + 1) * share]
        return carry

    lax.fori_loop(0, resid.shape[1] // 512, norm_part, 0)
    second_w = scatter_middle(rest, rest_sum, wide_bufs, place, first_w)
    stores = [fetch(grad_one, grad_one_far, loads.at[36])]
    share_end(gathered, sems, tp_at, started, passed)
    stores.append(fetch(gathered, gathered_far, loads.at[37]))
    low_one = dot_nt(grad_one[:, :narrow], b_in[...]).astype(BF)
    for k in range(8):
        part_out[k, :, model : model + rank] = low_one[k * share : (k + 1) * share]
    scatter_end(both, dkv_sum, bufs, first, second)
    kv_rows[...] = jnp.zeros(kv_rows.shape, F32)
    kv_rows[mine] = dkv_sum[...]
    group = tp // (QHEADS // KVH)
    for k in range(KVH):
        on = jnp.where(group == k, 1.0, 0.0)
        for v in range(2):
            lo = 2 * STATE + (v * KVH + k) * HD
            grad_two[:, lo : lo + HD] = (kv_rows[:, v * HD : (v + 1) * HD] * on).astype(BF)

    def finish(j):
        cols = pl.ds(512 * j, 512)
        full = dot_nt(grad_two[:, 512:768], kv[j, 2]) + dot_nt(grad_two[:, 768:], kv[j, 3])
        for k in range(8):
            some = part_out[k, :, cols].astype(F32) + full[k * share : (k + 1) * share]
            part_out[k, :, cols] = some.astype(BF)
        return fetch(part_out.at[:, :, cols], part_out_far.at[:, :, cols], loads.at[38 + j])

    stores += [
        fetch(grad_two.at[:, pl.ds(128 * k, 128)], two_out_far.at[k], loads.at[43 + k])
        for k in range(8)
    ]
    low_two = dot_nt(grad_two[...], b_sh[...]).astype(BF)
    for k in range(8):
        part_out[k, :, model + rank :] = low_two[k * share : (k + 1) * share]
    cols = pl.ds(model, 2 * rank)
    stores.append(fetch(part_out.at[:, :, cols], part_out_far.at[:, :, cols], loads.at[42]))
    stores += [finish(j) for j in range(model // 512)]
    scatter_end(rest, rest_sum, wide_bufs, first_w, second_w)
    for cp in one + two:
        cp.wait_send()
    for cp in stores:
        cp.wait()


def back_exchange(scale, *args):
    resid, bc, xs, b_in, kv, part, w_sh, rest = (args[k] for k in (2, 4, 5, 11, 24, 25, 27, 28))
    rows, width = xs.shape
    heads = width // MHEAD
    half = rows // 2
    cols = 2 * HD
    _, share, wide = part.shape
    model = resid.shape[1]
    rank = b_in.shape[0]
    return call(
        functools.partial(back_kernel, scale),
        [
            (part.shape, BF),
            ((8, share, model + 2 * rank), BF),
            ((8, rows, w_sh.shape[1] // 8), BF),
            ((rows, 2 * width + HD + 128), BF),
            ((8, 128), F32),
            ((rows, rank), BF),
            (rest.shape[2:], F32),
        ],
        list(args),
        [
            pltpu.VMEM(args[18].shape, args[18].dtype),
            pltpu.VMEM(args[20].shape, args[20].dtype),
            pltpu.VMEM(args[22].shape, args[22].dtype),
            pltpu.VMEM(args[23].shape, args[23].dtype),
            pltpu.VMEM(args[6].shape, args[6].dtype),
            pltpu.VMEM(args[16].shape, args[16].dtype),
            pltpu.VMEM(args[14].shape, args[14].dtype),
            DMA((7,)),
            pltpu.VMEM(args[2].shape, args[2].dtype),
            pltpu.VMEM(args[3].shape, args[3].dtype),
            pltpu.VMEM(args[5].shape, args[5].dtype),
            pltpu.VMEM(args[7].shape, args[7].dtype),
            pltpu.VMEM(args[8].shape, args[8].dtype),
            pltpu.VMEM(args[10].shape, args[10].dtype),
            pltpu.VMEM(args[11].shape, args[11].dtype),
            pltpu.VMEM(args[12].shape, args[12].dtype),
            pltpu.VMEM(args[13].shape, args[13].dtype),
            DMA((9,)),
            pltpu.VMEM(part.shape, BF),
            pltpu.VMEM((8, share, model + 2 * rank), BF),
            pltpu.VMEM((rows, 2 * width + HD + 128), BF),
            pltpu.VMEM(kv.shape, BF),
            pltpu.VMEM(part.shape, BF),
            pltpu.VMEM(rest.shape, BF),
            pltpu.VMEM(kv.shape, BF),
            pltpu.VMEM((rows, HD), BF),
            pltpu.VMEM((rows, width), F32),
            pltpu.VMEM((rows, width), BF),
            pltpu.VMEM((rows, width), BF),
            pltpu.VMEM((16, 16, width + 128), BF),
            pltpu.VMEM((16, 16, width + 128), BF),
            pltpu.VMEM((16, 16, width), BF),
            pltpu.VMEM((16, 16, width), BF),
            pltpu.VMEM((4, 4, half, cols), BF),
            pltpu.VMEM((half, cols), F32),
            pltpu.VMEM((rows, cols), F32),
            pltpu.VMEM((rows, w_sh.shape[1]), BF),
            pltpu.VMEM((128, rows), F32),
            pltpu.VMEM((128, rows), F32),
            pltpu.VMEM((128, rows), F32),
            pltpu.VMEM((rows, 128), F32),
            pltpu.VMEM((heads, rows, 128), BF),
            pltpu.VMEM((heads, rows, 128), BF),
            pltpu.VMEM((rows, width), F32),
            pltpu.VMEM((rows, STATE), F32),
            pltpu.VMEM((rows, STATE), F32),
            pltpu.VMEM((rows, 128), F32),
            DMA((51,)),
            *pair(15),
            *pair(15),
            *pair(4),
            *scatter_bufs(half, cols),
            *reduce_bufs(share, wide),
            *share_sems(),
            *scatter_bufs(rest.shape[2], 128),
        ],
        5,
        "back_exchange",
        [SM, VM, HB, HB, VM, HB, HB, HB, HB, VM, HB, HB, HB, HB, HB, VM, HB, VM, HB, VM, HB, VM, HB, HB, HB, HB, HB, HB, HB],
        [HB, HB, HB, HB, VM, VM, VM],
    )


def tail_kernel(
    part_far,
    part_two_far,
    gain,
    mask_far,
    gain_two,
    grad_resid_far,
    low_in,
    low_sh,
    grad_low_out,
    grad_low_gu,
    low_out,
    head,
    a_in_far,
    a_sh_far,
    hidden_far,
    normed_far,
    grad_one_far,
    merged_far,
    normed_mine_far,
    mixer_mine_far,
    grad_mine_far,
    rows_far,
    gathered_far,
    big_out,
    small_out,
    shared,
    head_out,
    part,
    part_two,
    a_in,
    a_sh,
    mask,
    grad_resid,
    far,
    gathered,
    source,
    normed_one,
    grad_one,
    merged,
    normed_mine,
    mixer_mine,
    grad_mine,
    low_dn,
    lows,
    turned,
    mine,
    big,
    small,
    two,
    two_t,
    picks,
    heads,
    loads,
    *scratch,
):
    place = ctx_place()
    tp_at = tp_place()
    ctx, tp = place[:2]
    peers = ctx_peers(ctx, tp) + all_tp(*tp_at)
    greet(peers)
    share, width = source.shape
    rank = a_in.shape[1]
    rows = normed_one.shape[0]
    rows_mine = pl.ds(pl.multiple_of(tp * share, share), share)
    get = [
        fetch(src, dst, loads.at[k])
        for k, (src, dst) in enumerate(
            (
                (grad_one_far, grad_one),
                (normed_far, normed_one),
                (merged_far, merged),
                (normed_mine_far, normed_mine),
                (mixer_mine_far, mixer_mine),
                (grad_mine_far, grad_mine),
                (rows_far.at[:, :, pl.ds(width, rank)], low_dn),
                (hidden_far.at[rows_mine], source),
            )
        )
    ]
    bring = [
        fetch(src, dst, far.at[k])
        for k, (src, dst) in enumerate(
            (
                (part_far, part),
                (part_two_far, part_two),
                (a_in_far, a_in),
                (a_sh_far, a_sh),
                (mask_far, mask),
                (grad_resid_far, grad_resid),
            )
        )
    ]
    bufs_z, more_z, sems, sems_l = scratch[:7], scratch[7:14], scratch[14:18], scratch[18:20]
    bufs, more, s_head, sems_s = scratch[20:28], scratch[28:36], scratch[36:38], scratch[38:]
    get[0].wait()
    turned[...] = grad_one[...].T
    deep = grad_one.shape[1]
    get[1].wait()

    def weights(j, carry):
        split_out(big, 0, dot(turned[...], normed_one[:, lanes(j, 256)]), 2 * j)
        return carry

    lax.fori_loop(0, 8, weights, 0)
    eights(big, deep, dot_tn(low_in[...], grad_one[...]))
    for k in range(2, 8):
        get[k].wait()
    row = deep + 64
    a_out_sum = dot_tn(merged[...], grad_low_out[...])
    for j in range(16):
        big[j // 4, j % 4, row : row + 32] = a_out_sum[j * 32 : (j + 1) * 32].astype(BF)
    for k, full in enumerate(
        (
            dot_tn(normed_mine[...], grad_low_gu[...]),
            dot_tn(mixer_mine[...], low_out[...]),
            dot_tn(grad_mine[...], low_dn[...].reshape(rows, rank)),
        )
    ):
        at = row + 32 + 16 * k
        big[:, :, at : at + 16] = full.astype(BF).reshape(4, 4, 16, rank)
    for cp in bring:
        cp.wait()
    met(peers)
    first_z = reduce_start(part, bufs_z, tp_at)
    first_two = reduce_start(part_two, more_z, tp_at)
    first = scatter_start(big, bufs, place)
    second_z = reduce_middle(part, bufs_z, tp_at, first_z)
    second_two = reduce_middle(part_two, more_z, tp_at, first_two)
    picks[...] = chooser(tp)
    half = width // 2
    for k in range(2):
        cols = slice(half * k, half * (k + 1))
        mine[:, 128 * k : 128 * (k + 1)] = dot(normed_one[:, cols], picks[...]).astype(BF)
    reduce_relay(part, bufs_z, tp_at, first_z, second_z)
    reduce_relay(part_two, more_z, tp_at, first_two, second_two)
    scatter_relay(big, bufs, place, first)
    total = reduce_end(part, bufs_z, tp_at, first_z, second_z)
    mask_mine = mask[rows_mine]
    low_one = (total[:, width : width + rank] * mask_mine).astype(BF)
    low_two = (total[:, width + rank :] * mask_mine).astype(BF)
    lows[tp, :, :rank] = low_one
    lows[tp, :, rank:] = low_two
    started_l = share_direct(lows, sems_l, tp_at)
    grad = total[:, :width] + dot_nt(low_one, a_in[...]) + dot_nt(low_two, a_sh[...])
    grad_v, grad_gain = norm_back(source[...].astype(F32), gain[0:1], grad)
    gathered[tp] = (grad_resid[...] + grad_v).astype(BF)
    started = share_start(gathered, sems, tp_at)
    two[...] = reduce_end(part_two, more_z, tp_at, first_two, second_two).astype(BF)
    b_sh_sum = dot_tn(low_sh[...], two[...])
    two_t[...] = two[...].T

    def shared_maps(j, carry):
        split_out(small, 0, dot(two_t[...], normed_one[:, lanes(j, 512)]), 4 * j)
        return carry

    lax.fori_loop(0, 4, shared_maps, 0)
    gain_rows = jnp.concatenate([grad_gain, gain_two[...], jnp.zeros((6, width), F32)], axis=0)
    for j in range(16):
        small[j // 4, j % 4, 144:160] = jnp.concatenate(
            [b_sh_sum[8 * j : 8 * j + 8], gain_rows[:, 128 * j : 128 * (j + 1)]], axis=0
        ).astype(BF)
    for cp in started_l:
        cp.wait_recv()
    full = dot_tn(mine[...], lows[...].reshape(rows, 2 * rank)).astype(BF)
    small[:, :, 160:176] = full[:, :rank].reshape(4, 4, 16, rank)
    small[:, :, 128:144] = full[:, rank:].reshape(4, 4, 16, rank)
    first_s = scatter_direct(small, more, place)
    sent = [send(head, heads.at[ctx], s_head, d - 1, ((ctx + d) % 16, tp)) for d in range(1, 16)]
    heads[ctx] = head[...]
    passed = [share_pass(gathered, sems, tp_at, started, k) for k in (0, 1)]
    second_s = scatter_middle(small, small_out, more, place, first_s)
    second = scatter_middle(big, big_out, bufs, place, first)
    passed.append(share_pass(gathered, sems, tp_at, started, 2))
    scatter_end(small, small_out, more, first_s, second_s)
    shared[tp] = small_out[pl.ds(0, shared.shape[1])].astype(BF)
    started_s = share_direct(shared, sems_s, tp_at)
    share_end(gathered, sems, tp_at, started, passed)
    store = fetch(gathered, gathered_far, loads.at[8])
    scatter_end(big, big_out, bufs, first, second)
    for cp in sent:
        cp.wait_recv()
    head_out[...] = jnp.sum(heads[...], axis=0)
    for cp in started_s:
        cp.wait_recv()
    for cp in sent + started_l + started_s:
        cp.wait_send()
    store.wait()


def tail_exchange(*args):
    part, part_two, grad_resid, head, grad_one, merged, rows_in = (
        args[k] for k in (0, 1, 5, 11, 16, 17, 21)
    )
    _, share, wide = part.shape
    _, rows, cols = part_two.shape
    width = grad_resid.shape[1]
    rank = (wide - width) // 2
    deep = grad_one.shape[1]
    return call(
        tail_kernel,
        [
            ((8, share, width), BF),
            ((deep + 144, 128), F32),
            ((176, 128), F32),
            ((8, 160, 128), BF),
            (head.shape, F32),
        ],
        list(args),
        [
            pltpu.VMEM(args[0].shape, args[0].dtype),
            pltpu.VMEM(args[1].shape, args[1].dtype),
            pltpu.VMEM(args[12].shape, args[12].dtype),
            pltpu.VMEM(args[13].shape, args[13].dtype),
            pltpu.VMEM(args[3].shape, args[3].dtype),
            pltpu.VMEM(args[5].shape, args[5].dtype),
            DMA((6,)),
            pltpu.VMEM((8, share, width), BF),
            pltpu.VMEM((share, width), BF),
            pltpu.VMEM((rows, width), BF),
            pltpu.VMEM(grad_one.shape, BF),
            pltpu.VMEM(merged.shape, BF),
            pltpu.VMEM((rows, 256), BF),
            pltpu.VMEM((rows, 256), BF),
            pltpu.VMEM((rows, 256), BF),
            pltpu.VMEM((8, share, rank), BF),
            pltpu.VMEM((8, share, 2 * rank), BF),
            pltpu.VMEM((deep, rows), BF),
            pltpu.VMEM((rows, 256), BF),
            pltpu.VMEM((4, 4, deep + 144, 128), BF),
            pltpu.VMEM((4, 4, 176, 128), BF),
            pltpu.VMEM((rows, 128), BF),
            pltpu.VMEM((128, rows), BF),
            pltpu.VMEM((1024, 128), BF),
            pltpu.VMEM((16,) + head.shape, F32),
            DMA((9,)),
            *reduce_bufs(share, wide),
            *reduce_bufs(rows, cols),
            *share_sems(),
            *pair(7),
            *scatter_bufs(deep + 144, 128),
            *scatter_bufs(176, 128),
            *pair(15),
            *pair(7),
        ],
        6,
        "tail_exchange",
        [HB, HB, VM, HB, VM, HB, VM, VM, VM, VM, VM, VM, HB, HB, HB, HB, HB, HB, HB, HB, HB, HB],
        [HB] + [VM] * 4,
    )


def finish_kernel(
    mixed_in,
    input_in,
    big,
    small,
    shared,
    head,
    early,
    rest_in,
    mixed,
    input_grad,
    gains,
    w_in,
    w_sh,
    w_dt,
    params,
    w_out,
    w_gu,
    w_down,
    a_in,
    b_in,
    a_sh,
    b_sh,
    a_out,
    b_out,
    a_gu,
    b_gu,
    a_dn,
    b_dn,
):
    width = mixed.shape[1]
    mixed[...] = mixed_in[0, :, :width].astype(F32)
    input_grad[...] = input_in[0, :, :width].astype(F32)

    @pl.when(pl.program_id(0) == 0)
    def rest():
        narrow = w_in.shape[2]
        hidden = w_down.shape[0]
        heads = w_dt.shape[0]
        w_in[:, 0, :] = big[0:narrow].T
        w_dt[...] = big[narrow : narrow + heads]
        deep = narrow + 128
        for k in range(narrow // 128):
            cols = slice(128 * k, 128 * (k + 1))
            b_in[:, 0, cols] = big[deep + 8 * k : deep + 8 * (k + 1)]
        params[...] = head[0:3, 0:heads]
        total = jnp.zeros((8, 128), F32)
        for k in range(8):
            block = shared[k].astype(F32)
            cols = slice(128 * k, 128 * (k + 1))
            w_sh[:, cols] = block[0:128].T
            a_sh[16 * k : 16 * (k + 1)] = block[128:144]
            b_sh[:, cols] = block[144:152]
            total = total + block[152:160]
        gains[...] = total[0:2]
        maps = deep + 64
        a_out[0] = big[maps : maps + 32]
        a_gu[...] = big[maps + 32 : maps + 48]
        b_out[...] = big[maps + 48 : maps + 64]
        b_dn[...] = big[maps + 64 : maps + 80]
        a_in[...] = small[160:176]
        w_gu[:, 0, :] = early[0:hidden].T
        w_gu[:, 1, :] = early[hidden : 2 * hidden].T
        w_down[...] = rest_in[0:hidden]
        w_out[0] = rest_in[hidden : 2 * hidden]
        for k in range(hidden // 128):
            cols = slice(128 * k, 128 * (k + 1))
            row = 2 * hidden + 8 * k
            b_gu[:, 0, cols] = early[row : row + 8]
            b_gu[:, 1, cols] = early[row + 32 : row + 40]
            a_dn[:, cols] = rest_in[row : row + 8]


def finish(mixed, input_grad, big, small, shared, head, early, rest, narrow, heads):
    _, rows, wide = mixed.shape
    _, _, wide_two = input_grad.shape
    width = wide - 128
    hidden = early.shape[0] // 2 // 128 * 128
    outs = [
        (8 * rows, width),
        (8 * rows, width),
        (2, 128),
        (128, 1, narrow),
        (128, 1024),
        (heads, 128),
        (3, heads),
        (1, hidden, 128),
        (128, 2, hidden),
        (hidden, 128),
        (16, 128),
        (8, 1, narrow),
        (128, 128),
        (8, 1024),
        (1, 32, 128),
        (16, 128),
        (16, 128),
        (8, 2, hidden),
        (8, hidden),
        (16, 128),
    ]

    def whole(shape):
        return pl.BlockSpec(shape, lambda i: (0,) * len(shape))

    done = pl.pallas_call(
        finish_kernel,
        grid=(8,),
        out_shape=[jax.ShapeDtypeStruct(s, F32) for s in outs],
        in_specs=[
            pl.BlockSpec((1, rows, wide), lambda i: (i, 0, 0)),
            pl.BlockSpec((1, rows, wide_two), lambda i: (i, 0, 0)),
        ]
        + [whole(a.shape) for a in (big, small, shared, head, early, rest)],
        out_specs=[pl.BlockSpec((rows, width), lambda i: (i, 0))] * 2 + [whole(s) for s in outs[2:]],
        compiler_params=pltpu.CompilerParams(vmem_limit_bytes=61 << 20),
        name="finish",
    )(mixed, input_grad, big, small, shared, head, early, rest)
    return tuple(a.T if k in (5, 15, 18, 19) else a for k, a in enumerate(done))


def body(
    hidden_in,
    norm_gains,
    w_in,
    w_shared,
    w_dt,
    head_params,
    w_out,
    w_gu,
    w_down,
    a_in,
    b_in,
    a_sh,
    b_sh,
    a_out,
    b_out,
    a_gu,
    b_gu,
    a_dn,
    b_dn,
    adapter_ids,
    doc_lengths,
    out_grad,
):
    rows, width = hidden_in.shape
    heads = head_params.shape[1]
    w_in = w_in.reshape(width, -1)
    b_in = b_in.reshape(b_in.shape[0], -1)
    w_out = w_out.reshape(-1, width)
    a_out = a_out.reshape(-1, a_out.shape[2])
    w_gu = w_gu.reshape(width, -1)
    b_gu = b_gu.reshape(b_gu.shape[0], -1)
    w_dt = jnp.pad(w_dt.T, ((0, 128 - heads), (0, 0)))
    scale = HD ** (-0.5)
    (
        normed_one,
        low_in,
        low_sh,
        z,
        xs,
        q,
        bc,
        mask,
        decay,
        dt,
        pre,
        total,
        entering,
        ssd,
        kv_all,
        mix_part,
        attn_t,
        lse,
        merged,
        params,
    ) = front_exchange(
        scale,
        doc_lengths,
        adapter_ids,
        hidden_in,
        norm_gains,
        w_dt,
        b_in,
        b_sh,
        head_params,
        a_out,
        a_in,
        a_sh,
        w_in,
        w_shared,
        w_out,
    )
    (
        low_out,
        grad_mixer,
        grad_low_gu,
        resid,
        grad_resid,
        gain_part_two,
        early,
        rest,
        mlp_part,
        normed_mine,
        grad_mine,
        mixer_mine,
    ) = mlp_exchange(
        mix_part,
        norm_gains,
        b_out,
        a_gu,
        b_gu,
        a_dn,
        b_dn,
        mask,
        merged,
        hidden_in,
        w_gu,
        w_down,
        out_grad,
    )
    mixed, part, two_blocks, grad_one, grad_head, grad_low_out, rest = back_exchange(
        scale,
        doc_lengths,
        total,
        resid,
        b_dn,
        bc,
        xs,
        decay,
        dt,
        pre,
        params,
        entering,
        b_in,
        b_sh,
        w_dt,
        q,
        lse,
        attn_t,
        grad_mixer,
        w_out,
        b_out,
        a_out,
        mask,
        z,
        ssd,
        kv_all,
        mlp_part,
        w_in,
        w_shared,
        rest,
    )
    input_grad, big, small, shared, head = tail_exchange(
        part,
        two_blocks,
        norm_gains,
        mask,
        gain_part_two,
        grad_resid,
        low_in,
        low_sh,
        grad_low_out,
        grad_low_gu,
        low_out,
        grad_head,
        a_in,
        a_sh,
        hidden_in,
        normed_one,
        grad_one,
        merged,
        normed_mine,
        mixer_mine,
        grad_mine,
        mixed,
    )
    return finish(mixed, input_grad, big, small, shared, head, early, rest, w_in.shape[1], heads)


def solution(mesh):
    placed = (
        P("ctx", None),
        P(),
        P(None, "tp", None),
        P(),
        P(None, "tp"),
        P(None, "tp"),
        P("tp", None, None),
        P(None, None, "tp"),
        P("tp", None),
        P(),
        P(None, "tp", None),
        P(),
        P(),
        P("tp", None, None),
        P(),
        P(),
        P(None, None, "tp"),
        P("tp", None),
        P(),
        P(),
        P(),
        P("ctx", None),
    )
    return jax.shard_map(
        body,
        mesh=mesh,
        in_specs=placed,
        out_specs=(
            P("ctx", None),
            P("ctx", None),
            P(None, "ctx"),
            P("ctx", "tp", None),
            P("ctx", None),
            P("ctx", "tp"),
            P(None, "tp"),
            P("tp", None, "ctx"),
            P("ctx", None, "tp"),
            P("tp", "ctx"),
            P(("ctx", "tp"), None),
            P("ctx", "tp", None),
            P("ctx", None),
            P("ctx", None),
            P("tp", "ctx", None),
            P(None, ("ctx", "tp")),
            P(("ctx", "tp"), None),
            P("ctx", None, "tp"),
            P("tp", "ctx"),
            P(None, ("ctx", "tp")),
        ),
        check_vma=False,
    )
```
